32 devices in a mesh: seq: 4 (over z), ctx: 8 (over y, x, core).
Axes of the slice: x: 2, y: 2, z: 4, core: 2. Of those that a mesh axis runs over, the one named last changes fastest.
Arguments:
- tokens: bfloat16 [6144, 2048], P(('seq', 'ctx')), may hold values from -6 to 6
- block_ids: int32 [4, 16], P('seq'), may hold values from 0 to 15, as said below
- cotangent: bfloat16 [6144, 2048], P(('seq', 'ctx')), may hold values from -6 to 6
- norm1_gain: bfloat16 [2048], P('seq'), may hold values from 0.25 to 1.75
- norm1_bias: bfloat16 [2048], P('seq'), may hold values from -3 to 3
- norm2_gain: bfloat16 [2048], P('seq'), may hold values from 0.25 to 1.75
- norm2_bias: bfloat16 [2048], P('seq'), may hold values from -3 to 3
- w_qkv: bfloat16 [2048, 6144], P('seq'), may hold values from -0.125 to 0.125
- b_qkv: bfloat16 [6144], P('seq'), may hold values from -3 to 3
- w_dense: bfloat16 [2048, 2048], P('seq'), may hold values from -1 to 1
- b_dense: bfloat16 [2048], P('seq'), may hold values from -3 to 3
- w_in: bfloat16 [2048, 8192], P('seq'), may hold values from -0.125 to 0.125
- b_in: bfloat16 [8192], P('seq'), may hold values from -3 to 3
- w_out: bfloat16 [8192, 2048], P('seq'), may hold values from -0.0625 to 0.0625
- b_out: bfloat16 [2048], P('seq'), may hold values from -3 to 3
Outputs:
- output: bfloat16 [6144, 2048], P(('seq', 'ctx'))
- grad_tokens: bfloat16 [6144, 2048], P(('seq', 'ctx'))
- grad_norm1_gain: float32 [2048], P('seq')
- grad_norm1_bias: float32 [2048], P('seq')
- grad_norm2_gain: float32 [2048], P('seq')
- grad_norm2_bias: float32 [2048], P('seq')
- grad_w_qkv: float32 [2048, 6144], P('seq')
- grad_b_qkv: float32 [6144], P('seq')
- grad_w_dense: float32 [2048, 2048], P('seq')
- grad_b_dense: float32 [2048], P('seq')
- grad_w_in: float32 [2048, 8192], P('seq')
- grad_b_in: float32 [8192], P('seq')
- grad_w_out: float32 [8192, 2048], P('seq')
- grad_b_out: float32 [2048], P('seq')
The draws below stay inside these ranges and needn't reach their ends.
Inputs may be any that keep to these rules, and one draw needn't show every extreme that they name: In each row of block_ids (one sequence), the slots 2 * j and 2 * j + 1 hold two blocks whose numbers sum to 15, and every block number appears once in the row.
All inputs are finite; a program needn't handle non-finite values.
Results may differ from the reference program's by a relative error of at most 0.011.
Values may be sent and summed in bfloat16 or wider, within the bound.
A program may use at most 408 MiB of HBM per device.

```python
import math
import jax
import jax.numpy as jnp
from jax import lax

D = 2048
H = 8
HD = 256
ROT = 64
FF = 8192
BLOCK = 96
BLOCKS = 16
LEN = 1536
SEQS = 4
TOKENS = 6144


def draw_block_ids(key, part):
    half_count = BLOCKS // 2
    seq_keys = jax.random.split(key, SEQS)

    def one_sequence(seq_key):
        key_order, key_flip = jax.random.split(seq_key)
        lower_ids = jax.random.permutation(key_order, half_count).astype(jnp.int32)
        upper_ids = (BLOCKS - 1 - lower_ids).astype(jnp.int32)
        flipped = jax.random.randint(key_flip, (half_count,), 0, 2)
        first_slot = jnp.where(flipped == 1, upper_ids, lower_ids)
        second_slot = jnp.where(flipped == 1, lower_ids, upper_ids)
        return jnp.stack([first_slot, second_slot], axis=1).reshape(BLOCKS)
    return jax.vmap(one_sequence)(seq_keys).astype(jnp.int32)


def level_of(own_key, shape, cuts, low, top_value):
    gain, own = 1.0, jax.random.fold_in(own_key, 6)
    for position, parts in cuts:
        heights = jnp.exp(jax.random.uniform(jax.random.fold_in(own, position), (parts,), jnp.float32, low / len(cuts), top_value / len(cuts)))
        gain = gain * jnp.repeat(heights, shape[position] // parts).reshape([-1 if axis == position else 1 for axis in range(len(shape))])
    return gain


def noise(rng, extent, width, reach, cuts=(), held_as=jnp.bfloat16):
    values = jax.random.normal(rng, extent, jnp.float32) * width
    if len(cuts) > 0:
        values = level_of(rng, extent, cuts, -0.22, 0.18) * values
    return jnp.clip(values, min=-reach, max=reach).astype(held_as)


def setup_inputs(seed: int = 0) -> dict:
    splits = jax.random.split(jax.random.key(seed), 16)
    tokens = noise(splits[0], (TOKENS, D), 1.0, 6.0, ((0, 32),))
    block_ids = draw_block_ids(jax.random.fold_in(splits[15], 71), 0)
    cotangent = noise(splits[2], (TOKENS, D), 1.0, 6.0, ((0, 32),))
    norm1_gain = jnp.clip(1.0 + 0.15 * jax.random.normal(splits[3], (D,), jnp.float32), 0.25, 1.75).astype(jnp.bfloat16)
    norm1_bias = noise(splits[4], (D,), 0.5, 3.0, ((0, 4),))
    norm2_gain = jnp.clip(1.0 + 0.15 * jax.random.normal(splits[5], (D,), jnp.float32), 0.25, 1.75).astype(jnp.bfloat16)
    norm2_bias = noise(splits[6], (D,), 0.5, 3.0, ((0, 4),))
    w_qkv = noise(splits[7], (D, 3 * D), D ** -0.5, 0.125, ((0, 4),))
    b_qkv = noise(splits[8], (3 * D,), 0.5, 3.0, ((0, 4),))
    w_dense = noise(splits[9], (D, D), (D // 64) ** -0.5, 1.0, ((0, 4),))
    b_dense = noise(splits[10], (D,), 0.5, 3.0, ((0, 4),))
    w_in = noise(splits[11], (D, FF), D ** -0.5, 0.125, ((0, 4),))
    b_in = noise(splits[12], (FF,), 0.5, 3.0, ((0, 4),))
    w_out = noise(splits[13], (FF, D), FF ** -0.5, 0.0625, ((0, 4),))
    b_out = noise(splits[14], (D,), 0.5, 3.0, ((0, 4),))
    return dict(tokens=tokens, block_ids=block_ids, cotangent=cotangent, norm1_gain=norm1_gain, norm1_bias=norm1_bias, norm2_gain=norm2_gain, norm2_bias=norm2_bias, w_qkv=w_qkv, b_qkv=b_qkv, w_dense=w_dense, b_dense=b_dense, w_in=w_in, b_in=b_in, w_out=w_out, b_out=b_out)


HIGHEST = lax.Precision.HIGHEST
EPSILON = 1e-05
ROT_BASE = 10000.0

@jax.custom_vjp
def low(v):
    return lax.optimization_barrier(v.astype(jnp.bfloat16)).astype(jnp.float32)

@jax.custom_vjp
def low_back(v):
    return v

def low_keep(v):
    return (low(v), None)

def low_pass(kept, grad):
    return (grad,)

def back_keep(v):
    return (v, None)

def back_low(kept, grad):
    return (low(grad),)
low.defvjp(low_keep, low_pass)
low_back.defvjp(back_keep, back_low)

def layer_norm(values, norm_gain, offset):
    center = values - lax.optimization_barrier(jnp.mean(values, axis=-1, keepdims=True))
    spread = lax.optimization_barrier(jnp.mean(center * center, axis=-1, keepdims=True))
    return center * lax.rsqrt(spread + EPSILON) * norm_gain + offset

def rotate(vectors, positions, rot_dims):
    half_rot = rot_dims // 2
    inverse_freq = jnp.power(ROT_BASE, -(jnp.arange(half_rot, dtype=jnp.float32) * 2.0) / rot_dims)
    angles = positions.astype(jnp.float32)[:, None] * inverse_freq[None, :]
    cosine = jnp.cos(angles)[:, None, :]
    sine_part = jnp.sin(angles)[:, None, :]
    first_half = vectors[..., :half_rot]
    second = vectors[..., half_rot:rot_dims]
    return jnp.concatenate([first_half * cosine - second * sine_part, second * cosine + first_half * sine_part, vectors[..., rot_dims:]], axis=-1)

def attend_sequence(group):
    queries, keys_all, values_all, positions = group
    query_block = math.gcd(LEN, 512)
    block_count = LEN // query_block
    query_blocks = queries.reshape(block_count, query_block, H, HD)
    position_blocks = positions.reshape(block_count, query_block)
    scale_attn = HD ** (-0.5)

    def one_block(pair):
        query_part, query_pos = pair
        scores = jnp.einsum('qhd,khd->hqk', query_part, keys_all, precision=HIGHEST) * scale_attn
        scores = low_back(scores)
        allowed = (query_pos[:, None] >= positions[None, :])[None]
        scores = jnp.where(allowed, scores, -1e+30)
        row_max = lax.optimization_barrier(jnp.max(scores, axis=-1, keepdims=True))
        exponent = jnp.where(allowed, jnp.exp(scores - row_max), 0.0)
        probabilities = low(exponent / lax.optimization_barrier(jnp.sum(exponent, axis=-1, keepdims=True)))
        return jnp.einsum('hqk,khd->qhd', probabilities, values_all, precision=HIGHEST)
    attended = lax.map(jax.checkpoint(one_block), (query_blocks, position_blocks))
    return attended.reshape(LEN, H * HD)

def forward(inputs, params, positions):
    norm1_gain, norm1_bias, norm2_gain, norm2_bias, w_qkv, b_qkv, w_dense, b_dense, w_in, b_in, w_out, b_out = params
    model_width = H * HD
    flat_pos = positions.reshape(TOKENS)
    normed1 = low(layer_norm(inputs, norm1_gain, norm1_bias))
    normed2 = low(layer_norm(inputs, norm2_gain, norm2_bias))
    project = low_back(jnp.dot(normed1, w_qkv, precision=HIGHEST) + b_qkv)
    queries = low(rotate(project[:, :model_width].reshape(TOKENS, H, HD), flat_pos, ROT))
    keys_all = low(rotate(project[:, model_width:2 * model_width].reshape(TOKENS, H, HD), flat_pos, ROT))
    values_all = low(project[:, 2 * model_width:].reshape(TOKENS, H, HD))
    attended = lax.map(attend_sequence, (queries.reshape(SEQS, LEN, H, HD), keys_all.reshape(SEQS, LEN, H, HD), values_all.reshape(SEQS, LEN, H, HD), positions))
    mixed = low(low_back(attended.reshape(TOKENS, model_width)))
    attn_out = jnp.dot(mixed, w_dense, precision=HIGHEST) + b_dense
    hidden = low_back(jnp.dot(normed2, w_in, precision=HIGHEST) + b_in)
    active = low(jax.nn.gelu(hidden, approximate=False))
    mlp_out = jnp.dot(active, w_out, precision=HIGHEST) + b_out
    return inputs + attn_out + mlp_out

def reference(tokens, block_ids, cotangent, norm1_gain, norm1_bias, norm2_gain, norm2_bias, w_qkv, b_qkv, w_dense, b_dense, w_in, b_in, w_out, b_out):
    offsets = jnp.tile(jnp.arange(BLOCK, dtype=jnp.int32), BLOCKS)[None, :]
    positions = (jnp.repeat(block_ids, BLOCK, axis=1) * BLOCK + offsets).astype(jnp.int32)
    params = tuple((member.astype(jnp.float32) for member in (norm1_gain, norm1_bias, norm2_gain, norm2_bias, w_qkv, b_qkv, w_dense, b_dense, w_in, b_in, w_out, b_out)))
    inputs = tokens.astype(jnp.float32)

    def apply_layer(layer_in, layer_params):
        return forward(layer_in, layer_params, positions)
    result, backward = jax.vjp(apply_layer, inputs, params)
    grad_inputs, grad_params = backward(cotangent.astype(jnp.float32))
    grad_norm1_gain, grad_norm1_bias, grad_norm2_gain, grad_norm2_bias, grad_w_qkv, grad_b_qkv, grad_w_dense, grad_b_dense, grad_w_in, grad_b_in, grad_w_out, grad_b_out = grad_params
    return (result.astype(jnp.bfloat16), grad_inputs.astype(jnp.bfloat16), grad_norm1_gain, grad_norm1_bias, grad_norm2_gain, grad_norm2_bias, grad_w_qkv, grad_b_qkv, grad_w_dense, grad_b_dense, grad_w_in, grad_b_in, grad_w_out, grad_b_out)
```

```python
import functools

import jax
import jax.numpy as jnp
from jax import lax
from jax.experimental import pallas as pl
from jax.experimental.pallas import tpu as pltpu
from jax.sharding import Mesh, PartitionSpec as P

H = 8
HD = 256
ROT = 64
BLOCK = 96
EPSILON = 1e-05
ROT_BASE = 10000.0
SCALE = HD ** (-0.5)

f32 = jnp.float32
bf16 = jnp.bfloat16
TP = ("seq", "core")


def angles_of(positions):
    half = ROT // 2
    inverse_freq = jnp.power(ROT_BASE, -(jnp.arange(half, dtype=f32) * 2.0) / ROT)
    angles = positions.astype(f32)[:, None] * inverse_freq[None, :]
    return jnp.cos(angles), jnp.sin(angles)


def rotate(u, cosine, sine):
    half = ROT // 2
    a, b = u[..., :half], u[..., half:ROT]
    return jnp.concatenate([a * cosine - b * sine, b * cosine + a * sine, u[..., ROT:]], axis=-1)


def attention_forward(q, k, v, row_pos, col_pos, tile):
    rows = q.shape[0]

    def kernel(q_ref, k_ref, v_ref, rp_ref, cp_ref, o_ref, lse_ref):
        s = lax.dot_general(
            q_ref[...], k_ref[...], (((1,), (1,)), ((), ())), preferred_element_type=f32
        ) * SCALE
        allowed = rp_ref[...] >= cp_ref[...]
        s = jnp.where(allowed, s, -1e30)
        top = jnp.max(s, axis=-1, keepdims=True)
        e = jnp.exp(s - top)
        total = jnp.sum(e, axis=-1, keepdims=True)
        p = (e / total).astype(bf16)
        o_ref[...] = jnp.dot(p, v_ref[...], preferred_element_type=f32).astype(bf16)
        lse_ref[...] = top + jnp.log(total)

    whole = pl.BlockSpec((rows, HD), lambda i: (0, 0))
    part = pl.BlockSpec((tile, HD), lambda i: (i, 0))
    one = pl.BlockSpec((tile, 1), lambda i: (i, 0))
    return pl.pallas_call(
        kernel,
        grid=(rows // tile,),
        in_specs=[part, whole, whole, one, pl.BlockSpec((1, rows), lambda i: (0, 0))],
        out_specs=[part, one],
        out_shape=[
            jax.ShapeDtypeStruct((rows, HD), bf16),
            jax.ShapeDtypeStruct((rows, 1), f32),
        ],
        compiler_params=pltpu.CompilerParams(vmem_limit_bytes=56 * 2**20),
        cost_estimate=pl.CostEstimate(
            flops=4 * rows * rows * HD, bytes_accessed=8 * rows * HD, transcendentals=rows * rows
        ),
        name="attention_forward",
    )(q, k, v, row_pos, col_pos)


def attention_backward(q, k, v, g, lse, row_pos, col_pos, tile):
    rows = q.shape[0]

    def kernel(q_ref, k_ref, v_ref, g_ref, lse_ref, rp_ref, cp_ref, dq_ref, dk_ref, dv_ref):
        nt = (((1,), (1,)), ((), ()))
        tn = (((0,), (0,)), ((), ()))

        @pl.when(pl.program_id(0) == 0)
        def _():
            dk_ref[...] = jnp.zeros_like(dk_ref)
            dv_ref[...] = jnp.zeros_like(dv_ref)

        s = lax.dot_general(q_ref[...], k_ref[...], nt, preferred_element_type=f32) * SCALE
        allowed = rp_ref[...] >= cp_ref[...]
        p = jnp.where(allowed, jnp.exp(s - lse_ref[...]), 0.0)
        dp = lax.dot_general(g_ref[...], v_ref[...], nt, preferred_element_type=f32)
        shift = jnp.sum(p * dp, axis=-1, keepdims=True)
        ds = (p * (dp - shift)).astype(bf16)
        dq_ref[...] = jnp.dot(ds, k_ref[...], preferred_element_type=f32) * SCALE
        dk_ref[...] += lax.dot_general(ds, q_ref[...], tn, preferred_element_type=f32) * SCALE
        dv_ref[...] += lax.dot_general(p.astype(bf16), g_ref[...], tn, preferred_element_type=f32)

    whole = pl.BlockSpec((rows, HD), lambda i: (0, 0))
    part = pl.BlockSpec((tile, HD), lambda i: (i, 0))
    one = pl.BlockSpec((tile, 1), lambda i: (i, 0))
    return pl.pallas_call(
        kernel,
        grid=(rows // tile,),
        in_specs=[part, whole, whole, part, one, one, pl.BlockSpec((1, rows), lambda i: (0, 0))],
        out_specs=[part, whole, whole],
        out_shape=[jax.ShapeDtypeStruct((rows, HD), f32)] * 3,
        compiler_params=pltpu.CompilerParams(vmem_limit_bytes=56 * 2**20),
        cost_estimate=pl.CostEstimate(
            flops=10 * rows * rows * HD, bytes_accessed=20 * rows * HD, transcendentals=rows * rows
        ),
        name="attention_backward",
    )(q, k, v, g, lse, row_pos, col_pos)


def on_device(
    nz,
    nchip,
    ncore,
    tokens,
    block_ids,
    cotangent,
    norm1_gain,
    norm1_bias,
    norm2_gain,
    norm2_bias,
    w_qkv,
    b_qkv,
    w_dense,
    b_dense,
    w_in,
    b_in,
    w_out,
    b_out,
):
    own, width = tokens.shape
    z = lax.axis_index("seq")
    chip = lax.axis_index("chip")
    core = lax.axis_index("core")
    ranks = nz * ncore
    rank = z * ncore + core
    rows = ranks * own
    ff = w_out.shape[0] * nz
    ffr = ff // ranks
    hc = width // ranks
    split = max(1, HD // hc)
    wrows = width // nz
    piece = wrows // nchip // ncore

    small = jnp.concatenate(
        [norm1_gain, norm1_bias, norm2_gain, norm2_bias, b_qkv, b_dense, b_in, b_out,
         block_ids.reshape(-1).astype(bf16)]
    )
    small = lax.all_gather(small, "seq", axis=0, tiled=False)
    d4 = wrows
    f4 = b_in.shape[0]
    q4 = b_qkv.shape[0]
    cuts = [0, d4, 2 * d4, 3 * d4, 4 * d4, 4 * d4 + q4, 5 * d4 + q4, 5 * d4 + q4 + f4,
            6 * d4 + q4 + f4, small.shape[1]]
    gain1, bias1, gain2, bias2, full_bqkv, full_bdense, full_bin, full_bout, ids = [
        small[:, cuts[i] : cuts[i + 1]].reshape(-1) for i in range(9)
    ]
    gain1, bias1, gain2, bias2 = [v.astype(f32) for v in (gain1, bias1, gain2, bias2)]
    ids = ids.reshape(nz, -1).astype(jnp.int32)

    tok = lax.all_gather(tokens, TP, axis=0, tiled=True)
    cot = lax.all_gather(cotangent, TP, axis=0, tiled=True)

    def reshard(w, groups):
        c = w.shape[1] // groups // ranks
        mine = lax.dynamic_slice_in_dim(
            w.reshape(nchip * ncore, piece, groups, nz, ncore * c), chip * ncore + core, 1, 0
        )[0]
        mine = mine.transpose(2, 0, 1, 3)
        got = lax.all_to_all(mine, "seq", 0, 0, tiled=True)
        every = lax.all_gather(got, ("chip", "core"), axis=0, tiled=False)
        every = every.transpose(1, 0, 2, 3, 4).reshape(width, groups, ncore, c)
        return lax.dynamic_index_in_dim(every, core, 2, keepdims=False).reshape(width, groups * c)

    w_in_c = reshard(w_in, 1)
    w_qkv_c = reshard(w_qkv, 3)
    w_out_r = lax.dynamic_slice_in_dim(w_out, core * ffr, ffr, 0)
    w_dense_r = lax.dynamic_slice_in_dim(w_dense, core * hc, hc, 0)

    def layer_stats(x):
        mean = jnp.mean(x, axis=-1, keepdims=True)
        center = x - mean
        spread = jnp.mean(center * center, axis=-1, keepdims=True)
        inv = lax.rsqrt(spread + EPSILON)
        return center * inv, inv

    xhat, unused = layer_stats(tok.astype(f32))
    normed1 = (xhat * gain1 + bias1).astype(bf16)
    normed2 = (xhat * gain2 + bias2).astype(bf16)

    project = jnp.dot(normed1, w_qkv_c, preferred_element_type=f32)
    bias_c = lax.dynamic_slice_in_dim(full_bqkv.reshape(3, ranks, hc), rank, 1, 1)
    project = (project + bias_c.reshape(1, 3 * hc).astype(f32)).reshape(rows, 3, hc)
    blocks = ids.shape[1]
    pos_all = jnp.repeat(ids, BLOCK, axis=1) * BLOCK + jnp.tile(
        jnp.arange(BLOCK, dtype=jnp.int32), blocks
    )
    pos_seq = lax.dynamic_index_in_dim(pos_all, chip, 0, keepdims=False)
    length = pos_seq.shape[0]

    def heads_of(x):
        if split > 1:
            x = lax.all_gather(x, "core", axis=2, tiled=True)
        x = x.reshape(nz, rows // nz, x.shape[1], HD).transpose(0, 2, 1, 3)
        x = lax.all_to_all(x, "chip", 0, 0, tiled=True)
        return x.transpose(1, 0, 2, 3).reshape(x.shape[1], length, HD)

    def heads_back(x):
        g = x.shape[0]
        x = x.reshape(g, nchip, length // nchip, HD).transpose(1, 0, 2, 3)
        x = lax.all_to_all(x, "chip", 0, 0, tiled=True)
        x = x.transpose(0, 2, 1, 3).reshape(rows, g, HD)
        if split > 1:
            x = lax.dynamic_slice_in_dim(x, core * hc, hc, 2)
        return x

    cosine, sine = angles_of(pos_seq)
    if split == 1:
        pos_rows = lax.dynamic_slice_in_dim(pos_all, chip * (rows // nz), rows // nz, 1).reshape(-1)
        cos_r, sin_r = angles_of(pos_rows)
        q = rotate(project[:, 0], cos_r, sin_r).astype(bf16)
        k = rotate(project[:, 1], cos_r, sin_r).astype(bf16)
        v = project[:, 2].astype(bf16)
        q, k, v = heads_of(jnp.stack([q, k, v], axis=1))
    else:
        q, k, v = heads_of(project)
        q = rotate(q, cosine, sine).astype(bf16)
        k = rotate(k, cosine, sine).astype(bf16)
        v = v.astype(bf16)
    row_pos, col_pos = pos_seq[:, None], pos_seq[None, :]
    tile = 256
    attended, lse = attention_forward(q, k, v, row_pos, col_pos, tile)
    mixed = heads_back(attended[None]).reshape(rows, hc)

    hidden = jnp.dot(normed2, w_in_c, preferred_element_type=f32)
    hidden = hidden + lax.dynamic_slice_in_dim(full_bin, rank * ffr, ffr).astype(f32)
    active, gelu_back = jax.vjp(functools.partial(jax.nn.gelu, approximate=False), hidden)
    active = active.astype(bf16)
    part_out = jnp.dot(mixed, w_dense_r, preferred_element_type=f32) + jnp.dot(
        active, w_out_r, preferred_element_type=f32
    )
    summed_out = lax.psum_scatter(part_out.astype(bf16), TP, scatter_dimension=0, tiled=True)
    output = (
        tokens.astype(f32)
        + summed_out.astype(f32)
        + full_bdense.astype(f32)
        + full_bout.astype(f32)
    ).astype(bf16)

    tn = (((0,), (0,)), ((), ()))
    nt = (((1,), (1,)), ((), ()))
    grad_active = lax.dot_general(cot, w_out_r, nt, preferred_element_type=f32)
    grad_hidden32 = gelu_back(grad_active)[0]
    grad_hidden = grad_hidden32.astype(bf16)
    dw_out = lax.dot_general(active, cot, tn, preferred_element_type=f32).astype(bf16)
    dw_in = lax.dot_general(normed2, grad_hidden, tn, preferred_element_type=f32).astype(bf16)
    gn2 = lax.dot_general(grad_hidden, w_in_c, nt, preferred_element_type=f32)

    dw_dense = lax.dot_general(mixed, cot, tn, preferred_element_type=f32).astype(bf16)
    grad_mixed = lax.dot_general(cot, w_dense_r, nt, preferred_element_type=f32).astype(bf16)
    g = heads_of(grad_mixed[:, None])[0]
    dq, dk, dv = attention_backward(q, k, v, g, lse, row_pos, col_pos, tile)
    dq = rotate(dq, cosine, -sine).astype(bf16)
    dk = rotate(dk, cosine, -sine).astype(bf16)
    grad_project = heads_back(jnp.stack([dq, dk, dv.astype(bf16)])).reshape(rows, 3 * hc)
    dw_qkv = lax.dot_general(normed1, grad_project, tn, preferred_element_type=f32).astype(bf16)
    gn1 = lax.dot_general(grad_project, w_qkv_c, nt, preferred_element_type=f32)

    e_part = (gn1 * gain1 + gn2 * gain2).astype(bf16)
    e = lax.psum_scatter(e_part, TP, scatter_dimension=0, tiled=True).astype(f32)
    xhat_own, inv_own = layer_stats(tokens.astype(f32))
    terms = (
        e
        - jnp.mean(e, axis=-1, keepdims=True)
        - xhat_own * jnp.mean(e * xhat_own, axis=-1, keepdims=True)
    ) * inv_own
    grad_tokens = (cotangent.astype(f32) + terms).astype(bf16)

    sum_cot = jnp.sum(cotangent.astype(f32), axis=0)
    mine_bin = jnp.zeros((ranks, ffr), f32)
    mine_bin = lax.dynamic_update_slice_in_dim(
        mine_bin, jnp.sum(grad_hidden.astype(f32), axis=0)[None], rank, 0
    ).reshape(-1)
    mine_bqkv = jnp.zeros((3, ranks, hc), f32)
    mine_bqkv = lax.dynamic_update_slice_in_dim(
        mine_bqkv, jnp.sum(grad_project.astype(f32), axis=0).reshape(3, 1, hc), rank, 1
    ).reshape(-1)
    vectors = [
        jnp.sum(gn1 * xhat, axis=0),
        jnp.sum(gn1, axis=0),
        jnp.sum(gn2 * xhat, axis=0),
        jnp.sum(gn2, axis=0),
        mine_bqkv,
        sum_cot,
        mine_bin,
    ]
    sizes = [v.shape[0] for v in vectors]
    sums = lax.psum(jnp.concatenate(vectors), ("seq", "chip", "core"))
    at = 0
    small_out = []
    for size in sizes:
        small_out.append(lax.dynamic_slice_in_dim(sums, at + z * (size // nz), size // nz))
        at += size
    g_gain1, g_bias1, g_gain2, g_bias2, g_bqkv, g_bdense, g_bin = small_out

    def rows_back(dw):
        part = lax.psum_scatter(dw, "chip", scatter_dimension=0, tiled=True)
        every = lax.all_gather(part, ("core", "chip"), axis=0, tiled=True)
        return every.astype(f32)

    def columns_back(dw, groups):
        c = dw.shape[1] // groups
        part = dw.reshape(nz, nchip, wrows // nchip, groups * c).transpose(1, 0, 2, 3)
        part = lax.psum_scatter(part, "chip", scatter_dimension=0, tiled=True)[0]
        part = lax.all_to_all(part, "seq", 0, 0, tiled=True)
        every = lax.all_gather(part, ("chip", "core"), axis=0, tiled=False)
        every = every.reshape(nchip, ncore, nz, wrows // nchip, groups, c)
        every = every.transpose(0, 3, 4, 2, 1, 5)
        return every.reshape(wrows, groups * ranks * c).astype(f32)

    g_wout = rows_back(dw_out)
    g_wdense = rows_back(dw_dense)
    g_win = columns_back(dw_in, 1)
    g_wqkv = columns_back(dw_qkv, 3)
    return (
        output,
        grad_tokens,
        g_gain1,
        g_bias1,
        g_gain2,
        g_bias2,
        g_wqkv,
        g_bqkv,
        g_wdense,
        g_bdense,
        g_win,
        g_bin,
        g_wout,
        g_bdense,
    )


def solution(mesh):
    nz, nctx = mesh.shape["seq"], mesh.shape["ctx"]
    ncore = 2
    nchip = nctx // ncore
    fine = Mesh(mesh.devices.reshape(nz, nchip, ncore), ("seq", "chip", "core"))
    own = P(("seq", "chip", "core"), None)
    vec = P("seq")
    mat = P("seq", None)
    return jax.shard_map(
        functools.partial(on_device, nz, nchip, ncore),
        mesh=fine,
        in_specs=(own, mat, own, vec, vec, vec, vec, mat, vec, mat, vec, mat, vec, mat, vec),
        out_specs=(own, own, vec, vec, vec, vec, mat, vec, mat, vec, mat, vec, mat, vec),
        check_vma=False,
    )
```

```python
import functools

import jax
import jax.numpy as jnp
from jax import lax
from jax.experimental import pallas as pl
from jax.experimental.pallas import tpu as pltpu
from jax.sharding import Mesh, PartitionSpec as P

H = 8
HD = 256
ROT = 64
BLOCK = 96
EPSILON = 1e-05
ROT_BASE = 10000.0
SCALE = HD ** (-0.5)

f32 = jnp.float32
bf16 = jnp.bfloat16
TP = ("seq", "core")
MESH = pl.DeviceIdType.MESH


def remote(src, dst, send, recv, target):
    return pltpu.make_async_remote_copy(
        src_ref=src, dst_ref=dst, send_sem=send, recv_sem=recv, device_id=target,
        device_id_type=MESH,
    )


def greet(targets):
    barrier = pltpu.get_barrier_semaphore()
    for target in targets:
        pl.semaphore_signal(barrier, inc=1, device_id=target, device_id_type=MESH)
    pl.semaphore_wait(barrier, len(targets))


def front(nz, nchip, ncore, tokens, w_in, w_qkv):
    own, width = tokens.shape
    wrows, ff = w_in.shape
    heads3 = w_qkv.shape[1]
    nctx = nchip * ncore
    piece = wrows // nctx
    zi, zq = ff // nz, heads3 // 3 // nz
    ci, cq = zi // ncore, zq // ncore

    def kernel(
        tok_ref, wi_ref, wq_ref, tok_out, wi_out, wq_out, buf_i, buf_q,
        up_s, up_r, dn_s, dn_r, sib_s, sib_r, zi_s, zi_r, zq_s, zq_r, pi_s, pi_r, pq_s, pq_r, loc,
    ):
        z = lax.axis_index("seq")
        chip = lax.axis_index("chip")
        core = lax.axis_index("core")
        share = chip * ncore + core
        sibling = {"core": 1 - core}

        def z_at(d):
            return lax.rem(z + d, nz)

        def plane_at(d):
            other = lax.rem(share + d, nctx)
            return other // ncore, lax.rem(other, ncore)

        greet(
            [{"seq": z_at(d)} for d in range(1, nz)]
            + [{"chip": plane_at(d)[0], "core": plane_at(d)[1]} for d in range(1, nctx)]
        )

        rows = pl.ds(share * piece, piece)
        hop = []
        for d in range(1, nz):
            to = z_at(d)
            hop.append(
                remote(
                    wi_ref.at[rows, pl.ds(to * zi, zi)], buf_i.at[z], zi_s.at[d], zi_r.at[z],
                    {"seq": to},
                )
            )
            for g in range(3):
                hop.append(
                    remote(
                        wq_ref.at[rows, pl.ds(g * zq * nz + to * zq, zq)], buf_q.at[z, g],
                        zq_s.at[d, g], zq_r.at[z, g], {"seq": to},
                    )
                )
        def up(s):
            shard = z - s
            src = tok_ref if s == 0 else tok_out.at[jnp.maximum(shard, 0), core]
            return remote(
                src, tok_out.at[jnp.maximum(shard, 0), core], up_s.at[s], up_r.at[s],
                {"seq": jnp.minimum(z + 1, nz - 1)},
            )

        def down(s):
            shard = z + s
            src = tok_ref if s == 0 else tok_out.at[jnp.minimum(shard, nz - 1), core]
            return remote(
                src, tok_out.at[jnp.minimum(shard, nz - 1), core], dn_s.at[s], dn_r.at[s],
                {"seq": jnp.maximum(z - 1, 0)},
            )

        def side(shard, own_rows=False):
            src = tok_ref if own_rows else tok_out.at[shard, core]
            return remote(src, tok_out.at[shard, core], sib_s.at[shard], sib_r.at[shard], sibling)

        for copy in hop:
            copy.start()

        @pl.when(z + 1 < nz)
        def _():
            up(0).start()

        @pl.when(z > 0)
        def _():
            down(0).start()

        side(z, True).start()
        locals_ = [
            pltpu.make_async_copy(tok_ref, tok_out.at[z, core], loc.at[0]),
            pltpu.make_async_copy(wi_ref.at[rows, pl.ds(z * zi, zi)], buf_i.at[z], loc.at[1]),
        ] + [
            pltpu.make_async_copy(
                wq_ref.at[rows, pl.ds(g * zq * nz + z * zq, zq)], buf_q.at[z, g], loc.at[2 + g]
            )
            for g in range(3)
        ]
        for copy in locals_:
            copy.start()

        def spread_i(source, d):
            to_chip, to_core = plane_at(d)
            dst = wi_out.at[pl.ds(source * wrows + share * piece, piece), :]
            src = buf_i.at[source, :, pl.ds(to_core * ci, ci)]
            return src, dst, to_chip, to_core

        def spread(source, d):
            to_chip, to_core = plane_at(d)
            target_rows = pl.ds(source * wrows + share * piece, piece)
            pairs = [
                (
                    buf_i.at[source, :, pl.ds(to_core * ci, ci)], wi_out.at[target_rows, :],
                    pi_s.at[source, d], pi_r.at[source, share],
                )
            ] + [
                (
                    buf_q.at[source, g, :, pl.ds(to_core * cq, cq)],
                    wq_out.at[target_rows, pl.ds(g * cq, cq)],
                    pq_s.at[source, d, g], pq_r.at[source, share, g],
                )
                for g in range(3)
            ]
            if d == 0:
                return [pltpu.make_async_copy(a, b, c) for a, b, c, r in pairs]
            return [remote(a, b, c, r, {"chip": to_chip, "core": to_core}) for a, b, c, r in pairs]

        def hop_arrival(source):
            remote(buf_i.at[source], buf_i.at[source], zi_s.at[0], zi_r.at[source], sibling).wait_recv()
            for g in range(3):
                remote(
                    buf_q.at[source, g], buf_q.at[source, g], zq_s.at[0, 0], zq_r.at[source, g],
                    sibling,
                ).wait_recv()

        for copy in locals_[1:]:
            copy.wait()
        for d in range(nctx):
            for copy in spread(z, d):
                copy.start()
        for dz in range(1, nz):
            source = z_at(dz if dz % 2 else nz - dz // 2) if False else z_at(dz)
            hop_arrival(source)
            for d in range(nctx):
                for copy in spread(source, d):
                    copy.start()

        for s in range(nz - 1):
            from_below = z - 1 - s
            from_above = z + 1 + s

            @pl.when(from_below >= 0)
            def _():
                shard = jnp.maximum(from_below, 0)
                remote(tok_ref, tok_out.at[shard, core], up_s.at[s], up_r.at[s], sibling).wait_recv()
                if s + 1 < nz - 1:
                    @pl.when(z + 1 < nz)
                    def _():
                        up(s + 1).start()
                side(shard).start()

            @pl.when(from_above < nz)
            def _():
                shard = jnp.minimum(from_above, nz - 1)
                remote(tok_ref, tok_out.at[shard, core], dn_s.at[s], dn_r.at[s], sibling).wait_recv()
                if s + 1 < nz - 1:
                    @pl.when(z > 0)
                    def _():
                        down(s + 1).start()
                side(shard).start()

        locals_[0].wait()
        for shard in range(nz):
            remote(tok_ref, tok_out.at[shard, 1 - core], sib_s.at[shard], sib_r.at[shard], sibling).wait()
        for s in range(nz - 1):
            @pl.when(jnp.logical_and(z + 1 < nz, z - s >= 0))
            def _():
                up(s).wait_send()

            @pl.when(jnp.logical_and(z > 0, z + s < nz))
            def _():
                down(s).wait_send()
        for copy in hop:
            copy.wait_send()
        for source in range(nz):
            for d in range(nctx):
                if d == 0:
                    for copy in spread(source, d):
                        copy.wait()
                    continue
                for copy in spread(source, d):
                    copy.wait_send()
                other = lax.rem(share + d, nctx)
                rows_there = pl.ds(source * wrows + other * piece, piece)
                remote(
                    wi_out.at[rows_there, :], wi_out.at[rows_there, :], pi_s.at[source, d],
                    pi_r.at[source, other], sibling,
                ).wait_recv()
                for g in range(3):
                    cols = pl.ds(g * cq, cq)
                    remote(
                        wq_out.at[rows_there, cols], wq_out.at[rows_there, cols],
                        pq_s.at[source, d, g], pq_r.at[source, other, g], sibling,
                    ).wait_recv()

    dma = pltpu.SemaphoreType.DMA
    anywhere = pl.BlockSpec(memory_space=pl.ANY)
    return pl.pallas_call(
        kernel,
        in_specs=[anywhere] * 3,
        out_specs=[anywhere] * 3,
        out_shape=[
            jax.ShapeDtypeStruct((nz, ncore, own, width), bf16),
            jax.ShapeDtypeStruct((nz * wrows, ci), bf16),
            jax.ShapeDtypeStruct((nz * wrows, 3 * cq), bf16),
        ],
        scratch_shapes=[
            pltpu.VMEM((nz, piece, zi), bf16),
            pltpu.VMEM((nz, 3, piece, zq), bf16),
            dma((nz,)), dma((nz,)), dma((nz,)), dma((nz,)),
            dma((nz,)), dma((nz,)),
            dma((nz,)), dma((nz,)), dma((nz, 3)), dma((nz, 3)),
            dma((nz, nctx)), dma((nz, nctx)), dma((nz, nctx, 3)), dma((nz, nctx, 3)),
            dma((5,)),
        ],
        compiler_params=pltpu.CompilerParams(collective_id=1, has_side_effects=True),
        name="front",
    )(tokens, w_in, w_qkv)


def tail(nz, nchip, ncore, dwo, dwd, dwi, dwq, part_e, part_o, vectors):
    width = dwo.shape[1]
    ro, rd = dwo.shape[0] // nchip, dwd.shape[0] // nchip
    ci, cq = dwi.shape[1], dwq.shape[1] // 3
    wrows = width // nz
    ri = wrows // nchip
    own = part_e.shape[0] // nz // ncore
    vr = vectors.shape[0]
    dwi = dwi.reshape(nz, nchip, ri, ci)
    dwq = dwq.reshape(nz, nchip, ri, 3 * cq)
    part_e = part_e.reshape(nz, ncore, own, width)
    part_o = part_o.reshape(nz, ncore, own, width)

    def kernel(
        dwo_ref, dwd_ref, dwi_ref, dwq_ref, pe_ref, po_ref, vec_ref,
        go_ref, gd_ref, gi_ref, gq_ref, e_ref, o_ref, vsum_ref,
        bo, bd, bi, bq, ti, tq, se, so, me, mo, ze, zo, v1, v2, v3,
        rs_s, rs_r, rs_l, x_s, x_r, x_l, ez_s, ez_r, t_s, t_r, t_l,
        go_s, go_r, gd_s, gd_r, gi_s, gi_r, gq_s, gq_r, own_l, fin_l,
        v_s, v_r, v_l,
    ):
        z = lax.axis_index("seq")
        chip = lax.axis_index("chip")
        core = lax.axis_index("core")
        sibling = {"core": 1 - core}

        def z_at(d):
            return lax.rem(z + d, nz)

        def chip_at(d):
            return lax.rem(chip + d, nchip)

        greet(
            [{"seq": z_at(d)} for d in range(1, nz)]
            + [{"chip": chip_at(d)} for d in range(1, nchip)]
            + [sibling]
        )

        halves = [
            remote(pe_ref.at[:, 1 - core], se, x_s.at[0], x_r.at[0], sibling),
            remote(po_ref.at[:, 1 - core], so, x_s.at[1], x_r.at[1], sibling),
        ]
        keep = [
            pltpu.make_async_copy(pe_ref.at[:, core], me, x_l.at[0]),
            pltpu.make_async_copy(po_ref.at[:, core], mo, x_l.at[1]),
        ]
        for copy in halves + keep:
            copy.start()

        def rs(d):
            to = chip_at(d)
            pairs = [
                (dwi_ref.at[:, to], bi.at[d]),
                (dwq_ref.at[:, to], bq.at[d]),
                (dwo_ref.at[pl.ds(to * ro, ro), :], bo.at[d]),
                (dwd_ref.at[pl.ds(to * rd, rd), :], bd.at[d]),
            ]
            if d == 0:
                return [pltpu.make_async_copy(a, b, rs_l.at[i]) for i, (a, b) in enumerate(pairs)]
            return [
                remote(a, b, rs_s.at[d, i], rs_r.at[d, i], {"chip": to})
                for i, (a, b) in enumerate(pairs)
            ]

        scattered = [rs(d) for d in range(nchip)]
        for kind in range(4):
            for d in range(1, nchip):
                scattered[d][kind].start()
            scattered[0][kind].start()

        v_own = pltpu.make_async_copy(vec_ref, v1.at[chip], v_l.at[0])
        v_own.start()
        v_chips = [
            remote(vec_ref, v1.at[chip], v_s.at[d], v_r.at[chip], {"chip": chip_at(d)})
            for d in range(1, nchip)
        ]
        for copy in v_chips:
            copy.start()

        def add_rows(total, count, step, body):
            @pl.loop(0, count // step)
            def _(i):
                body(pl.ds(pl.multiple_of(i * step, step), step))

        z_copies = []
        for which, (mine, theirs, landing) in enumerate(((me, se, ze), (mo, so, zo))):
            halves[which].wait_recv()
            keep[which].wait()

            @pl.loop(0, nz)
            def _(b):
                @pl.loop(0, own // 16)
                def _(i):
                    at = pl.ds(pl.multiple_of(i * 16, 16), 16)
                    mine[b, at, :] = (
                        mine[b, at, :].astype(f32) + theirs[b, at, :].astype(f32)
                    ).astype(bf16)

            for d in range(1, nz):
                copy = remote(
                    mine.at[z_at(d)], landing.at[d], ez_s.at[which, d], ez_r.at[which, d],
                    {"seq": z_at(d)},
                )
                copy.start()
                z_copies.append(copy)

        v_own.wait()
        for d in range(1, nchip):
            other = chip_at(d)
            remote(vec_ref, v1.at[other], v_s.at[d], v_r.at[other], sibling).wait_recv()
        total = v1[0]
        for d in range(1, nchip):
            total = total + v1[d]
        v2[core] = total
        v_side = remote(v2.at[core], v2.at[core], v_s.at[nchip], v_r.at[nchip], sibling)
        v_side.start()

        def add_four(buf, count, pieces):
            @pl.loop(0, count // 16)
            def _(i):
                at = pl.ds(pl.multiple_of(i * 16, 16), 16)
                acc = buf[(0,) + pieces + (at,)].astype(f32)
                for d in range(1, nchip):
                    acc = acc + buf[(d,) + pieces + (at,)].astype(f32)
                buf[(0,) + pieces + (at,)] = acc.astype(bf16)

        turns = []
        for kind, (buf, turned) in enumerate(((bi, ti), (bq, tq))):
            scattered[0][kind].wait()
            for d in range(1, nchip):
                scattered[d][kind].wait_recv()

            @pl.loop(0, nz)
            def _(b):
                add_four(buf, ri, (b,))

            for d in range(1, nz):
                to = z_at(d)
                copy = remote(
                    buf.at[0, to], turned.at[z], t_s.at[kind, d], t_r.at[kind, z], {"seq": to}
                )
                copy.start()
                turns.append(copy)
            local = pltpu.make_async_copy(buf.at[0, z], turned.at[z], t_l.at[kind])
            local.start()
            turns.append(local)

        v_side.wait_recv()
        vz = v2[0]
        for c in range(1, ncore):
            vz = vz + v2[c]
        v3[z] = vz
        v_zs = [
            remote(v3.at[z], v3.at[z], v_s.at[nchip + d], v_r.at[nchip + 1 + z], {"seq": z_at(d)})
            for d in range(1, nz)
        ]
        for copy in v_zs:
            copy.start()

        def spread(src, dst_of, send, recv, local):
            copies = [pltpu.make_async_copy(src, dst_of(chip, core), local)]
            copies += [
                remote(src, dst_of(chip, core), send.at[d], recv.at[chip], {"chip": chip_at(d)})
                for d in range(1, nchip)
            ]
            copies.append(
                remote(
                    src, dst_of(chip, core), send.at[nchip + chip], recv.at[nchip + chip], sibling
                )
            )
            for copy in copies:
                copy.start()
            return copies

        go_at = lambda c, k: go_ref.at[pl.ds(k * (ro * nchip) + c * ro, ro), :]
        gd_at = lambda c, k: gd_ref.at[pl.ds(k * (rd * nchip) + c * rd, rd), :]
        gi_at = lambda c, k, s: gi_ref.at[
            pl.ds(c * ri, ri), pl.ds((s * ncore + k) * ci, ci)
        ]
        gq_at = lambda c, k, s, g: gq_ref.at[
            pl.ds(c * ri, ri), pl.ds(g * nz * ncore * cq + (s * ncore + k) * cq, cq)
        ]
        groups = []
        for kind, (buf, count) in enumerate(((bo, ro), (bd, rd))):
            scattered[0][2 + kind].wait()
            for d in range(1, nchip):
                scattered[d][2 + kind].wait_recv()
            add_four(buf, count, ())
            group = (
                (bo.at[0], go_at, go_s, go_r, own_l.at[0])
                if kind == 0
                else (bd.at[0], gd_at, gd_s, gd_r, own_l.at[1])
            )
            groups.append(group + (spread(*group),))
        for dz in range(nz):
            source = z_at(dz)
            if dz > 0:
                remote(bi.at[0, 0], ti.at[source], t_s.at[0, dz], t_r.at[0, source], sibling).wait_recv()
            else:
                turns[nz - 1].wait()
            group = (
                ti.at[source], functools.partial(gi_at, s=source), gi_s.at[source], gi_r.at[source],
                own_l.at[2 + source],
            )
            groups.append(group + (spread(*group),))
        for dz in range(nz):
            source = z_at(dz)
            if dz > 0:
                remote(bq.at[0, 0], tq.at[source], t_s.at[1, dz], t_r.at[1, source], sibling).wait_recv()
            else:
                turns[2 * nz - 1].wait()
            for g in range(3):
                group = (
                    tq.at[source, :, pl.ds(g * cq, cq)],
                    functools.partial(gq_at, s=source, g=g),
                    gq_s.at[source, g], gq_r.at[source, g], own_l.at[2 + nz + 3 * source + g],
                )
                groups.append(group + (spread(*group),))

        for which, (mine, landing, out) in enumerate(((me, ze, e_ref), (mo, zo, o_ref))):
            for d in range(1, nz):
                z_copies[which * (nz - 1) + d - 1].wait_recv()

            @pl.loop(0, own // 16)
            def _(i):
                at = pl.ds(pl.multiple_of(i * 16, 16), 16)
                acc = mine[z, at, :].astype(f32)
                for d in range(1, nz):
                    acc = acc + landing[d, at, :].astype(f32)
                out[at, :] = acc

        for d in range(1, nz):
            other = z_at(d)
            remote(v3.at[0], v3.at[other], v_s.at[0], v_r.at[nchip + 1 + other], sibling).wait_recv()
        total = v3[0]
        for d in range(1, nz):
            total = total + v3[d]
        vsum_ref[...] = total

        passed = []
        for src, dst_of, send, recv, local, copies in groups:
            for d in range(1, nchip):
                other = chip_at(d)
                here = dst_of(other, core)
                remote(here, here, send.at[0], recv.at[other], sibling).wait_recv()
                copy = remote(here, here, send.at[nchip + other], recv.at[nchip + other], sibling)
                copy.start()
                passed.append(copy)
        for src, dst_of, send, recv, local, copies in groups:
            copies[0].wait()
            for copy in copies[1:]:
                copy.wait_send()
            for d in range(nchip):
                other = chip_at(d)
                there = dst_of(other, 1 - core)
                remote(there, there, send.at[0], recv.at[nchip + other], sibling).wait_recv()
        for copy in passed:
            copy.wait_send()
        for d in range(1, nchip):
            for copy in scattered[d]:
                copy.wait_send()
        for copy in halves + z_copies + v_chips + v_zs + [v_side]:
            copy.wait_send()
        for kind in range(2):
            for d in range(1, nz):
                turns[kind * nz + d - 1].wait_send()

    dma = pltpu.SemaphoreType.DMA
    anywhere = pl.BlockSpec(memory_space=pl.ANY)
    vmem = pl.BlockSpec(memory_space=pltpu.VMEM)
    out_shape = [
        jax.ShapeDtypeStruct((ncore * nchip * ro, width), bf16),
        jax.ShapeDtypeStruct((ncore * nchip * rd, width), bf16),
        jax.ShapeDtypeStruct((wrows, nz * ncore * ci), bf16),
        jax.ShapeDtypeStruct((wrows, 3 * nz * ncore * cq), bf16),
        jax.ShapeDtypeStruct((own, width), f32),
        jax.ShapeDtypeStruct((own, width), f32),
        jax.ShapeDtypeStruct((vr, 128), f32),
    ]
    ranked = (nz, own, width)
    return pl.pallas_call(
        kernel,
        in_specs=[anywhere] * 6 + [vmem],
        out_specs=[anywhere] * 4 + [vmem] * 3,
        out_shape=out_shape,
        scratch_shapes=[
            pltpu.VMEM((nchip, ro, width), bf16),
            pltpu.VMEM((nchip, rd, width), bf16),
            pltpu.VMEM((nchip, nz, ri, ci), bf16),
            pltpu.VMEM((nchip, nz, ri, 3 * cq), bf16),
            pltpu.VMEM((nz, ri, ci), bf16),
            pltpu.VMEM((nz, ri, 3 * cq), bf16),
            pltpu.VMEM(ranked, bf16),
            pltpu.VMEM(ranked, bf16),
            pltpu.VMEM(ranked, bf16),
            pltpu.VMEM(ranked, bf16),
            pltpu.VMEM(ranked, bf16),
            pltpu.VMEM(ranked, bf16),
            pltpu.VMEM((nchip, vr, 128), f32),
            pltpu.VMEM((ncore, vr, 128), f32),
            pltpu.VMEM((nz, vr, 128), f32),
            dma((nchip, 4)), dma((nchip, 4)), dma((4,)),
            dma((2,)), dma((2,)), dma((2,)),
            dma((2, nz)), dma((2, nz)),
            dma((2, nz)), dma((2, nz)), dma((2,)),
            dma((2 * nchip,)), dma((2 * nchip,)),
            dma((2 * nchip,)), dma((2 * nchip,)),
            dma((nz, 2 * nchip)), dma((nz, 2 * nchip)),
            dma((nz, 3, 2 * nchip)), dma((nz, 3, 2 * nchip)),
            dma((2 + 4 * nz,)), dma((2,)),
            dma((nchip + nz,)), dma((nchip + nz + 1,)), dma((1,)),
        ],
        compiler_params=pltpu.CompilerParams(
            collective_id=2, has_side_effects=True, vmem_limit_bytes=60 * 2**20
        ),
        name="tail",
    )(dwo, dwd, dwi, dwq, part_e, part_o, vectors)


def angles_of(positions):
    half = ROT // 2
    inverse_freq = jnp.power(ROT_BASE, -(jnp.arange(half, dtype=f32) * 2.0) / ROT)
    angles = positions.astype(f32)[:, None] * inverse_freq[None, :]
    return jnp.cos(angles), jnp.sin(angles)


def rotate(u, cosine, sine):
    half = ROT // 2
    a, b = u[..., :half], u[..., half:ROT]
    return jnp.concatenate([a * cosine - b * sine, b * cosine + a * sine, u[..., ROT:]], axis=-1)


def attention_forward(q, k, v, row_pos, col_pos, tile):
    rows = q.shape[0]

    def kernel(q_ref, k_ref, v_ref, rp_ref, cp_ref, o_ref, lse_ref):
        s = lax.dot_general(
            q_ref[...], k_ref[...], (((1,), (1,)), ((), ())), preferred_element_type=f32
        ) * SCALE
        allowed = rp_ref[...] >= cp_ref[...]
        s = jnp.where(allowed, s, -1e30)
        top = jnp.max(s, axis=-1, keepdims=True)
        e = jnp.exp(s - top)
        total = jnp.sum(e, axis=-1, keepdims=True)
        p = (e / total).astype(bf16)
        o_ref[...] = jnp.dot(p, v_ref[...], preferred_element_type=f32).astype(bf16)
        lse_ref[...] = top + jnp.log(total)

    whole = pl.BlockSpec((rows, HD), lambda i: (0, 0))
    part = pl.BlockSpec((tile, HD), lambda i: (i, 0))
    one = pl.BlockSpec((tile, 1), lambda i: (i, 0))
    return pl.pallas_call(
        kernel,
        grid=(rows // tile,),
        in_specs=[part, whole, whole, one, pl.BlockSpec((1, rows), lambda i: (0, 0))],
        out_specs=[part, one],
        out_shape=[
            jax.ShapeDtypeStruct((rows, HD), bf16),
            jax.ShapeDtypeStruct((rows, 1), f32),
        ],
        compiler_params=pltpu.CompilerParams(vmem_limit_bytes=56 * 2**20),
        cost_estimate=pl.CostEstimate(
            flops=4 * rows * rows * HD, bytes_accessed=8 * rows * HD, transcendentals=rows * rows
        ),
        name="attention_forward",
    )(q, k, v, row_pos, col_pos)


def attention_backward(q, k, v, g, lse, row_pos, col_pos, tile):
    rows = q.shape[0]

    def kernel(q_ref, k_ref, v_ref, g_ref, lse_ref, rp_ref, cp_ref, dq_ref, dk_ref, dv_ref):
        nt = (((1,), (1,)), ((), ()))
        tn = (((0,), (0,)), ((), ()))

        @pl.when(pl.program_id(0) == 0)
        def _():
            dk_ref[...] = jnp.zeros_like(dk_ref)
            dv_ref[...] = jnp.zeros_like(dv_ref)

        s = lax.dot_general(q_ref[...], k_ref[...], nt, preferred_element_type=f32) * SCALE
        allowed = rp_ref[...] >= cp_ref[...]
        p = jnp.where(allowed, jnp.exp(s - lse_ref[...]), 0.0)
        dp = lax.dot_general(g_ref[...], v_ref[...], nt, preferred_element_type=f32)
        shift = jnp.sum(p * dp, axis=-1, keepdims=True)
        ds = (p * (dp - shift)).astype(bf16)
        dq_ref[...] = jnp.dot(ds, k_ref[...], preferred_element_type=f32) * SCALE
        dk_ref[...] += lax.dot_general(ds, q_ref[...], tn, preferred_element_type=f32) * SCALE
        dv_ref[...] += lax.dot_general(p.astype(bf16), g_ref[...], tn, preferred_element_type=f32)

    whole = pl.BlockSpec((rows, HD), lambda i: (0, 0))
    part = pl.BlockSpec((tile, HD), lambda i: (i, 0))
    one = pl.BlockSpec((tile, 1), lambda i: (i, 0))
    return pl.pallas_call(
        kernel,
        grid=(rows // tile,),
        in_specs=[part, whole, whole, part, one, one, pl.BlockSpec((1, rows), lambda i: (0, 0))],
        out_specs=[part, whole, whole],
        out_shape=[jax.ShapeDtypeStruct((rows, HD), f32)] * 3,
        compiler_params=pltpu.CompilerParams(vmem_limit_bytes=56 * 2**20),
        cost_estimate=pl.CostEstimate(
            flops=10 * rows * rows * HD, bytes_accessed=20 * rows * HD, transcendentals=rows * rows
        ),
        name="attention_backward",
    )(q, k, v, g, lse, row_pos, col_pos)


def on_device(
    nz,
    nchip,
    ncore,
    tokens,
    block_ids,
    cotangent,
    norm1_gain,
    norm1_bias,
    norm2_gain,
    norm2_bias,
    w_qkv,
    b_qkv,
    w_dense,
    b_dense,
    w_in,
    b_in,
    w_out,
    b_out,
):
    own, width = tokens.shape
    z = lax.axis_index("seq")
    chip = lax.axis_index("chip")
    core = lax.axis_index("core")
    ranks = nz * ncore
    rank = z * ncore + core
    rows = ranks * own
    ff = w_out.shape[0] * nz
    ffr = ff // ranks
    hc = width // ranks
    split = max(1, HD // hc)
    wrows = width // nz
    piece = wrows // nchip // ncore

    small = jnp.concatenate(
        [norm1_gain, norm1_bias, norm2_gain, norm2_bias, b_qkv, b_dense, b_in, b_out,
         block_ids.reshape(-1).astype(bf16)]
    )
    small = lax.all_gather(small, "seq", axis=0, tiled=False)
    d4 = wrows
    f4 = b_in.shape[0]
    q4 = b_qkv.shape[0]
    cuts = [0, d4, 2 * d4, 3 * d4, 4 * d4, 4 * d4 + q4, 5 * d4 + q4, 5 * d4 + q4 + f4,
            6 * d4 + q4 + f4, small.shape[1]]
    gain1, bias1, gain2, bias2, full_bqkv, full_bdense, full_bin, full_bout, ids = [
        small[:, cuts[i] : cuts[i + 1]].reshape(-1) for i in range(9)
    ]
    gain1, bias1, gain2, bias2 = [v.astype(f32) for v in (gain1, bias1, gain2, bias2)]
    ids = ids.reshape(nz, -1).astype(jnp.int32)

    tok, w_in_c, w_qkv_c = front(nz, nchip, ncore, tokens, w_in, w_qkv)
    tok = tok.reshape(rows, width)
    tok, cot_own = lax.optimization_barrier((tok, cotangent))
    cot = lax.all_gather(cot_own, TP, axis=0, tiled=True)
    w_out_r = lax.dynamic_slice_in_dim(w_out, core * ffr, ffr, 0)
    w_dense_r = lax.dynamic_slice_in_dim(w_dense, core * hc, hc, 0)

    def layer_stats(x):
        mean = jnp.mean(x, axis=-1, keepdims=True)
        center = x - mean
        spread = jnp.mean(center * center, axis=-1, keepdims=True)
        inv = lax.rsqrt(spread + EPSILON)
        return center * inv, inv

    xhat, unused = layer_stats(tok.astype(f32))
    normed1 = (xhat * gain1 + bias1).astype(bf16)
    normed2 = (xhat * gain2 + bias2).astype(bf16)

    project = jnp.dot(normed1, w_qkv_c, preferred_element_type=f32)
    bias_c = lax.dynamic_slice_in_dim(full_bqkv.reshape(3, ranks, hc), rank, 1, 1)
    project = (project + bias_c.reshape(1, 3 * hc).astype(f32)).reshape(rows, 3, hc)
    blocks = ids.shape[1]
    pos_all = jnp.repeat(ids, BLOCK, axis=1) * BLOCK + jnp.tile(
        jnp.arange(BLOCK, dtype=jnp.int32), blocks
    )
    pos_seq = lax.dynamic_index_in_dim(pos_all, chip, 0, keepdims=False)
    length = pos_seq.shape[0]

    def heads_of(x):
        if split > 1:
            x = lax.all_gather(x, "core", axis=2, tiled=True)
        x = x.reshape(nz, rows // nz, x.shape[1], HD).transpose(0, 2, 1, 3)
        x = lax.all_to_all(x, "chip", 0, 0, tiled=True)
        return x.transpose(1, 0, 2, 3).reshape(x.shape[1], length, HD)

    def heads_back(x):
        g = x.shape[0]
        x = x.reshape(g, nchip, length // nchip, HD).transpose(1, 0, 2, 3)
        x = lax.all_to_all(x, "chip", 0, 0, tiled=True)
        x = x.transpose(0, 2, 1, 3).reshape(rows, g, HD)
        if split > 1:
            x = lax.dynamic_slice_in_dim(x, core * hc, hc, 2)
        return x

    cosine, sine = angles_of(pos_seq)
    if split == 1:
        pos_rows = lax.dynamic_slice_in_dim(pos_all, chip * (rows // nz), rows // nz, 1).reshape(-1)
        cos_r, sin_r = angles_of(pos_rows)
        q = rotate(project[:, 0], cos_r, sin_r).astype(bf16)
        k = rotate(project[:, 1], cos_r, sin_r).astype(bf16)
        v = project[:, 2].astype(bf16)
        q, k, v = heads_of(jnp.stack([q, k, v], axis=1))
    else:
        q, k, v = heads_of(project)
        q = rotate(q, cosine, sine).astype(bf16)
        k = rotate(k, cosine, sine).astype(bf16)
        v = v.astype(bf16)
    row_pos, col_pos = pos_seq[:, None], pos_seq[None, :]
    tile = 256
    attended, lse = attention_forward(q, k, v, row_pos, col_pos, tile)
    mixed = heads_back(attended[None]).reshape(rows, hc)

    hidden = jnp.dot(normed2, w_in_c, preferred_element_type=f32)
    hidden = hidden + lax.dynamic_slice_in_dim(full_bin, rank * ffr, ffr).astype(f32)
    active, gelu_back = jax.vjp(functools.partial(jax.nn.gelu, approximate=False), hidden)
    active = active.astype(bf16)
    part_out = jnp.dot(mixed, w_dense_r, preferred_element_type=f32) + jnp.dot(
        active, w_out_r, preferred_element_type=f32
    )
    tn = (((0,), (0,)), ((), ()))
    nt = (((1,), (1,)), ((), ()))
    grad_active = lax.dot_general(cot, w_out_r, nt, preferred_element_type=f32)
    grad_hidden32 = gelu_back(grad_active)[0]
    grad_hidden = grad_hidden32.astype(bf16)
    dw_out = lax.dot_general(active, cot, tn, preferred_element_type=f32).astype(bf16)
    dw_in = lax.dot_general(normed2, grad_hidden, tn, preferred_element_type=f32).astype(bf16)
    gn2 = lax.dot_general(grad_hidden, w_in_c, nt, preferred_element_type=f32)

    dw_dense = lax.dot_general(mixed, cot, tn, preferred_element_type=f32).astype(bf16)
    grad_mixed = lax.dot_general(cot, w_dense_r, nt, preferred_element_type=f32).astype(bf16)
    g = heads_of(grad_mixed[:, None])[0]
    dq, dk, dv = attention_backward(q, k, v, g, lse, row_pos, col_pos, tile)
    dq = rotate(dq, cosine, -sine).astype(bf16)
    dk = rotate(dk, cosine, -sine).astype(bf16)
    grad_project = heads_back(jnp.stack([dq, dk, dv.astype(bf16)])).reshape(rows, 3 * hc)
    dw_qkv = lax.dot_general(normed1, grad_project, tn, preferred_element_type=f32).astype(bf16)
    gn1 = lax.dot_general(grad_project, w_qkv_c, nt, preferred_element_type=f32)

    e_part = (gn1 * gain1 + gn2 * gain2).astype(bf16)
    sum_cot = jnp.sum(cotangent.astype(f32), axis=0)
    mine_bin = jnp.zeros((ranks, ffr), f32)
    mine_bin = lax.dynamic_update_slice_in_dim(
        mine_bin, jnp.sum(grad_hidden.astype(f32), axis=0)[None], rank, 0
    ).reshape(-1)
    mine_bqkv = jnp.zeros((3, ranks, hc), f32)
    mine_bqkv = lax.dynamic_update_slice_in_dim(
        mine_bqkv, jnp.sum(grad_project.astype(f32), axis=0).reshape(3, 1, hc), rank, 1
    ).reshape(-1)
    vectors = [
        jnp.sum(gn1 * xhat, axis=0),
        jnp.sum(gn1, axis=0),
        jnp.sum(gn2 * xhat, axis=0),
        jnp.sum(gn2, axis=0),
        mine_bqkv,
        sum_cot,
        mine_bin,
    ]
    sizes = [v.shape[0] for v in vectors]
    vectors = jnp.concatenate(vectors).reshape(-1, 128)
    g_wout, g_wdense, g_win, g_wqkv, e, summed_out, sums = tail(
        nz, nchip, ncore, dw_out, dw_dense, dw_in, dw_qkv, e_part, part_out.astype(bf16), vectors
    )
    sums = sums.reshape(-1)
    at = 0
    small_out = []
    for size in sizes:
        small_out.append(lax.dynamic_slice_in_dim(sums, at + z * (size // nz), size // nz))
        at += size
    g_gain1, g_bias1, g_gain2, g_bias2, g_bqkv, g_bdense, g_bin = small_out

    output = (
        tokens.astype(f32) + summed_out + full_bdense.astype(f32) + full_bout.astype(f32)
    ).astype(bf16)
    xhat_own, inv_own = layer_stats(tokens.astype(f32))
    terms = (
        e
        - jnp.mean(e, axis=-1, keepdims=True)
        - xhat_own * jnp.mean(e * xhat_own, axis=-1, keepdims=True)
    ) * inv_own
    grad_tokens = (cotangent.astype(f32) + terms).astype(bf16)

    g_wout, g_wdense, g_win, g_wqkv = [g.astype(f32) for g in (g_wout, g_wdense, g_win, g_wqkv)]
    return (
        output,
        grad_tokens,
        g_gain1,
        g_bias1,
        g_gain2,
        g_bias2,
        g_wqkv,
        g_bqkv,
        g_wdense,
        g_bdense,
        g_win,
        g_bin,
        g_wout,
        g_bdense,
    )


def solution(mesh):
    nz, nctx = mesh.shape["seq"], mesh.shape["ctx"]
    ncore = 2
    nchip = nctx // ncore
    fine = Mesh(mesh.devices.reshape(nz, nchip, ncore), ("seq", "chip", "core"))
    own = P(("seq", "chip", "core"), None)
    vec = P("seq")
    mat = P("seq", None)
    return jax.shard_map(
        functools.partial(on_device, nz, nchip, ncore),
        mesh=fine,
        in_specs=(own, mat, own, vec, vec, vec, vec, mat, vec, mat, vec, mat, vec, mat, vec),
        out_specs=(own, own, vec, vec, vec, vec, mat, vec, mat, vec, mat, vec, mat, vec),
        check_vma=False,
    )
```

```python
import functools
import math

import jax
import jax.numpy as jnp
import numpy as np
from jax import lax
from jax.experimental import pallas as pl
from jax.experimental.pallas import tpu as pltpu
from jax.sharding import Mesh, PartitionSpec as P

HD = 256
ROT = 64
BLOCK = 96
EPSILON = 1e-05
ROT_BASE = 10000.0
SCALE = HD ** (-0.5)
f32 = jnp.float32
bf16 = jnp.bfloat16
TP = ("seq", "core")
MESH = pl.DeviceIdType.MESH
NT = (((1,), (1,)), ((), ()))
TN = (((0,), (0,)), ((), ()))
BIG = pltpu.CompilerParams(vmem_limit_bytes=56 * 2**20)


def remote(src, dst, send, recv, target):
    return pltpu.make_async_remote_copy(
        src_ref=src, dst_ref=dst, send_sem=send, recv_sem=recv, device_id=target,
        device_id_type=MESH,
    )


def greet(targets):
    barrier = pltpu.get_barrier_semaphore()
    for target in targets:
        pl.semaphore_signal(barrier, inc=1, device_id=target, device_id_type=MESH)
    pl.semaphore_wait(barrier, len(targets))


def front(nz, nchip, ncore, tokens, w_in, w_qkv, small):
    own, width = tokens.shape
    wrows, ff = w_in.shape
    heads3 = w_qkv.shape[1]
    nctx = nchip * ncore
    piece = wrows // nctx
    zi, zq = ff // nz, heads3 // 3 // nz
    ci, cq = zi // ncore, zq // ncore

    def kernel(
        tok_ref, wi_ref, wq_ref, sm_ref, tok_out, wi_out, wq_out, sm_out, buf_i, buf_q,
        up_s, up_r, dn_s, dn_r, sib_s, sib_r, zi_s, zi_r, zq_s, zq_r, pi_s, pi_r, pq_s, pq_r, loc, sm_s, sm_r,
    ):
        z = lax.axis_index("seq")
        chip = lax.axis_index("chip")
        core = lax.axis_index("core")
        share = chip * ncore + core
        sibling = {"core": 1 - core}

        def z_at(d):
            return lax.rem(z + d, nz)

        def plane_at(d):
            other = lax.rem(share + d, nctx)
            return other // ncore, lax.rem(other, ncore)

        greet(
            [{"seq": z_at(d)} for d in range(1, nz)]
            + [{"chip": plane_at(d)[0], "core": plane_at(d)[1]} for d in range(1, nctx)]
        )

        rows = pl.ds(share * piece, piece)
        def hop(to):
            to = jnp.clip(to, 0, nz - 1)
            copies = [
                remote(
                    wi_ref.at[rows, pl.ds(to * zi, zi)], buf_i.at[z], zi_s.at[to], zi_r.at[z],
                    {"seq": to},
                )
            ]
            for g in range(3):
                copies.append(
                    remote(
                        wq_ref.at[rows, pl.ds(g * zq * nz + to * zq, zq)], buf_q.at[z, g],
                        zq_s.at[to, g], zq_r.at[z, g], {"seq": to},
                    )
                )
            return copies

        def around(body):
            for distance in range(1, nz):
                for other in (z + distance, z - distance):
                    @pl.when(jnp.logical_and(other >= 0, other < nz))
                    def _():
                        body(jnp.clip(other, 0, nz - 1))

        def up(s):
            shard = z - s
            src = tok_ref if s == 0 else tok_out.at[jnp.maximum(shard, 0), core]
            return remote(
                src, tok_out.at[jnp.maximum(shard, 0), core], up_s.at[s], up_r.at[s],
                {"seq": jnp.minimum(z + 1, nz - 1)},
            )

        def down(s):
            shard = z + s
            src = tok_ref if s == 0 else tok_out.at[jnp.minimum(shard, nz - 1), core]
            return remote(
                src, tok_out.at[jnp.minimum(shard, nz - 1), core], dn_s.at[s], dn_r.at[s],
                {"seq": jnp.maximum(z - 1, 0)},
            )

        def side(shard, own_rows=False):
            src = tok_ref if own_rows else tok_out.at[shard, core]
            return remote(src, tok_out.at[shard, core], sib_s.at[shard], sib_r.at[shard], sibling)

        smalls = [
            remote(sm_ref, sm_out.at[z], sm_s.at[d], sm_r.at[z], {"seq": z_at(d)})
            for d in range(1, nz)
        ]
        for copy in smalls:
            copy.start()

        def send_hop(to):
            for copy in hop(to):
                copy.start()

        around(send_hop)

        @pl.when(z + 1 < nz)
        def _():
            up(0).start()

        @pl.when(z > 0)
        def _():
            down(0).start()

        side(z, True).start()
        locals_ = [
            pltpu.make_async_copy(tok_ref, tok_out.at[z, core], loc.at[0]),
            pltpu.make_async_copy(wi_ref.at[rows, pl.ds(z * zi, zi)], buf_i.at[z], loc.at[1]),
            pltpu.make_async_copy(sm_ref, sm_out.at[z], sm_s.at[0]),
        ] + [
            pltpu.make_async_copy(
                wq_ref.at[rows, pl.ds(g * zq * nz + z * zq, zq)], buf_q.at[z, g], loc.at[2 + g]
            )
            for g in range(3)
        ]
        for copy in locals_:
            copy.start()

        def spread(source, d):
            to_chip, to_core = plane_at(d)
            target_rows = pl.ds(source * wrows + share * piece, piece)
            pairs = [
                (
                    buf_i.at[source, :, pl.ds(to_core * ci, ci)], wi_out.at[target_rows, :],
                    pi_s.at[source, d], pi_r.at[source, share],
                )
            ] + [
                (
                    buf_q.at[source, g, :, pl.ds(to_core * cq, cq)],
                    wq_out.at[target_rows, pl.ds(g * cq, cq)],
                    pq_s.at[source, d, g], pq_r.at[source, share, g],
                )
                for g in range(3)
            ]
            if d == 0:
                return [pltpu.make_async_copy(a, b, c) for a, b, c, r in pairs]
            return [remote(a, b, c, r, {"chip": to_chip, "core": to_core}) for a, b, c, r in pairs]

        def hop_arrival(source):
            remote(buf_i.at[source], buf_i.at[source], zi_s.at[0], zi_r.at[source], sibling).wait_recv()
            for g in range(3):
                remote(
                    buf_q.at[source, g], buf_q.at[source, g], zq_s.at[0, 0], zq_r.at[source, g],
                    sibling,
                ).wait_recv()

        for copy in locals_[1:]:
            copy.wait()
        for d in range(nctx):
            for copy in spread(z, d):
                copy.start()
        def hand_on(source):
            hop_arrival(source)
            for d in range(nctx):
                for copy in spread(source, d):
                    copy.start()

        around(hand_on)

        for s in range(nz - 1):
            from_below = z - 1 - s
            from_above = z + 1 + s

            @pl.when(from_below >= 0)
            def _():
                shard = jnp.maximum(from_below, 0)
                remote(tok_ref, tok_out.at[shard, core], up_s.at[s], up_r.at[s], sibling).wait_recv()
                if s + 1 < nz - 1:
                    @pl.when(z + 1 < nz)
                    def _():
                        up(s + 1).start()
                side(shard).start()

            @pl.when(from_above < nz)
            def _():
                shard = jnp.minimum(from_above, nz - 1)
                remote(tok_ref, tok_out.at[shard, core], dn_s.at[s], dn_r.at[s], sibling).wait_recv()
                if s + 1 < nz - 1:
                    @pl.when(z > 0)
                    def _():
                        down(s + 1).start()
                side(shard).start()

        locals_[0].wait()
        for shard in range(nz):
            remote(tok_ref, tok_out.at[shard, 1 - core], sib_s.at[shard], sib_r.at[shard], sibling).wait()
        for s in range(nz - 1):
            @pl.when(jnp.logical_and(z + 1 < nz, z - s >= 0))
            def _():
                up(s).wait_send()

            @pl.when(jnp.logical_and(z > 0, z + s < nz))
            def _():
                down(s).wait_send()
        for copy in smalls:
            copy.wait_send()

        def hop_left(to):
            for copy in hop(to):
                copy.wait_send()

        around(hop_left)
        for d in range(1, nz):
            other = z_at(d)
            remote(sm_ref, sm_out.at[other], sm_s.at[d], sm_r.at[other], sibling).wait_recv()
        for source in range(nz):
            for d in range(nctx):
                if d == 0:
                    for copy in spread(source, d):
                        copy.wait()
                    continue
                for copy in spread(source, d):
                    copy.wait_send()
                other = lax.rem(share + d, nctx)
                rows_there = pl.ds(source * wrows + other * piece, piece)
                remote(
                    wi_out.at[rows_there, :], wi_out.at[rows_there, :], pi_s.at[source, d],
                    pi_r.at[source, other], sibling,
                ).wait_recv()
                for g in range(3):
                    cols = pl.ds(g * cq, cq)
                    remote(
                        wq_out.at[rows_there, cols], wq_out.at[rows_there, cols],
                        pq_s.at[source, d, g], pq_r.at[source, other, g], sibling,
                    ).wait_recv()

    dma = pltpu.SemaphoreType.DMA
    anywhere = pl.BlockSpec(memory_space=pl.ANY)
    return pl.pallas_call(
        kernel,
        in_specs=[anywhere] * 4,
        out_specs=[anywhere] * 4,
        out_shape=[
            jax.ShapeDtypeStruct((nz, ncore, own, width), bf16),
            jax.ShapeDtypeStruct((nz * wrows, ci), bf16),
            jax.ShapeDtypeStruct((nz * wrows, 3 * cq), bf16),
            jax.ShapeDtypeStruct((nz,) + small.shape, bf16),
        ],
        scratch_shapes=[
            pltpu.VMEM((nz, piece, zi), bf16),
            pltpu.VMEM((nz, 3, piece, zq), bf16),
            dma((nz,)), dma((nz,)), dma((nz,)), dma((nz,)),
            dma((nz,)), dma((nz,)),
            dma((nz,)), dma((nz,)), dma((nz, 3)), dma((nz, 3)),
            dma((nz, nctx)), dma((nz, nctx)), dma((nz, nctx, 3)), dma((nz, nctx, 3)),
            dma((5,)), dma((nz,)), dma((nz,)),
        ],
        compiler_params=pltpu.CompilerParams(collective_id=1, has_side_effects=True),
        name="front",
    )(tokens, w_in, w_qkv, small)


def turn_table(length):
    half = ROT // 2
    power = -(np.arange(half, dtype=np.float32) * np.float32(2.0)) / np.float32(ROT)
    angles = np.arange(length, dtype=np.float32)[:, None] * np.power(np.float32(ROT_BASE), power)
    table = np.zeros((3, length, 128), np.float32)
    table[0] = 1.0
    table[0, :, :half] = table[0, :, half:ROT] = np.cos(angles)
    table[1, :, :half] = -np.sin(angles)
    table[2, :, half:ROT] = np.sin(angles)
    return table


def turned(u, cosine, minus, plus):
    half = ROT // 2
    return u * cosine + pltpu.roll(u, 128 - half, 1) * minus + pltpu.roll(u, half, 1) * plus


def stats(x):
    center = x - jnp.mean(x, axis=-1, keepdims=True)
    inv = lax.rsqrt(jnp.mean(center * center, axis=-1, keepdims=True) + EPSILON)
    return center * inv, inv


def cost(flops, nbytes, trans=0):
    return pl.CostEstimate(flops=int(flops), bytes_accessed=int(nbytes), transcendentals=int(trans))


def projections(nz, ids, place, tok, w, bias, gain, offset, table):
    rows, width = tok.shape
    step = rows // nz
    blocks = step // BLOCK
    cols = w.shape[1]
    hc = cols // 3

    def kernel(ids_ref, place_ref, tok_ref, w_ref, b_ref, g_ref, o_ref, t_ref, n_ref, out_ref):
        xhat, inv = stats(tok_ref[...].astype(f32))
        normed = (xhat * g_ref[...] + o_ref[...]).astype(bf16)
        n_ref[...] = normed
        project = jnp.dot(normed, w_ref[...], preferred_element_type=f32) + b_ref[...]
        out_ref[...] = project.astype(bf16)
        first = place_ref[0] == 1

        @pl.when(first)
        def _():
            for b in range(blocks):
                at = pl.ds(pl.multiple_of(ids_ref[pl.program_id(0) * blocks + b] * BLOCK, BLOCK), BLOCK)
                c, m, p = t_ref[0, at, :], t_ref[1, at, :], t_ref[2, at, :]
                for g in range(2):
                    u = project[b * BLOCK : (b + 1) * BLOCK, g * hc : g * hc + 128]
                    out_ref[b * BLOCK : (b + 1) * BLOCK, g * hc : g * hc + 128] = turned(
                        u, c, m, p
                    ).astype(bf16)

    whole = lambda shape: pl.BlockSpec(shape, lambda i, *_: (0,) * len(shape))
    return pl.pallas_call(
        kernel,
        grid_spec=pltpu.PrefetchScalarGridSpec(
            num_scalar_prefetch=2,
            grid=(nz,),
            in_specs=[
                pl.BlockSpec((step, width), lambda i, *_: (i, 0)),
                whole((width, cols)),
                whole((1, cols)),
                whole((1, width)),
                whole((1, width)),
                whole(table.shape),
            ],
            out_specs=[
                pl.BlockSpec((step, width), lambda i, *_: (i, 0)),
                pl.BlockSpec((step, cols), lambda i, *_: (i, 0)),
            ],
        ),
        out_shape=[
            jax.ShapeDtypeStruct((rows, width), bf16),
            jax.ShapeDtypeStruct((rows, cols), bf16),
        ],
        compiler_params=BIG,
        cost_estimate=cost(2 * rows * width * cols, 4 * rows * width + 2 * width * cols),
        name="projections",
    )(ids, place, tok, w, bias, gain, offset, table)


def feed_forward(nz, tok, w, bias, gain, offset):
    rows, width = tok.shape
    step = rows // nz
    cols = w.shape[1]

    def kernel(tok_ref, w_ref, b_ref, g_ref, o_ref, n_ref, a_ref, d_ref):
        xhat, inv = stats(tok_ref[...].astype(f32))
        normed = (xhat * g_ref[...] + o_ref[...]).astype(bf16)
        n_ref[...] = normed
        v = jnp.dot(normed, w_ref[...], preferred_element_type=f32) + b_ref[...]
        gate = 0.5 * (1.0 + lax.erf(v * (0.5**0.5)))
        a_ref[...] = (v * gate).astype(bf16)
        bell = jnp.exp(v * v * -0.5) * ((2.0 * math.pi) ** -0.5)
        d_ref[...] = (gate + v * bell).astype(bf16)

    whole = lambda shape: pl.BlockSpec(shape, lambda i: (0, 0))
    part = lambda n: pl.BlockSpec((step, n), lambda i: (i, 0))
    return pl.pallas_call(
        kernel,
        grid=(nz,),
        in_specs=[part(width), whole((width, cols)), whole((1, cols)), whole((1, width)), whole((1, width))],
        out_specs=[part(width), part(cols), part(cols)],
        out_shape=[
            jax.ShapeDtypeStruct((rows, width), bf16),
            jax.ShapeDtypeStruct((rows, cols), bf16),
            jax.ShapeDtypeStruct((rows, cols), bf16),
        ],
        compiler_params=BIG,
        cost_estimate=cost(2 * rows * width * cols, 4 * rows * width + 2 * width * cols, 2 * rows * cols),
        name="feed_forward",
    )(tok, w, bias, gain, offset)


def layer_out(nz, core, mixed, w_dense, active, w_out):
    rows, hc = mixed.shape
    width = w_out.shape[1]
    step = rows // nz
    units = active.shape[1]

    def kernel(core_ref, m_ref, wd_ref, a_ref, wo_ref, out_ref):
        out_ref[...] = (
            jnp.dot(m_ref[...], wd_ref[...], preferred_element_type=f32)
            + jnp.dot(a_ref[...], wo_ref[...], preferred_element_type=f32)
        ).astype(bf16)

    part = lambda n: pl.BlockSpec((step, n), lambda i, c: (i, 0))
    held = lambda n: pl.BlockSpec((n, width), lambda i, c: (c[0], 0))
    return pl.pallas_call(
        kernel,
        grid_spec=pltpu.PrefetchScalarGridSpec(
            num_scalar_prefetch=1,
            grid=(nz,),
            in_specs=[part(hc), held(hc), part(units), held(units)],
            out_specs=part(width),
        ),
        out_shape=jax.ShapeDtypeStruct((rows, width), bf16),
        compiler_params=BIG,
        cost_estimate=cost(2 * rows * width * (hc + units), 4 * rows * width + 2 * width * units),
        name="layer_out",
    )(core, mixed, w_dense, active, w_out)


def grad_of_mixed(nz, core, cot, w_dense, hc):
    rows, width = cot.shape
    step = rows // nz

    def kernel(core_ref, c_ref, w_ref, out_ref):
        out_ref[...] = lax.dot_general(
            c_ref[...], w_ref[...], NT, preferred_element_type=f32
        ).astype(bf16)

    return pl.pallas_call(
        kernel,
        grid_spec=pltpu.PrefetchScalarGridSpec(
            num_scalar_prefetch=1,
            grid=(nz,),
            in_specs=[
                pl.BlockSpec((step, width), lambda i, c: (i, 0)),
                pl.BlockSpec((hc, width), lambda i, c: (c[0], 0)),
            ],
            out_specs=pl.BlockSpec((step, hc), lambda i, c: (i, 0)),
        ),
        out_shape=jax.ShapeDtypeStruct((rows, hc), bf16),
        compiler_params=BIG,
        cost_estimate=cost(2 * rows * width * hc, 2 * rows * width),
        name="grad_of_mixed",
    )(core, cot, w_dense)


def grad_of_hidden(nz, core, cot, w_out, slope):
    rows, width = cot.shape
    step = rows // nz
    units = slope.shape[1]

    def kernel(core_ref, c_ref, w_ref, d_ref, out_ref, sum_ref):
        g = lax.dot_general(c_ref[...], w_ref[...], NT, preferred_element_type=f32)
        g = (g * d_ref[...].astype(f32)).astype(bf16)
        out_ref[...] = g

        @pl.when(pl.program_id(0) == 0)
        def _():
            sum_ref[...] = jnp.zeros_like(sum_ref)

        sum_ref[...] += jnp.sum(g.astype(f32), axis=0, keepdims=True)

    return pl.pallas_call(
        kernel,
        grid_spec=pltpu.PrefetchScalarGridSpec(
            num_scalar_prefetch=1,
            grid=(nz,),
            in_specs=[
                pl.BlockSpec((step, width), lambda i, c: (i, 0)),
                pl.BlockSpec((units, width), lambda i, c: (c[0], 0)),
                pl.BlockSpec((step, units), lambda i, c: (i, 0)),
            ],
            out_specs=[
                pl.BlockSpec((step, units), lambda i, c: (i, 0)),
                pl.BlockSpec((1, units), lambda i, c: (0, 0)),
            ],
        ),
        out_shape=[
            jax.ShapeDtypeStruct((rows, units), bf16),
            jax.ShapeDtypeStruct((1, units), f32),
        ],
        compiler_params=BIG,
        cost_estimate=cost(2 * rows * width * units, 2 * rows * width + 2 * width * units),
        name="grad_of_hidden",
    )(core, cot, w_out, slope)


def norm_back(nz, grad, w, tok, gain, other, sums):
    rows, width = tok.shape
    step = rows // nz
    cols = grad.shape[1]

    def kernel(*refs):
        g_ref, w_ref, t_ref, gain_ref = refs[:4]
        at = 4
        if other is not None:
            other_ref = refs[at]
            at += 1
        e_ref, s_ref = refs[at : at + 2]
        gn = lax.dot_general(g_ref[...], w_ref[...], NT, preferred_element_type=f32)
        xhat, inv = stats(t_ref[...].astype(f32))
        e = gn * gain_ref[...]
        if other is not None:
            e = e + other_ref[...].astype(f32)
        e_ref[...] = e.astype(bf16)

        @pl.when(pl.program_id(0) == 0)
        def _():
            s_ref[...] = jnp.zeros_like(s_ref)
            if sums:
                refs[at + 2][...] = jnp.zeros_like(refs[at + 2])

        s_ref[0:1, :] += jnp.sum(gn * xhat, axis=0, keepdims=True)
        s_ref[1:2, :] += jnp.sum(gn, axis=0, keepdims=True)
        if sums:
            refs[at + 2][...] += jnp.sum(g_ref[...].astype(f32), axis=0, keepdims=True)

    part = lambda n: pl.BlockSpec((step, n), lambda i: (i, 0))
    whole = lambda shape: pl.BlockSpec(shape, lambda i: (0, 0))
    ins = [grad, w, tok, gain] + ([] if other is None else [other])
    return pl.pallas_call(
        kernel,
        grid=(nz,),
        in_specs=[part(cols), whole((width, cols)), part(width), whole((1, width))]
        + ([] if other is None else [part(width)]),
        out_specs=[part(width), whole((2, width))] + ([whole((1, cols))] if sums else []),
        out_shape=[
            jax.ShapeDtypeStruct((rows, width), bf16),
            jax.ShapeDtypeStruct((2, width), f32),
        ]
        + ([jax.ShapeDtypeStruct((1, cols), f32)] if sums else []),
        compiler_params=BIG,
        cost_estimate=cost(2 * rows * width * cols, 6 * rows * width + 2 * width * cols),
        name="norm_back",
    )(*ins)


def attention_forward(ids, order, qkv, tile):
    rows = qkv.shape[0]
    blocks = rows // BLOCK

    def kernel(ids_ref, order_ref, x_ref, o_ref, lse_ref, q_ref, k_ref, v_ref, s_ref):
        for b in range(blocks):
            at = pl.ds(pl.multiple_of(order_ref[b] * BLOCK, BLOCK), BLOCK)
            here = slice(b * BLOCK, (b + 1) * BLOCK)
            for i, ref in enumerate((q_ref, k_ref, v_ref)):
                ref[here, :] = x_ref[at, i * HD : (i + 1) * HD]
        for t in range(rows // tile):
            mine = slice(t * tile, (t + 1) * tile)
            n = (t + 1) * tile
            s = lax.dot_general(q_ref[mine, :], k_ref[:n, :], NT, preferred_element_type=f32)
            s = s * SCALE
            seen = t * tile + lax.broadcasted_iota(jnp.int32, (tile, n), 0) >= (
                lax.broadcasted_iota(jnp.int32, (tile, n), 1)
            )
            s = jnp.where(seen, s, -1e30)
            top = jnp.max(s, axis=-1, keepdims=True)
            e = jnp.exp(s - top)
            total = jnp.sum(e, axis=-1, keepdims=True)
            p = (e * (1.0 / total)).astype(bf16)
            s_ref[mine, :] = jnp.dot(p, v_ref[:n, :], preferred_element_type=f32).astype(bf16)
            lse_ref[mine, :] = top + jnp.log(total)
        for b in range(blocks):
            at = pl.ds(pl.multiple_of(ids_ref[b] * BLOCK, BLOCK), BLOCK)
            o_ref[b * BLOCK : (b + 1) * BLOCK, :] = s_ref[at, :]

    smem = pl.BlockSpec(memory_space=pltpu.SMEM)
    vmem = pl.BlockSpec(memory_space=pltpu.VMEM)
    return pl.pallas_call(
        kernel,
        in_specs=[smem, smem, vmem],
        out_specs=[vmem, vmem],
        out_shape=[
            jax.ShapeDtypeStruct((rows, HD), bf16),
            jax.ShapeDtypeStruct((rows, 1), f32),
        ],
        scratch_shapes=[pltpu.VMEM((rows, HD), bf16)] * 4,
        compiler_params=BIG,
        cost_estimate=cost(2.3 * rows * rows * HD, 8 * rows * HD, rows * rows / 2),
        name="attention_forward",
    )(ids, order, qkv)


def attention_backward(ids, order, qkv, grad, lse, table, tile):
    rows = qkv.shape[0]
    blocks = rows // BLOCK

    def kernel(ids_ref, order_ref, x_ref, g_ref, lse_ref, t_ref, out_ref, q_ref, k_ref, v_ref, m_ref,
               r_ref, dk_ref, dv_ref):
        for b in range(blocks):
            at = pl.ds(pl.multiple_of(order_ref[b] * BLOCK, BLOCK), BLOCK)
            here = slice(b * BLOCK, (b + 1) * BLOCK)
            for i, ref in enumerate((q_ref, k_ref, v_ref)):
                ref[here, :] = x_ref[at, i * HD : (i + 1) * HD]
            m_ref[here, :] = g_ref[at, :]
        for t in reversed(range(rows // tile)):
            mine = slice(t * tile, (t + 1) * tile)
            n = (t + 1) * tile
            q, g = q_ref[mine, :], m_ref[mine, :]
            s = lax.dot_general(q, k_ref[:n, :], NT, preferred_element_type=f32) * SCALE
            seen = t * tile + lax.broadcasted_iota(jnp.int32, (tile, n), 0) >= (
                lax.broadcasted_iota(jnp.int32, (tile, n), 1)
            )
            p = jnp.where(seen, jnp.exp(s - lse_ref[mine, :]), 0.0)
            dp = lax.dot_general(g, v_ref[:n, :], NT, preferred_element_type=f32)
            shift = jnp.sum(p * dp, axis=-1, keepdims=True)
            ds = (p * (dp - shift)).astype(bf16)
            low = p.astype(bf16)
            dq = jnp.dot(ds, k_ref[:n, :], preferred_element_type=f32) * SCALE
            r_ref[mine, :128] = turned(
                dq[:, :128], t_ref[0, mine, :], -t_ref[1, mine, :], -t_ref[2, mine, :]
            ).astype(bf16)
            r_ref[mine, 128:HD] = dq[:, 128:].astype(bf16)
            dk = lax.dot_general(ds, q, TN, preferred_element_type=f32) * SCALE
            dv = lax.dot_general(low, g, TN, preferred_element_type=f32)
            if n == rows:
                dk_ref[...] = dk
                dv_ref[...] = dv
            else:
                dk_ref[:n, :] += dk
                dv_ref[:n, :] += dv
        r_ref[:, HD : HD + 128] = turned(
            dk_ref[:, :128], t_ref[0], -t_ref[1], -t_ref[2]
        ).astype(bf16)
        r_ref[:, HD + 128 : 2 * HD] = dk_ref[:, 128:].astype(bf16)
        r_ref[:, 2 * HD :] = dv_ref[...].astype(bf16)
        for b in range(blocks):
            at = pl.ds(pl.multiple_of(ids_ref[b] * BLOCK, BLOCK), BLOCK)
            out_ref[b * BLOCK : (b + 1) * BLOCK, :] = r_ref[at, :]

    smem = pl.BlockSpec(memory_space=pltpu.SMEM)
    vmem = pl.BlockSpec(memory_space=pltpu.VMEM)
    return pl.pallas_call(
        kernel,
        in_specs=[smem, smem, vmem, vmem, vmem, vmem],
        out_specs=vmem,
        out_shape=jax.ShapeDtypeStruct((rows, 3 * HD), bf16),
        scratch_shapes=[pltpu.VMEM((rows, HD), bf16)] * 4
        + [pltpu.VMEM((rows, 3 * HD), bf16)]
        + [pltpu.VMEM((rows, HD), f32)] * 2,
        compiler_params=BIG,
        cost_estimate=cost(6 * rows * rows * HD, 20 * rows * HD, rows * rows / 2),
        name="attention_backward",
    )(ids, order, qkv, grad, lse, table)


def gather_plane(nchip, chip, core, src, dst_of, send, recv, local):
    sibling = {"core": 1 - core}
    rows = src.shape[0]
    half = rows // 2
    here = dst_of(chip, core)
    begun = [pltpu.make_async_copy(src, here, local)]
    begun.append(remote(src, here, send.at[0], recv.at[0], sibling))
    relays = []
    arrivals = []

    def cut(ref, h):
        return ref.at[pl.ds(h * half, half), :]

    if nchip == 4:
        beside = chip + 1 - 2 * lax.rem(chip, 2)
        below = lax.rem(chip + 2, 4)
        across = 3 - chip
        order = ((beside, 0, 1), (below, 1, 2), (beside, 1, 1), (below, 0, 2))
        for i, (to, h, d) in enumerate(order):
            slot = 4 + 2 * d + h
            begun.append(
                remote(cut(src, h), cut(here, h), send.at[slot], recv.at[slot], {"chip": to})
            )

        def passing(owner, h, to):
            part = cut(dst_of(owner, core), h)
            return remote(part, part, send.at[10 + h], recv.at[10 + h], {"chip": to})

        relays = [(passing(beside, 0, below), beside, 0, 6), (passing(below, 1, beside), below, 1, 9)]
        arrivals = [(beside, 1, 7, 1), (below, 0, 8, 2), (across, 0, 10, 3), (across, 1, 11, 3)]
        others = [(beside, 1), (below, 2), (across, 3)]
    else:
        others = [(lax.rem(chip + d, nchip), d) for d in range(1, nchip)]
        for to, d in others:
            begun.append(
                remote(src, here, send.at[nchip + d], recv.at[nchip + chip], {"chip": to})
            )

    def side(owner, slot):
        part = dst_of(owner, core)
        return remote(part, part, send.at[slot], recv.at[slot], sibling)

    def slot_of(owner, d):
        return d if nchip == 4 else 2 * nchip + owner

    def first():
        for copy in begun:
            copy.start()

    def onward():
        if nchip == 4:
            for copy, owner, h, slot in relays:
                part = cut(dst_of(owner, core), h)
                remote(part, part, send.at[0], recv.at[slot], sibling).wait_recv()
                copy.start()

    def pass_on():
        if nchip == 4:
            for owner, h, slot, d in arrivals:
                part = cut(dst_of(owner, core), h)
                remote(part, part, send.at[0], recv.at[slot], sibling).wait_recv()
                if slot != 10:
                    side(owner, d).start()
        else:
            for owner, d in others:
                part = dst_of(owner, core)
                remote(part, part, send.at[0], recv.at[nchip + owner], sibling).wait_recv()
                side(owner, slot_of(owner, d)).start()

    def last():
        begun[0].wait()
        for copy in begun[1:]:
            copy.wait_send()
        for copy, owner, h, slot in relays:
            copy.wait_send()
        there = dst_of(chip, 1 - core)
        remote(there, there, send.at[0], recv.at[0], sibling).wait_recv()
        for owner, d in others:
            side(owner, slot_of(owner, d)).wait_send()
            there = dst_of(owner, 1 - core)
            remote(there, there, send.at[0], recv.at[slot_of(owner, d)], sibling).wait_recv()

    return first, onward, pass_on, last


def scatter_plane(nchip, chip, part, own, first, second, send, recv, local):
    halves = own.shape[0]
    copies = []
    shape = own.shape[2:]

    def add(dst, terms):
        def rows(lead):
            @pl.loop(0, shape[-2] // 16)
            def _(i):
                at = lead + (pl.ds(pl.multiple_of(i * 16, 16), 16), slice(None))
                acc = dst[at].astype(f32)
                for term in terms:
                    acc = acc + term[at].astype(f32)
                dst[at] = acc.astype(bf16)

        if len(shape) == 2:
            rows(())
        else:

            @pl.loop(0, shape[0])
            def _(b):
                rows((b,))

    if nchip == 4:
        beside = chip + 1 - 2 * lax.rem(chip, 2)
        below = lax.rem(chip + 2, 4)
        across = 3 - chip
        ways = [(beside, below), (below, beside)]
        kept = [
            [
                pltpu.make_async_copy(part(chip, h), own.at[h, 0], local.at[h, 0]),
                pltpu.make_async_copy(part(ways[h][1], h), own.at[h, 1], local.at[h, 1]),
            ]
            for h in range(2)
        ]
        leave = [
            [
                remote(
                    part(across, h), first.at[h, 1], send.at[h, 1], recv.at[h, 1],
                    {"chip": ways[h][0]},
                ),
                remote(
                    part(ways[h][0], h), first.at[h, 0], send.at[h, 0], recv.at[h, 0],
                    {"chip": ways[h][0]},
                ),
            ]
            for h in range(2)
        ]
        follow = [
            remote(
                own.at[h, 1], second.at[h], send.at[h, 2], recv.at[h, 2], {"chip": ways[h][1]}
            )
            for h in range(2)
        ]

        def begin():
            for i in range(2):
                for h in range(2):
                    leave[h][i].start()
            for h in range(2):
                kept[h][1].start()
                kept[h][0].start()

        def middle():
            for h in range(2):
                kept[h][1].wait()
                leave[h][0].wait_recv()
                add(own.at[h, 1], [first.at[h, 1]])
                follow[h].start()

        def finish():
            for h in range(2):
                kept[h][0].wait()
                leave[h][1].wait_recv()
                follow[h].wait_recv()
                add(own.at[h, 0], [first.at[h, 0], second.at[h]])

        def last():
            for h in range(2):
                for copy in leave[h] + [follow[h]]:
                    copy.wait_send()
    else:
        to = [lax.rem(chip + d, nchip) for d in range(nchip)]
        kept = pltpu.make_async_copy(part(chip, 0), own.at[0, 0], local.at[0, 0])
        leave = [
            remote(part(to[d], 0), first.at[0, d], send.at[0, d], recv.at[0, d], {"chip": to[d]})
            for d in range(1, nchip)
        ]

        def begin():
            for copy in leave:
                copy.start()
            kept.start()

        def middle():
            pass

        def finish():
            kept.wait()
            for copy in leave:
                copy.wait_recv()
            add(own.at[0, 0], [first.at[0, d] for d in range(1, nchip)])

        def last():
            for copy in leave:
                copy.wait_send()

    return begin, middle, finish, last


def tail(nz, nchip, ncore, dwo, dwd, dwi, dwq, part_e, vectors):
    width = dwo.shape[1]
    ro, rd = dwo.shape[0] // nchip, dwd.shape[0] // nchip
    halves = 2 if nchip == 4 else 1
    hz = nz // halves
    ho, hd = ro // halves, rd // halves
    ci, cq = dwi.shape[2], dwq.shape[1] // 3
    wrows = width // nz
    ri = wrows // nchip
    own = part_e.shape[0] // nz // ncore
    vr = vectors.shape[0]
    dwo = dwo.reshape(nchip, ro, width)
    dwq = dwq.reshape(nz, nchip, ri, 3 * cq)
    dwd = dwd.reshape(nchip, rd, width)
    part_e = part_e.reshape(nz, ncore, own, width)

    def kernel(
        dwo_ref, dwd_ref, dwi_ref, dwq_ref, pe_ref, vec_ref,
        go_ref, gd_ref, gi_ref, gq_ref, e_ref, vsum_ref,
        oo, fo, so, oq, fq, sq, od, fd, sd, ti, tq, se, me, ze, v1, v2, v3,
        ro_s, ro_r, ro_l, rq_s, rq_r, rq_l, rd_s, rd_r, rd_l, x_s, x_r, x_l, ez_s, ez_r, t_s, t_r, t_l,
        go_s, go_r, gd_s, gd_r, gi_s, gi_r, gq_s, gq_r, own_l,
        v_s, v_r, v_l,
    ):
        z = lax.axis_index("seq")
        chip = lax.axis_index("chip")
        core = lax.axis_index("core")
        sibling = {"core": 1 - core}

        def z_at(d):
            return lax.rem(z + d, nz)

        def chip_at(d):
            return lax.rem(chip + d, nchip)

        greet(
            [{"seq": z_at(d)} for d in range(1, nz)]
            + [{"chip": chip_at(d)} for d in range(1, nchip)]
            + [sibling]
        )

        def turn(kind, part, turned):
            copies = [
                remote(
                    part(z_at(d)), turned.at[z], t_s.at[kind, d], t_r.at[kind, z],
                    {"seq": z_at(d)},
                )
                for d in range(1, nz)
            ]
            copies.append(pltpu.make_async_copy(part(z), turned.at[z], t_l.at[kind]))
            for copy in copies:
                copy.start()
            return copies

        def turned_at(kind, part, turned, source):
            return remote(part, turned.at[source], t_s.at[kind, 0], t_r.at[kind, source], sibling)

        sum_q = scatter_plane(
            nchip, chip, lambda c, h: dwq_ref.at[pl.ds(h * hz, hz), c], oq, fq, sq, rq_s, rq_r, rq_l
        )
        sum_o = scatter_plane(
            nchip, chip, lambda c, h: dwo_ref.at[c, pl.ds(h * ho, ho)], oo, fo, so, ro_s, ro_r, ro_l
        )
        sum_d = scatter_plane(
            nchip, chip, lambda c, h: dwd_ref.at[c, pl.ds(h * hd, hd)], od, fd, sd, rd_s, rd_r, rd_l
        )
        turn_i = turn(0, lambda to: dwi_ref.at[to], ti)
        sum_q[0]()

        exchanged = [
            remote(pe_ref.at[:, 1 - core], se, x_s.at[0], x_r.at[0], sibling),
        ]
        keep = [
            pltpu.make_async_copy(pe_ref.at[:, core], me, x_l.at[0]),
        ]
        for copy in exchanged + keep:
            copy.start()

        v_own = pltpu.make_async_copy(vec_ref, v1.at[chip], v_l.at[0])
        v_own.start()
        v_chips = [
            remote(vec_ref, v1.at[chip], v_s.at[d], v_r.at[chip], {"chip": chip_at(d)})
            for d in range(1, nchip)
        ]
        for copy in v_chips:
            copy.start()

        def pair_sum(which, mine, theirs):
            exchanged[which].wait_recv()
            keep[which].wait()

            @pl.loop(0, nz)
            def _(b):
                @pl.loop(0, own // 16)
                def _(i):
                    at = pl.ds(pl.multiple_of(i * 16, 16), 16)
                    mine[b, at, :] = (
                        mine[b, at, :].astype(f32) + theirs[b, at, :].astype(f32)
                    ).astype(bf16)

        def z_sends(which, mine, landing):
            return [
                remote(
                    mine.at[z_at(d)], landing.at[d], ez_s.at[which, d], ez_r.at[which, d],
                    {"seq": z_at(d)},
                )
                for d in range(1, nz)
            ]

        def z_sum(copies, mine, landing, out):
            for copy in copies:
                copy.wait_recv()

            @pl.loop(0, own // 16)
            def _(i):
                at = pl.ds(pl.multiple_of(i * 16, 16), 16)
                acc = mine[z, at, :].astype(f32)
                for d in range(1, nz):
                    acc = acc + landing[d, at, :].astype(f32)
                out[at, :] = acc

        pair_sum(0, me, se)
        sum_q[1]()
        sum_o[0]()
        sum_d[0]()

        go_at = lambda c, k, h: go_ref.at[pl.ds(k * (ro * nchip) + c * ro + h * ho, ho), :]
        gd_at = lambda c, k, h: gd_ref.at[pl.ds(k * (rd * nchip) + c * rd + h * hd, hd), :]
        gi_at = lambda c, k, s: gi_ref.at[
            pl.ds(c * ri, ri), pl.ds((s * ncore + k) * ci, ci)
        ]
        gq_at = lambda c, k, s, g: gq_ref.at[
            pl.ds(c * ri, ri), pl.ds(g * nz * ncore * cq + (s * ncore + k) * cq, cq)
        ]
        group = functools.partial(gather_plane, nchip, chip, core)
        groups = []
        for dz in range(1, nz):
            turned_at(0, dwi_ref.at[0], ti, z_at(dz)).wait_recv()
        turn_i[-1].wait()
        for source in range(nz):
            groups.append(
                group(
                    ti.at[source], functools.partial(gi_at, s=source), gi_s.at[source],
                    gi_r.at[source], own_l.at[source],
                )
            )
            groups[-1][0]()
        sent_e = z_sends(0, me, ze)
        for copy in sent_e:
            copy.start()
        sum_q[2]()
        turn_q = turn(1, lambda to: oq.at[to // hz, 0, lax.rem(to, hz)], tq)

        v_own.wait()
        for d in range(1, nchip):
            other = chip_at(d)
            remote(vec_ref, v1.at[other], v_s.at[d], v_r.at[other], sibling).wait_recv()
        total = v1[0]
        for d in range(1, nchip):
            total = total + v1[d]
        v2[core] = total
        v_side = remote(v2.at[core], v2.at[core], v_s.at[nchip], v_r.at[nchip], sibling)
        v_side.start()

        v_side.wait_recv()
        vz = v2[0]
        for c in range(1, ncore):
            vz = vz + v2[c]
        v3[z] = vz
        v_zs = [
            remote(v3.at[z], v3.at[z], v_s.at[nchip + d], v_r.at[nchip + 1 + z], {"seq": z_at(d)})
            for d in range(1, nz)
        ]
        for copy in v_zs:
            copy.start()

        sum_o[1]()
        sum_d[1]()
        for first, onward, pass_on, last in groups:
            onward()
        sum_o[2]()
        sum_d[2]()
        for h in range(halves):
            for at, (buf, place, sends, recvs) in enumerate(
                ((oo, go_at, go_s, go_r), (od, gd_at, gd_s, gd_r))
            ):
                groups.append(
                    group(
                        buf.at[h, 0], functools.partial(place, h=h), sends.at[h], recvs.at[h],
                        own_l.at[nz + 2 * at + h],
                    )
                )
                groups[-1][0]()

        for dz in range(1, nz):
            turned_at(1, oq.at[0, 0, 0], tq, z_at(dz)).wait_recv()
        turn_q[-1].wait()
        later = []
        for source in range(nz):
            for g in range(3):
                later.append(
                    group(
                        tq.at[source, :, pl.ds(g * cq, cq)],
                        functools.partial(gq_at, s=source, g=g),
                        gq_s.at[source, g], gq_r.at[source, g], own_l.at[4 + nz + 3 * source + g],
                    )
                )
        for first, onward, pass_on, last in later:
            first()
        for first, onward, pass_on, last in groups[nz:]:
            onward()
        for first, onward, pass_on, last in groups[:nz]:
            pass_on()
        for first, onward, pass_on, last in later:
            onward()
        for first, onward, pass_on, last in groups[nz:]:
            pass_on()

        for d in range(1, nz):
            other = z_at(d)
            remote(v3.at[0], v3.at[other], v_s.at[0], v_r.at[nchip + 1 + other], sibling).wait_recv()
        total = v3[0]
        for d in range(1, nz):
            total = total + v3[d]
        vsum_ref[...] = total

        z_sum(sent_e, me, ze, e_ref)
        for first, onward, pass_on, last in later:
            pass_on()

        for first, onward, pass_on, last in groups + later:
            last()
        for begin, middle, finish, last in (sum_o, sum_q, sum_d):
            last()
        for copy in exchanged + sent_e + v_chips + v_zs + [v_side]:
            copy.wait_send()
        for copy in turn_i[:-1] + turn_q[:-1]:
            copy.wait_send()

    dma = pltpu.SemaphoreType.DMA
    anywhere = pl.BlockSpec(memory_space=pl.ANY)
    vmem = pl.BlockSpec(memory_space=pltpu.VMEM)
    out_shape = [
        jax.ShapeDtypeStruct((ncore * nchip * ro, width), bf16),
        jax.ShapeDtypeStruct((ncore * nchip * rd, width), bf16),
        jax.ShapeDtypeStruct((wrows, nz * ncore * ci), bf16),
        jax.ShapeDtypeStruct((wrows, 3 * nz * ncore * cq), bf16),
        jax.ShapeDtypeStruct((own, width), f32),
        jax.ShapeDtypeStruct((vr, 128), f32),
    ]
    ranked = (nz, own, width)
    slots = max(3 * nchip, 12)
    pair = 2 if nchip == 4 else 1
    nfirst = 2 if nchip == 4 else nchip
    return pl.pallas_call(
        kernel,
        in_specs=[anywhere] * 5 + [vmem],
        out_specs=[anywhere] * 4 + [vmem] * 2,
        out_shape=out_shape,
        scratch_shapes=[
            pltpu.VMEM((halves, pair, ho, width), bf16),
            pltpu.VMEM((halves, nfirst, ho, width), bf16),
            pltpu.VMEM((halves, ho, width), bf16),
            pltpu.VMEM((halves, pair, hz, ri, 3 * cq), bf16),
            pltpu.VMEM((halves, nfirst, hz, ri, 3 * cq), bf16),
            pltpu.VMEM((halves, hz, ri, 3 * cq), bf16),
            pltpu.VMEM((halves, pair, hd, width), bf16),
            pltpu.VMEM((halves, nfirst, hd, width), bf16),
            pltpu.VMEM((halves, hd, width), bf16),
            pltpu.VMEM((nz, ri, ci), bf16),
            pltpu.VMEM((nz, ri, 3 * cq), bf16),
            pltpu.VMEM(ranked, bf16),
            pltpu.VMEM(ranked, bf16),
            pltpu.VMEM(ranked, bf16),
            pltpu.VMEM((nchip, vr, 128), f32),
            pltpu.VMEM((ncore, vr, 128), f32),
            pltpu.VMEM((nz, vr, 128), f32),
            dma((halves, nchip)), dma((halves, nchip)), dma((halves, 2)),
            dma((halves, nchip)), dma((halves, nchip)), dma((halves, 2)),
            dma((halves, nchip)), dma((halves, nchip)), dma((halves, 2)),
            dma((2,)), dma((2,)), dma((2,)),
            dma((2, nz)), dma((2, nz)),
            dma((2, nz)), dma((2, nz)), dma((2,)),
            dma((halves, slots)), dma((halves, slots)),
            dma((halves, slots)), dma((halves, slots)),
            dma((nz, slots)), dma((nz, slots)),
            dma((nz, 3, slots)), dma((nz, 3, slots)),
            dma((4 + 4 * nz,)),
            dma((nchip + nz,)), dma((nchip + nz + 1,)), dma((1,)),
        ],
        compiler_params=pltpu.CompilerParams(
            collective_id=2, has_side_effects=True, vmem_limit_bytes=60 * 2**20
        ),
        name="tail",
    )(dwo, dwd, dwi, dwq, part_e, vectors)


def on_device(
    nz,
    nchip,
    ncore,
    tokens,
    block_ids,
    cotangent,
    norm1_gain,
    norm1_bias,
    norm2_gain,
    norm2_bias,
    w_qkv,
    b_qkv,
    w_dense,
    b_dense,
    w_in,
    b_in,
    w_out,
    b_out,
):
    own, width = tokens.shape
    z = lax.axis_index("seq")
    chip = lax.axis_index("chip")
    core = lax.axis_index("core")
    ranks = nz * ncore
    rank = z * ncore + core
    rows = ranks * own
    ffr = w_out.shape[0] // ncore
    hc = width // ranks
    split = max(1, HD // hc)
    wrows = width // nz
    blocks = block_ids.shape[1]
    length = blocks * BLOCK
    core_at = core.reshape(1)

    parts = [norm1_gain, norm1_bias, norm2_gain, norm2_bias, b_qkv, b_dense + 0, b_in, b_out,
             block_ids.reshape(-1)]
    sizes = [p.shape[0] for p in parts]
    total = -(-sum(sizes) // 2048) * 2048
    starts = [sum(sizes[:i]) for i in range(len(sizes))]
    small = sum(
        jnp.pad(p.astype(f32), (at, total - at - p.shape[0])) for p, at in zip(parts, starts)
    )
    small = small.astype(bf16).reshape(-1, 128)
    tok, w_in_c, w_qkv_c, small = front(nz, nchip, ncore, tokens, w_in, w_qkv, small)
    tok = tok.reshape(rows, width)
    small = small.reshape(nz, total)

    def vector(i):
        return small[:, starts[i] : starts[i] + sizes[i]].astype(f32).reshape(1, -1)

    gain1, bias1, gain2, bias2 = [vector(i) for i in range(4)]
    bias_c = lax.dynamic_index_in_dim(vector(4).reshape(3, ranks, hc), rank, 1, keepdims=False)
    bias_c = bias_c.reshape(1, 3 * hc)
    bias_in = lax.dynamic_slice_in_dim(vector(6), rank * ffr, ffr, 1)
    ids = vector(8).astype(jnp.int32).reshape(nz, blocks)
    tok, cot_own = lax.optimization_barrier((tok, cotangent))
    cot = lax.all_gather(cot_own, TP, axis=0, tiled=True)

    per_chip = blocks // nchip
    ids_rows = lax.dynamic_slice_in_dim(ids, chip * per_chip, per_chip, 1).reshape(-1)
    ids_seq = lax.dynamic_index_in_dim(ids, chip, 0, keepdims=False)
    slots = jnp.arange(blocks, dtype=jnp.int32)
    order = jnp.sum(jnp.where(ids_seq[None, :] == slots[:, None], slots[None, :], 0), axis=1)
    place = (lax.rem(rank, split) == 0).astype(jnp.int32).reshape(1)
    table = jnp.asarray(turn_table(length))

    def heads_of(x):
        g = x.shape[1] // hc
        if split > 1:
            x = lax.all_gather(x.reshape(rows, g, hc), "core", axis=2, tiled=True)
        x = x.reshape(nz, rows // nz, g * HD)
        return lax.all_to_all(x, "chip", 0, 0, tiled=True).reshape(length, g * HD)

    def heads_back(x):
        g = x.shape[1] // HD
        x = x.reshape(nchip, length // nchip, g * HD)
        x = lax.all_to_all(x, "chip", 0, 0, tiled=True).reshape(rows, g * HD)
        if split > 1:
            x = lax.dynamic_slice_in_dim(x.reshape(rows, g, HD), core * hc, hc, 2)
        return x.reshape(rows, g * hc)

    tile = 256
    normed1, qkv = projections(nz, ids_rows, place, tok, w_qkv_c, bias_c, gain1, bias1, table)
    qkv = heads_of(qkv)
    normed2, active, slope = feed_forward(nz, tok, w_in_c, bias_in, gain2, bias2)
    qkv, active, slope, normed2 = lax.optimization_barrier((qkv, active, slope, normed2))
    attended, lse = attention_forward(ids_seq, order, qkv, tile)
    attended, cot = lax.optimization_barrier((attended, cot))
    mixed = heads_back(attended)

    grad_mixed = grad_of_mixed(nz, core_at, cot, w_dense, hc)
    grad_mixed, cot = lax.optimization_barrier((grad_mixed, cot))
    g = heads_of(grad_mixed)
    grad_hidden, sum_bin = grad_of_hidden(nz, core_at, cot, w_out, slope)
    dw_in = lax.dot_general(normed2, grad_hidden, TN, preferred_element_type=f32).astype(bf16)
    dw_in = dw_in.reshape(nz, nchip, wrows // nchip, ffr).transpose(1, 0, 2, 3)
    dw_in = dw_in.reshape(width, ffr)
    g, dw_in, mixed = lax.optimization_barrier((g, dw_in, mixed))
    s_in = lax.psum_scatter(dw_in, "chip", scatter_dimension=0, tiled=True)
    s_in = s_in.reshape(nz, wrows // nchip, ffr)
    dqkv = attention_backward(ids_seq, order, qkv, g, lse, table, tile)
    dqkv, mixed, active, cot, grad_hidden = lax.optimization_barrier(
        (dqkv, mixed, active, cot, grad_hidden)
    )
    grad_project = heads_back(dqkv)
    part_out = layer_out(nz, core_at, mixed, w_dense, active, w_out)
    dw_out = lax.dot_general(active, cot, TN, preferred_element_type=f32).astype(bf16)
    dw_dense = lax.dot_general(mixed, cot, TN, preferred_element_type=f32).astype(bf16)
    e2, sums2 = norm_back(nz, grad_hidden, w_in_c, tok, gain2, None, False)
    grad_project, part_out, dw_out, dw_dense, e2, s_in = lax.optimization_barrier(
        (grad_project, part_out, dw_out, dw_dense, e2, s_in)
    )
    summed_out = lax.psum_scatter(part_out, TP, scatter_dimension=0, tiled=True).astype(f32)
    dw_qkv = lax.dot_general(normed1, grad_project, TN, preferred_element_type=f32).astype(bf16)
    e_part, sums1, sum_bqkv = norm_back(nz, grad_project, w_qkv_c, tok, gain1, e2, True)

    here = jnp.arange(ranks, dtype=jnp.int32) == rank
    mine_bqkv = jnp.where(here[None, :, None], sum_bqkv.reshape(3, 1, hc), 0.0)
    mine_bin = jnp.where(here[:, None], sum_bin.reshape(1, ffr), 0.0)
    vectors = [
        sums1.reshape(-1),
        sums2.reshape(-1),
        mine_bqkv.reshape(-1),
        jnp.sum(cotangent.astype(f32), axis=0),
        mine_bin.reshape(-1),
    ]
    vectors = jnp.concatenate([v.reshape(-1, 128) for v in vectors])
    g_wout, g_wdense, g_win, g_wqkv, e, sums = tail(
        nz, nchip, ncore, dw_out, dw_dense, s_in, dw_qkv, e_part, vectors
    )
    sums = sums.reshape(-1)
    at = 0
    small_out = []
    for size in (width, width, width, width, 3 * width, width, ranks * ffr):
        small_out.append(lax.dynamic_slice_in_dim(sums, at + z * (size // nz), size // nz))
        at += size
    g_gain1, g_bias1, g_gain2, g_bias2, g_bqkv, g_bdense, g_bin = small_out

    output = (tokens.astype(f32) + summed_out + vector(5) + vector(7)).astype(bf16)
    xhat_own, inv_own = stats(tokens.astype(f32))
    terms = (
        e
        - jnp.mean(e, axis=-1, keepdims=True)
        - xhat_own * jnp.mean(e * xhat_own, axis=-1, keepdims=True)
    ) * inv_own
    grad_tokens = (cotangent.astype(f32) + terms).astype(bf16)
    g_wout, g_wdense, g_win, g_wqkv = [g.astype(f32) for g in (g_wout, g_wdense, g_win, g_wqkv)]
    return (
        output,
        grad_tokens,
        g_gain1,
        g_bias1,
        g_gain2,
        g_bias2,
        g_wqkv,
        g_bqkv,
        g_wdense,
        g_bdense,
        g_win,
        g_bin,
        g_wout,
        g_bdense,
    )


def solution(mesh):
    nz, nctx = mesh.shape["seq"], mesh.shape["ctx"]
    ncore = 2
    nchip = nctx // ncore
    fine = Mesh(mesh.devices.reshape(nz, nchip, ncore), ("seq", "chip", "core"))
    own = P(("seq", "chip", "core"), None)
    vec = P("seq")
    mat = P("seq", None)
    return jax.shard_map(
        functools.partial(on_device, nz, nchip, ncore),
        mesh=fine,
        in_specs=(own, mat, own, vec, vec, vec, vec, mat, vec, mat, vec, mat, vec, mat, vec),
        out_specs=(own, own, vec, vec, vec, vec, mat, vec, mat, vec, mat, vec, mat, vec),
        check_vma=False,
    )
```

```python
import functools
import math

import jax
import jax.numpy as jnp
import numpy as np
from jax import lax
from jax.experimental import pallas as pl
from jax.experimental.pallas import tpu as pltpu
from jax.sharding import Mesh, PartitionSpec as P

HD = 256
ROT = 64
BLOCK = 96
EPSILON = 1e-05
ROT_BASE = 10000.0
SCALE = HD ** (-0.5)
f32 = jnp.float32
bf16 = jnp.bfloat16
TP = ("seq", "core")
MESH = pl.DeviceIdType.MESH
NT = (((1,), (1,)), ((), ()))
TN = (((0,), (0,)), ((), ()))
BIG = pltpu.CompilerParams(vmem_limit_bytes=56 * 2**20)


def remote(src, dst, send, recv, target):
    return pltpu.make_async_remote_copy(
        src_ref=src, dst_ref=dst, send_sem=send, recv_sem=recv, device_id=target,
        device_id_type=MESH,
    )


def greet(targets):
    barrier = pltpu.get_barrier_semaphore()
    for target in targets:
        pl.semaphore_signal(barrier, inc=1, device_id=target, device_id_type=MESH)
    pl.semaphore_wait(barrier, len(targets))


def front(nz, nchip, ncore, tokens, w_in, w_qkv, small):
    own, width = tokens.shape
    wrows, ff = w_in.shape
    heads3 = w_qkv.shape[1]
    nctx = nchip * ncore
    piece = wrows // nctx
    zi, zq = ff // nz, heads3 // 3 // nz
    ci, cq = zi // ncore, zq // ncore

    def kernel(
        tok_ref, wi_ref, wq_ref, sm_ref, tok_out, wi_out, wq_out, sm_out, buf_i, buf_q,
        up_s, up_r, dn_s, dn_r, sib_s, sib_r, zi_s, zi_r, zq_s, zq_r, pi_s, pi_r, pq_s, pq_r, loc, sm_s, sm_r,
    ):
        z = lax.axis_index("seq")
        chip = lax.axis_index("chip")
        core = lax.axis_index("core")
        share = chip * ncore + core
        sibling = {"core": 1 - core}

        def z_at(d):
            return lax.rem(z + d, nz)

        def plane_at(d):
            other = lax.rem(share + d, nctx)
            return other // ncore, lax.rem(other, ncore)

        greet(
            [{"seq": z_at(d)} for d in range(1, nz)]
            + [{"chip": plane_at(d)[0], "core": plane_at(d)[1]} for d in range(1, nctx)]
        )

        rows = pl.ds(share * piece, piece)
        def hop(to):
            to = jnp.clip(to, 0, nz - 1)
            copies = [
                remote(
                    wi_ref.at[rows, pl.ds(to * zi, zi)], buf_i.at[z], zi_s.at[to], zi_r.at[z],
                    {"seq": to},
                )
            ]
            for g in range(3):
                copies.append(
                    remote(
                        wq_ref.at[rows, pl.ds(g * zq * nz + to * zq, zq)], buf_q.at[z, g],
                        zq_s.at[to, g], zq_r.at[z, g], {"seq": to},
                    )
                )
            return copies

        def around(body):
            for distance in range(1, nz):
                for other in (z + distance, z - distance):
                    @pl.when(jnp.logical_and(other >= 0, other < nz))
                    def _():
                        body(jnp.clip(other, 0, nz - 1))

        def up(s):
            shard = z - s
            src = tok_ref if s == 0 else tok_out.at[jnp.maximum(shard, 0), core]
            return remote(
                src, tok_out.at[jnp.maximum(shard, 0), core], up_s.at[s], up_r.at[s],
                {"seq": jnp.minimum(z + 1, nz - 1)},
            )

        def down(s):
            shard = z + s
            src = tok_ref if s == 0 else tok_out.at[jnp.minimum(shard, nz - 1), core]
            return remote(
                src, tok_out.at[jnp.minimum(shard, nz - 1), core], dn_s.at[s], dn_r.at[s],
                {"seq": jnp.maximum(z - 1, 0)},
            )

        def side(shard, own_rows=False):
            src = tok_ref if own_rows else tok_out.at[shard, core]
            return remote(src, tok_out.at[shard, core], sib_s.at[shard], sib_r.at[shard], sibling)

        smalls = [
            remote(sm_ref, sm_out.at[z], sm_s.at[d], sm_r.at[z], {"seq": z_at(d)})
            for d in range(1, nz)
        ]
        for copy in smalls:
            copy.start()

        def send_hop(to):
            for copy in hop(to):
                copy.start()

        around(send_hop)

        @pl.when(z + 1 < nz)
        def _():
            up(0).start()

        @pl.when(z > 0)
        def _():
            down(0).start()

        side(z, True).start()
        locals_ = [
            pltpu.make_async_copy(tok_ref, tok_out.at[z, core], loc.at[0]),
            pltpu.make_async_copy(wi_ref.at[rows, pl.ds(z * zi, zi)], buf_i.at[z], loc.at[1]),
            pltpu.make_async_copy(sm_ref, sm_out.at[z], sm_s.at[0]),
        ] + [
            pltpu.make_async_copy(
                wq_ref.at[rows, pl.ds(g * zq * nz + z * zq, zq)], buf_q.at[z, g], loc.at[2 + g]
            )
            for g in range(3)
        ]
        for copy in locals_:
            copy.start()

        def spread(source, d):
            to_chip, to_core = plane_at(d)
            target_rows = pl.ds(source * wrows + share * piece, piece)
            pairs = [
                (
                    buf_i.at[source, :, pl.ds(to_core * ci, ci)], wi_out.at[target_rows, :],
                    pi_s.at[source, d], pi_r.at[source, share],
                )
            ] + [
                (
                    buf_q.at[source, g, :, pl.ds(to_core * cq, cq)],
                    wq_out.at[target_rows, pl.ds(g * cq, cq)],
                    pq_s.at[source, d, g], pq_r.at[source, share, g],
                )
                for g in range(3)
            ]
            if d == 0:
                return [pltpu.make_async_copy(a, b, c) for a, b, c, r in pairs]
            return [remote(a, b, c, r, {"chip": to_chip, "core": to_core}) for a, b, c, r in pairs]

        def hop_arrival(source):
            remote(buf_i.at[source], buf_i.at[source], zi_s.at[0], zi_r.at[source], sibling).wait_recv()
            for g in range(3):
                remote(
                    buf_q.at[source, g], buf_q.at[source, g], zq_s.at[0, 0], zq_r.at[source, g],
                    sibling,
                ).wait_recv()

        for copy in locals_[1:]:
            copy.wait()
        for d in range(nctx):
            for copy in spread(z, d):
                copy.start()
        def hand_on(source):
            hop_arrival(source)
            for d in range(nctx):
                for copy in spread(source, d):
                    copy.start()

        around(hand_on)

        for s in range(nz - 1):
            from_below = z - 1 - s
            from_above = z + 1 + s

            @pl.when(from_below >= 0)
            def _():
                shard = jnp.maximum(from_below, 0)
                remote(tok_ref, tok_out.at[shard, core], up_s.at[s], up_r.at[s], sibling).wait_recv()
                if s + 1 < nz - 1:
                    @pl.when(z + 1 < nz)
                    def _():
                        up(s + 1).start()
                side(shard).start()

            @pl.when(from_above < nz)
            def _():
                shard = jnp.minimum(from_above, nz - 1)
                remote(tok_ref, tok_out.at[shard, core], dn_s.at[s], dn_r.at[s], sibling).wait_recv()
                if s + 1 < nz - 1:
                    @pl.when(z > 0)
                    def _():
                        down(s + 1).start()
                side(shard).start()

        locals_[0].wait()
        for shard in range(nz):
            remote(tok_ref, tok_out.at[shard, 1 - core], sib_s.at[shard], sib_r.at[shard], sibling).wait()
        for s in range(nz - 1):
            @pl.when(jnp.logical_and(z + 1 < nz, z - s >= 0))
            def _():
                up(s).wait_send()

            @pl.when(jnp.logical_and(z > 0, z + s < nz))
            def _():
                down(s).wait_send()
        for copy in smalls:
            copy.wait_send()

        def hop_left(to):
            for copy in hop(to):
                copy.wait_send()

        around(hop_left)
        for d in range(1, nz):
            other = z_at(d)
            remote(sm_ref, sm_out.at[other], sm_s.at[d], sm_r.at[other], sibling).wait_recv()
        for source in range(nz):
            for d in range(nctx):
                if d == 0:
                    for copy in spread(source, d):
                        copy.wait()
                    continue
                for copy in spread(source, d):
                    copy.wait_send()
                other = lax.rem(share + d, nctx)
                rows_there = pl.ds(source * wrows + other * piece, piece)
                remote(
                    wi_out.at[rows_there, :], wi_out.at[rows_there, :], pi_s.at[source, d],
                    pi_r.at[source, other], sibling,
                ).wait_recv()
                for g in range(3):
                    cols = pl.ds(g * cq, cq)
                    remote(
                        wq_out.at[rows_there, cols], wq_out.at[rows_there, cols],
                        pq_s.at[source, d, g], pq_r.at[source, other, g], sibling,
                    ).wait_recv()

    dma = pltpu.SemaphoreType.DMA
    anywhere = pl.BlockSpec(memory_space=pl.ANY)
    return pl.pallas_call(
        kernel,
        in_specs=[anywhere] * 4,
        out_specs=[anywhere] * 4,
        out_shape=[
            jax.ShapeDtypeStruct((nz, ncore, own, width), bf16),
            jax.ShapeDtypeStruct((nz * wrows, ci), bf16),
            jax.ShapeDtypeStruct((nz * wrows, 3 * cq), bf16),
            jax.ShapeDtypeStruct((nz,) + small.shape, bf16),
        ],
        scratch_shapes=[
            pltpu.VMEM((nz, piece, zi), bf16),
            pltpu.VMEM((nz, 3, piece, zq), bf16),
            dma((nz,)), dma((nz,)), dma((nz,)), dma((nz,)),
            dma((nz,)), dma((nz,)),
            dma((nz,)), dma((nz,)), dma((nz, 3)), dma((nz, 3)),
            dma((nz, nctx)), dma((nz, nctx)), dma((nz, nctx, 3)), dma((nz, nctx, 3)),
            dma((5,)), dma((nz,)), dma((nz,)),
        ],
        compiler_params=pltpu.CompilerParams(collective_id=1, has_side_effects=True),
        name="front",
    )(tokens, w_in, w_qkv, small)


def turn_table(length):
    half = ROT // 2
    power = -(np.arange(half, dtype=np.float32) * np.float32(2.0)) / np.float32(ROT)
    angles = np.arange(length, dtype=np.float32)[:, None] * np.power(np.float32(ROT_BASE), power)
    table = np.zeros((3, length, 128), np.float32)
    table[0] = 1.0
    table[0, :, :half] = table[0, :, half:ROT] = np.cos(angles)
    table[1, :, :half] = -np.sin(angles)
    table[2, :, half:ROT] = np.sin(angles)
    return table


def turned(u, cosine, minus, plus):
    half = ROT // 2
    return u * cosine + pltpu.roll(u, 128 - half, 1) * minus + pltpu.roll(u, half, 1) * plus


def stats(x):
    center = x - jnp.mean(x, axis=-1, keepdims=True)
    inv = lax.rsqrt(jnp.mean(center * center, axis=-1, keepdims=True) + EPSILON)
    return center * inv, inv


def cost(flops, nbytes, trans=0):
    return pl.CostEstimate(flops=int(flops), bytes_accessed=int(nbytes), transcendentals=int(trans))


def projections(nz, ids, place, tok, w, bias, gain, offset, table):
    rows, width = tok.shape
    step = rows // nz
    blocks = step // BLOCK
    cols = w.shape[1]
    hc = cols // 3

    def kernel(ids_ref, place_ref, tok_ref, w_ref, b_ref, g_ref, o_ref, t_ref, n_ref, out_ref):
        xhat, inv = stats(tok_ref[...].astype(f32))
        normed = (xhat * g_ref[...] + o_ref[...]).astype(bf16)
        n_ref[...] = normed
        project = jnp.dot(normed, w_ref[...], preferred_element_type=f32) + b_ref[...]
        out_ref[...] = project.astype(bf16)
        first = place_ref[0] == 1

        @pl.when(first)
        def _():
            for b in range(blocks):
                at = pl.ds(pl.multiple_of(ids_ref[pl.program_id(0) * blocks + b] * BLOCK, BLOCK), BLOCK)
                c, m, p = t_ref[0, at, :], t_ref[1, at, :], t_ref[2, at, :]
                for g in range(2):
                    u = project[b * BLOCK : (b + 1) * BLOCK, g * hc : g * hc + 128]
                    out_ref[b * BLOCK : (b + 1) * BLOCK, g * hc : g * hc + 128] = turned(
                        u, c, m, p
                    ).astype(bf16)

    whole = lambda shape: pl.BlockSpec(shape, lambda i, *_: (0,) * len(shape))
    return pl.pallas_call(
        kernel,
        grid_spec=pltpu.PrefetchScalarGridSpec(
            num_scalar_prefetch=2,
            grid=(nz,),
            in_specs=[
                pl.BlockSpec((step, width), lambda i, *_: (i, 0)),
                whole((width, cols)),
                whole((1, cols)),
                whole((1, width)),
                whole((1, width)),
                whole(table.shape),
            ],
            out_specs=[
                pl.BlockSpec((step, width), lambda i, *_: (i, 0)),
                pl.BlockSpec((step, cols), lambda i, *_: (i, 0)),
            ],
        ),
        out_shape=[
            jax.ShapeDtypeStruct((rows, width), bf16),
            jax.ShapeDtypeStruct((rows, cols), bf16),
        ],
        compiler_params=BIG,
        cost_estimate=cost(2 * rows * width * cols, 4 * rows * width + 2 * width * cols),
        name="projections",
    )(ids, place, tok, w, bias, gain, offset, table)


def feed_forward(nz, tok, w, bias, gain, offset):
    rows, width = tok.shape
    step = rows // nz
    cols = w.shape[1]

    def kernel(tok_ref, w_ref, b_ref, g_ref, o_ref, n_ref, a_ref, d_ref):
        xhat, inv = stats(tok_ref[...].astype(f32))
        normed = (xhat * g_ref[...] + o_ref[...]).astype(bf16)
        n_ref[...] = normed
        v = jnp.dot(normed, w_ref[...], preferred_element_type=f32) + b_ref[...]
        gate = 0.5 * (1.0 + lax.erf(v * (0.5**0.5)))
        a_ref[...] = (v * gate).astype(bf16)
        bell = jnp.exp(v * v * -0.5) * ((2.0 * math.pi) ** -0.5)
        d_ref[...] = (gate + v * bell).astype(bf16)

    whole = lambda shape: pl.BlockSpec(shape, lambda i: (0, 0))
    part = lambda n: pl.BlockSpec((step, n), lambda i: (i, 0))
    return pl.pallas_call(
        kernel,
        grid=(nz,),
        in_specs=[part(width), whole((width, cols)), whole((1, cols)), whole((1, width)), whole((1, width))],
        out_specs=[part(width), part(cols), part(cols)],
        out_shape=[
            jax.ShapeDtypeStruct((rows, width), bf16),
            jax.ShapeDtypeStruct((rows, cols), bf16),
            jax.ShapeDtypeStruct((rows, cols), bf16),
        ],
        compiler_params=BIG,
        cost_estimate=cost(2 * rows * width * cols, 4 * rows * width + 2 * width * cols, 2 * rows * cols),
        name="feed_forward",
    )(tok, w, bias, gain, offset)


def layer_out(nz, core, mixed, w_dense, active, w_out):
    rows, hc = mixed.shape
    width = w_out.shape[1]
    step = rows // nz
    units = active.shape[1]

    def kernel(core_ref, m_ref, wd_ref, a_ref, wo_ref, out_ref):
        out_ref[...] = (
            jnp.dot(m_ref[...], wd_ref[...], preferred_element_type=f32)
            + jnp.dot(a_ref[...], wo_ref[...], preferred_element_type=f32)
        ).astype(bf16)

    part = lambda n: pl.BlockSpec((step, n), lambda i, c: (i, 0))
    held = lambda n: pl.BlockSpec((n, width), lambda i, c: (c[0], 0))
    return pl.pallas_call(
        kernel,
        grid_spec=pltpu.PrefetchScalarGridSpec(
            num_scalar_prefetch=1,
            grid=(nz,),
            in_specs=[part(hc), held(hc), part(units), held(units)],
            out_specs=part(width),
        ),
        out_shape=jax.ShapeDtypeStruct((rows, width), bf16),
        compiler_params=BIG,
        cost_estimate=cost(2 * rows * width * (hc + units), 4 * rows * width + 2 * width * units),
        name="layer_out",
    )(core, mixed, w_dense, active, w_out)


def widen(x):
    rows, cols = x.shape
    step = min(rows, 128 if cols > 4096 else 512)

    def kernel(x_ref, o_ref):
        o_ref[...] = x_ref[...].astype(f32)

    part = pl.BlockSpec((step, cols), lambda i: (i, 0))
    return pl.pallas_call(
        kernel,
        grid=(rows // step,),
        in_specs=[part],
        out_specs=part,
        out_shape=jax.ShapeDtypeStruct((rows, cols), f32),
        compiler_params=BIG,
        cost_estimate=cost(rows * cols, 6 * rows * cols),
        name="widen",
    )(x)


def grad_of_mixed(nz, core, cot, w_dense, hc):
    rows, width = cot.shape
    step = rows // nz

    def kernel(core_ref, c_ref, w_ref, out_ref):
        out_ref[...] = lax.dot_general(
            c_ref[...], w_ref[...], NT, preferred_element_type=f32
        ).astype(bf16)

    return pl.pallas_call(
        kernel,
        grid_spec=pltpu.PrefetchScalarGridSpec(
            num_scalar_prefetch=1,
            grid=(nz,),
            in_specs=[
                pl.BlockSpec((step, width), lambda i, c: (i, 0)),
                pl.BlockSpec((hc, width), lambda i, c: (c[0], 0)),
            ],
            out_specs=pl.BlockSpec((step, hc), lambda i, c: (i, 0)),
        ),
        out_shape=jax.ShapeDtypeStruct((rows, hc), bf16),
        compiler_params=BIG,
        cost_estimate=cost(2 * rows * width * hc, 2 * rows * width),
        name="grad_of_mixed",
    )(core, cot, w_dense)


def grad_of_hidden(nz, core, cot, w_out, slope):
    rows, width = cot.shape
    step = rows // nz
    units = slope.shape[1]

    def kernel(core_ref, c_ref, w_ref, d_ref, out_ref, sum_ref):
        g = lax.dot_general(c_ref[...], w_ref[...], NT, preferred_element_type=f32)
        g = (g * d_ref[...].astype(f32)).astype(bf16)
        out_ref[...] = g

        @pl.when(pl.program_id(0) == 0)
        def _():
            sum_ref[...] = jnp.zeros_like(sum_ref)

        sum_ref[...] += jnp.sum(g.astype(f32), axis=0, keepdims=True)

    return pl.pallas_call(
        kernel,
        grid_spec=pltpu.PrefetchScalarGridSpec(
            num_scalar_prefetch=1,
            grid=(nz,),
            in_specs=[
                pl.BlockSpec((step, width), lambda i, c: (i, 0)),
                pl.BlockSpec((units, width), lambda i, c: (c[0], 0)),
                pl.BlockSpec((step, units), lambda i, c: (i, 0)),
            ],
            out_specs=[
                pl.BlockSpec((step, units), lambda i, c: (i, 0)),
                pl.BlockSpec((1, units), lambda i, c: (0, 0)),
            ],
        ),
        out_shape=[
            jax.ShapeDtypeStruct((rows, units), bf16),
            jax.ShapeDtypeStruct((1, units), f32),
        ],
        compiler_params=BIG,
        cost_estimate=cost(2 * rows * width * units, 2 * rows * width + 2 * width * units),
        name="grad_of_hidden",
    )(core, cot, w_out, slope)


def norm_back(nz, grad, w, tok, gain, other, sums):
    rows, width = tok.shape
    step = rows // nz
    cols = grad.shape[1]

    def kernel(*refs):
        g_ref, w_ref, t_ref, gain_ref = refs[:4]
        at = 4
        if other is not None:
            other_ref = refs[at]
            at += 1
        e_ref, s_ref = refs[at : at + 2]
        gn = lax.dot_general(g_ref[...], w_ref[...], NT, preferred_element_type=f32)
        xhat, inv = stats(t_ref[...].astype(f32))
        e = gn * gain_ref[...]
        if other is not None:
            e = e + other_ref[...].astype(f32)
        e_ref[...] = e.astype(bf16)

        @pl.when(pl.program_id(0) == 0)
        def _():
            s_ref[...] = jnp.zeros_like(s_ref)
            if sums:
                refs[at + 2][...] = jnp.zeros_like(refs[at + 2])

        s_ref[0:1, :] += jnp.sum(gn * xhat, axis=0, keepdims=True)
        s_ref[1:2, :] += jnp.sum(gn, axis=0, keepdims=True)
        if sums:
            refs[at + 2][...] += jnp.sum(g_ref[...].astype(f32), axis=0, keepdims=True)

    part = lambda n: pl.BlockSpec((step, n), lambda i: (i, 0))
    whole = lambda shape: pl.BlockSpec(shape, lambda i: (0, 0))
    ins = [grad, w, tok, gain] + ([] if other is None else [other])
    return pl.pallas_call(
        kernel,
        grid=(nz,),
        in_specs=[part(cols), whole((width, cols)), part(width), whole((1, width))]
        + ([] if other is None else [part(width)]),
        out_specs=[part(width), whole((2, width))] + ([whole((1, cols))] if sums else []),
        out_shape=[
            jax.ShapeDtypeStruct((rows, width), bf16),
            jax.ShapeDtypeStruct((2, width), f32),
        ]
        + ([jax.ShapeDtypeStruct((1, cols), f32)] if sums else []),
        compiler_params=BIG,
        cost_estimate=cost(2 * rows * width * cols, 6 * rows * width + 2 * width * cols),
        name="norm_back",
    )(*ins)


def attention_forward(ids, order, qkv, tile):
    rows = qkv.shape[0]
    blocks = rows // BLOCK

    def kernel(ids_ref, order_ref, x_ref, o_ref, lse_ref, q_ref, k_ref, v_ref, s_ref):
        for b in range(blocks):
            at = pl.ds(pl.multiple_of(order_ref[b] * BLOCK, BLOCK), BLOCK)
            here = slice(b * BLOCK, (b + 1) * BLOCK)
            for i, ref in enumerate((q_ref, k_ref, v_ref)):
                ref[here, :] = x_ref[at, i * HD : (i + 1) * HD]
        for t in range(rows // tile):
            mine = slice(t * tile, (t + 1) * tile)
            n = (t + 1) * tile
            s = lax.dot_general(q_ref[mine, :], k_ref[:n, :], NT, preferred_element_type=f32)
            s = s * SCALE
            seen = t * tile + lax.broadcasted_iota(jnp.int32, (tile, n), 0) >= (
                lax.broadcasted_iota(jnp.int32, (tile, n), 1)
            )
            s = jnp.where(seen, s, -1e30)
            top = jnp.max(s, axis=-1, keepdims=True)
            e = jnp.exp(s - top)
            total = jnp.sum(e, axis=-1, keepdims=True)
            p = (e * (1.0 / total)).astype(bf16)
            s_ref[mine, :] = jnp.dot(p, v_ref[:n, :], preferred_element_type=f32).astype(bf16)
            lse_ref[mine, :] = top + jnp.log(total)
        for b in range(blocks):
            at = pl.ds(pl.multiple_of(ids_ref[b] * BLOCK, BLOCK), BLOCK)
            o_ref[b * BLOCK : (b + 1) * BLOCK, :] = s_ref[at, :]

    smem = pl.BlockSpec(memory_space=pltpu.SMEM)
    vmem = pl.BlockSpec(memory_space=pltpu.VMEM)
    return pl.pallas_call(
        kernel,
        in_specs=[smem, smem, vmem],
        out_specs=[vmem, vmem],
        out_shape=[
            jax.ShapeDtypeStruct((rows, HD), bf16),
            jax.ShapeDtypeStruct((rows, 1), f32),
        ],
        scratch_shapes=[pltpu.VMEM((rows, HD), bf16)] * 4,
        compiler_params=BIG,
        cost_estimate=cost(2.3 * rows * rows * HD, 8 * rows * HD, rows * rows / 2),
        name="attention_forward",
    )(ids, order, qkv)


def attention_backward(ids, order, qkv, grad, lse, table, tile):
    rows = qkv.shape[0]
    blocks = rows // BLOCK

    def kernel(ids_ref, order_ref, x_ref, g_ref, lse_ref, t_ref, out_ref, q_ref, k_ref, v_ref, m_ref,
               r_ref, dk_ref, dv_ref):
        for b in range(blocks):
            at = pl.ds(pl.multiple_of(order_ref[b] * BLOCK, BLOCK), BLOCK)
            here = slice(b * BLOCK, (b + 1) * BLOCK)
            for i, ref in enumerate((q_ref, k_ref, v_ref)):
                ref[here, :] = x_ref[at, i * HD : (i + 1) * HD]
            m_ref[here, :] = g_ref[at, :]
        for t in reversed(range(rows // tile)):
            mine = slice(t * tile, (t + 1) * tile)
            n = (t + 1) * tile
            q, g = q_ref[mine, :], m_ref[mine, :]
            s = lax.dot_general(q, k_ref[:n, :], NT, preferred_element_type=f32) * SCALE
            seen = t * tile + lax.broadcasted_iota(jnp.int32, (tile, n), 0) >= (
                lax.broadcasted_iota(jnp.int32, (tile, n), 1)
            )
            p = jnp.where(seen, jnp.exp(s - lse_ref[mine, :]), 0.0)
            dp = lax.dot_general(g, v_ref[:n, :], NT, preferred_element_type=f32)
            shift = jnp.sum(p * dp, axis=-1, keepdims=True)
            ds = (p * (dp - shift)).astype(bf16)
            low = p.astype(bf16)
            dq = jnp.dot(ds, k_ref[:n, :], preferred_element_type=f32) * SCALE
            r_ref[mine, :128] = turned(
                dq[:, :128], t_ref[0, mine, :], -t_ref[1, mine, :], -t_ref[2, mine, :]
            ).astype(bf16)
            r_ref[mine, 128:HD] = dq[:, 128:].astype(bf16)
            dk = lax.dot_general(ds, q, TN, preferred_element_type=f32) * SCALE
            dv = lax.dot_general(low, g, TN, preferred_element_type=f32)
            if n == rows:
                dk_ref[...] = dk
                dv_ref[...] = dv
            else:
                dk_ref[:n, :] += dk
                dv_ref[:n, :] += dv
        r_ref[:, HD : HD + 128] = turned(
            dk_ref[:, :128], t_ref[0], -t_ref[1], -t_ref[2]
        ).astype(bf16)
        r_ref[:, HD + 128 : 2 * HD] = dk_ref[:, 128:].astype(bf16)
        r_ref[:, 2 * HD :] = dv_ref[...].astype(bf16)
        for b in range(blocks):
            at = pl.ds(pl.multiple_of(ids_ref[b] * BLOCK, BLOCK), BLOCK)
            out_ref[b * BLOCK : (b + 1) * BLOCK, :] = r_ref[at, :]

    smem = pl.BlockSpec(memory_space=pltpu.SMEM)
    vmem = pl.BlockSpec(memory_space=pltpu.VMEM)
    return pl.pallas_call(
        kernel,
        in_specs=[smem, smem, vmem, vmem, vmem, vmem],
        out_specs=vmem,
        out_shape=jax.ShapeDtypeStruct((rows, 3 * HD), bf16),
        scratch_shapes=[pltpu.VMEM((rows, HD), bf16)] * 4
        + [pltpu.VMEM((rows, 3 * HD), bf16)]
        + [pltpu.VMEM((rows, HD), f32)] * 2,
        compiler_params=BIG,
        cost_estimate=cost(6 * rows * rows * HD, 20 * rows * HD, rows * rows / 2),
        name="attention_backward",
    )(ids, order, qkv, grad, lse, table)


def gather_plane(nchip, chip, core, src, dst_of, send, recv, local):
    sibling = {"core": 1 - core}
    rows = src.shape[0]
    half = rows // 2
    here = dst_of(chip, core)
    begun = [pltpu.make_async_copy(src, here, local)]
    begun.append(remote(src, here, send.at[0], recv.at[0], sibling))
    relays = []
    arrivals = []

    def cut(ref, h):
        return ref.at[pl.ds(h * half, half), :]

    if nchip == 4:
        beside = chip + 1 - 2 * lax.rem(chip, 2)
        below = lax.rem(chip + 2, 4)
        across = 3 - chip
        order = ((beside, 0, 1), (below, 1, 2), (beside, 1, 1), (below, 0, 2))
        for i, (to, h, d) in enumerate(order):
            slot = 4 + 2 * d + h
            begun.append(
                remote(cut(src, h), cut(here, h), send.at[slot], recv.at[slot], {"chip": to})
            )

        def passing(owner, h, to):
            part = cut(dst_of(owner, core), h)
            return remote(part, part, send.at[10 + h], recv.at[10 + h], {"chip": to})

        relays = [(passing(beside, 0, below), beside, 0, 6), (passing(below, 1, beside), below, 1, 9)]
        arrivals = [(beside, 1, 7, 1), (below, 0, 8, 2), (across, 0, 10, 3), (across, 1, 11, 3)]
        others = [(beside, 1), (below, 2), (across, 3)]
    else:
        others = [(lax.rem(chip + d, nchip), d) for d in range(1, nchip)]
        for to, d in others:
            begun.append(
                remote(src, here, send.at[nchip + d], recv.at[nchip + chip], {"chip": to})
            )

    def side(owner, slot):
        part = dst_of(owner, core)
        return remote(part, part, send.at[slot], recv.at[slot], sibling)

    def slot_of(owner, d):
        return d if nchip == 4 else 2 * nchip + owner

    def first():
        for copy in begun:
            copy.start()

    def onward():
        if nchip == 4:
            for copy, owner, h, slot in relays:
                part = cut(dst_of(owner, core), h)
                remote(part, part, send.at[0], recv.at[slot], sibling).wait_recv()
                copy.start()

    def pass_on():
        if nchip == 4:
            for owner, h, slot, d in arrivals:
                part = cut(dst_of(owner, core), h)
                remote(part, part, send.at[0], recv.at[slot], sibling).wait_recv()
                if slot != 10:
                    side(owner, d).start()
        else:
            for owner, d in others:
                part = dst_of(owner, core)
                remote(part, part, send.at[0], recv.at[nchip + owner], sibling).wait_recv()
                side(owner, slot_of(owner, d)).start()

    def last():
        begun[0].wait()
        for copy in begun[1:]:
            copy.wait_send()
        for copy, owner, h, slot in relays:
            copy.wait_send()
        there = dst_of(chip, 1 - core)
        remote(there, there, send.at[0], recv.at[0], sibling).wait_recv()
        for owner, d in others:
            side(owner, slot_of(owner, d)).wait_send()
            there = dst_of(owner, 1 - core)
            remote(there, there, send.at[0], recv.at[slot_of(owner, d)], sibling).wait_recv()

    return first, onward, pass_on, last


def scatter_plane(nchip, chip, part, own, first, second, send, recv, local):
    halves = own.shape[0]
    copies = []
    shape = own.shape[2:]

    def add(dst, terms):
        def rows(lead):
            @pl.loop(0, shape[-2] // 16)
            def _(i):
                at = lead + (pl.ds(pl.multiple_of(i * 16, 16), 16), slice(None))
                acc = dst[at].astype(f32)
                for term in terms:
                    acc = acc + term[at].astype(f32)
                dst[at] = acc.astype(bf16)

        if len(shape) == 2:
            rows(())
        else:

            @pl.loop(0, shape[0])
            def _(b):
                rows((b,))

    if nchip == 4:
        beside = chip + 1 - 2 * lax.rem(chip, 2)
        below = lax.rem(chip + 2, 4)
        across = 3 - chip
        ways = [(beside, below), (below, beside)]
        kept = [
            [
                pltpu.make_async_copy(part(chip, h), own.at[h, 0], local.at[h, 0]),
                pltpu.make_async_copy(part(ways[h][1], h), own.at[h, 1], local.at[h, 1]),
            ]
            for h in range(2)
        ]
        leave = [
            [
                remote(
                    part(across, h), first.at[h, 1], send.at[h, 1], recv.at[h, 1],
                    {"chip": ways[h][0]},
                ),
                remote(
                    part(ways[h][0], h), first.at[h, 0], send.at[h, 0], recv.at[h, 0],
                    {"chip": ways[h][0]},
                ),
            ]
            for h in range(2)
        ]
        follow = [
            remote(
                own.at[h, 1], second.at[h], send.at[h, 2], recv.at[h, 2], {"chip": ways[h][1]}
            )
            for h in range(2)
        ]

        def begin():
            for i in range(2):
                for h in range(2):
                    leave[h][i].start()
            for h in range(2):
                kept[h][1].start()
                kept[h][0].start()

        def middle():
            for h in range(2):
                kept[h][1].wait()
                leave[h][0].wait_recv()
                add(own.at[h, 1], [first.at[h, 1]])
                follow[h].start()

        def finish():
            for h in range(2):
                kept[h][0].wait()
                leave[h][1].wait_recv()
                follow[h].wait_recv()
                add(own.at[h, 0], [first.at[h, 0], second.at[h]])

        def last():
            for h in range(2):
                for copy in leave[h] + [follow[h]]:
                    copy.wait_send()
    else:
        to = [lax.rem(chip + d, nchip) for d in range(nchip)]
        kept = pltpu.make_async_copy(part(chip, 0), own.at[0, 0], local.at[0, 0])
        leave = [
            remote(part(to[d], 0), first.at[0, d], send.at[0, d], recv.at[0, d], {"chip": to[d]})
            for d in range(1, nchip)
        ]

        def begin():
            for copy in leave:
                copy.start()
            kept.start()

        def middle():
            pass

        def finish():
            kept.wait()
            for copy in leave:
                copy.wait_recv()
            add(own.at[0, 0], [first.at[0, d] for d in range(1, nchip)])

        def last():
            for copy in leave:
                copy.wait_send()

    return begin, middle, finish, last


def tail(nz, nchip, ncore, dwo, dwd, dwi, vectors, normed1, grad_project, grad_hidden, tok, w_qkv, w_in, gain1, gain2):
    width = dwo.shape[1]
    ro, rd = dwo.shape[0], dwd.shape[0] // nchip
    halves = 2 if nchip == 4 else 1
    hz = nz // halves
    hd = rd // halves
    ci, cq = dwi.shape[1], grad_project.shape[1] // 3
    wrows = width // nz
    ri = wrows // nchip
    rows = tok.shape[0]
    step = rows // nz
    own = step // ncore
    vr = vectors.shape[0]
    chunk = 512
    dwi = dwi.reshape(nz, nchip, ri, ci)
    dwd = dwd.reshape(nchip, rd, width)

    def kernel(
        dwo_ref, dwd_ref, dwi_ref, vec_ref, n_hbm, gp_hbm, gh_hbm, tok_hbm, wq_hbm, wi_hbm, g1_ref, g2_ref,
        go_ref, gd_ref, gi_ref, gq_ref, e_ref, vsum_ref,
        x_ref, gp_ref, gh_ref, wq_ref, wi_ref, dwq_ref, eb,
        oi, fi, si, oq, fq, sq, od, fd, sd, ti, tq, se, ze, cs, v0, v1, v2, v3,
        ld, ri_s, ri_r, ri_l, rq_s, rq_r, rq_l, rd_s, rd_r, rd_l, x_s, x_r, ez_s, ez_r, t_s, t_r, t_l,
        go_s, go_r, gd_s, gd_r, gi_s, gi_r, gq_s, gq_r, own_l,
        v_s, v_r,
    ):
        z = lax.axis_index("seq")
        chip = lax.axis_index("chip")
        core = lax.axis_index("core")
        sibling = {"core": 1 - core}

        def z_at(d):
            return lax.rem(z + d, nz)

        def chip_at(d):
            return lax.rem(chip + d, nchip)

        loads = [
            pltpu.make_async_copy(a, b, ld.at[i])
            for i, (a, b) in enumerate(
                ((n_hbm, x_ref), (gp_hbm, gp_ref), (gh_hbm, gh_ref), (wi_hbm, wi_ref), (wq_hbm, wq_ref))
            )
        ]
        for copy in loads:
            copy.start()
        greet(
            [{"seq": z_at(d)} for d in range(1, nz)]
            + [{"chip": chip_at(d)} for d in range(1, nchip)]
            + [sibling]
        )

        def turn(kind, part, turned):
            copies = [
                remote(
                    part(z_at(d)), turned.at[z], t_s.at[kind, d], t_r.at[kind, z],
                    {"seq": z_at(d)},
                )
                for d in range(1, nz)
            ]
            copies.append(pltpu.make_async_copy(part(z), turned.at[z], t_l.at[kind]))
            for copy in copies:
                copy.start()
            return copies

        def turned_at(kind, part, turned, source):
            return remote(part, turned.at[source], t_s.at[kind, 0], t_r.at[kind, source], sibling)

        sum_i = scatter_plane(
            nchip, chip, lambda c, h: dwi_ref.at[pl.ds(h * hz, hz), c], oi, fi, si, ri_s, ri_r, ri_l
        )
        sum_q = scatter_plane(
            nchip, chip, lambda c, h: dwq_ref.at[pl.ds(h * hz, hz), pl.ds(c * ri, ri)], oq, fq, sq,
            rq_s, rq_r, rq_l,
        )
        sum_d = scatter_plane(
            nchip, chip, lambda c, h: dwd_ref.at[c, pl.ds(h * hd, hd)], od, fd, sd, rd_s, rd_r, rd_l
        )
        sum_i[0]()

        loads[0].wait()
        loads[1].wait()
        for b in range(nz):
            dwq_ref[b] = lax.dot_general(
                x_ref[:, b * wrows : (b + 1) * wrows], gp_ref[...], TN, preferred_element_type=f32
            ).astype(bf16)
        load_tok = pltpu.make_async_copy(tok_hbm, x_ref, ld.at[5])
        load_tok.start()
        sum_i[1]()
        sum_q[0]()
        sum_d[0]()

        for copy in loads[2:] + [load_tok]:
            copy.wait()
        cs[...] = jnp.zeros_like(cs)

        def norm_back(b):
            at = pl.ds(b * step, step)
            x = x_ref[at, :].astype(f32)
            mean = jnp.mean(x, axis=-1, keepdims=True)
            x = x - mean
            inv = lax.rsqrt(jnp.mean(x * x, axis=-1, keepdims=True) + EPSILON)

            @pl.loop(0, width // chunk)
            def _(c):
                cols = pl.ds(pl.multiple_of(c * chunk, chunk), chunk)
                xhat = (x_ref[at, cols].astype(f32) - mean) * inv
                gn = lax.dot_general(
                    gp_ref[at, :], wq_ref[cols, :], NT, preferred_element_type=f32
                )
                cs[0:1, cols] += jnp.sum(gn * xhat, axis=0, keepdims=True)
                cs[1:2, cols] += jnp.sum(gn, axis=0, keepdims=True)
                e = gn * g1_ref[:, cols]
                gn = lax.dot_general(
                    gh_ref[at, :], wi_ref[cols, :], NT, preferred_element_type=f32
                )
                cs[2:3, cols] += jnp.sum(gn * xhat, axis=0, keepdims=True)
                cs[3:4, cols] += jnp.sum(gn, axis=0, keepdims=True)
                e = (e + gn * g2_ref[:, cols]).astype(bf16)
                for k in range(ncore):
                    eb[b, k, :, cols] = e[k * own : (k + 1) * own]

            copy = remote(eb.at[b, 1 - core], se.at[b], x_s.at[b], x_r.at[b], sibling)
            copy.start()
            return copy

        exchanged = [norm_back(b) for b in range(nz)]
        sum_i[2]()
        turn_i = turn(0, lambda to: oi.at[to // hz, 0, lax.rem(to, hz)], ti)
        sum_q[1]()

        v0[...] = vec_ref[...]
        lanes = width // 128
        for k in range(4):
            for j in range(lanes):
                v0[k * lanes + j : k * lanes + j + 1, :] = cs[k : k + 1, j * 128 : (j + 1) * 128]
        v_chips = [
            remote(v0, v1.at[chip], v_s.at[d], v_r.at[chip], {"chip": chip_at(d)})
            for d in range(1, nchip)
        ]
        for copy in v_chips:
            copy.start()
        v1[chip] = v0[...]

        go_at = lambda c, k: go_ref.at[pl.ds(k * (ro * nchip) + c * ro, ro), :]
        gd_at = lambda c, k, h: gd_ref.at[pl.ds(k * (rd * nchip) + c * rd + h * hd, hd), :]
        gi_at = lambda c, k, s: gi_ref.at[
            pl.ds(c * ri, ri), pl.ds((s * ncore + k) * ci, ci)
        ]
        gq_at = lambda c, k, s, g: gq_ref.at[
            pl.ds(c * ri, ri), pl.ds(g * nz * ncore * cq + (s * ncore + k) * cq, cq)
        ]
        group = functools.partial(gather_plane, nchip, chip, core)
        rows_o = group(dwo_ref, go_at, go_s, go_r, own_l.at[nz])
        rows_o[0]()

        for b in range(nz):
            exchanged[b].wait_recv()

            @pl.loop(0, own // 16)
            def _(i):
                at = pl.ds(pl.multiple_of(i * 16, 16), 16)
                eb[b, core, at, :] = (
                    eb[b, core, at, :].astype(f32) + se[b, at, :].astype(f32)
                ).astype(bf16)

        sum_q[2]()
        turn_q = turn(1, lambda to: oq.at[to // hz, 0, lax.rem(to, hz)], tq)
        sum_d[1]()

        for d in range(1, nchip):
            other = chip_at(d)
            remote(v0, v1.at[other], v_s.at[d], v_r.at[other], sibling).wait_recv()
        total = v1[0]
        for d in range(1, nchip):
            total = total + v1[d]
        v2[core] = total
        v_side = remote(v2.at[core], v2.at[core], v_s.at[nchip], v_r.at[nchip], sibling)
        v_side.start()

        groups = []
        for dz in range(1, nz):
            turned_at(0, oi.at[0, 0, 0], ti, z_at(dz)).wait_recv()
        turn_i[-1].wait()
        for source in range(nz):
            groups.append(
                group(
                    ti.at[source], functools.partial(gi_at, s=source), gi_s.at[source],
                    gi_r.at[source], own_l.at[source],
                )
            )
            groups[-1][0]()
        sent_e = [
            remote(
                eb.at[z_at(d), core], ze.at[d], ez_s.at[d], ez_r.at[d], {"seq": z_at(d)}
            )
            for d in range(1, nz)
        ]
        for copy in sent_e:
            copy.start()

        v_side.wait_recv()
        vz = v2[0]
        for c in range(1, ncore):
            vz = vz + v2[c]
        v3[z] = vz
        v_zs = [
            remote(v3.at[z], v3.at[z], v_s.at[nchip + d], v_r.at[nchip + 1 + z], {"seq": z_at(d)})
            for d in range(1, nz)
        ]
        for copy in v_zs:
            copy.start()
        sum_d[2]()
        rows_d = [
            group(od.at[h, 0], functools.partial(gd_at, h=h), gd_s.at[h], gd_r.at[h], own_l.at[nz + 1 + h])
            for h in range(halves)
        ]
        for first, onward, pass_on, last in rows_d:
            first()
        rows_o[1]()
        for first, onward, pass_on, last in groups:
            onward()

        for dz in range(1, nz):
            turned_at(1, oq.at[0, 0, 0], tq, z_at(dz)).wait_recv()
        turn_q[-1].wait()
        later = []
        for source in range(nz):
            for g in range(3):
                later.append(
                    group(
                        tq.at[source, :, pl.ds(g * cq, cq)],
                        functools.partial(gq_at, s=source, g=g),
                        gq_s.at[source, g], gq_r.at[source, g], own_l.at[4 + nz + 3 * source + g],
                    )
                )
        for first, onward, pass_on, last in later:
            first()
        rows_o[2]()
        for first, onward, pass_on, last in rows_d:
            onward()
        for first, onward, pass_on, last in groups:
            pass_on()
        for first, onward, pass_on, last in later:
            onward()
        for first, onward, pass_on, last in rows_d:
            pass_on()

        for d in range(1, nz):
            other = z_at(d)
            remote(v3.at[0], v3.at[other], v_s.at[0], v_r.at[nchip + 1 + other], sibling).wait_recv()
        total = v3[0]
        for d in range(1, nz):
            total = total + v3[d]
        vsum_ref[...] = total

        for copy in sent_e:
            copy.wait_recv()

        @pl.loop(0, own // 16)
        def _(i):
            at = pl.ds(pl.multiple_of(i * 16, 16), 16)
            acc = eb[z, core, at, :].astype(f32)
            for d in range(1, nz):
                acc = acc + ze[d, at, :].astype(f32)
            e_ref[at, :] = acc

        for first, onward, pass_on, last in later:
            pass_on()

        for first, onward, pass_on, last in [rows_o] + rows_d + groups + later:
            last()
        for begin, middle, finish, last in (sum_i, sum_q, sum_d):
            last()
        for copy in exchanged + sent_e + v_chips + v_zs + [v_side]:
            copy.wait_send()
        for copy in turn_i[:-1] + turn_q[:-1]:
            copy.wait_send()

    dma = pltpu.SemaphoreType.DMA
    anywhere = pl.BlockSpec(memory_space=pl.ANY)
    vmem = pl.BlockSpec(memory_space=pltpu.VMEM)
    out_shape = [
        jax.ShapeDtypeStruct((ncore * nchip * ro, width), bf16),
        jax.ShapeDtypeStruct((ncore * nchip * rd, width), bf16),
        jax.ShapeDtypeStruct((wrows, nz * ncore * ci), bf16),
        jax.ShapeDtypeStruct((wrows, 3 * nz * ncore * cq), bf16),
        jax.ShapeDtypeStruct((own, width), f32),
        jax.ShapeDtypeStruct((vr, 128), f32),
    ]
    slots = max(3 * nchip, 12)
    pair = 2 if nchip == 4 else 1
    nfirst = 2 if nchip == 4 else nchip

    def three(*shape):
        return [
            pltpu.VMEM((halves, pair) + shape, bf16),
            pltpu.VMEM((halves, nfirst) + shape, bf16),
            pltpu.VMEM((halves,) + shape, bf16),
        ]

    return pl.pallas_call(
        kernel,
        in_specs=[anywhere] * 3 + [vmem] + [anywhere] * 6 + [vmem] * 2,
        out_specs=[anywhere] * 4 + [vmem] * 2,
        out_shape=out_shape,
        scratch_shapes=[
            pltpu.VMEM((rows, width), bf16),
            pltpu.VMEM(grad_project.shape, bf16),
            pltpu.VMEM(grad_hidden.shape, bf16),
            pltpu.VMEM(w_qkv.shape, bf16),
            pltpu.VMEM(w_in.shape, bf16),
            pltpu.VMEM((nz, wrows, 3 * cq), bf16),
            pltpu.VMEM((nz, ncore, own, width), bf16),
        ]
        + three(hz, ri, ci)
        + three(hz, ri, 3 * cq)
        + three(hd, width)
        + [
            pltpu.VMEM((nz, ri, ci), bf16),
            pltpu.VMEM((nz, ri, 3 * cq), bf16),
            pltpu.VMEM((nz, own, width), bf16),
            pltpu.VMEM((nz, own, width), bf16),
            pltpu.VMEM((8, width), f32),
            pltpu.VMEM((vr, 128), f32),
            pltpu.VMEM((nchip, vr, 128), f32),
            pltpu.VMEM((ncore, vr, 128), f32),
            pltpu.VMEM((nz, vr, 128), f32),
            dma((6,)),
            dma((halves, nchip)), dma((halves, nchip)), dma((halves, 2)),
            dma((halves, nchip)), dma((halves, nchip)), dma((halves, 2)),
            dma((halves, nchip)), dma((halves, nchip)), dma((halves, 2)),
            dma((nz,)), dma((nz,)),
            dma((nz,)), dma((nz,)),
            dma((2, nz)), dma((2, nz)), dma((2,)),
            dma((slots,)), dma((slots,)),
            dma((halves, slots)), dma((halves, slots)),
            dma((nz, slots)), dma((nz, slots)),
            dma((nz, 3, slots)), dma((nz, 3, slots)),
            dma((4 + 4 * nz,)),
            dma((nchip + nz,)), dma((nchip + nz + 1,)),
        ],
        compiler_params=pltpu.CompilerParams(
            collective_id=2, has_side_effects=True, vmem_limit_bytes=62 * 2**20
        ),
        cost_estimate=cost(4 * rows * width * (3 * cq + ci), 20 * rows * width),
        name="tail",
    )(dwo, dwd, dwi, vectors, normed1, grad_project, grad_hidden, tok, w_qkv, w_in, gain1, gain2)


def on_device(
    nz,
    nchip,
    ncore,
    tokens,
    block_ids,
    cotangent,
    norm1_gain,
    norm1_bias,
    norm2_gain,
    norm2_bias,
    w_qkv,
    b_qkv,
    w_dense,
    b_dense,
    w_in,
    b_in,
    w_out,
    b_out,
):
    own, width = tokens.shape
    z = lax.axis_index("seq")
    chip = lax.axis_index("chip")
    core = lax.axis_index("core")
    ranks = nz * ncore
    rank = z * ncore + core
    rows = ranks * own
    ffr = w_out.shape[0] // ncore
    hc = width // ranks
    split = max(1, HD // hc)
    wrows = width // nz
    blocks = block_ids.shape[1]
    length = blocks * BLOCK
    core_at = core.reshape(1)

    parts = [norm1_gain, norm1_bias, norm2_gain, norm2_bias, b_qkv, b_dense + 0, b_in, b_out,
             block_ids.reshape(-1)]
    sizes = [p.shape[0] for p in parts]
    total = -(-sum(sizes) // 2048) * 2048
    starts = [sum(sizes[:i]) for i in range(len(sizes))]
    small = sum(
        jnp.pad(p.astype(f32), (at, total - at - p.shape[0])) for p, at in zip(parts, starts)
    )
    small = small.astype(bf16).reshape(-1, 128)
    tok, w_in_c, w_qkv_c, small = front(nz, nchip, ncore, tokens, w_in, w_qkv, small)
    tok = tok.reshape(rows, width)
    small = small.reshape(nz, total)

    def vector(i):
        return small[:, starts[i] : starts[i] + sizes[i]].astype(f32).reshape(1, -1)

    gain1, bias1, gain2, bias2 = [vector(i) for i in range(4)]
    bias_c = lax.dynamic_index_in_dim(vector(4).reshape(3, ranks, hc), rank, 1, keepdims=False)
    bias_c = bias_c.reshape(1, 3 * hc)
    bias_in = lax.dynamic_slice_in_dim(vector(6), rank * ffr, ffr, 1)
    ids = vector(8).astype(jnp.int32).reshape(nz, blocks)
    tok, cot_own = lax.optimization_barrier((tok, cotangent))
    cot = lax.all_gather(cot_own, TP, axis=0, tiled=True)

    per_chip = blocks // nchip
    ids_rows = lax.dynamic_slice_in_dim(ids, chip * per_chip, per_chip, 1).reshape(-1)
    ids_seq = lax.dynamic_index_in_dim(ids, chip, 0, keepdims=False)
    slots = jnp.arange(blocks, dtype=jnp.int32)
    order = jnp.sum(jnp.where(ids_seq[None, :] == slots[:, None], slots[None, :], 0), axis=1)
    place = (lax.rem(rank, split) == 0).astype(jnp.int32).reshape(1)
    table = jnp.asarray(turn_table(length))

    def heads_of(x):
        g = x.shape[1] // hc
        if split > 1:
            x = lax.all_gather(x.reshape(rows, g, hc), "core", axis=2, tiled=True)
        x = x.reshape(nz, rows // nz, g * HD)
        return lax.all_to_all(x, "chip", 0, 0, tiled=True).reshape(length, g * HD)

    def heads_back(x):
        g = x.shape[1] // HD
        x = x.reshape(nchip, length // nchip, g * HD)
        x = lax.all_to_all(x, "chip", 0, 0, tiled=True).reshape(rows, g * HD)
        if split > 1:
            x = lax.dynamic_slice_in_dim(x.reshape(rows, g, HD), core * hc, hc, 2)
        return x.reshape(rows, g * hc)

    tile = 256
    normed1, qkv = projections(nz, ids_rows, place, tok, w_qkv_c, bias_c, gain1, bias1, table)
    qkv = heads_of(qkv)
    normed2, active, slope = feed_forward(nz, tok, w_in_c, bias_in, gain2, bias2)
    qkv, active, slope, normed2 = lax.optimization_barrier((qkv, active, slope, normed2))
    attended, lse = attention_forward(ids_seq, order, qkv, tile)
    attended, cot = lax.optimization_barrier((attended, cot))
    mixed = heads_back(attended)

    grad_mixed = grad_of_mixed(nz, core_at, cot, w_dense, hc)
    grad_mixed, cot = lax.optimization_barrier((grad_mixed, cot))
    g = heads_of(grad_mixed)
    dw_out = lax.dot_general(active, cot, TN, preferred_element_type=f32).astype(bf16)
    dw_out, cot = lax.optimization_barrier((dw_out, cot))
    s_out = lax.psum_scatter(dw_out, "chip", scatter_dimension=0, tiled=True)
    grad_hidden, sum_bin = grad_of_hidden(nz, core_at, cot, w_out, slope)
    g, grad_hidden, mixed = lax.optimization_barrier((g, grad_hidden, mixed))
    dqkv = attention_backward(ids_seq, order, qkv, g, lse, table, tile)
    dqkv, mixed, active, cot, grad_hidden = lax.optimization_barrier(
        (dqkv, mixed, active, cot, grad_hidden)
    )
    grad_project = heads_back(dqkv)
    part_out = layer_out(nz, core_at, mixed, w_dense, active, w_out)
    part_out, cot, mixed, grad_hidden = lax.optimization_barrier((part_out, cot, mixed, grad_hidden))
    summed_out = lax.psum_scatter(part_out, TP, scatter_dimension=0, tiled=True).astype(f32)
    dw_in = lax.dot_general(normed2, grad_hidden, TN, preferred_element_type=f32).astype(bf16)
    dw_dense = lax.dot_general(mixed, cot, TN, preferred_element_type=f32).astype(bf16)
    grad_project, dw_in, dw_dense = lax.optimization_barrier((grad_project, dw_in, dw_dense))
    sum_bqkv = jnp.sum(grad_project.astype(f32), axis=0)

    here = jnp.arange(ranks, dtype=jnp.int32) == rank
    mine_bqkv = jnp.where(here[None, :, None], sum_bqkv.reshape(3, 1, hc), 0.0)
    mine_bin = jnp.where(here[:, None], sum_bin.reshape(1, ffr), 0.0)
    vectors = [
        jnp.zeros(4 * width, f32),
        mine_bqkv.reshape(-1),
        jnp.sum(cotangent.astype(f32), axis=0),
        mine_bin.reshape(-1),
    ]
    vectors = jnp.concatenate([v.reshape(-1, 128) for v in vectors])
    g_wout, g_wdense, g_win, g_wqkv, e, sums = tail(
        nz, nchip, ncore, s_out, dw_dense, dw_in, vectors, normed1, grad_project, grad_hidden, tok,
        w_qkv_c, w_in_c, gain1, gain2
    )
    sums = sums.reshape(-1)
    at = 0
    small_out = []
    for size in (width, width, width, width, 3 * width, width, ranks * ffr):
        small_out.append(lax.dynamic_slice_in_dim(sums, at + z * (size // nz), size // nz))
        at += size
    g_gain1, g_bias1, g_gain2, g_bias2, g_bqkv, g_bdense, g_bin = small_out

    output = (tokens.astype(f32) + summed_out + vector(5) + vector(7)).astype(bf16)
    xhat_own, inv_own = stats(tokens.astype(f32))
    terms = (
        e
        - jnp.mean(e, axis=-1, keepdims=True)
        - xhat_own * jnp.mean(e * xhat_own, axis=-1, keepdims=True)
    ) * inv_own
    grad_tokens = (cotangent.astype(f32) + terms).astype(bf16)
    g_wout, g_wdense, g_win, g_wqkv = [widen(g) for g in (g_wout, g_wdense, g_win, g_wqkv)]
    return (
        output,
        grad_tokens,
        g_gain1,
        g_bias1,
        g_gain2,
        g_bias2,
        g_wqkv,
        g_bqkv,
        g_wdense,
        g_bdense,
        g_win,
        g_bin,
        g_wout,
        g_bdense,
    )


def solution(mesh):
    nz, nctx = mesh.shape["seq"], mesh.shape["ctx"]
    ncore = 2
    nchip = nctx // ncore
    fine = Mesh(mesh.devices.reshape(nz, nchip, ncore), ("seq", "chip", "core"))
    own = P(("seq", "chip", "core"), None)
    vec = P("seq")
    mat = P("seq", None)
    return jax.shard_map(
        functools.partial(on_device, nz, nchip, ncore),
        mesh=fine,
        in_specs=(own, mat, own, vec, vec, vec, vec, mat, vec, mat, vec, mat, vec, mat, vec),
        out_specs=(own, own, vec, vec, vec, vec, mat, vec, mat, vec, mat, vec, mat, vec),
        check_vma=False,
    )
```

```python
import functools
import math

import jax
import jax.numpy as jnp
import numpy as np
from jax import lax
from jax.experimental import pallas as pl
from jax.experimental.pallas import tpu as pltpu
from jax.sharding import Mesh, PartitionSpec as P

HD = 256
ROT = 64
BLOCK = 96
EPSILON = 1e-05
ROT_BASE = 10000.0
SCALE = HD ** (-0.5)
f32 = jnp.float32
bf16 = jnp.bfloat16
TP = ("seq", "core")
MESH = pl.DeviceIdType.MESH
NT = (((1,), (1,)), ((), ()))
TN = (((0,), (0,)), ((), ()))
BIG = pltpu.CompilerParams(vmem_limit_bytes=62 * 2**20)


def remote(src, dst, send, recv, target):
    return pltpu.make_async_remote_copy(
        src_ref=src, dst_ref=dst, send_sem=send, recv_sem=recv, device_id=target,
        device_id_type=MESH,
    )


def greet(targets):
    barrier = pltpu.get_barrier_semaphore()
    for target in targets:
        pl.semaphore_signal(barrier, inc=1, device_id=target, device_id_type=MESH)
    pl.semaphore_wait(barrier, len(targets))


def front(nz, nchip, ncore, tokens, w_in, w_qkv, small):
    own, width = tokens.shape
    wrows, ff = w_in.shape
    heads3 = w_qkv.shape[1]
    nctx = nchip * ncore
    piece = wrows // nctx
    zi, zq = ff // nz, heads3 // 3 // nz
    ci, cq = zi // ncore, zq // ncore

    def kernel(
        tok_ref, wi_ref, wq_ref, sm_ref, tok_out, wi_out, wq_out, sm_out, buf_i, buf_q,
        up_s, up_r, dn_s, dn_r, sib_s, sib_r, zi_s, zi_r, zq_s, zq_r, pi_s, pi_r, pq_s, pq_r, loc, sm_s, sm_r,
    ):
        z = lax.axis_index("seq")
        chip = lax.axis_index("chip")
        core = lax.axis_index("core")
        share = chip * ncore + core
        sibling = {"core": 1 - core}

        def z_at(d):
            return lax.rem(z + d, nz)

        def plane_at(d):
            other = lax.rem(share + d, nctx)
            return other // ncore, lax.rem(other, ncore)

        greet(
            [{"seq": z_at(d)} for d in range(1, nz)]
            + [{"chip": plane_at(d)[0], "core": plane_at(d)[1]} for d in range(1, nctx)]
        )

        rows = pl.ds(share * piece, piece)
        def hop(to):
            to = jnp.clip(to, 0, nz - 1)
            copies = [
                remote(
                    wi_ref.at[rows, pl.ds(to * zi, zi)], buf_i.at[z], zi_s.at[to], zi_r.at[z],
                    {"seq": to},
                )
            ]
            for g in range(3):
                copies.append(
                    remote(
                        wq_ref.at[rows, pl.ds(g * zq * nz + to * zq, zq)], buf_q.at[z, g],
                        zq_s.at[to, g], zq_r.at[z, g], {"seq": to},
                    )
                )
            return copies

        def around(body):
            for distance in range(1, nz):
                for other in (z + distance, z - distance):
                    @pl.when(jnp.logical_and(other >= 0, other < nz))
                    def _():
                        body(jnp.clip(other, 0, nz - 1))

        def up(s):
            shard = z - s
            src = tok_ref if s == 0 else tok_out.at[jnp.maximum(shard, 0), core]
            return remote(
                src, tok_out.at[jnp.maximum(shard, 0), core], up_s.at[s], up_r.at[s],
                {"seq": jnp.minimum(z + 1, nz - 1)},
            )

        def down(s):
            shard = z + s
            src = tok_ref if s == 0 else tok_out.at[jnp.minimum(shard, nz - 1), core]
            return remote(
                src, tok_out.at[jnp.minimum(shard, nz - 1), core], dn_s.at[s], dn_r.at[s],
                {"seq": jnp.maximum(z - 1, 0)},
            )

        def side(shard, own_rows=False):
            src = tok_ref if own_rows else tok_out.at[shard, core]
            return remote(src, tok_out.at[shard, core], sib_s.at[shard], sib_r.at[shard], sibling)

        smalls = [
            remote(sm_ref, sm_out.at[z], sm_s.at[d], sm_r.at[z], {"seq": z_at(d)})
            for d in range(1, nz)
        ]
        for copy in smalls:
            copy.start()

        def send_hop(to):
            for copy in hop(to):
                copy.start()

        around(send_hop)

        @pl.when(z + 1 < nz)
        def _():
            up(0).start()

        @pl.when(z > 0)
        def _():
            down(0).start()

        side(z, True).start()
        locals_ = [
            pltpu.make_async_copy(tok_ref, tok_out.at[z, core], loc.at[0]),
            pltpu.make_async_copy(wi_ref.at[rows, pl.ds(z * zi, zi)], buf_i.at[z], loc.at[1]),
            pltpu.make_async_copy(sm_ref, sm_out.at[z], sm_s.at[0]),
        ] + [
            pltpu.make_async_copy(
                wq_ref.at[rows, pl.ds(g * zq * nz + z * zq, zq)], buf_q.at[z, g], loc.at[2 + g]
            )
            for g in range(3)
        ]
        for copy in locals_:
            copy.start()

        def spread(source, d):
            to_chip, to_core = plane_at(d)
            target_rows = pl.ds(source * wrows + share * piece, piece)
            pairs = [
                (
                    buf_i.at[source, :, pl.ds(to_core * ci, ci)], wi_out.at[target_rows, :],
                    pi_s.at[source, d], pi_r.at[source, share],
                )
            ] + [
                (
                    buf_q.at[source, g, :, pl.ds(to_core * cq, cq)],
                    wq_out.at[target_rows, pl.ds(g * cq, cq)],
                    pq_s.at[source, d, g], pq_r.at[source, share, g],
                )
                for g in range(3)
            ]
            if d == 0:
                return [pltpu.make_async_copy(a, b, c) for a, b, c, r in pairs]
            return [remote(a, b, c, r, {"chip": to_chip, "core": to_core}) for a, b, c, r in pairs]

        def hop_arrival(source):
            remote(buf_i.at[source], buf_i.at[source], zi_s.at[0], zi_r.at[source], sibling).wait_recv()
            for g in range(3):
                remote(
                    buf_q.at[source, g], buf_q.at[source, g], zq_s.at[0, 0], zq_r.at[source, g],
                    sibling,
                ).wait_recv()

        for copy in locals_[1:]:
            copy.wait()
        for d in range(nctx):
            for copy in spread(z, d):
                copy.start()
        def hand_on(source):
            hop_arrival(source)
            for d in range(nctx):
                for copy in spread(source, d):
                    copy.start()

        around(hand_on)

        for s in range(nz - 1):
            from_below = z - 1 - s
            from_above = z + 1 + s

            @pl.when(from_below >= 0)
            def _():
                shard = jnp.maximum(from_below, 0)
                remote(tok_ref, tok_out.at[shard, core], up_s.at[s], up_r.at[s], sibling).wait_recv()
                if s + 1 < nz - 1:
                    @pl.when(z + 1 < nz)
                    def _():
                        up(s + 1).start()
                side(shard).start()

            @pl.when(from_above < nz)
            def _():
                shard = jnp.minimum(from_above, nz - 1)
                remote(tok_ref, tok_out.at[shard, core], dn_s.at[s], dn_r.at[s], sibling).wait_recv()
                if s + 1 < nz - 1:
                    @pl.when(z > 0)
                    def _():
                        down(s + 1).start()
                side(shard).start()

        locals_[0].wait()
        for shard in range(nz):
            remote(tok_ref, tok_out.at[shard, 1 - core], sib_s.at[shard], sib_r.at[shard], sibling).wait()
        for s in range(nz - 1):
            @pl.when(jnp.logical_and(z + 1 < nz, z - s >= 0))
            def _():
                up(s).wait_send()

            @pl.when(jnp.logical_and(z > 0, z + s < nz))
            def _():
                down(s).wait_send()
        for copy in smalls:
            copy.wait_send()

        def hop_left(to):
            for copy in hop(to):
                copy.wait_send()

        around(hop_left)
        for d in range(1, nz):
            other = z_at(d)
            remote(sm_ref, sm_out.at[other], sm_s.at[d], sm_r.at[other], sibling).wait_recv()
        for source in range(nz):
            for d in range(nctx):
                if d == 0:
                    for copy in spread(source, d):
                        copy.wait()
                    continue
                for copy in spread(source, d):
                    copy.wait_send()
                other = lax.rem(share + d, nctx)
                rows_there = pl.ds(source * wrows + other * piece, piece)
                remote(
                    wi_out.at[rows_there, :], wi_out.at[rows_there, :], pi_s.at[source, d],
                    pi_r.at[source, other], sibling,
                ).wait_recv()
                for g in range(3):
                    cols = pl.ds(g * cq, cq)
                    remote(
                        wq_out.at[rows_there, cols], wq_out.at[rows_there, cols],
                        pq_s.at[source, d, g], pq_r.at[source, other, g], sibling,
                    ).wait_recv()

    dma = pltpu.SemaphoreType.DMA
    anywhere = pl.BlockSpec(memory_space=pl.ANY)
    return pl.pallas_call(
        kernel,
        in_specs=[anywhere] * 4,
        out_specs=[anywhere] * 4,
        out_shape=[
            jax.ShapeDtypeStruct((nz, ncore, own, width), bf16),
            jax.ShapeDtypeStruct((nz * wrows, ci), bf16),
            jax.ShapeDtypeStruct((nz * wrows, 3 * cq), bf16),
            jax.ShapeDtypeStruct((nz,) + small.shape, bf16),
        ],
        scratch_shapes=[
            pltpu.VMEM((nz, piece, zi), bf16),
            pltpu.VMEM((nz, 3, piece, zq), bf16),
            dma((nz,)), dma((nz,)), dma((nz,)), dma((nz,)),
            dma((nz,)), dma((nz,)),
            dma((nz,)), dma((nz,)), dma((nz, 3)), dma((nz, 3)),
            dma((nz, nctx)), dma((nz, nctx)), dma((nz, nctx, 3)), dma((nz, nctx, 3)),
            dma((5,)), dma((nz,)), dma((nz,)),
        ],
        compiler_params=pltpu.CompilerParams(collective_id=1, has_side_effects=True),
        name="front",
    )(tokens, w_in, w_qkv, small)


def turn_table(length):
    half = ROT // 2
    power = -(np.arange(half, dtype=np.float32) * np.float32(2.0)) / np.float32(ROT)
    angles = np.arange(length, dtype=np.float32)[:, None] * np.power(np.float32(ROT_BASE), power)
    table = np.zeros((3, length, 128), np.float32)
    table[0] = 1.0
    table[0, :, :half] = table[0, :, half:ROT] = np.cos(angles)
    table[1, :, :half] = -np.sin(angles)
    table[2, :, half:ROT] = np.sin(angles)
    return table


def turned(u, cosine, minus, plus):
    half = ROT // 2
    return u * cosine + pltpu.roll(u, 128 - half, 1) * minus + pltpu.roll(u, half, 1) * plus


def stats(x):
    center = x - jnp.mean(x, axis=-1, keepdims=True)
    inv = lax.rsqrt(jnp.mean(center * center, axis=-1, keepdims=True) + EPSILON)
    return center * inv, inv


def cost(flops, nbytes, trans=0):
    return pl.CostEstimate(flops=int(flops), bytes_accessed=int(nbytes), transcendentals=int(trans))


def projections(nz, ids, place, tok, w, bias, gain, offset, table):
    rows, width = tok.shape
    step = rows // nz
    blocks = step // BLOCK
    cols = w.shape[1]
    hc = cols // 3

    def kernel(ids_ref, place_ref, tok_ref, w_ref, b_ref, g_ref, o_ref, t_ref, n_ref, out_ref):
        xhat, inv = stats(tok_ref[...].astype(f32))
        normed = (xhat * g_ref[...] + o_ref[...]).astype(bf16)
        n_ref[...] = normed
        project = jnp.dot(normed, w_ref[...], preferred_element_type=f32) + b_ref[...]
        out_ref[...] = project.astype(bf16)
        first = place_ref[0] == 1

        @pl.when(first)
        def _():
            for b in range(blocks):
                at = pl.ds(pl.multiple_of(ids_ref[pl.program_id(0) * blocks + b] * BLOCK, BLOCK), BLOCK)
                c, m, p = t_ref[0, at, :], t_ref[1, at, :], t_ref[2, at, :]
                for g in range(2):
                    u = project[b * BLOCK : (b + 1) * BLOCK, g * hc : g * hc + 128]
                    out_ref[b * BLOCK : (b + 1) * BLOCK, g * hc : g * hc + 128] = turned(
                        u, c, m, p
                    ).astype(bf16)

    whole = lambda shape: pl.BlockSpec(shape, lambda i, *_: (0,) * len(shape))
    return pl.pallas_call(
        kernel,
        grid_spec=pltpu.PrefetchScalarGridSpec(
            num_scalar_prefetch=2,
            grid=(nz,),
            in_specs=[
                pl.BlockSpec((step, width), lambda i, *_: (i, 0)),
                whole((width, cols)),
                whole((1, cols)),
                whole((1, width)),
                whole((1, width)),
                whole(table.shape),
            ],
            out_specs=[
                pl.BlockSpec((step, width), lambda i, *_: (i, 0)),
                pl.BlockSpec((step, cols), lambda i, *_: (i, 0)),
            ],
        ),
        out_shape=[
            jax.ShapeDtypeStruct((rows, width), bf16),
            jax.ShapeDtypeStruct((rows, cols), bf16),
        ],
        compiler_params=BIG,
        cost_estimate=cost(2 * rows * width * cols, 4 * rows * width + 2 * width * cols),
        name="projections",
    )(ids, place, tok, w, bias, gain, offset, table)


def feed_forward(nz, tok, w, bias, gain, offset):
    rows, width = tok.shape
    step = rows // nz
    cols = w.shape[1]

    def kernel(tok_ref, w_ref, b_ref, g_ref, o_ref, n_ref, a_ref, d_ref):
        xhat, inv = stats(tok_ref[...].astype(f32))
        normed = (xhat * g_ref[...] + o_ref[...]).astype(bf16)
        n_ref[...] = normed
        v = jnp.dot(normed, w_ref[...], preferred_element_type=f32) + b_ref[...]
        gate = 0.5 * (1.0 + lax.erf(v * (0.5**0.5)))
        a_ref[...] = (v * gate).astype(bf16)
        bell = jnp.exp(v * v * -0.5) * ((2.0 * math.pi) ** -0.5)
        d_ref[...] = (gate + v * bell).astype(bf16)

    whole = lambda shape: pl.BlockSpec(shape, lambda i: (0, 0))
    part = lambda n: pl.BlockSpec((step, n), lambda i: (i, 0))
    return pl.pallas_call(
        kernel,
        grid=(nz,),
        in_specs=[part(width), whole((width, cols)), whole((1, cols)), whole((1, width)), whole((1, width))],
        out_specs=[part(width), part(cols), part(cols)],
        out_shape=[
            jax.ShapeDtypeStruct((rows, width), bf16),
            jax.ShapeDtypeStruct((rows, cols), bf16),
            jax.ShapeDtypeStruct((rows, cols), bf16),
        ],
        compiler_params=BIG,
        cost_estimate=cost(2 * rows * width * cols, 4 * rows * width + 2 * width * cols, 2 * rows * cols),
        name="feed_forward",
    )(tok, w, bias, gain, offset)


def layer_out(nz, core, mixed, w_dense, active, w_out):
    rows, hc = mixed.shape
    width = w_out.shape[1]
    step = rows // nz
    units = active.shape[1]

    def kernel(core_ref, m_ref, wd_ref, a_ref, wo_ref, out_ref):
        out_ref[...] = (
            jnp.dot(m_ref[...], wd_ref[...], preferred_element_type=f32)
            + jnp.dot(a_ref[...], wo_ref[...], preferred_element_type=f32)
        ).astype(bf16)

    part = lambda n: pl.BlockSpec((step, n), lambda i, c: (i, 0))
    held = lambda n: pl.BlockSpec((n, width), lambda i, c: (c[0], 0))
    return pl.pallas_call(
        kernel,
        grid_spec=pltpu.PrefetchScalarGridSpec(
            num_scalar_prefetch=1,
            grid=(nz,),
            in_specs=[part(hc), held(hc), part(units), held(units)],
            out_specs=part(width),
        ),
        out_shape=jax.ShapeDtypeStruct((rows, width), bf16),
        compiler_params=BIG,
        cost_estimate=cost(2 * rows * width * (hc + units), 4 * rows * width + 2 * width * units),
        name="layer_out",
    )(core, mixed, w_dense, active, w_out)


def widen(arrays):
    steps = [min(x.shape[0], 128 if x.shape[1] > 4096 else 512) for x in arrays]
    counts = [x.shape[0] // step for x, step in zip(arrays, steps)]
    starts = [sum(counts[:i]) for i in range(len(counts))]

    def kernel(*refs):
        n = len(arrays)
        for i in range(n):
            here = pl.program_id(0) - starts[i]

            @pl.when(jnp.logical_and(here >= 0, here < counts[i]))
            def _():
                refs[n + i][...] = refs[i][...].astype(f32)

    def part(i):
        return pl.BlockSpec(
            (steps[i], arrays[i].shape[1]),
            lambda s: (jnp.clip(s - starts[i], 0, counts[i] - 1), 0),
        )

    specs = [part(i) for i in range(len(arrays))]
    size = sum(x.size for x in arrays)
    return pl.pallas_call(
        kernel,
        grid=(sum(counts),),
        in_specs=specs,
        out_specs=specs,
        out_shape=[jax.ShapeDtypeStruct(x.shape, f32) for x in arrays],
        compiler_params=BIG,
        cost_estimate=cost(size, 6 * size),
        name="widen",
    )(*arrays)


def grad_of_mixed(nz, core, cot, w_dense, hc):
    rows, width = cot.shape
    step = rows // nz

    def kernel(core_ref, c_ref, w_ref, out_ref):
        out_ref[...] = lax.dot_general(
            c_ref[...], w_ref[...], NT, preferred_element_type=f32
        ).astype(bf16)

    return pl.pallas_call(
        kernel,
        grid_spec=pltpu.PrefetchScalarGridSpec(
            num_scalar_prefetch=1,
            grid=(nz,),
            in_specs=[
                pl.BlockSpec((step, width), lambda i, c: (i, 0)),
                pl.BlockSpec((hc, width), lambda i, c: (c[0], 0)),
            ],
            out_specs=pl.BlockSpec((step, hc), lambda i, c: (i, 0)),
        ),
        out_shape=jax.ShapeDtypeStruct((rows, hc), bf16),
        compiler_params=BIG,
        cost_estimate=cost(2 * rows * width * hc, 2 * rows * width),
        name="grad_of_mixed",
    )(core, cot, w_dense)


def grad_of_hidden(nz, core, cot, w_out, slope):
    rows, width = cot.shape
    step = rows // nz
    units = slope.shape[1]

    def kernel(core_ref, c_ref, w_ref, d_ref, out_ref, sum_ref):
        g = lax.dot_general(c_ref[...], w_ref[...], NT, preferred_element_type=f32)
        g = (g * d_ref[...].astype(f32)).astype(bf16)
        out_ref[...] = g

        @pl.when(pl.program_id(0) == 0)
        def _():
            sum_ref[...] = jnp.zeros_like(sum_ref)

        sum_ref[...] += jnp.sum(g.astype(f32), axis=0, keepdims=True)

    return pl.pallas_call(
        kernel,
        grid_spec=pltpu.PrefetchScalarGridSpec(
            num_scalar_prefetch=1,
            grid=(nz,),
            in_specs=[
                pl.BlockSpec((step, width), lambda i, c: (i, 0)),
                pl.BlockSpec((units, width), lambda i, c: (c[0], 0)),
                pl.BlockSpec((step, units), lambda i, c: (i, 0)),
            ],
            out_specs=[
                pl.BlockSpec((step, units), lambda i, c: (i, 0)),
                pl.BlockSpec((1, units), lambda i, c: (0, 0)),
            ],
        ),
        out_shape=[
            jax.ShapeDtypeStruct((rows, units), bf16),
            jax.ShapeDtypeStruct((1, units), f32),
        ],
        compiler_params=BIG,
        cost_estimate=cost(2 * rows * width * units, 2 * rows * width + 2 * width * units),
        name="grad_of_hidden",
    )(core, cot, w_out, slope)


def norm_back(nz, grad, w, tok, gain, other, sums):
    rows, width = tok.shape
    step = rows // nz
    cols = grad.shape[1]

    def kernel(*refs):
        g_ref, w_ref, t_ref, gain_ref = refs[:4]
        at = 4
        if other is not None:
            other_ref = refs[at]
            at += 1
        e_ref, s_ref = refs[at : at + 2]
        gn = lax.dot_general(g_ref[...], w_ref[...], NT, preferred_element_type=f32)
        xhat, inv = stats(t_ref[...].astype(f32))
        e = gn * gain_ref[...]
        if other is not None:
            e = e + other_ref[...].astype(f32)
        e_ref[...] = e.astype(bf16)

        @pl.when(pl.program_id(0) == 0)
        def _():
            s_ref[...] = jnp.zeros_like(s_ref)
            if sums:
                refs[at + 2][...] = jnp.zeros_like(refs[at + 2])

        s_ref[0:1, :] += jnp.sum(gn * xhat, axis=0, keepdims=True)
        s_ref[1:2, :] += jnp.sum(gn, axis=0, keepdims=True)
        if sums:
            refs[at + 2][...] += jnp.sum(g_ref[...].astype(f32), axis=0, keepdims=True)

    part = lambda n: pl.BlockSpec((step, n), lambda i: (i, 0))
    whole = lambda shape: pl.BlockSpec(shape, lambda i: (0, 0))
    ins = [grad, w, tok, gain] + ([] if other is None else [other])
    return pl.pallas_call(
        kernel,
        grid=(nz,),
        in_specs=[part(cols), whole((width, cols)), part(width), whole((1, width))]
        + ([] if other is None else [part(width)]),
        out_specs=[part(width), whole((2, width))] + ([whole((1, cols))] if sums else []),
        out_shape=[
            jax.ShapeDtypeStruct((rows, width), bf16),
            jax.ShapeDtypeStruct((2, width), f32),
        ]
        + ([jax.ShapeDtypeStruct((1, cols), f32)] if sums else []),
        compiler_params=BIG,
        cost_estimate=cost(2 * rows * width * cols, 6 * rows * width + 2 * width * cols),
        name="norm_back",
    )(*ins)


def attention_forward(ids, order, qkv, tile):
    rows = qkv.shape[0]
    blocks = rows // BLOCK

    def kernel(ids_ref, order_ref, x_ref, o_ref, lse_ref, q_ref, k_ref, v_ref, s_ref):
        for b in range(blocks):
            at = pl.ds(pl.multiple_of(order_ref[b] * BLOCK, BLOCK), BLOCK)
            here = slice(b * BLOCK, (b + 1) * BLOCK)
            for i, ref in enumerate((q_ref, k_ref, v_ref)):
                ref[here, :] = x_ref[at, i * HD : (i + 1) * HD]
        for t in range(rows // tile):
            mine = slice(t * tile, (t + 1) * tile)
            n = (t + 1) * tile
            s = lax.dot_general(q_ref[mine, :], k_ref[:n, :], NT, preferred_element_type=f32)
            s = s * SCALE
            seen = t * tile + lax.broadcasted_iota(jnp.int32, (tile, n), 0) >= (
                lax.broadcasted_iota(jnp.int32, (tile, n), 1)
            )
            s = jnp.where(seen, s, -1e30)
            top = jnp.max(s, axis=-1, keepdims=True)
            e = jnp.exp(s - top)
            total = jnp.sum(e, axis=-1, keepdims=True)
            p = (e * (1.0 / total)).astype(bf16)
            s_ref[mine, :] = jnp.dot(p, v_ref[:n, :], preferred_element_type=f32).astype(bf16)
            lse_ref[mine, :] = top + jnp.log(total)
        for b in range(blocks):
            at = pl.ds(pl.multiple_of(ids_ref[b] * BLOCK, BLOCK), BLOCK)
            o_ref[b * BLOCK : (b + 1) * BLOCK, :] = s_ref[at, :]

    smem = pl.BlockSpec(memory_space=pltpu.SMEM)
    vmem = pl.BlockSpec(memory_space=pltpu.VMEM)
    return pl.pallas_call(
        kernel,
        in_specs=[smem, smem, vmem],
        out_specs=[vmem, vmem],
        out_shape=[
            jax.ShapeDtypeStruct((rows, HD), bf16),
            jax.ShapeDtypeStruct((rows, 1), f32),
        ],
        scratch_shapes=[pltpu.VMEM((rows, HD), bf16)] * 4,
        compiler_params=BIG,
        cost_estimate=cost(2.3 * rows * rows * HD, 8 * rows * HD, rows * rows / 2),
        name="attention_forward",
    )(ids, order, qkv)


def attention_backward(ids, order, qkv, grad, lse, table, tile):
    rows = qkv.shape[0]
    blocks = rows // BLOCK

    def kernel(ids_ref, order_ref, x_ref, g_ref, lse_ref, t_ref, out_ref, q_ref, k_ref, v_ref, m_ref,
               r_ref, dk_ref, dv_ref):
        for b in range(blocks):
            at = pl.ds(pl.multiple_of(order_ref[b] * BLOCK, BLOCK), BLOCK)
            here = slice(b * BLOCK, (b + 1) * BLOCK)
            for i, ref in enumerate((q_ref, k_ref, v_ref)):
                ref[here, :] = x_ref[at, i * HD : (i + 1) * HD]
            m_ref[here, :] = g_ref[at, :]
        for t in reversed(range(rows // tile)):
            mine = slice(t * tile, (t + 1) * tile)
            n = (t + 1) * tile
            q, g = q_ref[mine, :], m_ref[mine, :]
            s = lax.dot_general(q, k_ref[:n, :], NT, preferred_element_type=f32) * SCALE
            seen = t * tile + lax.broadcasted_iota(jnp.int32, (tile, n), 0) >= (
                lax.broadcasted_iota(jnp.int32, (tile, n), 1)
            )
            p = jnp.where(seen, jnp.exp(s - lse_ref[mine, :]), 0.0)
            dp = lax.dot_general(g, v_ref[:n, :], NT, preferred_element_type=f32)
            shift = jnp.sum(p * dp, axis=-1, keepdims=True)
            ds = (p * (dp - shift)).astype(bf16)
            low = p.astype(bf16)
            dq = jnp.dot(ds, k_ref[:n, :], preferred_element_type=f32) * SCALE
            r_ref[mine, :128] = turned(
                dq[:, :128], t_ref[0, mine, :], -t_ref[1, mine, :], -t_ref[2, mine, :]
            ).astype(bf16)
            r_ref[mine, 128:HD] = dq[:, 128:].astype(bf16)
            dk = lax.dot_general(ds, q, TN, preferred_element_type=f32) * SCALE
            dv = lax.dot_general(low, g, TN, preferred_element_type=f32)
            if n == rows:
                dk_ref[...] = dk
                dv_ref[...] = dv
            else:
                dk_ref[:n, :] += dk
                dv_ref[:n, :] += dv
        r_ref[:, HD : HD + 128] = turned(
            dk_ref[:, :128], t_ref[0], -t_ref[1], -t_ref[2]
        ).astype(bf16)
        r_ref[:, HD + 128 : 2 * HD] = dk_ref[:, 128:].astype(bf16)
        r_ref[:, 2 * HD :] = dv_ref[...].astype(bf16)
        for b in range(blocks):
            at = pl.ds(pl.multiple_of(ids_ref[b] * BLOCK, BLOCK), BLOCK)
            out_ref[b * BLOCK : (b + 1) * BLOCK, :] = r_ref[at, :]

    smem = pl.BlockSpec(memory_space=pltpu.SMEM)
    vmem = pl.BlockSpec(memory_space=pltpu.VMEM)
    return pl.pallas_call(
        kernel,
        in_specs=[smem, smem, vmem, vmem, vmem, vmem],
        out_specs=vmem,
        out_shape=jax.ShapeDtypeStruct((rows, 3 * HD), bf16),
        scratch_shapes=[pltpu.VMEM((rows, HD), bf16)] * 4
        + [pltpu.VMEM((rows, 3 * HD), bf16)]
        + [pltpu.VMEM((rows, HD), f32)] * 2,
        compiler_params=BIG,
        cost_estimate=cost(6 * rows * rows * HD, 20 * rows * HD, rows * rows / 2),
        name="attention_backward",
    )(ids, order, qkv, grad, lse, table)


def exchange_heads(nz, nchip, ncore, attended, cot, w_dense, active):
    rows, width = cot.shape
    step = rows // nz
    length, hc = attended.shape
    part = length // nchip
    units = active.shape[1]
    tile = 256

    def kernel(att_ref, cot_hbm, w_hbm, act_hbm, mix_out, g_out, dw_out, cot_ref, w_ref, act_ref, gm_ref, dw_ref,
               ld, m_s, m_r, g_s, g_r, own_l, dw_l):
        chip = lax.axis_index("chip")
        core = lax.axis_index("core")
        loads = [
            pltpu.make_async_copy(w_hbm.at[pl.ds(core * hc, hc), :], w_ref, ld.at[0]),
            pltpu.make_async_copy(cot_hbm, cot_ref, ld.at[1]),
            pltpu.make_async_copy(act_hbm, act_ref, ld.at[2]),
        ]
        for copy in loads:
            copy.start()

        def chip_at(d):
            return lax.rem(chip + d, nchip)

        greet([{"chip": chip_at(d)} for d in range(1, nchip)])
        sent = [
            remote(
                att_ref.at[pl.ds(chip_at(d) * part, part), :],
                mix_out.at[pl.ds(chip * step, step), :], m_s.at[d], m_r.at[d], {"chip": chip_at(d)},
            )
            for d in range(1, nchip)
        ]
        kept = [
            pltpu.make_async_copy(
                att_ref.at[pl.ds(chip * part, part), :], mix_out.at[pl.ds(chip * step, step), :],
                own_l.at[0],
            )
        ]
        for copy in sent + kept:
            copy.start()
        loads[0].wait()
        loads[1].wait()
        for d in range(1, nchip + 1):
            to = chip_at(d)
            at = pl.ds(pl.multiple_of(to * step, step), step)
            gm_ref[at, :] = lax.dot_general(
                cot_ref[at, :], w_ref[...], NT, preferred_element_type=f32
            ).astype(bf16)
            there = g_out.at[pl.ds(chip * part, part), :]
            if d < nchip:
                copy = remote(gm_ref.at[at, :], there, g_s.at[d], g_r.at[d], {"chip": to})
                sent.append(copy)
            else:
                copy = pltpu.make_async_copy(gm_ref.at[at, :], there, own_l.at[1])
                kept.append(copy)
            copy.start()
        loads[2].wait()
        for t in range(units // tile):
            at = pl.ds(t * tile, tile)
            dw_ref[at, :] = lax.dot_general(
                act_ref[:, at], cot_ref[...], TN, preferred_element_type=f32
            ).astype(bf16)
            copy = pltpu.make_async_copy(dw_ref.at[at, :], dw_out.at[at, :], dw_l.at[t])
            copy.start()
            kept.append(copy)
        for copy in kept + sent:
            copy.wait()

    dma = pltpu.SemaphoreType.DMA
    anywhere = pl.BlockSpec(memory_space=pl.ANY)
    return pl.pallas_call(
        kernel,
        in_specs=[anywhere] * 4,
        out_specs=[anywhere] * 3,
        out_shape=[
            jax.ShapeDtypeStruct((rows, hc), bf16),
            jax.ShapeDtypeStruct((length, hc), bf16),
            jax.ShapeDtypeStruct((units, width), bf16),
        ],
        scratch_shapes=[
            pltpu.VMEM((rows, width), bf16),
            pltpu.VMEM((hc, width), bf16),
            pltpu.VMEM((rows, units), bf16),
            pltpu.VMEM((rows, hc), bf16),
            pltpu.VMEM((units, width), bf16),
            dma((3,)), dma((nchip,)), dma((nchip,)), dma((nchip,)), dma((nchip,)), dma((2,)),
            dma((units // tile,)),
        ],
        compiler_params=pltpu.CompilerParams(
            collective_id=3, has_side_effects=True, vmem_limit_bytes=62 * 2**20
        ),
        cost_estimate=cost(2 * rows * width * (hc + units), 4 * rows * width),
        name="exchange_heads",
    )(attended, cot, w_dense, active)


def gather_plane(nchip, chip, core, src, dst_of, send, recv, local):
    sibling = {"core": 1 - core}
    rows = src.shape[0]
    half = rows // 2
    here = dst_of(chip, core)
    begun = [pltpu.make_async_copy(src, here, local)]
    begun.append(remote(src, here, send.at[0], recv.at[0], sibling))
    relays = []
    arrivals = []

    def cut(ref, h):
        return ref.at[pl.ds(h * half, half), :]

    if nchip == 4:
        beside = chip + 1 - 2 * lax.rem(chip, 2)
        below = lax.rem(chip + 2, 4)
        across = 3 - chip
        order = ((beside, 0, 1), (below, 1, 2), (beside, 1, 1), (below, 0, 2))
        for i, (to, h, d) in enumerate(order):
            slot = 4 + 2 * d + h
            begun.append(
                remote(cut(src, h), cut(here, h), send.at[slot], recv.at[slot], {"chip": to})
            )

        def passing(owner, h, to):
            part = cut(dst_of(owner, core), h)
            return remote(part, part, send.at[10 + h], recv.at[10 + h], {"chip": to})

        relays = [(passing(beside, 0, below), beside, 0, 6), (passing(below, 1, beside), below, 1, 9)]
        arrivals = [(beside, 1, 7, 1), (below, 0, 8, 2), (across, 0, 10, 3), (across, 1, 11, 3)]
        others = [(beside, 1), (below, 2), (across, 3)]
    else:
        others = [(lax.rem(chip + d, nchip), d) for d in range(1, nchip)]
        for to, d in others:
            begun.append(
                remote(src, here, send.at[nchip + d], recv.at[nchip + chip], {"chip": to})
            )

    def side(owner, slot):
        part = dst_of(owner, core)
        return remote(part, part, send.at[slot], recv.at[slot], sibling)

    def slot_of(owner, d):
        return d if nchip == 4 else 2 * nchip + owner

    def first():
        for copy in begun:
            copy.start()

    def onward():
        if nchip == 4:
            for copy, owner, h, slot in relays:
                part = cut(dst_of(owner, core), h)
                remote(part, part, send.at[0], recv.at[slot], sibling).wait_recv()
                copy.start()

    def pass_on():
        if nchip == 4:
            for owner, h, slot, d in arrivals:
                part = cut(dst_of(owner, core), h)
                remote(part, part, send.at[0], recv.at[slot], sibling).wait_recv()
                if slot != 10:
                    side(owner, d).start()
        else:
            for owner, d in others:
                part = dst_of(owner, core)
                remote(part, part, send.at[0], recv.at[nchip + owner], sibling).wait_recv()
                side(owner, slot_of(owner, d)).start()

    def last():
        begun[0].wait()
        for copy in begun[1:]:
            copy.wait_send()
        for copy, owner, h, slot in relays:
            copy.wait_send()
        there = dst_of(chip, 1 - core)
        remote(there, there, send.at[0], recv.at[0], sibling).wait_recv()
        for owner, d in others:
            side(owner, slot_of(owner, d)).wait_send()
            there = dst_of(owner, 1 - core)
            remote(there, there, send.at[0], recv.at[slot_of(owner, d)], sibling).wait_recv()

    return first, onward, pass_on, last


def scatter_plane(nchip, chip, part, own, first, second, send, recv, local):
    halves = own.shape[0]
    copies = []
    shape = own.shape[2:]

    def add(dst, terms):
        def rows(lead):
            @pl.loop(0, shape[-2] // 16)
            def _(i):
                at = lead + (pl.ds(pl.multiple_of(i * 16, 16), 16), slice(None))
                acc = dst[at].astype(f32)
                for term in terms:
                    acc = acc + term[at].astype(f32)
                dst[at] = acc.astype(bf16)

        if len(shape) == 2:
            rows(())
        else:

            @pl.loop(0, shape[0])
            def _(b):
                rows((b,))

    if nchip == 4:
        beside = chip + 1 - 2 * lax.rem(chip, 2)
        below = lax.rem(chip + 2, 4)
        across = 3 - chip
        ways = [(beside, below), (below, beside)]
        kept = [
            [
                pltpu.make_async_copy(part(chip, h), own.at[h, 0], local.at[h, 0]),
                pltpu.make_async_copy(part(ways[h][1], h), own.at[h, 1], local.at[h, 1]),
            ]
            for h in range(2)
        ]
        leave = [
            [
                remote(
                    part(across, h), first.at[h, 1], send.at[h, 1], recv.at[h, 1],
                    {"chip": ways[h][0]},
                ),
                remote(
                    part(ways[h][0], h), first.at[h, 0], send.at[h, 0], recv.at[h, 0],
                    {"chip": ways[h][0]},
                ),
            ]
            for h in range(2)
        ]
        follow = [
            remote(
                own.at[h, 1], second.at[h], send.at[h, 2], recv.at[h, 2], {"chip": ways[h][1]}
            )
            for h in range(2)
        ]

        def begin():
            for i in range(2):
                for h in range(2):
                    leave[h][i].start()
            for h in range(2):
                kept[h][1].start()
                kept[h][0].start()

        def middle():
            for h in range(2):
                kept[h][1].wait()
                leave[h][0].wait_recv()
                add(own.at[h, 1], [first.at[h, 1]])
                follow[h].start()

        def finish():
            for h in range(2):
                kept[h][0].wait()
                leave[h][1].wait_recv()
                follow[h].wait_recv()
                add(own.at[h, 0], [first.at[h, 0], second.at[h]])

        def last():
            for h in range(2):
                for copy in leave[h] + [follow[h]]:
                    copy.wait_send()
    else:
        to = [lax.rem(chip + d, nchip) for d in range(nchip)]
        kept = pltpu.make_async_copy(part(chip, 0), own.at[0, 0], local.at[0, 0])
        leave = [
            remote(part(to[d], 0), first.at[0, d], send.at[0, d], recv.at[0, d], {"chip": to[d]})
            for d in range(1, nchip)
        ]

        def begin():
            for copy in leave:
                copy.start()
            kept.start()

        def middle():
            pass

        def finish():
            kept.wait()
            for copy in leave:
                copy.wait_recv()
            add(own.at[0, 0], [first.at[0, d] for d in range(1, nchip)])

        def last():
            for copy in leave:
                copy.wait_send()

    return begin, middle, finish, last


def tail(nz, nchip, ncore, dwo, dwd, dwi, vectors, normed1, grad_project, grad_hidden, tok, w_qkv, w_in, gain1, gain2):
    width = dwo.shape[1]
    ro, rd = dwo.shape[0], dwd.shape[0] // nchip
    halves = 2 if nchip == 4 else 1
    hz = nz // halves
    hd = rd // halves
    ci, cq = dwi.shape[1], grad_project.shape[1] // 3
    wrows = width // nz
    ri = wrows // nchip
    rows = tok.shape[0]
    step = rows // nz
    own = step // ncore
    vr = vectors.shape[0]
    chunk = 512
    dwi = dwi.reshape(nz, nchip, ri, ci)
    dwd = dwd.reshape(nchip, rd, width)

    def kernel(
        dwo_ref, dwd_ref, dwi_ref, vec_ref, n_hbm, gp_hbm, gh_hbm, tok_hbm, wq_hbm, wi_hbm, g1_ref, g2_ref,
        go_ref, gd_ref, gi_ref, gq_ref, e_ref, vsum_ref,
        x_ref, gp_ref, gh_ref, wq_ref, wi_ref, dwq_ref, eb,
        oi, fi, si, oq, fq, sq, od, fd, sd, ti, tq, se, ze, cs, v0, v1, v2, v3,
        ld, ri_s, ri_r, ri_l, rq_s, rq_r, rq_l, rd_s, rd_r, rd_l, x_s, x_r, ez_s, ez_r, t_s, t_r, t_l,
        go_s, go_r, gd_s, gd_r, gi_s, gi_r, gq_s, gq_r, own_l,
        v_s, v_r,
    ):
        z = lax.axis_index("seq")
        chip = lax.axis_index("chip")
        core = lax.axis_index("core")
        sibling = {"core": 1 - core}

        def z_at(d):
            return lax.rem(z + d, nz)

        def chip_at(d):
            return lax.rem(chip + d, nchip)

        loads = [
            pltpu.make_async_copy(a, b, ld.at[i])
            for i, (a, b) in enumerate(
                ((n_hbm, x_ref), (gp_hbm, gp_ref), (gh_hbm, gh_ref), (wi_hbm, wi_ref), (wq_hbm, wq_ref))
            )
        ]
        for copy in loads:
            copy.start()
        greet(
            [{"seq": z_at(d)} for d in range(1, nz)]
            + [{"chip": chip_at(d)} for d in range(1, nchip)]
            + [sibling]
        )

        def turn(kind, part, turned):
            copies = [
                remote(
                    part(z_at(d)), turned.at[z], t_s.at[kind, d], t_r.at[kind, z],
                    {"seq": z_at(d)},
                )
                for d in range(1, nz)
            ]
            copies.append(pltpu.make_async_copy(part(z), turned.at[z], t_l.at[kind]))
            for copy in copies:
                copy.start()
            return copies

        def turned_at(kind, part, turned, source):
            return remote(part, turned.at[source], t_s.at[kind, 0], t_r.at[kind, source], sibling)

        sum_i = scatter_plane(
            nchip, chip, lambda c, h: dwi_ref.at[pl.ds(h * hz, hz), c], oi, fi, si, ri_s, ri_r, ri_l
        )
        sum_q = scatter_plane(
            nchip, chip, lambda c, h: dwq_ref.at[pl.ds(h * hz, hz), pl.ds(c * ri, ri)], oq, fq, sq,
            rq_s, rq_r, rq_l,
        )
        sum_d = scatter_plane(
            nchip, chip, lambda c, h: dwd_ref.at[c, pl.ds(h * hd, hd)], od, fd, sd, rd_s, rd_r, rd_l
        )
        sum_i[0]()

        loads[0].wait()
        loads[1].wait()
        for b in range(nz):
            dwq_ref[b] = lax.dot_general(
                x_ref[:, b * wrows : (b + 1) * wrows], gp_ref[...], TN, preferred_element_type=f32
            ).astype(bf16)
        load_tok = pltpu.make_async_copy(tok_hbm, x_ref, ld.at[5])
        load_tok.start()
        sum_i[1]()
        sum_q[0]()
        sum_d[0]()

        for copy in loads[2:] + [load_tok]:
            copy.wait()
        cs[...] = jnp.zeros_like(cs)

        def norm_back(b):
            at = pl.ds(b * step, step)
            x = x_ref[at, :].astype(f32)
            mean = jnp.mean(x, axis=-1, keepdims=True)
            x = x - mean
            inv = lax.rsqrt(jnp.mean(x * x, axis=-1, keepdims=True) + EPSILON)

            @pl.loop(0, width // chunk)
            def _(c):
                cols = pl.ds(pl.multiple_of(c * chunk, chunk), chunk)
                xhat = (x_ref[at, cols].astype(f32) - mean) * inv
                gn = lax.dot_general(
                    gp_ref[at, :], wq_ref[cols, :], NT, preferred_element_type=f32
                )
                cs[0:1, cols] += jnp.sum(gn * xhat, axis=0, keepdims=True)
                cs[1:2, cols] += jnp.sum(gn, axis=0, keepdims=True)
                e = gn * g1_ref[:, cols]
                gn = lax.dot_general(
                    gh_ref[at, :], wi_ref[cols, :], NT, preferred_element_type=f32
                )
                cs[2:3, cols] += jnp.sum(gn * xhat, axis=0, keepdims=True)
                cs[3:4, cols] += jnp.sum(gn, axis=0, keepdims=True)
                e = (e + gn * g2_ref[:, cols]).astype(bf16)
                for k in range(ncore):
                    eb[b, k, :, cols] = e[k * own : (k + 1) * own]

            copy = remote(eb.at[b, 1 - core], se.at[b], x_s.at[b], x_r.at[b], sibling)
            copy.start()
            return copy

        exchanged = [norm_back(b) for b in range(nz)]
        sum_i[2]()
        turn_i = turn(0, lambda to: oi.at[to // hz, 0, lax.rem(to, hz)], ti)
        sum_q[1]()

        v0[...] = vec_ref[...]
        lanes = width // 128
        for k in range(4):
            for j in range(lanes):
                v0[k * lanes + j : k * lanes + j + 1, :] = cs[k : k + 1, j * 128 : (j + 1) * 128]
        v_chips = [
            remote(v0, v1.at[chip], v_s.at[d], v_r.at[chip], {"chip": chip_at(d)})
            for d in range(1, nchip)
        ]
        for copy in v_chips:
            copy.start()
        v1[chip] = v0[...]

        go_at = lambda c, k: go_ref.at[pl.ds(k * (ro * nchip) + c * ro, ro), :]
        gd_at = lambda c, k, h: gd_ref.at[pl.ds(k * (rd * nchip) + c * rd + h * hd, hd), :]
        gi_at = lambda c, k, s: gi_ref.at[
            pl.ds(c * ri, ri), pl.ds((s * ncore + k) * ci, ci)
        ]
        gq_at = lambda c, k, s, g: gq_ref.at[
            pl.ds(c * ri, ri), pl.ds(g * nz * ncore * cq + (s * ncore + k) * cq, cq)
        ]
        group = functools.partial(gather_plane, nchip, chip, core)
        rows_o = group(dwo_ref, go_at, go_s, go_r, own_l.at[nz])
        rows_o[0]()

        for b in range(nz):
            exchanged[b].wait_recv()

            @pl.loop(0, own // 16)
            def _(i):
                at = pl.ds(pl.multiple_of(i * 16, 16), 16)
                eb[b, core, at, :] = (
                    eb[b, core, at, :].astype(f32) + se[b, at, :].astype(f32)
                ).astype(bf16)

        sum_q[2]()
        turn_q = turn(1, lambda to: oq.at[to // hz, 0, lax.rem(to, hz)], tq)
        sum_d[1]()

        for d in range(1, nchip):
            other = chip_at(d)
            remote(v0, v1.at[other], v_s.at[d], v_r.at[other], sibling).wait_recv()
        total = v1[0]
        for d in range(1, nchip):
            total = total + v1[d]
        v2[core] = total
        v_side = remote(v2.at[core], v2.at[core], v_s.at[nchip], v_r.at[nchip], sibling)
        v_side.start()

        groups = []
        for dz in range(1, nz):
            turned_at(0, oi.at[0, 0, 0], ti, z_at(dz)).wait_recv()
        turn_i[-1].wait()
        for source in range(nz):
            groups.append(
                group(
                    ti.at[source], functools.partial(gi_at, s=source), gi_s.at[source],
                    gi_r.at[source], own_l.at[source],
                )
            )
            groups[-1][0]()
        sent_e = [
            remote(
                eb.at[z_at(d), core], ze.at[d], ez_s.at[d], ez_r.at[d], {"seq": z_at(d)}
            )
            for d in range(1, nz)
        ]
        for copy in sent_e:
            copy.start()

        v_side.wait_recv()
        vz = v2[0]
        for c in range(1, ncore):
            vz = vz + v2[c]
        v3[z] = vz
        v_zs = [
            remote(v3.at[z], v3.at[z], v_s.at[nchip + d], v_r.at[nchip + 1 + z], {"seq": z_at(d)})
            for d in range(1, nz)
        ]
        for copy in v_zs:
            copy.start()
        sum_d[2]()
        rows_d = [
            group(od.at[h, 0], functools.partial(gd_at, h=h), gd_s.at[h], gd_r.at[h], own_l.at[nz + 1 + h])
            for h in range(halves)
        ]
        for first, onward, pass_on, last in rows_d:
            first()
        rows_o[1]()
        for first, onward, pass_on, last in groups:
            onward()

        for dz in range(1, nz):
            turned_at(1, oq.at[0, 0, 0], tq, z_at(dz)).wait_recv()
        turn_q[-1].wait()
        later = []
        for source in range(nz):
            for g in range(3):
                later.append(
                    group(
                        tq.at[source, :, pl.ds(g * cq, cq)],
                        functools.partial(gq_at, s=source, g=g),
                        gq_s.at[source, g], gq_r.at[source, g], own_l.at[4 + nz + 3 * source + g],
                    )
                )
        for first, onward, pass_on, last in later:
            first()
        rows_o[2]()
        for first, onward, pass_on, last in rows_d:
            onward()
        for first, onward, pass_on, last in groups:
            pass_on()
        for first, onward, pass_on, last in later:
            onward()
        for first, onward, pass_on, last in rows_d:
            pass_on()

        for d in range(1, nz):
            other = z_at(d)
            remote(v3.at[0], v3.at[other], v_s.at[0], v_r.at[nchip + 1 + other], sibling).wait_recv()
        total = v3[0]
        for d in range(1, nz):
            total = total + v3[d]
        vsum_ref[...] = total

        for copy in sent_e:
            copy.wait_recv()

        @pl.loop(0, own // 16)
        def _(i):
            at = pl.ds(pl.multiple_of(i * 16, 16), 16)
            acc = eb[z, core, at, :].astype(f32)
            for d in range(1, nz):
                acc = acc + ze[d, at, :].astype(f32)
            e_ref[at, :] = acc

        for first, onward, pass_on, last in later:
            pass_on()

        for first, onward, pass_on, last in [rows_o] + rows_d + groups + later:
            last()
        for begin, middle, finish, last in (sum_i, sum_q, sum_d):
            last()
        for copy in exchanged + sent_e + v_chips + v_zs + [v_side]:
            copy.wait_send()
        for copy in turn_i[:-1] + turn_q[:-1]:
            copy.wait_send()

    dma = pltpu.SemaphoreType.DMA
    anywhere = pl.BlockSpec(memory_space=pl.ANY)
    vmem = pl.BlockSpec(memory_space=pltpu.VMEM)
    out_shape = [
        jax.ShapeDtypeStruct((ncore * nchip * ro, width), bf16),
        jax.ShapeDtypeStruct((ncore * nchip * rd, width), bf16),
        jax.ShapeDtypeStruct((wrows, nz * ncore * ci), bf16),
        jax.ShapeDtypeStruct((wrows, 3 * nz * ncore * cq), bf16),
        jax.ShapeDtypeStruct((own, width), f32),
        jax.ShapeDtypeStruct((vr, 128), f32),
    ]
    slots = max(3 * nchip, 12)
    pair = 2 if nchip == 4 else 1
    nfirst = 2 if nchip == 4 else nchip

    def three(*shape):
        return [
            pltpu.VMEM((halves, pair) + shape, bf16),
            pltpu.VMEM((halves, nfirst) + shape, bf16),
            pltpu.VMEM((halves,) + shape, bf16),
        ]

    return pl.pallas_call(
        kernel,
        in_specs=[anywhere] * 3 + [vmem] + [anywhere] * 6 + [vmem] * 2,
        out_specs=[anywhere] * 4 + [vmem] * 2,
        out_shape=out_shape,
        scratch_shapes=[
            pltpu.VMEM((rows, width), bf16),
            pltpu.VMEM(grad_project.shape, bf16),
            pltpu.VMEM(grad_hidden.shape, bf16),
            pltpu.VMEM(w_qkv.shape, bf16),
            pltpu.VMEM(w_in.shape, bf16),
            pltpu.VMEM((nz, wrows, 3 * cq), bf16),
            pltpu.VMEM((nz, ncore, own, width), bf16),
        ]
        + three(hz, ri, ci)
        + three(hz, ri, 3 * cq)
        + three(hd, width)
        + [
            pltpu.VMEM((nz, ri, ci), bf16),
            pltpu.VMEM((nz, ri, 3 * cq), bf16),
            pltpu.VMEM((nz, own, width), bf16),
            pltpu.VMEM((nz, own, width), bf16),
            pltpu.VMEM((8, width), f32),
            pltpu.VMEM((vr, 128), f32),
            pltpu.VMEM((nchip, vr, 128), f32),
            pltpu.VMEM((ncore, vr, 128), f32),
            pltpu.VMEM((nz, vr, 128), f32),
            dma((6,)),
            dma((halves, nchip)), dma((halves, nchip)), dma((halves, 2)),
            dma((halves, nchip)), dma((halves, nchip)), dma((halves, 2)),
            dma((halves, nchip)), dma((halves, nchip)), dma((halves, 2)),
            dma((nz,)), dma((nz,)),
            dma((nz,)), dma((nz,)),
            dma((2, nz)), dma((2, nz)), dma((2,)),
            dma((slots,)), dma((slots,)),
            dma((halves, slots)), dma((halves, slots)),
            dma((nz, slots)), dma((nz, slots)),
            dma((nz, 3, slots)), dma((nz, 3, slots)),
            dma((4 + 4 * nz,)),
            dma((nchip + nz,)), dma((nchip + nz + 1,)),
        ],
        compiler_params=pltpu.CompilerParams(
            collective_id=2, has_side_effects=True, vmem_limit_bytes=62 * 2**20
        ),
        cost_estimate=cost(4 * rows * width * (3 * cq + ci), 20 * rows * width),
        name="tail",
    )(dwo, dwd, dwi, vectors, normed1, grad_project, grad_hidden, tok, w_qkv, w_in, gain1, gain2)


def on_device(
    nz,
    nchip,
    ncore,
    tokens,
    block_ids,
    cotangent,
    norm1_gain,
    norm1_bias,
    norm2_gain,
    norm2_bias,
    w_qkv,
    b_qkv,
    w_dense,
    b_dense,
    w_in,
    b_in,
    w_out,
    b_out,
):
    own, width = tokens.shape
    z = lax.axis_index("seq")
    chip = lax.axis_index("chip")
    core = lax.axis_index("core")
    ranks = nz * ncore
    rank = z * ncore + core
    rows = ranks * own
    ffr = w_out.shape[0] // ncore
    hc = width // ranks
    split = max(1, HD // hc)
    wrows = width // nz
    blocks = block_ids.shape[1]
    length = blocks * BLOCK
    core_at = core.reshape(1)

    parts = [norm1_gain, norm1_bias, norm2_gain, norm2_bias, b_qkv, b_dense + 0, b_in, b_out,
             block_ids.reshape(-1)]
    sizes = [p.shape[0] for p in parts]
    total = -(-sum(sizes) // 2048) * 2048
    starts = [sum(sizes[:i]) for i in range(len(sizes))]
    small = sum(
        jnp.pad(p.astype(f32), (at, total - at - p.shape[0])) for p, at in zip(parts, starts)
    )
    small = small.astype(bf16).reshape(-1, 128)
    tok, w_in_c, w_qkv_c, small = front(nz, nchip, ncore, tokens, w_in, w_qkv, small)
    tok = tok.reshape(rows, width)
    small = small.reshape(nz, total)

    def vector(i):
        return small[:, starts[i] : starts[i] + sizes[i]].astype(f32).reshape(1, -1)

    gain1, bias1, gain2, bias2 = [vector(i) for i in range(4)]
    bias_c = lax.dynamic_index_in_dim(vector(4).reshape(3, ranks, hc), rank, 1, keepdims=False)
    bias_c = bias_c.reshape(1, 3 * hc)
    bias_in = lax.dynamic_slice_in_dim(vector(6), rank * ffr, ffr, 1)
    ids = vector(8).astype(jnp.int32).reshape(nz, blocks)
    tok, cot_own = lax.optimization_barrier((tok, cotangent))
    cot = lax.all_gather(cot_own, TP, axis=0, tiled=True)

    per_chip = blocks // nchip
    ids_rows = lax.dynamic_slice_in_dim(ids, chip * per_chip, per_chip, 1).reshape(-1)
    ids_seq = lax.dynamic_index_in_dim(ids, chip, 0, keepdims=False)
    slots = jnp.arange(blocks, dtype=jnp.int32)
    order = jnp.sum(jnp.where(ids_seq[None, :] == slots[:, None], slots[None, :], 0), axis=1)
    place = (lax.rem(rank, split) == 0).astype(jnp.int32).reshape(1)
    table = jnp.asarray(turn_table(length))

    def heads_of(x):
        g = x.shape[1] // hc
        if split > 1:
            x = lax.all_gather(x.reshape(rows, g, hc), "core", axis=2, tiled=True)
        x = x.reshape(nz, rows // nz, g * HD)
        return lax.all_to_all(x, "chip", 0, 0, tiled=True).reshape(length, g * HD)

    def heads_back(x):
        g = x.shape[1] // HD
        x = x.reshape(nchip, length // nchip, g * HD)
        x = lax.all_to_all(x, "chip", 0, 0, tiled=True).reshape(rows, g * HD)
        if split > 1:
            x = lax.dynamic_slice_in_dim(x.reshape(rows, g, HD), core * hc, hc, 2)
        return x.reshape(rows, g * hc)

    tile = 256
    normed1, qkv = projections(nz, ids_rows, place, tok, w_qkv_c, bias_c, gain1, bias1, table)
    qkv = heads_of(qkv)
    normed2, active, slope = feed_forward(nz, tok, w_in_c, bias_in, gain2, bias2)
    qkv, active, slope, normed2 = lax.optimization_barrier((qkv, active, slope, normed2))
    attended, lse = attention_forward(ids_seq, order, qkv, tile)
    attended, cot = lax.optimization_barrier((attended, cot))

    if split == 1:
        mixed, g, dw_out = exchange_heads(nz, nchip, ncore, attended, cot, w_dense, active)
    else:
        mixed = heads_back(attended)
        g = heads_of(grad_of_mixed(nz, core_at, cot, w_dense, hc))
        dw_out = lax.dot_general(active, cot, TN, preferred_element_type=f32).astype(bf16)
    mixed, g, dw_out, cot = lax.optimization_barrier((mixed, g, dw_out, cot))
    s_out = lax.psum_scatter(dw_out, "chip", scatter_dimension=0, tiled=True)
    part_out = layer_out(nz, core_at, mixed, w_dense, active, w_out)
    g, part_out = lax.optimization_barrier((g, part_out))
    dqkv = attention_backward(ids_seq, order, qkv, g, lse, table, tile)
    dqkv, cot, mixed, part_out = lax.optimization_barrier((dqkv, cot, mixed, part_out))
    grad_project = heads_back(dqkv)
    grad_hidden, sum_bin = grad_of_hidden(nz, core_at, cot, w_out, slope)
    dw_in = lax.dot_general(normed2, grad_hidden, TN, preferred_element_type=f32).astype(bf16)
    dw_dense = lax.dot_general(mixed, cot, TN, preferred_element_type=f32).astype(bf16)
    grad_project, dw_in, dw_dense, s_out, part_out = lax.optimization_barrier(
        (grad_project, dw_in, dw_dense, s_out, part_out)
    )
    summed_out = lax.psum_scatter(part_out, TP, scatter_dimension=0, tiled=True).astype(f32)
    sum_bqkv = jnp.sum(grad_project.astype(f32), axis=0)

    here = jnp.arange(ranks, dtype=jnp.int32) == rank
    mine_bqkv = jnp.where(here[None, :, None], sum_bqkv.reshape(3, 1, hc), 0.0)
    mine_bin = jnp.where(here[:, None], sum_bin.reshape(1, ffr), 0.0)
    vectors = [
        jnp.zeros(4 * width, f32),
        mine_bqkv.reshape(-1),
        jnp.sum(cotangent.astype(f32), axis=0),
        mine_bin.reshape(-1),
    ]
    vectors = jnp.concatenate([v.reshape(-1, 128) for v in vectors])
    g_wout, g_wdense, g_win, g_wqkv, e, sums = tail(
        nz, nchip, ncore, s_out, dw_dense, dw_in, vectors, normed1, grad_project, grad_hidden, tok,
        w_qkv_c, w_in_c, gain1, gain2
    )
    sums = sums.reshape(-1)
    at = 0
    small_out = []
    for size in (width, width, width, width, 3 * width, width, ranks * ffr):
        small_out.append(lax.dynamic_slice_in_dim(sums, at + z * (size // nz), size // nz))
        at += size
    g_gain1, g_bias1, g_gain2, g_bias2, g_bqkv, g_bdense, g_bin = small_out

    output = (tokens.astype(f32) + summed_out + vector(5) + vector(7)).astype(bf16)
    xhat_own, inv_own = stats(tokens.astype(f32))
    terms = (
        e
        - jnp.mean(e, axis=-1, keepdims=True)
        - xhat_own * jnp.mean(e * xhat_own, axis=-1, keepdims=True)
    ) * inv_own
    grad_tokens = (cotangent.astype(f32) + terms).astype(bf16)
    g_wout, g_wdense, g_win, g_wqkv = widen([g_wout, g_wdense, g_win, g_wqkv])
    return (
        output,
        grad_tokens,
        g_gain1,
        g_bias1,
        g_gain2,
        g_bias2,
        g_wqkv,
        g_bqkv,
        g_wdense,
        g_bdense,
        g_win,
        g_bin,
        g_wout,
        g_bdense,
    )


def solution(mesh):
    nz, nctx = mesh.shape["seq"], mesh.shape["ctx"]
    ncore = 2
    nchip = nctx // ncore
    fine = Mesh(mesh.devices.reshape(nz, nchip, ncore), ("seq", "chip", "core"))
    own = P(("seq", "chip", "core"), None)
    vec = P("seq")
    mat = P("seq", None)
    return jax.shard_map(
        functools.partial(on_device, nz, nchip, ncore),
        mesh=fine,
        in_specs=(own, mat, own, vec, vec, vec, vec, mat, vec, mat, vec, mat, vec, mat, vec),
        out_specs=(own, own, vec, vec, vec, vec, mat, vec, mat, vec, mat, vec, mat, vec),
        check_vma=False,
    )
```

```python
import functools
import math

import jax
import jax.numpy as jnp
import numpy as np
from jax import lax
from jax.experimental import pallas as pl
from jax.experimental.pallas import tpu as pltpu
from jax.sharding import Mesh, PartitionSpec as P

HD = 256
ROT = 64
BLOCK = 96
EPSILON = 1e-05
ROT_BASE = 10000.0
SCALE = HD ** (-0.5)
f32 = jnp.float32
bf16 = jnp.bfloat16
TP = ("seq", "core")
MESH = pl.DeviceIdType.MESH
NT = (((1,), (1,)), ((), ()))
TN = (((0,), (0,)), ((), ()))
BIG = pltpu.CompilerParams(vmem_limit_bytes=62 * 2**20)


def remote(src, dst, send, recv, target):
    return pltpu.make_async_remote_copy(
        src_ref=src, dst_ref=dst, send_sem=send, recv_sem=recv, device_id=target,
        device_id_type=MESH,
    )


def greet(targets):
    barrier = pltpu.get_barrier_semaphore()
    for target in targets:
        pl.semaphore_signal(barrier, inc=1, device_id=target, device_id_type=MESH)
    pl.semaphore_wait(barrier, len(targets))


def front(nz, nchip, ncore, tokens, w_in, w_qkv, small):
    own, width = tokens.shape
    wrows, ff = w_in.shape
    heads3 = w_qkv.shape[1]
    nctx = nchip * ncore
    piece = wrows // nctx
    half = piece // 2
    zi, zq = ff // nz, heads3 // 3 // nz
    ci, cq = zi // ncore, zq // ncore

    def kernel(
        tok_ref, wi_ref, wq_ref, sm_ref, tok_out, wi_out, wq_out, sm_out, buf_i, buf_q,
        up_s, up_r, dn_s, dn_r, sib_s, sib_r, zi_s, zi_r, zq_s, zq_r, p_s, p_r, r_s, loc, loc_p, sm_s, sm_r,
    ):
        z = lax.axis_index("seq")
        chip = lax.axis_index("chip")
        core = lax.axis_index("core")
        share = chip * ncore + core
        sibling = {"core": 1 - core}

        def z_at(d):
            return lax.rem(z + d, nz)

        def plane_at(d):
            other = lax.rem(share + d, nctx)
            return other // ncore, lax.rem(other, ncore)

        greet(
            [{"seq": z_at(d)} for d in range(1, nz)]
            + [{"chip": plane_at(d)[0], "core": plane_at(d)[1]} for d in range(1, nctx)]
        )

        def around(body, distances=range(1, nz)):
            for distance in distances:
                for other in (z + distance, z - distance):

                    @pl.when(jnp.logical_and(other >= 0, other < nz))
                    def _():
                        body(jnp.clip(other, 0, nz - 1))

        rows = pl.ds(share * piece, piece)

        def hop(to):
            pairs = [(wi_ref.at[rows, pl.ds(to * zi, zi)], buf_i.at[z], zi_s.at[to], zi_r.at[z])]
            for k in range(ncore):
                for g in range(3):
                    pairs.append(
                        (
                            wq_ref.at[rows, pl.ds(g * zq * nz + to * zq + k * cq, cq)],
                            buf_q.at[z, k, :, pl.ds(g * cq, cq)],
                            zq_s.at[to, k, g], zq_r.at[z, k, g],
                        )
                    )
            return pairs

        def hop_to(to):
            return [remote(a, b, c, d, {"seq": to}) for a, b, c, d in hop(to)]

        def send_hop(to):
            for copy in hop_to(to):
                copy.start()

        def hop_left(to):
            for copy in hop_to(to):
                copy.wait_send()

        def hop_arrival(source):
            here = buf_i.at[source]
            remote(here, here, zi_s.at[0], zi_r.at[source], sibling).wait_recv()
            for k in range(ncore):
                for g in range(3):
                    here = buf_q.at[source, k, :, pl.ds(g * cq, cq)]
                    remote(here, here, zq_s.at[0, 0, 0], zq_r.at[source, k, g], sibling).wait_recv()

        def up(s):
            at = jnp.maximum(z - s, 0)
            src = tok_ref if s == 0 else tok_out.at[at, core]
            return remote(
                src, tok_out.at[at, core], up_s.at[s], up_r.at[s],
                {"seq": jnp.minimum(z + 1, nz - 1)},
            )

        def down(s):
            at = jnp.minimum(z + s, nz - 1)
            src = tok_ref if s == 0 else tok_out.at[at, core]
            return remote(
                src, tok_out.at[at, core], dn_s.at[s], dn_r.at[s],
                {"seq": jnp.maximum(z - 1, 0)},
            )

        def side(shard, own_rows=False):
            src = tok_ref if own_rows else tok_out.at[shard, core]
            return remote(src, tok_out.at[shard, core], sib_s.at[shard], sib_r.at[shard], sibling)

        def token_step(s):
            @pl.when(z - 1 - s >= 0)
            def _():
                shard = jnp.maximum(z - 1 - s, 0)
                here = tok_out.at[shard, core]
                remote(here, here, up_s.at[s], up_r.at[s], sibling).wait_recv()
                if s + 1 < nz - 1:

                    @pl.when(z + 1 < nz)
                    def _():
                        up(s + 1).start()

                side(shard).start()

            @pl.when(z + 1 + s < nz)
            def _():
                shard = jnp.minimum(z + 1 + s, nz - 1)
                here = tok_out.at[shard, core]
                remote(here, here, dn_s.at[s], dn_r.at[s], sibling).wait_recv()
                if s + 1 < nz - 1:

                    @pl.when(z > 0)
                    def _():
                        down(s + 1).start()

                side(shard).start()

        def pieces(source, k):
            return buf_i.at[source, :, pl.ds(k * ci, ci)], buf_q.at[source, k]

        def places(source, owner):
            at = pl.ds(source * wrows + owner * piece, piece)
            return wi_out.at[at, :], wq_out.at[at, :]

        def cut(ref, h):
            return ref if h is None else ref.at[pl.ds(h * half, half), :]

        def in_place(source):
            return [
                pltpu.make_async_copy(a, b, loc_p.at[source, i])
                for i, (a, b) in enumerate(zip(pieces(source, core), places(source, share)))
            ]

        if nchip == 4:
            beside = chip + 1 - 2 * lax.rem(chip, 2)
            below = lax.rem(chip + 2, 4)
            across = 3 - chip
            order = ((beside, 0), (below, 1), (beside, 1), (below, 0))

            def spread(source):
                copies = []
                for way, (to, h) in enumerate(order):
                    for k in range(ncore):
                        for i, (a, b) in enumerate(zip(pieces(source, k), places(source, share))):
                            copies.append(
                                remote(
                                    cut(a, h), cut(b, h), p_s.at[source, i, k, way],
                                    p_r.at[source, i, share, h], {"chip": to, "core": k},
                                )
                            )
                return copies

            def relays(source):
                copies = []
                for h, (came, to) in enumerate(((beside, below), (below, beside))):
                    for k in range(ncore):
                        owner = came * ncore + k
                        for i, ref in enumerate(places(source, owner)):
                            part = cut(ref, h)
                            copies.append(
                                remote(
                                    part, part, r_s.at[source, i, k, h],
                                    p_r.at[source, i, owner, h], {"chip": to},
                                )
                            )
                return copies

            def relay(source):
                for copy in relays(source):
                    copy.wait_recv()
                    copy.start()

            rest = [(beside, 1), (below, 0), (across, 0), (across, 1)]
        else:

            def spread(source):
                copies = []
                for d in range(1, nctx):
                    to, k = plane_at(d)
                    for i, (a, b) in enumerate(zip(pieces(source, k), places(source, share))):
                        copies.append(
                            remote(
                                a, b, p_s.at[source, i, 0, d], p_r.at[source, i, share, 0],
                                {"chip": to, "core": k},
                            )
                        )
                return copies

            def relay(source):
                pass

        def to_sibling(source):
            return [
                remote(a, b, p_s.at[source, i, 0, 4], p_r.at[source, i, share, 0], sibling)
                for i, (a, b) in enumerate(zip(pieces(source, 1 - core), places(source, share)))
            ]

        def hand_on(source):
            for copy in spread(source) + in_place(source):
                copy.start()
            if nchip == 4:
                for copy in to_sibling(source):
                    copy.start()

        def arrive(source):
            hop_arrival(source)
            hand_on(source)

        smalls = [
            remote(sm_ref, sm_out.at[z], sm_s.at[d], sm_r.at[z], {"seq": z_at(d)})
            for d in range(1, nz)
        ]
        for copy in smalls:
            copy.start()
        around(send_hop)

        @pl.when(z + 1 < nz)
        def _():
            up(0).start()

        @pl.when(z > 0)
        def _():
            down(0).start()

        side(z, True).start()
        mine = [
            pltpu.make_async_copy(tok_ref, tok_out.at[z, core], loc.at[0]),
            pltpu.make_async_copy(sm_ref, sm_out.at[z], loc.at[1]),
        ]
        held = [
            pltpu.make_async_copy(a, b, loc.at[2 + i]) for i, (a, b, c, d) in enumerate(hop(z))
        ]
        for copy in held + mine:
            copy.start()
        for copy in held:
            copy.wait()
        hand_on(z)
        for distance in range(1, nz):
            around(arrive, [distance])
            if distance == 1:
                relay(z)
            else:
                around(relay, [distance - 1])
            token_step(distance - 1)
        around(relay, [nz - 1])

        for copy in mine:
            copy.wait()
        for shard in range(nz):
            there = tok_out.at[shard, 1 - core]
            remote(there, there, sib_s.at[shard], sib_r.at[shard], sibling).wait_recv()
            side(shard).wait_send()
        for s in range(nz - 1):

            @pl.when(jnp.logical_and(z + 1 < nz, z - s >= 0))
            def _():
                up(s).wait_send()

            @pl.when(jnp.logical_and(z > 0, z + s < nz))
            def _():
                down(s).wait_send()

        around(hop_left)
        for copy in smalls:
            copy.wait_send()
        for d in range(1, nz):
            there = sm_out.at[z_at(d)]
            remote(there, there, sm_s.at[d], sm_r.at[z_at(d)], sibling).wait_recv()
        for source in range(nz):
            for copy in in_place(source):
                copy.wait()
            for copy in spread(source):
                copy.wait_send()
            if nchip == 4:
                for copy in to_sibling(source) + relays(source):
                    copy.wait_send()
                waits = [(chip * ncore + 1 - core, None, 0)] + [
                    (c * ncore + k, h, h) for c, h in rest for k in range(ncore)
                ]
            else:
                waits = [(lax.rem(share + d, nctx), None, 0) for d in range(1, nctx)]
            for owner, h, slot in waits:
                for i, ref in enumerate(places(source, owner)):
                    part = cut(ref, h)
                    remote(
                        part, part, p_s.at[source, i, 0, 0], p_r.at[source, i, owner, slot], sibling
                    ).wait_recv()

    dma = pltpu.SemaphoreType.DMA
    anywhere = pl.BlockSpec(memory_space=pl.ANY)
    return pl.pallas_call(
        kernel,
        in_specs=[anywhere] * 4,
        out_specs=[anywhere] * 4,
        out_shape=[
            jax.ShapeDtypeStruct((nz, ncore, own, width), bf16),
            jax.ShapeDtypeStruct((nz * wrows, ci), bf16),
            jax.ShapeDtypeStruct((nz * wrows, 3 * cq), bf16),
            jax.ShapeDtypeStruct((nz,) + small.shape, bf16),
        ],
        scratch_shapes=[
            pltpu.VMEM((nz, piece, zi), bf16),
            pltpu.VMEM((nz, ncore, piece, 3 * cq), bf16),
            dma((nz,)), dma((nz,)), dma((nz,)), dma((nz,)),
            dma((nz,)), dma((nz,)),
            dma((nz,)), dma((nz,)), dma((nz, ncore, 3)), dma((nz, ncore, 3)),
            dma((nz, 2, ncore, max(5, nctx))), dma((nz, 2, nctx, 2)), dma((nz, 2, ncore, 2)),
            dma((3 + 3 * ncore,)), dma((nz, 2)), dma((nz,)), dma((nz,)),
        ],
        compiler_params=pltpu.CompilerParams(
            collective_id=1, has_side_effects=True, vmem_limit_bytes=62 * 2**20
        ),
        name="front",
    )(tokens, w_in, w_qkv, small)


def turn_table(length):
    half = ROT // 2
    power = -(np.arange(half, dtype=np.float32) * np.float32(2.0)) / np.float32(ROT)
    angles = np.arange(length, dtype=np.float32)[:, None] * np.power(np.float32(ROT_BASE), power)
    table = np.zeros((3, length, 128), np.float32)
    table[0] = 1.0
    table[0, :, :half] = table[0, :, half:ROT] = np.cos(angles)
    table[1, :, :half] = -np.sin(angles)
    table[2, :, half:ROT] = np.sin(angles)
    return table


def turned(u, cosine, minus, plus):
    half = ROT // 2
    return u * cosine + pltpu.roll(u, 128 - half, 1) * minus + pltpu.roll(u, half, 1) * plus


def stats(x):
    center = x - jnp.mean(x, axis=-1, keepdims=True)
    inv = lax.rsqrt(jnp.mean(center * center, axis=-1, keepdims=True) + EPSILON)
    return center * inv, inv


def cost(flops, nbytes, trans=0):
    return pl.CostEstimate(flops=int(flops), bytes_accessed=int(nbytes), transcendentals=int(trans))


def projections(nz, ids, place, tok, w, bias, gain, offset, table):
    rows, width = tok.shape
    step = rows // nz
    blocks = step // BLOCK
    cols = w.shape[1]
    hc = cols // 3

    def kernel(ids_ref, place_ref, tok_ref, w_ref, b_ref, g_ref, o_ref, t_ref, n_ref, out_ref):
        xhat, inv = stats(tok_ref[...].astype(f32))
        normed = (xhat * g_ref[...] + o_ref[...]).astype(bf16)
        n_ref[...] = normed
        project = jnp.dot(normed, w_ref[...], preferred_element_type=f32) + b_ref[...]
        out_ref[...] = project.astype(bf16)
        first = place_ref[0] == 1

        @pl.when(first)
        def _():
            for b in range(blocks):
                at = pl.ds(pl.multiple_of(ids_ref[pl.program_id(0) * blocks + b] * BLOCK, BLOCK), BLOCK)
                c, m, p = t_ref[0, at, :], t_ref[1, at, :], t_ref[2, at, :]
                for g in range(2):
                    u = project[b * BLOCK : (b + 1) * BLOCK, g * hc : g * hc + 128]
                    out_ref[b * BLOCK : (b + 1) * BLOCK, g * hc : g * hc + 128] = turned(
                        u, c, m, p
                    ).astype(bf16)

    whole = lambda shape: pl.BlockSpec(shape, lambda i, *_: (0,) * len(shape))
    return pl.pallas_call(
        kernel,
        grid_spec=pltpu.PrefetchScalarGridSpec(
            num_scalar_prefetch=2,
            grid=(nz,),
            in_specs=[
                pl.BlockSpec((step, width), lambda i, *_: (i, 0)),
                whole((width, cols)),
                whole((1, cols)),
                whole((1, width)),
                whole((1, width)),
                whole(table.shape),
            ],
            out_specs=[
                pl.BlockSpec((step, width), lambda i, *_: (i, 0)),
                pl.BlockSpec((step, cols), lambda i, *_: (i, 0)),
            ],
        ),
        out_shape=[
            jax.ShapeDtypeStruct((rows, width), bf16),
            jax.ShapeDtypeStruct((rows, cols), bf16),
        ],
        compiler_params=BIG,
        cost_estimate=cost(2 * rows * width * cols, 4 * rows * width + 2 * width * cols),
        name="projections",
    )(ids, place, tok, w, bias, gain, offset, table)


def feed_forward(nz, tok, w, bias, gain, offset):
    rows, width = tok.shape
    step = rows // nz
    cols = w.shape[1]

    def kernel(tok_ref, w_ref, b_ref, g_ref, o_ref, n_ref, a_ref, d_ref):
        xhat, inv = stats(tok_ref[...].astype(f32))
        normed = (xhat * g_ref[...] + o_ref[...]).astype(bf16)
        n_ref[...] = normed
        v = jnp.dot(normed, w_ref[...], preferred_element_type=f32) + b_ref[...]
        gate = 0.5 * (1.0 + lax.erf(v * (0.5**0.5)))
        a_ref[...] = (v * gate).astype(bf16)
        bell = jnp.exp(v * v * -0.5) * ((2.0 * math.pi) ** -0.5)
        d_ref[...] = (gate + v * bell).astype(bf16)

    whole = lambda shape: pl.BlockSpec(shape, lambda i: (0, 0))
    part = lambda n: pl.BlockSpec((step, n), lambda i: (i, 0))
    return pl.pallas_call(
        kernel,
        grid=(nz,),
        in_specs=[part(width), whole((width, cols)), whole((1, cols)), whole((1, width)), whole((1, width))],
        out_specs=[part(width), part(cols), part(cols)],
        out_shape=[
            jax.ShapeDtypeStruct((rows, width), bf16),
            jax.ShapeDtypeStruct((rows, cols), bf16),
            jax.ShapeDtypeStruct((rows, cols), bf16),
        ],
        compiler_params=BIG,
        cost_estimate=cost(2 * rows * width * cols, 4 * rows * width + 2 * width * cols, 2 * rows * cols),
        name="feed_forward",
    )(tok, w, bias, gain, offset)


def layer_out(nz, core, mixed, w_dense, active, w_out):
    rows, hc = mixed.shape
    width = w_out.shape[1]
    step = rows // nz
    units = active.shape[1]

    def kernel(core_ref, m_ref, wd_ref, a_ref, wo_ref, out_ref):
        out_ref[...] = (
            jnp.dot(m_ref[...], wd_ref[...], preferred_element_type=f32)
            + jnp.dot(a_ref[...], wo_ref[...], preferred_element_type=f32)
        ).astype(bf16)

    part = lambda n: pl.BlockSpec((step, n), lambda i, c: (i, 0))
    held = lambda n: pl.BlockSpec((n, width), lambda i, c: (c[0], 0))
    return pl.pallas_call(
        kernel,
        grid_spec=pltpu.PrefetchScalarGridSpec(
            num_scalar_prefetch=1,
            grid=(nz,),
            in_specs=[part(hc), held(hc), part(units), held(units)],
            out_specs=part(width),
        ),
        out_shape=jax.ShapeDtypeStruct((rows, width), bf16),
        compiler_params=BIG,
        cost_estimate=cost(2 * rows * width * (hc + units), 4 * rows * width + 2 * width * units),
        name="layer_out",
    )(core, mixed, w_dense, active, w_out)


def widen(arrays):
    steps = [min(x.shape[0], 128 if x.shape[1] > 4096 else 512) for x in arrays]
    counts = [x.shape[0] // step for x, step in zip(arrays, steps)]
    starts = [sum(counts[:i]) for i in range(len(counts))]

    def kernel(*refs):
        n = len(arrays)
        for i in range(n):
            here = pl.program_id(0) - starts[i]

            @pl.when(jnp.logical_and(here >= 0, here < counts[i]))
            def _():
                refs[n + i][...] = refs[i][...].astype(f32)

    def part(i):
        return pl.BlockSpec(
            (steps[i], arrays[i].shape[1]),
            lambda s: (jnp.clip(s - starts[i], 0, counts[i] - 1), 0),
        )

    specs = [part(i) for i in range(len(arrays))]
    size = sum(x.size for x in arrays)
    return pl.pallas_call(
        kernel,
        grid=(sum(counts),),
        in_specs=specs,
        out_specs=specs,
        out_shape=[jax.ShapeDtypeStruct(x.shape, f32) for x in arrays],
        compiler_params=BIG,
        cost_estimate=cost(size, 6 * size),
        name="widen",
    )(*arrays)


def grad_of_mixed(nz, core, cot, w_dense, hc):
    rows, width = cot.shape
    step = rows // nz

    def kernel(core_ref, c_ref, w_ref, out_ref):
        out_ref[...] = lax.dot_general(
            c_ref[...], w_ref[...], NT, preferred_element_type=f32
        ).astype(bf16)

    return pl.pallas_call(
        kernel,
        grid_spec=pltpu.PrefetchScalarGridSpec(
            num_scalar_prefetch=1,
            grid=(nz,),
            in_specs=[
                pl.BlockSpec((step, width), lambda i, c: (i, 0)),
                pl.BlockSpec((hc, width), lambda i, c: (c[0], 0)),
            ],
            out_specs=pl.BlockSpec((step, hc), lambda i, c: (i, 0)),
        ),
        out_shape=jax.ShapeDtypeStruct((rows, hc), bf16),
        compiler_params=BIG,
        cost_estimate=cost(2 * rows * width * hc, 2 * rows * width),
        name="grad_of_mixed",
    )(core, cot, w_dense)


def grad_of_hidden(nz, core, cot, w_out, slope):
    rows, width = cot.shape
    step = rows // nz
    units = slope.shape[1]

    def kernel(core_ref, c_ref, w_ref, d_ref, out_ref, sum_ref):
        g = lax.dot_general(c_ref[...], w_ref[...], NT, preferred_element_type=f32)
        g = (g * d_ref[...].astype(f32)).astype(bf16)
        out_ref[...] = g

        @pl.when(pl.program_id(0) == 0)
        def _():
            sum_ref[...] = jnp.zeros_like(sum_ref)

        sum_ref[...] += jnp.sum(g.astype(f32), axis=0, keepdims=True)

    return pl.pallas_call(
        kernel,
        grid_spec=pltpu.PrefetchScalarGridSpec(
            num_scalar_prefetch=1,
            grid=(nz,),
            in_specs=[
                pl.BlockSpec((step, width), lambda i, c: (i, 0)),
                pl.BlockSpec((units, width), lambda i, c: (c[0], 0)),
                pl.BlockSpec((step, units), lambda i, c: (i, 0)),
            ],
            out_specs=[
                pl.BlockSpec((step, units), lambda i, c: (i, 0)),
                pl.BlockSpec((1, units), lambda i, c: (0, 0)),
            ],
        ),
        out_shape=[
            jax.ShapeDtypeStruct((rows, units), bf16),
            jax.ShapeDtypeStruct((1, units), f32),
        ],
        compiler_params=BIG,
        cost_estimate=cost(2 * rows * width * units, 2 * rows * width + 2 * width * units),
        name="grad_of_hidden",
    )(core, cot, w_out, slope)


def norm_back(nz, grad, w, tok, gain, other, sums):
    rows, width = tok.shape
    step = rows // nz
    cols = grad.shape[1]

    def kernel(*refs):
        g_ref, w_ref, t_ref, gain_ref = refs[:4]
        at = 4
        if other is not None:
            other_ref = refs[at]
            at += 1
        e_ref, s_ref = refs[at : at + 2]
        gn = lax.dot_general(g_ref[...], w_ref[...], NT, preferred_element_type=f32)
        xhat, inv = stats(t_ref[...].astype(f32))
        e = gn * gain_ref[...]
        if other is not None:
            e = e + other_ref[...].astype(f32)
        e_ref[...] = e.astype(bf16)

        @pl.when(pl.program_id(0) == 0)
        def _():
            s_ref[...] = jnp.zeros_like(s_ref)
            if sums:
                refs[at + 2][...] = jnp.zeros_like(refs[at + 2])

        s_ref[0:1, :] += jnp.sum(gn * xhat, axis=0, keepdims=True)
        s_ref[1:2, :] += jnp.sum(gn, axis=0, keepdims=True)
        if sums:
            refs[at + 2][...] += jnp.sum(g_ref[...].astype(f32), axis=0, keepdims=True)

    part = lambda n: pl.BlockSpec((step, n), lambda i: (i, 0))
    whole = lambda shape: pl.BlockSpec(shape, lambda i: (0, 0))
    ins = [grad, w, tok, gain] + ([] if other is None else [other])
    return pl.pallas_call(
        kernel,
        grid=(nz,),
        in_specs=[part(cols), whole((width, cols)), part(width), whole((1, width))]
        + ([] if other is None else [part(width)]),
        out_specs=[part(width), whole((2, width))] + ([whole((1, cols))] if sums else []),
        out_shape=[
            jax.ShapeDtypeStruct((rows, width), bf16),
            jax.ShapeDtypeStruct((2, width), f32),
        ]
        + ([jax.ShapeDtypeStruct((1, cols), f32)] if sums else []),
        compiler_params=BIG,
        cost_estimate=cost(2 * rows * width * cols, 6 * rows * width + 2 * width * cols),
        name="norm_back",
    )(*ins)


def attention_forward(ids, order, qkv, tile):
    rows = qkv.shape[0]
    blocks = rows // BLOCK

    def kernel(ids_ref, order_ref, x_ref, o_ref, lse_ref, q_ref, k_ref, v_ref, s_ref):
        for b in range(blocks):
            at = pl.ds(pl.multiple_of(order_ref[b] * BLOCK, BLOCK), BLOCK)
            here = slice(b * BLOCK, (b + 1) * BLOCK)
            for i, ref in enumerate((q_ref, k_ref, v_ref)):
                ref[here, :] = x_ref[at, i * HD : (i + 1) * HD]
        for t in range(rows // tile):
            mine = slice(t * tile, (t + 1) * tile)
            n = (t + 1) * tile
            s = lax.dot_general(q_ref[mine, :], k_ref[:n, :], NT, preferred_element_type=f32)
            s = s * SCALE
            seen = t * tile + lax.broadcasted_iota(jnp.int32, (tile, n), 0) >= (
                lax.broadcasted_iota(jnp.int32, (tile, n), 1)
            )
            s = jnp.where(seen, s, -1e30)
            top = jnp.max(s, axis=-1, keepdims=True)
            e = jnp.exp(s - top)
            total = jnp.sum(e, axis=-1, keepdims=True)
            p = (e * (1.0 / total)).astype(bf16)
            s_ref[mine, :] = jnp.dot(p, v_ref[:n, :], preferred_element_type=f32).astype(bf16)
            lse_ref[mine, :] = top + jnp.log(total)
        for b in range(blocks):
            at = pl.ds(pl.multiple_of(ids_ref[b] * BLOCK, BLOCK), BLOCK)
            o_ref[b * BLOCK : (b + 1) * BLOCK, :] = s_ref[at, :]

    smem = pl.BlockSpec(memory_space=pltpu.SMEM)
    vmem = pl.BlockSpec(memory_space=pltpu.VMEM)
    return pl.pallas_call(
        kernel,
        in_specs=[smem, smem, vmem],
        out_specs=[vmem, vmem],
        out_shape=[
            jax.ShapeDtypeStruct((rows, HD), bf16),
            jax.ShapeDtypeStruct((rows, 1), f32),
        ],
        scratch_shapes=[pltpu.VMEM((rows, HD), bf16)] * 4,
        compiler_params=BIG,
        cost_estimate=cost(2.3 * rows * rows * HD, 8 * rows * HD, rows * rows / 2),
        name="attention_forward",
    )(ids, order, qkv)


def attention_backward(ids, order, qkv, grad, lse, table, tile):
    rows = qkv.shape[0]
    blocks = rows // BLOCK

    def kernel(ids_ref, order_ref, x_ref, g_ref, lse_ref, t_ref, out_ref, q_ref, k_ref, v_ref, m_ref,
               r_ref, dk_ref, dv_ref):
        for b in range(blocks):
            at = pl.ds(pl.multiple_of(order_ref[b] * BLOCK, BLOCK), BLOCK)
            here = slice(b * BLOCK, (b + 1) * BLOCK)
            for i, ref in enumerate((q_ref, k_ref, v_ref)):
                ref[here, :] = x_ref[at, i * HD : (i + 1) * HD]
            m_ref[here, :] = g_ref[at, :]
        for t in reversed(range(rows // tile)):
            mine = slice(t * tile, (t + 1) * tile)
            n = (t + 1) * tile
            q, g = q_ref[mine, :], m_ref[mine, :]
            s = lax.dot_general(q, k_ref[:n, :], NT, preferred_element_type=f32) * SCALE
            seen = t * tile + lax.broadcasted_iota(jnp.int32, (tile, n), 0) >= (
                lax.broadcasted_iota(jnp.int32, (tile, n), 1)
            )
            p = jnp.where(seen, jnp.exp(s - lse_ref[mine, :]), 0.0)
            dp = lax.dot_general(g, v_ref[:n, :], NT, preferred_element_type=f32)
            shift = jnp.sum(p * dp, axis=-1, keepdims=True)
            ds = (p * (dp - shift)).astype(bf16)
            low = p.astype(bf16)
            dq = jnp.dot(ds, k_ref[:n, :], preferred_element_type=f32) * SCALE
            r_ref[mine, :128] = turned(
                dq[:, :128], t_ref[0, mine, :], -t_ref[1, mine, :], -t_ref[2, mine, :]
            ).astype(bf16)
            r_ref[mine, 128:HD] = dq[:, 128:].astype(bf16)
            dk = lax.dot_general(ds, q, TN, preferred_element_type=f32) * SCALE
            dv = lax.dot_general(low, g, TN, preferred_element_type=f32)
            if n == rows:
                dk_ref[...] = dk
                dv_ref[...] = dv
            else:
                dk_ref[:n, :] += dk
                dv_ref[:n, :] += dv
        r_ref[:, HD : HD + 128] = turned(
            dk_ref[:, :128], t_ref[0], -t_ref[1], -t_ref[2]
        ).astype(bf16)
        r_ref[:, HD + 128 : 2 * HD] = dk_ref[:, 128:].astype(bf16)
        r_ref[:, 2 * HD :] = dv_ref[...].astype(bf16)
        for b in range(blocks):
            at = pl.ds(pl.multiple_of(ids_ref[b] * BLOCK, BLOCK), BLOCK)
            out_ref[b * BLOCK : (b + 1) * BLOCK, :] = r_ref[at, :]

    smem = pl.BlockSpec(memory_space=pltpu.SMEM)
    vmem = pl.BlockSpec(memory_space=pltpu.VMEM)
    return pl.pallas_call(
        kernel,
        in_specs=[smem, smem, vmem, vmem, vmem, vmem],
        out_specs=vmem,
        out_shape=jax.ShapeDtypeStruct((rows, 3 * HD), bf16),
        scratch_shapes=[pltpu.VMEM((rows, HD), bf16)] * 4
        + [pltpu.VMEM((rows, 3 * HD), bf16)]
        + [pltpu.VMEM((rows, HD), f32)] * 2,
        compiler_params=BIG,
        cost_estimate=cost(6 * rows * rows * HD, 20 * rows * HD, rows * rows / 2),
        name="attention_backward",
    )(ids, order, qkv, grad, lse, table)


def exchange_heads(nz, nchip, ncore, attended, cot, w_dense, active):
    rows, width = cot.shape
    step = rows // nz
    length, hc = attended.shape
    part = length // nchip
    units = active.shape[1]
    tile = 256

    def kernel(att_ref, cot_hbm, w_hbm, act_hbm, mix_out, g_out, dw_out, cot_ref, w_ref, act_ref, gm_ref, dw_ref,
               ld, m_s, m_r, g_s, g_r, own_l, dw_l):
        chip = lax.axis_index("chip")
        core = lax.axis_index("core")
        loads = [
            pltpu.make_async_copy(w_hbm.at[pl.ds(core * hc, hc), :], w_ref, ld.at[0]),
            pltpu.make_async_copy(cot_hbm, cot_ref, ld.at[1]),
            pltpu.make_async_copy(act_hbm, act_ref, ld.at[2]),
        ]
        for copy in loads:
            copy.start()

        def chip_at(d):
            return lax.rem(chip + d, nchip)

        greet([{"chip": chip_at(d)} for d in range(1, nchip)])
        sent = [
            remote(
                att_ref.at[pl.ds(chip_at(d) * part, part), :],
                mix_out.at[pl.ds(chip * step, step), :], m_s.at[d], m_r.at[d], {"chip": chip_at(d)},
            )
            for d in range(1, nchip)
        ]
        kept = [
            pltpu.make_async_copy(
                att_ref.at[pl.ds(chip * part, part), :], mix_out.at[pl.ds(chip * step, step), :],
                own_l.at[0],
            )
        ]
        for copy in sent + kept:
            copy.start()
        loads[0].wait()
        loads[1].wait()
        for d in range(1, nchip + 1):
            to = chip_at(d)
            at = pl.ds(pl.multiple_of(to * step, step), step)
            gm_ref[at, :] = lax.dot_general(
                cot_ref[at, :], w_ref[...], NT, preferred_element_type=f32
            ).astype(bf16)
            there = g_out.at[pl.ds(chip * part, part), :]
            if d < nchip:
                copy = remote(gm_ref.at[at, :], there, g_s.at[d], g_r.at[d], {"chip": to})
                sent.append(copy)
            else:
                copy = pltpu.make_async_copy(gm_ref.at[at, :], there, own_l.at[1])
                kept.append(copy)
            copy.start()
        loads[2].wait()
        for t in range(units // tile):
            at = pl.ds(t * tile, tile)
            dw_ref[at, :] = lax.dot_general(
                act_ref[:, at], cot_ref[...], TN, preferred_element_type=f32
            ).astype(bf16)
            copy = pltpu.make_async_copy(dw_ref.at[at, :], dw_out.at[at, :], dw_l.at[t])
            copy.start()
            kept.append(copy)
        for copy in kept + sent:
            copy.wait()

    dma = pltpu.SemaphoreType.DMA
    anywhere = pl.BlockSpec(memory_space=pl.ANY)
    return pl.pallas_call(
        kernel,
        in_specs=[anywhere] * 4,
        out_specs=[anywhere] * 3,
        out_shape=[
            jax.ShapeDtypeStruct((rows, hc), bf16),
            jax.ShapeDtypeStruct((length, hc), bf16),
            jax.ShapeDtypeStruct((units, width), bf16),
        ],
        scratch_shapes=[
            pltpu.VMEM((rows, width), bf16),
            pltpu.VMEM((hc, width), bf16),
            pltpu.VMEM((rows, units), bf16),
            pltpu.VMEM((rows, hc), bf16),
            pltpu.VMEM((units, width), bf16),
            dma((3,)), dma((nchip,)), dma((nchip,)), dma((nchip,)), dma((nchip,)), dma((2,)),
            dma((units // tile,)),
        ],
        compiler_params=pltpu.CompilerParams(
            collective_id=3, has_side_effects=True, vmem_limit_bytes=62 * 2**20
        ),
        cost_estimate=cost(2 * rows * width * (hc + units), 4 * rows * width),
        name="exchange_heads",
    )(attended, cot, w_dense, active)


def gather_plane(nchip, chip, core, src, dst_of, send, recv, local):
    sibling = {"core": 1 - core}
    rows = src.shape[0]
    half = rows // 2
    here = dst_of(chip, core)
    begun = [pltpu.make_async_copy(src, here, local)]
    begun.append(remote(src, here, send.at[0], recv.at[0], sibling))
    relays = []
    arrivals = []

    def cut(ref, h):
        return ref.at[pl.ds(h * half, half), :]

    if nchip == 4:
        beside = chip + 1 - 2 * lax.rem(chip, 2)
        below = lax.rem(chip + 2, 4)
        across = 3 - chip
        order = ((beside, 0, 1), (below, 1, 2), (beside, 1, 1), (below, 0, 2))
        for i, (to, h, d) in enumerate(order):
            slot = 4 + 2 * d + h
            begun.append(
                remote(cut(src, h), cut(here, h), send.at[slot], recv.at[slot], {"chip": to})
            )

        def passing(owner, h, to):
            part = cut(dst_of(owner, core), h)
            return remote(part, part, send.at[10 + h], recv.at[10 + h], {"chip": to})

        relays = [(passing(beside, 0, below), beside, 0, 6), (passing(below, 1, beside), below, 1, 9)]
        arrivals = [(beside, 1, 7, 1), (below, 0, 8, 2), (across, 0, 10, 3), (across, 1, 11, 3)]
        others = [(beside, 1), (below, 2), (across, 3)]
    else:
        others = [(lax.rem(chip + d, nchip), d) for d in range(1, nchip)]
        for to, d in others:
            begun.append(
                remote(src, here, send.at[nchip + d], recv.at[nchip + chip], {"chip": to})
            )

    def side(owner, slot):
        part = dst_of(owner, core)
        return remote(part, part, send.at[slot], recv.at[slot], sibling)

    def slot_of(owner, d):
        return d if nchip == 4 else 2 * nchip + owner

    def first():
        for copy in begun:
            copy.start()

    def onward():
        if nchip == 4:
            for copy, owner, h, slot in relays:
                part = cut(dst_of(owner, core), h)
                remote(part, part, send.at[0], recv.at[slot], sibling).wait_recv()
                copy.start()

    def pass_on():
        if nchip == 4:
            for owner, h, slot, d in arrivals:
                part = cut(dst_of(owner, core), h)
                remote(part, part, send.at[0], recv.at[slot], sibling).wait_recv()
                if slot != 10:
                    side(owner, d).start()
        else:
            for owner, d in others:
                part = dst_of(owner, core)
                remote(part, part, send.at[0], recv.at[nchip + owner], sibling).wait_recv()
                side(owner, slot_of(owner, d)).start()

    def last():
        begun[0].wait()
        for copy in begun[1:]:
            copy.wait_send()
        for copy, owner, h, slot in relays:
            copy.wait_send()
        there = dst_of(chip, 1 - core)
        remote(there, there, send.at[0], recv.at[0], sibling).wait_recv()
        for owner, d in others:
            side(owner, slot_of(owner, d)).wait_send()
            there = dst_of(owner, 1 - core)
            remote(there, there, send.at[0], recv.at[slot_of(owner, d)], sibling).wait_recv()

    return first, onward, pass_on, last


def scatter_plane(nchip, chip, part, own, first, second, send, recv, local):
    halves = own.shape[0]
    copies = []
    shape = own.shape[2:]

    def add(dst, terms):
        def rows(lead):
            @pl.loop(0, shape[-2] // 16)
            def _(i):
                at = lead + (pl.ds(pl.multiple_of(i * 16, 16), 16), slice(None))
                acc = dst[at].astype(f32)
                for term in terms:
                    acc = acc + term[at].astype(f32)
                dst[at] = acc.astype(bf16)

        if len(shape) == 2:
            rows(())
        else:

            @pl.loop(0, shape[0])
            def _(b):
                rows((b,))

    if nchip == 4:
        beside = chip + 1 - 2 * lax.rem(chip, 2)
        below = lax.rem(chip + 2, 4)
        across = 3 - chip
        ways = [(beside, below), (below, beside)]
        kept = [
            [
                pltpu.make_async_copy(part(chip, h), own.at[h, 0], local.at[h, 0]),
                pltpu.make_async_copy(part(ways[h][1], h), own.at[h, 1], local.at[h, 1]),
            ]
            for h in range(2)
        ]
        leave = [
            [
                remote(
                    part(across, h), first.at[h, 1], send.at[h, 1], recv.at[h, 1],
                    {"chip": ways[h][0]},
                ),
                remote(
                    part(ways[h][0], h), first.at[h, 0], send.at[h, 0], recv.at[h, 0],
                    {"chip": ways[h][0]},
                ),
            ]
            for h in range(2)
        ]
        follow = [
            remote(
                own.at[h, 1], second.at[h], send.at[h, 2], recv.at[h, 2], {"chip": ways[h][1]}
            )
            for h in range(2)
        ]

        def begin():
            for i in range(2):
                for h in range(2):
                    leave[h][i].start()
            for h in range(2):
                kept[h][1].start()
                kept[h][0].start()

        def middle():
            for h in range(2):
                kept[h][1].wait()
                leave[h][0].wait_recv()
                add(own.at[h, 1], [first.at[h, 1]])
                follow[h].start()

        def finish():
            for h in range(2):
                kept[h][0].wait()
                leave[h][1].wait_recv()
                follow[h].wait_recv()
                add(own.at[h, 0], [first.at[h, 0], second.at[h]])

        def last():
            for h in range(2):
                for copy in leave[h] + [follow[h]]:
                    copy.wait_send()
    else:
        to = [lax.rem(chip + d, nchip) for d in range(nchip)]
        kept = pltpu.make_async_copy(part(chip, 0), own.at[0, 0], local.at[0, 0])
        leave = [
            remote(part(to[d], 0), first.at[0, d], send.at[0, d], recv.at[0, d], {"chip": to[d]})
            for d in range(1, nchip)
        ]

        def begin():
            for copy in leave:
                copy.start()
            kept.start()

        def middle():
            pass

        def finish():
            kept.wait()
            for copy in leave:
                copy.wait_recv()
            add(own.at[0, 0], [first.at[0, d] for d in range(1, nchip)])

        def last():
            for copy in leave:
                copy.wait_send()

    return begin, middle, finish, last


def tail(nz, nchip, ncore, dwo, dwd, dwi, vectors, normed1, grad_project, grad_hidden, tok, w_qkv, w_in, gain1, gain2):
    width = dwo.shape[1]
    ro, rd = dwo.shape[0], dwd.shape[0] // nchip
    halves = 2 if nchip == 4 else 1
    hz = nz // halves
    hd = rd // halves
    ci, cq = dwi.shape[1], grad_project.shape[1] // 3
    wrows = width // nz
    ri = wrows // nchip
    rows = tok.shape[0]
    step = rows // nz
    own = step // ncore
    vr = vectors.shape[0]
    chunk = 512
    dwi = dwi.reshape(nz, nchip, ri, ci)
    dwd = dwd.reshape(nchip, rd, width)

    def kernel(
        dwo_ref, dwd_ref, dwi_ref, vec_ref, n_hbm, gp_hbm, gh_hbm, tok_hbm, wq_hbm, wi_hbm, g1_ref, g2_ref,
        go_ref, gd_ref, gi_ref, gq_ref, e_ref, vsum_ref,
        x_ref, gp_ref, gh_ref, wq_ref, wi_ref, dwq_ref, eb,
        oi, fi, si, oq, fq, sq, od, fd, sd, ti, tq, se, ze, cs, v0, v1, v2, v3,
        ld, ri_s, ri_r, ri_l, rq_s, rq_r, rq_l, rd_s, rd_r, rd_l, x_s, x_r, ez_s, ez_r, t_s, t_r, t_l,
        go_s, go_r, gd_s, gd_r, gi_s, gi_r, gq_s, gq_r, own_l,
        v_s, v_r,
    ):
        z = lax.axis_index("seq")
        chip = lax.axis_index("chip")
        core = lax.axis_index("core")
        sibling = {"core": 1 - core}

        def z_at(d):
            return lax.rem(z + d, nz)

        def chip_at(d):
            return lax.rem(chip + d, nchip)

        loads = [
            pltpu.make_async_copy(a, b, ld.at[i])
            for i, (a, b) in enumerate(
                ((n_hbm, x_ref), (gp_hbm, gp_ref), (gh_hbm, gh_ref), (wi_hbm, wi_ref), (wq_hbm, wq_ref))
            )
        ]
        for copy in loads:
            copy.start()
        greet(
            [{"seq": z_at(d)} for d in range(1, nz)]
            + [{"chip": chip_at(d)} for d in range(1, nchip)]
            + [sibling]
        )

        def turn(kind, part, turned):
            copies = [
                remote(
                    part(z_at(d)), turned.at[z], t_s.at[kind, d], t_r.at[kind, z],
                    {"seq": z_at(d)},
                )
                for d in range(1, nz)
            ]
            copies.append(pltpu.make_async_copy(part(z), turned.at[z], t_l.at[kind]))
            for copy in copies:
                copy.start()
            return copies

        def turned_at(kind, part, turned, source):
            return remote(part, turned.at[source], t_s.at[kind, 0], t_r.at[kind, source], sibling)

        sum_i = scatter_plane(
            nchip, chip, lambda c, h: dwi_ref.at[pl.ds(h * hz, hz), c], oi, fi, si, ri_s, ri_r, ri_l
        )
        sum_q = scatter_plane(
            nchip, chip, lambda c, h: dwq_ref.at[pl.ds(h * hz, hz), pl.ds(c * ri, ri)], oq, fq, sq,
            rq_s, rq_r, rq_l,
        )
        sum_d = scatter_plane(
            nchip, chip, lambda c, h: dwd_ref.at[c, pl.ds(h * hd, hd)], od, fd, sd, rd_s, rd_r, rd_l
        )
        sum_i[0]()

        loads[0].wait()
        loads[1].wait()
        for b in range(nz):
            dwq_ref[b] = lax.dot_general(
                x_ref[:, b * wrows : (b + 1) * wrows], gp_ref[...], TN, preferred_element_type=f32
            ).astype(bf16)
        load_tok = pltpu.make_async_copy(tok_hbm, x_ref, ld.at[5])
        load_tok.start()
        sum_i[1]()
        sum_q[0]()
        sum_d[0]()

        for copy in loads[2:] + [load_tok]:
            copy.wait()
        cs[...] = jnp.zeros_like(cs)
        cs[4:5, : 3 * cq] = jnp.sum(gp_ref[...].astype(f32), axis=0, keepdims=True)

        def norm_back(b):
            at = pl.ds(b * step, step)
            x = x_ref[at, :].astype(f32)
            mean = jnp.mean(x, axis=-1, keepdims=True)
            x = x - mean
            inv = lax.rsqrt(jnp.mean(x * x, axis=-1, keepdims=True) + EPSILON)

            @pl.loop(0, width // chunk)
            def _(c):
                cols = pl.ds(pl.multiple_of(c * chunk, chunk), chunk)
                xhat = (x_ref[at, cols].astype(f32) - mean) * inv
                gn = lax.dot_general(
                    gp_ref[at, :], wq_ref[cols, :], NT, preferred_element_type=f32
                )
                cs[0:1, cols] += jnp.sum(gn * xhat, axis=0, keepdims=True)
                cs[1:2, cols] += jnp.sum(gn, axis=0, keepdims=True)
                e = gn * g1_ref[:, cols]
                gn = lax.dot_general(
                    gh_ref[at, :], wi_ref[cols, :], NT, preferred_element_type=f32
                )
                cs[2:3, cols] += jnp.sum(gn * xhat, axis=0, keepdims=True)
                cs[3:4, cols] += jnp.sum(gn, axis=0, keepdims=True)
                e = (e + gn * g2_ref[:, cols]).astype(bf16)
                for k in range(ncore):
                    eb[b, k, :, cols] = e[k * own : (k + 1) * own]

            copy = remote(eb.at[b, 1 - core], se.at[b], x_s.at[b], x_r.at[b], sibling)
            copy.start()
            return copy

        exchanged = [norm_back(b) for b in range(nz)]
        sum_i[2]()
        turn_i = turn(0, lambda to: oi.at[to // hz, 0, lax.rem(to, hz)], ti)
        sum_q[1]()

        v0[...] = vec_ref[...]
        lanes = width // 128
        for k in range(4):
            for j in range(lanes):
                v0[k * lanes + j : k * lanes + j + 1, :] = cs[k : k + 1, j * 128 : (j + 1) * 128]
        rank = z * ncore + core
        deep = (3 * cq) // 128 // 3
        for r in range(nz * ncore):

            @pl.when(rank == r)
            def _():
                for g in range(3):
                    for j in range(deep):
                        row = 4 * lanes + (g * nz * ncore + r) * deep + j
                        col = g * cq + j * 128
                        v0[row : row + 1, :] = cs[4:5, col : col + 128]

        v_chips = [
            remote(v0, v1.at[chip], v_s.at[d], v_r.at[chip], {"chip": chip_at(d)})
            for d in range(1, nchip)
        ]
        for copy in v_chips:
            copy.start()
        v1[chip] = v0[...]

        go_at = lambda c, k: go_ref.at[pl.ds(k * (ro * nchip) + c * ro, ro), :]
        gd_at = lambda c, k, h: gd_ref.at[pl.ds(k * (rd * nchip) + c * rd + h * hd, hd), :]
        gi_at = lambda c, k, s: gi_ref.at[
            pl.ds(c * ri, ri), pl.ds((s * ncore + k) * ci, ci)
        ]
        gq_at = lambda c, k, s, g: gq_ref.at[
            pl.ds(c * ri, ri), pl.ds(g * nz * ncore * cq + (s * ncore + k) * cq, cq)
        ]
        group = functools.partial(gather_plane, nchip, chip, core)
        rows_o = group(dwo_ref, go_at, go_s, go_r, own_l.at[nz])
        rows_o[0]()

        for b in range(nz):
            exchanged[b].wait_recv()

            @pl.loop(0, own // 16)
            def _(i):
                at = pl.ds(pl.multiple_of(i * 16, 16), 16)
                eb[b, core, at, :] = (
                    eb[b, core, at, :].astype(f32) + se[b, at, :].astype(f32)
                ).astype(bf16)

        sum_q[2]()
        turn_q = turn(1, lambda to: oq.at[to // hz, 0, lax.rem(to, hz)], tq)
        sum_d[1]()

        for d in range(1, nchip):
            other = chip_at(d)
            remote(v0, v1.at[other], v_s.at[d], v_r.at[other], sibling).wait_recv()
        total = v1[0]
        for d in range(1, nchip):
            total = total + v1[d]
        v2[core] = total
        v_side = remote(v2.at[core], v2.at[core], v_s.at[nchip], v_r.at[nchip], sibling)
        v_side.start()

        groups = []
        for dz in range(1, nz):
            turned_at(0, oi.at[0, 0, 0], ti, z_at(dz)).wait_recv()
        turn_i[-1].wait()
        for source in range(nz):
            groups.append(
                group(
                    ti.at[source], functools.partial(gi_at, s=source), gi_s.at[source],
                    gi_r.at[source], own_l.at[source],
                )
            )
            groups[-1][0]()
        sent_e = [
            remote(
                eb.at[z_at(d), core], ze.at[d], ez_s.at[d], ez_r.at[d], {"seq": z_at(d)}
            )
            for d in range(1, nz)
        ]
        for copy in sent_e:
            copy.start()

        v_side.wait_recv()
        vz = v2[0]
        for c in range(1, ncore):
            vz = vz + v2[c]
        v3[z] = vz
        v_zs = [
            remote(v3.at[z], v3.at[z], v_s.at[nchip + d], v_r.at[nchip + 1 + z], {"seq": z_at(d)})
            for d in range(1, nz)
        ]
        for copy in v_zs:
            copy.start()
        sum_d[2]()
        rows_d = [
            group(od.at[h, 0], functools.partial(gd_at, h=h), gd_s.at[h], gd_r.at[h], own_l.at[nz + 1 + h])
            for h in range(halves)
        ]
        for first, onward, pass_on, last in rows_d:
            first()
        rows_o[1]()
        for first, onward, pass_on, last in groups:
            onward()

        for dz in range(1, nz):
            turned_at(1, oq.at[0, 0, 0], tq, z_at(dz)).wait_recv()
        turn_q[-1].wait()
        later = []
        for source in range(nz):
            for g in range(3):
                later.append(
                    group(
                        tq.at[source, :, pl.ds(g * cq, cq)],
                        functools.partial(gq_at, s=source, g=g),
                        gq_s.at[source, g], gq_r.at[source, g], own_l.at[4 + nz + 3 * source + g],
                    )
                )
        for first, onward, pass_on, last in later:
            first()
        rows_o[2]()
        for first, onward, pass_on, last in rows_d:
            onward()
        for first, onward, pass_on, last in groups:
            pass_on()
        for first, onward, pass_on, last in later:
            onward()
        for first, onward, pass_on, last in rows_d:
            pass_on()

        for d in range(1, nz):
            other = z_at(d)
            remote(v3.at[0], v3.at[other], v_s.at[0], v_r.at[nchip + 1 + other], sibling).wait_recv()
        total = v3[0]
        for d in range(1, nz):
            total = total + v3[d]
        vsum_ref[...] = total

        for copy in sent_e:
            copy.wait_recv()

        @pl.loop(0, own // 16)
        def _(i):
            at = pl.ds(pl.multiple_of(i * 16, 16), 16)
            acc = eb[z, core, at, :].astype(f32)
            for d in range(1, nz):
                acc = acc + ze[d, at, :].astype(f32)
            e_ref[at, :] = acc

        for first, onward, pass_on, last in later:
            pass_on()

        for first, onward, pass_on, last in [rows_o] + rows_d + groups + later:
            last()
        for begin, middle, finish, last in (sum_i, sum_q, sum_d):
            last()
        for copy in exchanged + sent_e + v_chips + v_zs + [v_side]:
            copy.wait_send()
        for copy in turn_i[:-1] + turn_q[:-1]:
            copy.wait_send()

    dma = pltpu.SemaphoreType.DMA
    anywhere = pl.BlockSpec(memory_space=pl.ANY)
    vmem = pl.BlockSpec(memory_space=pltpu.VMEM)
    out_shape = [
        jax.ShapeDtypeStruct((ncore * nchip * ro, width), bf16),
        jax.ShapeDtypeStruct((ncore * nchip * rd, width), bf16),
        jax.ShapeDtypeStruct((wrows, nz * ncore * ci), bf16),
        jax.ShapeDtypeStruct((wrows, 3 * nz * ncore * cq), bf16),
        jax.ShapeDtypeStruct((own, width), f32),
        jax.ShapeDtypeStruct((vr, 128), f32),
    ]
    slots = max(3 * nchip, 12)
    pair = 2 if nchip == 4 else 1
    nfirst = 2 if nchip == 4 else nchip

    def three(*shape):
        return [
            pltpu.VMEM((halves, pair) + shape, bf16),
            pltpu.VMEM((halves, nfirst) + shape, bf16),
            pltpu.VMEM((halves,) + shape, bf16),
        ]

    return pl.pallas_call(
        kernel,
        in_specs=[anywhere] * 3 + [vmem] + [anywhere] * 6 + [vmem] * 2,
        out_specs=[anywhere] * 4 + [vmem] * 2,
        out_shape=out_shape,
        scratch_shapes=[
            pltpu.VMEM((rows, width), bf16),
            pltpu.VMEM(grad_project.shape, bf16),
            pltpu.VMEM(grad_hidden.shape, bf16),
            pltpu.VMEM(w_qkv.shape, bf16),
            pltpu.VMEM(w_in.shape, bf16),
            pltpu.VMEM((nz, wrows, 3 * cq), bf16),
            pltpu.VMEM((nz, ncore, own, width), bf16),
        ]
        + three(hz, ri, ci)
        + three(hz, ri, 3 * cq)
        + three(hd, width)
        + [
            pltpu.VMEM((nz, ri, ci), bf16),
            pltpu.VMEM((nz, ri, 3 * cq), bf16),
            pltpu.VMEM((nz, own, width), bf16),
            pltpu.VMEM((nz, own, width), bf16),
            pltpu.VMEM((8, width), f32),
            pltpu.VMEM((vr, 128), f32),
            pltpu.VMEM((nchip, vr, 128), f32),
            pltpu.VMEM((ncore, vr, 128), f32),
            pltpu.VMEM((nz, vr, 128), f32),
            dma((6,)),
            dma((halves, nchip)), dma((halves, nchip)), dma((halves, 2)),
            dma((halves, nchip)), dma((halves, nchip)), dma((halves, 2)),
            dma((halves, nchip)), dma((halves, nchip)), dma((halves, 2)),
            dma((nz,)), dma((nz,)),
            dma((nz,)), dma((nz,)),
            dma((2, nz)), dma((2, nz)), dma((2,)),
            dma((slots,)), dma((slots,)),
            dma((halves, slots)), dma((halves, slots)),
            dma((nz, slots)), dma((nz, slots)),
            dma((nz, 3, slots)), dma((nz, 3, slots)),
            dma((4 + 4 * nz,)),
            dma((nchip + nz,)), dma((nchip + nz + 1,)),
        ],
        compiler_params=pltpu.CompilerParams(
            collective_id=2, has_side_effects=True, vmem_limit_bytes=62 * 2**20
        ),
        cost_estimate=cost(4 * rows * width * (3 * cq + ci), 20 * rows * width),
        name="tail",
    )(dwo, dwd, dwi, vectors, normed1, grad_project, grad_hidden, tok, w_qkv, w_in, gain1, gain2)


def on_device(
    nz,
    nchip,
    ncore,
    tokens,
    block_ids,
    cotangent,
    norm1_gain,
    norm1_bias,
    norm2_gain,
    norm2_bias,
    w_qkv,
    b_qkv,
    w_dense,
    b_dense,
    w_in,
    b_in,
    w_out,
    b_out,
):
    own, width = tokens.shape
    z = lax.axis_index("seq")
    chip = lax.axis_index("chip")
    core = lax.axis_index("core")
    ranks = nz * ncore
    rank = z * ncore + core
    rows = ranks * own
    ffr = w_out.shape[0] // ncore
    hc = width // ranks
    split = max(1, HD // hc)
    wrows = width // nz
    blocks = block_ids.shape[1]
    length = blocks * BLOCK
    core_at = core.reshape(1)

    parts = [norm1_gain, norm1_bias, norm2_gain, norm2_bias, b_qkv, b_dense + 0, b_in, b_out,
             block_ids.reshape(-1)]
    sizes = [p.shape[0] for p in parts]
    total = -(-sum(sizes) // 2048) * 2048
    starts = [sum(sizes[:i]) for i in range(len(sizes))]
    small = sum(
        jnp.pad(p.astype(f32), (at, total - at - p.shape[0])) for p, at in zip(parts, starts)
    )
    small = small.astype(bf16).reshape(-1, 128)
    tok, w_in_c, w_qkv_c, small = front(nz, nchip, ncore, tokens, w_in, w_qkv, small)
    tok = tok.reshape(rows, width)
    small = small.reshape(nz, total)

    def vector(i):
        return small[:, starts[i] : starts[i] + sizes[i]].astype(f32).reshape(1, -1)

    gain1, bias1, gain2, bias2 = [vector(i) for i in range(4)]
    bias_c = lax.dynamic_index_in_dim(vector(4).reshape(3, ranks, hc), rank, 1, keepdims=False)
    bias_c = bias_c.reshape(1, 3 * hc)
    bias_in = lax.dynamic_slice_in_dim(vector(6), rank * ffr, ffr, 1)
    ids = vector(8).astype(jnp.int32).reshape(nz, blocks)
    tok, cot_own = lax.optimization_barrier((tok, cotangent))
    cot = lax.all_gather(cot_own, TP, axis=0, tiled=True)

    per_chip = blocks // nchip
    ids_rows = lax.dynamic_slice_in_dim(ids, chip * per_chip, per_chip, 1).reshape(-1)
    ids_seq = lax.dynamic_index_in_dim(ids, chip, 0, keepdims=False)
    slots = jnp.arange(blocks, dtype=jnp.int32)
    order = jnp.sum(jnp.where(ids_seq[None, :] == slots[:, None], slots[None, :], 0), axis=1)
    place = (lax.rem(rank, split) == 0).astype(jnp.int32).reshape(1)
    table = jnp.asarray(turn_table(length))

    def heads_of(x):
        g = x.shape[1] // hc
        if split > 1:
            x = lax.all_gather(x.reshape(rows, g, hc), "core", axis=2, tiled=True)
        x = x.reshape(nz, rows // nz, g * HD)
        return lax.all_to_all(x, "chip", 0, 0, tiled=True).reshape(length, g * HD)

    def heads_back(x):
        g = x.shape[1] // HD
        x = x.reshape(nchip, length // nchip, g * HD)
        x = lax.all_to_all(x, "chip", 0, 0, tiled=True).reshape(rows, g * HD)
        if split > 1:
            x = lax.dynamic_slice_in_dim(x.reshape(rows, g, HD), core * hc, hc, 2)
        return x.reshape(rows, g * hc)

    tile = 256
    normed1, qkv = projections(nz, ids_rows, place, tok, w_qkv_c, bias_c, gain1, bias1, table)
    qkv = heads_of(qkv)
    normed2, active, slope = feed_forward(nz, tok, w_in_c, bias_in, gain2, bias2)
    qkv, active, slope, normed2 = lax.optimization_barrier((qkv, active, slope, normed2))
    attended, lse = attention_forward(ids_seq, order, qkv, tile)
    attended, cot = lax.optimization_barrier((attended, cot))

    if split == 1:
        mixed, g, dw_out = exchange_heads(nz, nchip, ncore, attended, cot, w_dense, active)
    else:
        mixed = heads_back(attended)
        g = heads_of(grad_of_mixed(nz, core_at, cot, w_dense, hc))
        dw_out = lax.dot_general(active, cot, TN, preferred_element_type=f32).astype(bf16)
    mixed, g, dw_out, cot = lax.optimization_barrier((mixed, g, dw_out, cot))
    s_out = lax.psum_scatter(dw_out, "chip", scatter_dimension=0, tiled=True)
    part_out = layer_out(nz, core_at, mixed, w_dense, active, w_out)
    g, part_out = lax.optimization_barrier((g, part_out))
    dqkv = attention_backward(ids_seq, order, qkv, g, lse, table, tile)
    dqkv, cot, mixed, part_out = lax.optimization_barrier((dqkv, cot, mixed, part_out))
    grad_project = heads_back(dqkv)
    grad_hidden, sum_bin = grad_of_hidden(nz, core_at, cot, w_out, slope)
    dw_in = lax.dot_general(normed2, grad_hidden, TN, preferred_element_type=f32).astype(bf16)
    dw_dense = lax.dot_general(mixed, cot, TN, preferred_element_type=f32).astype(bf16)
    grad_project, dw_in, dw_dense, s_out, part_out = lax.optimization_barrier(
        (grad_project, dw_in, dw_dense, s_out, part_out)
    )
    summed_out = lax.psum_scatter(part_out, TP, scatter_dimension=0, tiled=True).astype(f32)

    here = jnp.arange(ranks, dtype=jnp.int32) == rank
    mine_bin = jnp.where(here[:, None], sum_bin.reshape(1, ffr), 0.0)
    vectors = [
        jnp.zeros(7 * width, f32),
        jnp.sum(cotangent.astype(f32), axis=0),
        mine_bin.reshape(-1),
    ]
    vectors = jnp.concatenate([v.reshape(-1, 128) for v in vectors])
    g_wout, g_wdense, g_win, g_wqkv, e, sums = tail(
        nz, nchip, ncore, s_out, dw_dense, dw_in, vectors, normed1, grad_project, grad_hidden, tok,
        w_qkv_c, w_in_c, gain1, gain2
    )
    sums = sums.reshape(-1)
    at = 0
    small_out = []
    for size in (width, width, width, width, 3 * width, width, ranks * ffr):
        small_out.append(lax.dynamic_slice_in_dim(sums, at + z * (size // nz), size // nz))
        at += size
    g_gain1, g_bias1, g_gain2, g_bias2, g_bqkv, g_bdense, g_bin = small_out

    output = (tokens.astype(f32) + summed_out + vector(5) + vector(7)).astype(bf16)
    xhat_own, inv_own = stats(tokens.astype(f32))
    terms = (
        e
        - jnp.mean(e, axis=-1, keepdims=True)
        - xhat_own * jnp.mean(e * xhat_own, axis=-1, keepdims=True)
    ) * inv_own
    grad_tokens = (cotangent.astype(f32) + terms).astype(bf16)
    g_wout, g_wdense, g_win, g_wqkv = widen([g_wout, g_wdense, g_win, g_wqkv])
    return (
        output,
        grad_tokens,
        g_gain1,
        g_bias1,
        g_gain2,
        g_bias2,
        g_wqkv,
        g_bqkv,
        g_wdense,
        g_bdense,
        g_win,
        g_bin,
        g_wout,
        g_bdense,
    )


def solution(mesh):
    nz, nctx = mesh.shape["seq"], mesh.shape["ctx"]
    ncore = 2
    nchip = nctx // ncore
    fine = Mesh(mesh.devices.reshape(nz, nchip, ncore), ("seq", "chip", "core"))
    own = P(("seq", "chip", "core"), None)
    vec = P("seq")
    mat = P("seq", None)
    return jax.shard_map(
        functools.partial(on_device, nz, nchip, ncore),
        mesh=fine,
        in_specs=(own, mat, own, vec, vec, vec, vec, mat, vec, mat, vec, mat, vec, mat, vec),
        out_specs=(own, own, vec, vec, vec, vec, mat, vec, mat, vec, mat, vec, mat, vec),
        check_vma=False,
    )
```

```python
import functools
import math

import jax
import jax.numpy as jnp
import numpy as np
from jax import lax
from jax.experimental import pallas as pl
from jax.experimental.pallas import tpu as pltpu
from jax.sharding import Mesh, PartitionSpec as P

HD = 256
ROT = 64
BLOCK = 96
EPSILON = 1e-05
ROT_BASE = 10000.0
SCALE = HD ** (-0.5)
f32 = jnp.float32
bf16 = jnp.bfloat16
TP = ("seq", "core")
MESH = pl.DeviceIdType.MESH
NT = (((1,), (1,)), ((), ()))
TN = (((0,), (0,)), ((), ()))
BIG = pltpu.CompilerParams(vmem_limit_bytes=62 * 2**20)


def remote(src, dst, send, recv, target):
    return pltpu.make_async_remote_copy(
        src_ref=src, dst_ref=dst, send_sem=send, recv_sem=recv, device_id=target,
        device_id_type=MESH,
    )


def greet(targets):
    barrier = pltpu.get_barrier_semaphore()
    for target in targets:
        pl.semaphore_signal(barrier, inc=1, device_id=target, device_id_type=MESH)
    pl.semaphore_wait(barrier, len(targets))


def front(nz, nchip, ncore, tokens, w_in, w_qkv, small):
    own, width = tokens.shape
    wrows, ff = w_in.shape
    heads3 = w_qkv.shape[1]
    nctx = nchip * ncore
    piece = wrows // nctx
    half = piece // 2
    zi, zq = ff // nz, heads3 // 3 // nz
    ci, cq = zi // ncore, zq // ncore

    def kernel(
        tok_ref, wi_ref, wq_ref, sm_ref, tok_out, wi_out, wq_out, sm_out, buf_i, buf_q,
        up_s, up_r, dn_s, dn_r, sib_s, sib_r, zi_s, zi_r, zq_s, zq_r, p_s, p_r, r_s, loc, loc_p, sm_s, sm_r,
    ):
        z = lax.axis_index("seq")
        chip = lax.axis_index("chip")
        core = lax.axis_index("core")
        share = chip * ncore + core
        sibling = {"core": 1 - core}

        def z_at(d):
            return lax.rem(z + d, nz)

        def plane_at(d):
            other = lax.rem(share + d, nctx)
            return other // ncore, lax.rem(other, ncore)

        greet(
            [{"seq": z_at(d)} for d in range(1, nz)]
            + [{"chip": plane_at(d)[0], "core": plane_at(d)[1]} for d in range(1, nctx)]
        )

        def around(body, distances=range(1, nz)):
            for distance in distances:
                for other in (z + distance, z - distance):

                    @pl.when(jnp.logical_and(other >= 0, other < nz))
                    def _():
                        body(jnp.clip(other, 0, nz - 1))

        rows = pl.ds(share * piece, piece)

        def hop(to):
            pairs = [(wi_ref.at[rows, pl.ds(to * zi, zi)], buf_i.at[z], zi_s.at[to], zi_r.at[z])]
            for k in range(ncore):
                for g in range(3):
                    pairs.append(
                        (
                            wq_ref.at[rows, pl.ds(g * zq * nz + to * zq + k * cq, cq)],
                            buf_q.at[z, k, :, pl.ds(g * cq, cq)],
                            zq_s.at[to, k, g], zq_r.at[z, k, g],
                        )
                    )
            return pairs

        def hop_to(to):
            return [remote(a, b, c, d, {"seq": to}) for a, b, c, d in hop(to)]

        def send_hop(to):
            for copy in hop_to(to):
                copy.start()

        def hop_left(to):
            for copy in hop_to(to):
                copy.wait_send()

        def hop_arrival(source):
            here = buf_i.at[source]
            remote(here, here, zi_s.at[0], zi_r.at[source], sibling).wait_recv()
            for k in range(ncore):
                for g in range(3):
                    here = buf_q.at[source, k, :, pl.ds(g * cq, cq)]
                    remote(here, here, zq_s.at[0, 0, 0], zq_r.at[source, k, g], sibling).wait_recv()

        def up(s):
            at = jnp.maximum(z - s, 0)
            src = tok_ref if s == 0 else tok_out.at[at, core]
            return remote(
                src, tok_out.at[at, core], up_s.at[s], up_r.at[s],
                {"seq": jnp.minimum(z + 1, nz - 1)},
            )

        def down(s):
            at = jnp.minimum(z + s, nz - 1)
            src = tok_ref if s == 0 else tok_out.at[at, core]
            return remote(
                src, tok_out.at[at, core], dn_s.at[s], dn_r.at[s],
                {"seq": jnp.maximum(z - 1, 0)},
            )

        def side(shard, own_rows=False):
            src = tok_ref if own_rows else tok_out.at[shard, core]
            return remote(src, tok_out.at[shard, core], sib_s.at[shard], sib_r.at[shard], sibling)

        def token_step(s):
            @pl.when(z - 1 - s >= 0)
            def _():
                shard = jnp.maximum(z - 1 - s, 0)
                here = tok_out.at[shard, core]
                remote(here, here, up_s.at[s], up_r.at[s], sibling).wait_recv()
                if s + 1 < nz - 1:

                    @pl.when(z + 1 < nz)
                    def _():
                        up(s + 1).start()

                side(shard).start()

            @pl.when(z + 1 + s < nz)
            def _():
                shard = jnp.minimum(z + 1 + s, nz - 1)
                here = tok_out.at[shard, core]
                remote(here, here, dn_s.at[s], dn_r.at[s], sibling).wait_recv()
                if s + 1 < nz - 1:

                    @pl.when(z > 0)
                    def _():
                        down(s + 1).start()

                side(shard).start()

        def pieces(source, k):
            return buf_i.at[source, :, pl.ds(k * ci, ci)], buf_q.at[source, k]

        def places(source, owner):
            at = pl.ds(source * wrows + owner * piece, piece)
            return wi_out.at[at, :], wq_out.at[at, :]

        def cut(ref, h):
            return ref if h is None else ref.at[pl.ds(h * half, half), :]

        def in_place(source):
            return [
                pltpu.make_async_copy(a, b, loc_p.at[source, i])
                for i, (a, b) in enumerate(zip(pieces(source, core), places(source, share)))
            ]

        if nchip == 4:
            beside = chip + 1 - 2 * lax.rem(chip, 2)
            below = lax.rem(chip + 2, 4)
            across = 3 - chip
            order = ((beside, 0), (below, 1), (beside, 1), (below, 0))

            def spread(source):
                copies = []
                for way, (to, h) in enumerate(order):
                    for k in range(ncore):
                        for i, (a, b) in enumerate(zip(pieces(source, k), places(source, share))):
                            copies.append(
                                remote(
                                    cut(a, h), cut(b, h), p_s.at[source, i, k, way],
                                    p_r.at[source, i, share, h], {"chip": to, "core": k},
                                )
                            )
                return copies

            def relays(source):
                copies = []
                for h, (came, to) in enumerate(((beside, below), (below, beside))):
                    for k in range(ncore):
                        owner = came * ncore + k
                        for i, ref in enumerate(places(source, owner)):
                            part = cut(ref, h)
                            copies.append(
                                remote(
                                    part, part, r_s.at[source, i, k, h],
                                    p_r.at[source, i, owner, h], {"chip": to},
                                )
                            )
                return copies

            def relay(source):
                for copy in relays(source):
                    copy.wait_recv()
                    copy.start()

            rest = [(beside, 1), (below, 0), (across, 0), (across, 1)]
        else:

            def spread(source):
                copies = []
                for d in range(1, nctx):
                    to, k = plane_at(d)
                    for i, (a, b) in enumerate(zip(pieces(source, k), places(source, share))):
                        copies.append(
                            remote(
                                a, b, p_s.at[source, i, 0, d], p_r.at[source, i, share, 0],
                                {"chip": to, "core": k},
                            )
                        )
                return copies

            def relay(source):
                pass

        def to_sibling(source):
            return [
                remote(a, b, p_s.at[source, i, 0, 4], p_r.at[source, i, share, 0], sibling)
                for i, (a, b) in enumerate(zip(pieces(source, 1 - core), places(source, share)))
            ]

        def hand_on(source):
            for copy in spread(source) + in_place(source):
                copy.start()
            if nchip == 4:
                for copy in to_sibling(source):
                    copy.start()

        def arrive(source):
            hop_arrival(source)
            hand_on(source)

        smalls = [
            remote(sm_ref, sm_out.at[z], sm_s.at[d], sm_r.at[z], {"seq": z_at(d)})
            for d in range(1, nz)
        ]
        for copy in smalls:
            copy.start()
        around(send_hop)

        @pl.when(z + 1 < nz)
        def _():
            up(0).start()

        @pl.when(z > 0)
        def _():
            down(0).start()

        side(z, True).start()
        mine = [
            pltpu.make_async_copy(tok_ref, tok_out.at[z, core], loc.at[0]),
            pltpu.make_async_copy(sm_ref, sm_out.at[z], loc.at[1]),
        ]
        held = [
            pltpu.make_async_copy(a, b, loc.at[2 + i]) for i, (a, b, c, d) in enumerate(hop(z))
        ]
        for copy in held + mine:
            copy.start()
        for copy in held:
            copy.wait()
        hand_on(z)
        for distance in range(1, nz):
            around(arrive, [distance])
            if distance == 1:
                relay(z)
            else:
                around(relay, [distance - 1])
            token_step(distance - 1)
        around(relay, [nz - 1])

        for copy in mine:
            copy.wait()
        for shard in range(nz):
            there = tok_out.at[shard, 1 - core]
            remote(there, there, sib_s.at[shard], sib_r.at[shard], sibling).wait_recv()
            side(shard).wait_send()
        for s in range(nz - 1):

            @pl.when(jnp.logical_and(z + 1 < nz, z - s >= 0))
            def _():
                up(s).wait_send()

            @pl.when(jnp.logical_and(z > 0, z + s < nz))
            def _():
                down(s).wait_send()

        around(hop_left)
        for copy in smalls:
            copy.wait_send()
        for d in range(1, nz):
            there = sm_out.at[z_at(d)]
            remote(there, there, sm_s.at[d], sm_r.at[z_at(d)], sibling).wait_recv()
        for source in range(nz):
            for copy in in_place(source):
                copy.wait()
            for copy in spread(source):
                copy.wait_send()
            if nchip == 4:
                for copy in to_sibling(source) + relays(source):
                    copy.wait_send()
                waits = [(chip * ncore + 1 - core, None, 0)] + [
                    (c * ncore + k, h, h) for c, h in rest for k in range(ncore)
                ]
            else:
                waits = [(lax.rem(share + d, nctx), None, 0) for d in range(1, nctx)]
            for owner, h, slot in waits:
                for i, ref in enumerate(places(source, owner)):
                    part = cut(ref, h)
                    remote(
                        part, part, p_s.at[source, i, 0, 0], p_r.at[source, i, owner, slot], sibling
                    ).wait_recv()

    dma = pltpu.SemaphoreType.DMA
    anywhere = pl.BlockSpec(memory_space=pl.ANY)
    return pl.pallas_call(
        kernel,
        in_specs=[anywhere] * 4,
        out_specs=[anywhere] * 4,
        out_shape=[
            jax.ShapeDtypeStruct((nz, ncore, own, width), bf16),
            jax.ShapeDtypeStruct((nz * wrows, ci), bf16),
            jax.ShapeDtypeStruct((nz * wrows, 3 * cq), bf16),
            jax.ShapeDtypeStruct((nz,) + small.shape, bf16),
        ],
        scratch_shapes=[
            pltpu.VMEM((nz, piece, zi), bf16),
            pltpu.VMEM((nz, ncore, piece, 3 * cq), bf16),
            dma((nz,)), dma((nz,)), dma((nz,)), dma((nz,)),
            dma((nz,)), dma((nz,)),
            dma((nz,)), dma((nz,)), dma((nz, ncore, 3)), dma((nz, ncore, 3)),
            dma((nz, 2, ncore, max(5, nctx))), dma((nz, 2, nctx, 2)), dma((nz, 2, ncore, 2)),
            dma((3 + 3 * ncore,)), dma((nz, 2)), dma((nz,)), dma((nz,)),
        ],
        compiler_params=pltpu.CompilerParams(
            collective_id=1, has_side_effects=True, vmem_limit_bytes=62 * 2**20
        ),
        name="front",
    )(tokens, w_in, w_qkv, small)


def turn_table(length):
    half = ROT // 2
    power = -(np.arange(half, dtype=np.float32) * np.float32(2.0)) / np.float32(ROT)
    angles = np.arange(length, dtype=np.float32)[:, None] * np.power(np.float32(ROT_BASE), power)
    table = np.zeros((3, length, 128), np.float32)
    table[0] = 1.0
    table[0, :, :half] = table[0, :, half:ROT] = np.cos(angles)
    table[1, :, :half] = -np.sin(angles)
    table[2, :, half:ROT] = np.sin(angles)
    return table


def turned(u, cosine, minus, plus):
    half = ROT // 2
    return u * cosine + pltpu.roll(u, 128 - half, 1) * minus + pltpu.roll(u, half, 1) * plus


def stats(x):
    center = x - jnp.mean(x, axis=-1, keepdims=True)
    inv = lax.rsqrt(jnp.mean(center * center, axis=-1, keepdims=True) + EPSILON)
    return center * inv, inv


def cost(flops, nbytes, trans=0):
    return pl.CostEstimate(flops=int(flops), bytes_accessed=int(nbytes), transcendentals=int(trans))


def projections(nz, ids, place, tok, w, bias, gain, offset, table):
    rows, width = tok.shape
    step = rows // nz
    blocks = step // BLOCK
    cols = w.shape[1]
    hc = cols // 3

    def kernel(ids_ref, place_ref, tok_ref, w_ref, b_ref, g_ref, o_ref, t_ref, n_ref, out_ref):
        xhat, inv = stats(tok_ref[...].astype(f32))
        normed = (xhat * g_ref[...] + o_ref[...]).astype(bf16)
        n_ref[...] = normed
        project = jnp.dot(normed, w_ref[...], preferred_element_type=f32) + b_ref[...]
        out_ref[...] = project.astype(bf16)
        first = place_ref[0] == 1

        @pl.when(first)
        def _():
            for b in range(blocks):
                at = pl.ds(pl.multiple_of(ids_ref[pl.program_id(0) * blocks + b] * BLOCK, BLOCK), BLOCK)
                c, m, p = t_ref[0, at, :], t_ref[1, at, :], t_ref[2, at, :]
                for g in range(2):
                    u = project[b * BLOCK : (b + 1) * BLOCK, g * hc : g * hc + 128]
                    out_ref[b * BLOCK : (b + 1) * BLOCK, g * hc : g * hc + 128] = turned(
                        u, c, m, p
                    ).astype(bf16)

    whole = lambda shape: pl.BlockSpec(shape, lambda i, *_: (0,) * len(shape))
    return pl.pallas_call(
        kernel,
        grid_spec=pltpu.PrefetchScalarGridSpec(
            num_scalar_prefetch=2,
            grid=(nz,),
            in_specs=[
                pl.BlockSpec((step, width), lambda i, *_: (i, 0)),
                whole((width, cols)),
                whole((1, cols)),
                whole((1, width)),
                whole((1, width)),
                whole(table.shape),
            ],
            out_specs=[
                pl.BlockSpec((step, width), lambda i, *_: (i, 0)),
                pl.BlockSpec((step, cols), lambda i, *_: (i, 0)),
            ],
        ),
        out_shape=[
            jax.ShapeDtypeStruct((rows, width), bf16),
            jax.ShapeDtypeStruct((rows, cols), bf16),
        ],
        compiler_params=BIG,
        cost_estimate=cost(2 * rows * width * cols, 4 * rows * width + 2 * width * cols),
        name="projections",
    )(ids, place, tok, w, bias, gain, offset, table)


def feed_forward(nz, tok, w, bias, gain, offset):
    rows, width = tok.shape
    step = rows // nz
    cols = w.shape[1]

    def kernel(tok_ref, w_ref, b_ref, g_ref, o_ref, n_ref, a_ref, d_ref):
        xhat, inv = stats(tok_ref[...].astype(f32))
        normed = (xhat * g_ref[...] + o_ref[...]).astype(bf16)
        n_ref[...] = normed
        v = jnp.dot(normed, w_ref[...], preferred_element_type=f32) + b_ref[...]
        gate = 0.5 * (1.0 + lax.erf(v * (0.5**0.5)))
        a_ref[...] = (v * gate).astype(bf16)
        bell = jnp.exp(v * v * -0.5) * ((2.0 * math.pi) ** -0.5)
        d_ref[...] = (gate + v * bell).astype(bf16)

    whole = lambda shape: pl.BlockSpec(shape, lambda i: (0, 0))
    part = lambda n: pl.BlockSpec((step, n), lambda i: (i, 0))
    return pl.pallas_call(
        kernel,
        grid=(nz,),
        in_specs=[part(width), whole((width, cols)), whole((1, cols)), whole((1, width)), whole((1, width))],
        out_specs=[part(width), part(cols), part(cols)],
        out_shape=[
            jax.ShapeDtypeStruct((rows, width), bf16),
            jax.ShapeDtypeStruct((rows, cols), bf16),
            jax.ShapeDtypeStruct((rows, cols), bf16),
        ],
        compiler_params=BIG,
        cost_estimate=cost(2 * rows * width * cols, 4 * rows * width + 2 * width * cols, 2 * rows * cols),
        name="feed_forward",
    )(tok, w, bias, gain, offset)


def layer_out(nz, core, mixed, w_dense, active, w_out):
    rows, hc = mixed.shape
    width = w_out.shape[1]
    step = rows // nz
    units = active.shape[1]

    def kernel(core_ref, m_ref, wd_ref, a_ref, wo_ref, out_ref):
        out_ref[...] = (
            jnp.dot(m_ref[...], wd_ref[...], preferred_element_type=f32)
            + jnp.dot(a_ref[...], wo_ref[...], preferred_element_type=f32)
        ).astype(bf16)

    part = lambda n: pl.BlockSpec((step, n), lambda i, c: (i, 0))
    held = lambda n: pl.BlockSpec((n, width), lambda i, c: (c[0], 0))
    return pl.pallas_call(
        kernel,
        grid_spec=pltpu.PrefetchScalarGridSpec(
            num_scalar_prefetch=1,
            grid=(nz,),
            in_specs=[part(hc), held(hc), part(units), held(units)],
            out_specs=part(width),
        ),
        out_shape=jax.ShapeDtypeStruct((rows, width), bf16),
        compiler_params=BIG,
        cost_estimate=cost(2 * rows * width * (hc + units), 4 * rows * width + 2 * width * units),
        name="layer_out",
    )(core, mixed, w_dense, active, w_out)


def widen(arrays, ranks):
    steps = [min(x.shape[0], 128 if x.shape[1] > 4096 else 512) for x in arrays]
    counts = [x.shape[0] // step for x, step in zip(arrays, steps)]
    starts = [sum(counts[:i]) for i in range(len(counts))]

    def kernel(*refs):
        n = len(arrays)
        for i in range(n):
            here = pl.program_id(0) - starts[i]

            @pl.when(jnp.logical_and(here >= 0, here < counts[i]))
            def _():
                if i < n - 1:
                    refs[n + i][...] = refs[i][...].astype(f32)
                else:
                    cols = arrays[i].shape[1] // 3 // ranks
                    for r in range(ranks):
                        for g in range(3):
                            to, at = (g * ranks + r) * cols, (3 * r + g) * cols
                            refs[n + i][:, to : to + cols] = refs[i][:, at : at + cols].astype(f32)

    def part(i):
        return pl.BlockSpec(
            (steps[i], arrays[i].shape[1]),
            lambda s: (jnp.clip(s - starts[i], 0, counts[i] - 1), 0),
        )

    specs = [part(i) for i in range(len(arrays))]
    size = sum(x.size for x in arrays)
    return pl.pallas_call(
        kernel,
        grid=(sum(counts),),
        in_specs=specs,
        out_specs=specs,
        out_shape=[jax.ShapeDtypeStruct(x.shape, f32) for x in arrays],
        compiler_params=BIG,
        cost_estimate=cost(size, 6 * size),
        name="widen",
    )(*arrays)


def grad_of_mixed(nz, core, cot, w_dense, hc):
    rows, width = cot.shape
    step = rows // nz

    def kernel(core_ref, c_ref, w_ref, out_ref):
        out_ref[...] = lax.dot_general(
            c_ref[...], w_ref[...], NT, preferred_element_type=f32
        ).astype(bf16)

    return pl.pallas_call(
        kernel,
        grid_spec=pltpu.PrefetchScalarGridSpec(
            num_scalar_prefetch=1,
            grid=(nz,),
            in_specs=[
                pl.BlockSpec((step, width), lambda i, c: (i, 0)),
                pl.BlockSpec((hc, width), lambda i, c: (c[0], 0)),
            ],
            out_specs=pl.BlockSpec((step, hc), lambda i, c: (i, 0)),
        ),
        out_shape=jax.ShapeDtypeStruct((rows, hc), bf16),
        compiler_params=BIG,
        cost_estimate=cost(2 * rows * width * hc, 2 * rows * width),
        name="grad_of_mixed",
    )(core, cot, w_dense)


def grad_of_hidden(nz, core, cot, w_out, slope):
    rows, width = cot.shape
    step = rows // nz
    units = slope.shape[1]

    def kernel(core_ref, c_ref, w_ref, d_ref, out_ref, sum_ref):
        g = lax.dot_general(c_ref[...], w_ref[...], NT, preferred_element_type=f32)
        g = (g * d_ref[...].astype(f32)).astype(bf16)
        out_ref[...] = g

        @pl.when(pl.program_id(0) == 0)
        def _():
            sum_ref[...] = jnp.zeros_like(sum_ref)

        sum_ref[...] += jnp.sum(g.astype(f32), axis=0, keepdims=True)

    return pl.pallas_call(
        kernel,
        grid_spec=pltpu.PrefetchScalarGridSpec(
            num_scalar_prefetch=1,
            grid=(nz,),
            in_specs=[
                pl.BlockSpec((step, width), lambda i, c: (i, 0)),
                pl.BlockSpec((units, width), lambda i, c: (c[0], 0)),
                pl.BlockSpec((step, units), lambda i, c: (i, 0)),
            ],
            out_specs=[
                pl.BlockSpec((step, units), lambda i, c: (i, 0)),
                pl.BlockSpec((1, units), lambda i, c: (0, 0)),
            ],
        ),
        out_shape=[
            jax.ShapeDtypeStruct((rows, units), bf16),
            jax.ShapeDtypeStruct((1, units), f32),
        ],
        compiler_params=BIG,
        cost_estimate=cost(2 * rows * width * units, 2 * rows * width + 2 * width * units),
        name="grad_of_hidden",
    )(core, cot, w_out, slope)


def norm_back(nz, grad, w, tok, gain, other, sums):
    rows, width = tok.shape
    step = rows // nz
    cols = grad.shape[1]

    def kernel(*refs):
        g_ref, w_ref, t_ref, gain_ref = refs[:4]
        at = 4
        if other is not None:
            other_ref = refs[at]
            at += 1
        e_ref, s_ref = refs[at : at + 2]
        gn = lax.dot_general(g_ref[...], w_ref[...], NT, preferred_element_type=f32)
        xhat, inv = stats(t_ref[...].astype(f32))
        e = gn * gain_ref[...]
        if other is not None:
            e = e + other_ref[...].astype(f32)
        e_ref[...] = e.astype(bf16)

        @pl.when(pl.program_id(0) == 0)
        def _():
            s_ref[...] = jnp.zeros_like(s_ref)
            if sums:
                refs[at + 2][...] = jnp.zeros_like(refs[at + 2])

        s_ref[0:1, :] += jnp.sum(gn * xhat, axis=0, keepdims=True)
        s_ref[1:2, :] += jnp.sum(gn, axis=0, keepdims=True)
        if sums:
            refs[at + 2][...] += jnp.sum(g_ref[...].astype(f32), axis=0, keepdims=True)

    part = lambda n: pl.BlockSpec((step, n), lambda i: (i, 0))
    whole = lambda shape: pl.BlockSpec(shape, lambda i: (0, 0))
    ins = [grad, w, tok, gain] + ([] if other is None else [other])
    return pl.pallas_call(
        kernel,
        grid=(nz,),
        in_specs=[part(cols), whole((width, cols)), part(width), whole((1, width))]
        + ([] if other is None else [part(width)]),
        out_specs=[part(width), whole((2, width))] + ([whole((1, cols))] if sums else []),
        out_shape=[
            jax.ShapeDtypeStruct((rows, width), bf16),
            jax.ShapeDtypeStruct((2, width), f32),
        ]
        + ([jax.ShapeDtypeStruct((1, cols), f32)] if sums else []),
        compiler_params=BIG,
        cost_estimate=cost(2 * rows * width * cols, 6 * rows * width + 2 * width * cols),
        name="norm_back",
    )(*ins)


def attention_forward(ids, order, qkv, tile):
    rows = qkv.shape[0]
    blocks = rows // BLOCK

    def kernel(ids_ref, order_ref, x_ref, o_ref, lse_ref, q_ref, k_ref, v_ref, s_ref):
        for b in range(blocks):
            at = pl.ds(pl.multiple_of(order_ref[b] * BLOCK, BLOCK), BLOCK)
            here = slice(b * BLOCK, (b + 1) * BLOCK)
            for i, ref in enumerate((q_ref, k_ref, v_ref)):
                ref[here, :] = x_ref[at, i * HD : (i + 1) * HD]
        for t in range(rows // tile):
            mine = slice(t * tile, (t + 1) * tile)
            n = (t + 1) * tile
            s = lax.dot_general(q_ref[mine, :], k_ref[:n, :], NT, preferred_element_type=f32)
            s = s * SCALE
            seen = t * tile + lax.broadcasted_iota(jnp.int32, (tile, n), 0) >= (
                lax.broadcasted_iota(jnp.int32, (tile, n), 1)
            )
            s = jnp.where(seen, s, -1e30)
            top = jnp.max(s, axis=-1, keepdims=True)
            e = jnp.exp(s - top)
            total = jnp.sum(e, axis=-1, keepdims=True)
            p = (e * (1.0 / total)).astype(bf16)
            s_ref[mine, :] = jnp.dot(p, v_ref[:n, :], preferred_element_type=f32).astype(bf16)
            lse_ref[mine, :] = top + jnp.log(total)
        for b in range(blocks):
            at = pl.ds(pl.multiple_of(ids_ref[b] * BLOCK, BLOCK), BLOCK)
            o_ref[b * BLOCK : (b + 1) * BLOCK, :] = s_ref[at, :]

    smem = pl.BlockSpec(memory_space=pltpu.SMEM)
    vmem = pl.BlockSpec(memory_space=pltpu.VMEM)
    return pl.pallas_call(
        kernel,
        in_specs=[smem, smem, vmem],
        out_specs=[vmem, vmem],
        out_shape=[
            jax.ShapeDtypeStruct((rows, HD), bf16),
            jax.ShapeDtypeStruct((rows, 1), f32),
        ],
        scratch_shapes=[pltpu.VMEM((rows, HD), bf16)] * 4,
        compiler_params=BIG,
        cost_estimate=cost(2.3 * rows * rows * HD, 8 * rows * HD, rows * rows / 2),
        name="attention_forward",
    )(ids, order, qkv)


def attention_backward(ids, order, qkv, grad, lse, table, tile):
    rows = qkv.shape[0]
    blocks = rows // BLOCK

    def kernel(ids_ref, order_ref, x_ref, g_ref, lse_ref, t_ref, out_ref, q_ref, k_ref, v_ref, m_ref,
               r_ref, dk_ref, dv_ref):
        for b in range(blocks):
            at = pl.ds(pl.multiple_of(order_ref[b] * BLOCK, BLOCK), BLOCK)
            here = slice(b * BLOCK, (b + 1) * BLOCK)
            for i, ref in enumerate((q_ref, k_ref, v_ref)):
                ref[here, :] = x_ref[at, i * HD : (i + 1) * HD]
            m_ref[here, :] = g_ref[at, :]
        for t in reversed(range(rows // tile)):
            mine = slice(t * tile, (t + 1) * tile)
            n = (t + 1) * tile
            q, g = q_ref[mine, :], m_ref[mine, :]
            s = lax.dot_general(q, k_ref[:n, :], NT, preferred_element_type=f32) * SCALE
            seen = t * tile + lax.broadcasted_iota(jnp.int32, (tile, n), 0) >= (
                lax.broadcasted_iota(jnp.int32, (tile, n), 1)
            )
            p = jnp.where(seen, jnp.exp(s - lse_ref[mine, :]), 0.0)
            dp = lax.dot_general(g, v_ref[:n, :], NT, preferred_element_type=f32)
            shift = jnp.sum(p * dp, axis=-1, keepdims=True)
            ds = (p * (dp - shift)).astype(bf16)
            low = p.astype(bf16)
            dq = jnp.dot(ds, k_ref[:n, :], preferred_element_type=f32) * SCALE
            r_ref[mine, :128] = turned(
                dq[:, :128], t_ref[0, mine, :], -t_ref[1, mine, :], -t_ref[2, mine, :]
            ).astype(bf16)
            r_ref[mine, 128:HD] = dq[:, 128:].astype(bf16)
            dk = lax.dot_general(ds, q, TN, preferred_element_type=f32) * SCALE
            dv = lax.dot_general(low, g, TN, preferred_element_type=f32)
            if n == rows:
                dk_ref[...] = dk
                dv_ref[...] = dv
            else:
                dk_ref[:n, :] += dk
                dv_ref[:n, :] += dv
        r_ref[:, HD : HD + 128] = turned(
            dk_ref[:, :128], t_ref[0], -t_ref[1], -t_ref[2]
        ).astype(bf16)
        r_ref[:, HD + 128 : 2 * HD] = dk_ref[:, 128:].astype(bf16)
        r_ref[:, 2 * HD :] = dv_ref[...].astype(bf16)
        for b in range(blocks):
            at = pl.ds(pl.multiple_of(ids_ref[b] * BLOCK, BLOCK), BLOCK)
            out_ref[b * BLOCK : (b + 1) * BLOCK, :] = r_ref[at, :]

    smem = pl.BlockSpec(memory_space=pltpu.SMEM)
    vmem = pl.BlockSpec(memory_space=pltpu.VMEM)
    return pl.pallas_call(
        kernel,
        in_specs=[smem, smem, vmem, vmem, vmem, vmem],
        out_specs=vmem,
        out_shape=jax.ShapeDtypeStruct((rows, 3 * HD), bf16),
        scratch_shapes=[pltpu.VMEM((rows, HD), bf16)] * 4
        + [pltpu.VMEM((rows, 3 * HD), bf16)]
        + [pltpu.VMEM((rows, HD), f32)] * 2,
        compiler_params=BIG,
        cost_estimate=cost(6 * rows * rows * HD, 20 * rows * HD, rows * rows / 2),
        name="attention_backward",
    )(ids, order, qkv, grad, lse, table)


def exchange_heads(nz, nchip, ncore, attended, cot, w_dense, active):
    rows, width = cot.shape
    step = rows // nz
    length, hc = attended.shape
    part = length // nchip
    units = active.shape[1]
    tile = 256

    def kernel(att_ref, cot_hbm, w_hbm, act_hbm, mix_out, g_out, dw_out, cot_ref, w_ref, act_ref, gm_ref, dw_ref,
               ld, m_s, m_r, g_s, g_r, own_l, dw_l):
        chip = lax.axis_index("chip")
        core = lax.axis_index("core")
        loads = [
            pltpu.make_async_copy(w_hbm.at[pl.ds(core * hc, hc), :], w_ref, ld.at[0]),
            pltpu.make_async_copy(cot_hbm, cot_ref, ld.at[1]),
            pltpu.make_async_copy(act_hbm, act_ref, ld.at[2]),
        ]
        for copy in loads:
            copy.start()

        def chip_at(d):
            return lax.rem(chip + d, nchip)

        greet([{"chip": chip_at(d)} for d in range(1, nchip)])
        sent = [
            remote(
                att_ref.at[pl.ds(chip_at(d) * part, part), :],
                mix_out.at[pl.ds(chip * step, step), :], m_s.at[d], m_r.at[d], {"chip": chip_at(d)},
            )
            for d in range(1, nchip)
        ]
        kept = [
            pltpu.make_async_copy(
                att_ref.at[pl.ds(chip * part, part), :], mix_out.at[pl.ds(chip * step, step), :],
                own_l.at[0],
            )
        ]
        for copy in sent + kept:
            copy.start()
        loads[0].wait()
        loads[1].wait()
        for d in range(1, nchip + 1):
            to = chip_at(d)
            at = pl.ds(pl.multiple_of(to * step, step), step)
            gm_ref[at, :] = lax.dot_general(
                cot_ref[at, :], w_ref[...], NT, preferred_element_type=f32
            ).astype(bf16)
            there = g_out.at[pl.ds(chip * part, part), :]
            if d < nchip:
                copy = remote(gm_ref.at[at, :], there, g_s.at[d], g_r.at[d], {"chip": to})
                sent.append(copy)
            else:
                copy = pltpu.make_async_copy(gm_ref.at[at, :], there, own_l.at[1])
                kept.append(copy)
            copy.start()
        loads[2].wait()
        for t in range(units // tile):
            at = pl.ds(t * tile, tile)
            dw_ref[at, :] = lax.dot_general(
                act_ref[:, at], cot_ref[...], TN, preferred_element_type=f32
            ).astype(bf16)
            copy = pltpu.make_async_copy(dw_ref.at[at, :], dw_out.at[at, :], dw_l.at[t])
            copy.start()
            kept.append(copy)
        for copy in kept + sent:
            copy.wait()

    dma = pltpu.SemaphoreType.DMA
    anywhere = pl.BlockSpec(memory_space=pl.ANY)
    return pl.pallas_call(
        kernel,
        in_specs=[anywhere] * 4,
        out_specs=[anywhere] * 3,
        out_shape=[
            jax.ShapeDtypeStruct((rows, hc), bf16),
            jax.ShapeDtypeStruct((length, hc), bf16),
            jax.ShapeDtypeStruct((units, width), bf16),
        ],
        scratch_shapes=[
            pltpu.VMEM((rows, width), bf16),
            pltpu.VMEM((hc, width), bf16),
            pltpu.VMEM((rows, units), bf16),
            pltpu.VMEM((rows, hc), bf16),
            pltpu.VMEM((units, width), bf16),
            dma((3,)), dma((nchip,)), dma((nchip,)), dma((nchip,)), dma((nchip,)), dma((2,)),
            dma((units // tile,)),
        ],
        compiler_params=pltpu.CompilerParams(
            collective_id=3, has_side_effects=True, vmem_limit_bytes=62 * 2**20
        ),
        cost_estimate=cost(2 * rows * width * (hc + units), 4 * rows * width),
        name="exchange_heads",
    )(attended, cot, w_dense, active)


def gather_plane(nchip, chip, core, src, dst_of, send, recv, local):
    sibling = {"core": 1 - core}
    rows = src.shape[0]
    half = rows // 2
    here = dst_of(chip, core)
    begun = [pltpu.make_async_copy(src, here, local)]
    begun.append(remote(src, here, send.at[0], recv.at[0], sibling))
    relays = []
    arrivals = []

    def cut(ref, h):
        return ref.at[pl.ds(h * half, half), :]

    if nchip == 4:
        beside = chip + 1 - 2 * lax.rem(chip, 2)
        below = lax.rem(chip + 2, 4)
        across = 3 - chip
        order = ((beside, 0, 1), (below, 1, 2), (beside, 1, 1), (below, 0, 2))
        for i, (to, h, d) in enumerate(order):
            slot = 4 + 2 * d + h
            begun.append(
                remote(cut(src, h), cut(here, h), send.at[slot], recv.at[slot], {"chip": to})
            )

        def passing(owner, h, to):
            part = cut(dst_of(owner, core), h)
            return remote(part, part, send.at[10 + h], recv.at[10 + h], {"chip": to})

        relays = [(passing(beside, 0, below), beside, 0, 6), (passing(below, 1, beside), below, 1, 9)]
        arrivals = [(beside, 1, 7, 1), (below, 0, 8, 2), (across, 0, 10, 3), (across, 1, 11, 3)]
        others = [(beside, 1), (below, 2), (across, 3)]
    else:
        others = [(lax.rem(chip + d, nchip), d) for d in range(1, nchip)]
        for to, d in others:
            begun.append(
                remote(src, here, send.at[nchip + d], recv.at[nchip + chip], {"chip": to})
            )

    def side(owner, slot):
        part = dst_of(owner, core)
        return remote(part, part, send.at[slot], recv.at[slot], sibling)

    def slot_of(owner, d):
        return d if nchip == 4 else 2 * nchip + owner

    def first():
        for copy in begun:
            copy.start()

    def onward():
        if nchip == 4:
            for copy, owner, h, slot in relays:
                part = cut(dst_of(owner, core), h)
                remote(part, part, send.at[0], recv.at[slot], sibling).wait_recv()
                copy.start()

    def pass_on():
        if nchip == 4:
            for owner, h, slot, d in arrivals:
                part = cut(dst_of(owner, core), h)
                remote(part, part, send.at[0], recv.at[slot], sibling).wait_recv()
                if slot != 10:
                    side(owner, d).start()
        else:
            for owner, d in others:
                part = dst_of(owner, core)
                remote(part, part, send.at[0], recv.at[nchip + owner], sibling).wait_recv()
                side(owner, slot_of(owner, d)).start()

    def last():
        begun[0].wait()
        for copy in begun[1:]:
            copy.wait_send()
        for copy, owner, h, slot in relays:
            copy.wait_send()
        there = dst_of(chip, 1 - core)
        remote(there, there, send.at[0], recv.at[0], sibling).wait_recv()
        for owner, d in others:
            side(owner, slot_of(owner, d)).wait_send()
            there = dst_of(owner, 1 - core)
            remote(there, there, send.at[0], recv.at[slot_of(owner, d)], sibling).wait_recv()

    return first, onward, pass_on, last


def scatter_plane(nchip, chip, part, own, first, second, send, recv, local):
    halves = own.shape[0]
    copies = []
    shape = own.shape[2:]

    def add(dst, terms):
        def rows(lead):
            @pl.loop(0, shape[-2] // 16)
            def _(i):
                at = lead + (pl.ds(pl.multiple_of(i * 16, 16), 16), slice(None))
                acc = dst[at].astype(f32)
                for term in terms:
                    acc = acc + term[at].astype(f32)
                dst[at] = acc.astype(bf16)

        if len(shape) == 2:
            rows(())
        else:

            @pl.loop(0, shape[0])
            def _(b):
                rows((b,))

    if nchip == 4:
        beside = chip + 1 - 2 * lax.rem(chip, 2)
        below = lax.rem(chip + 2, 4)
        across = 3 - chip
        ways = [(beside, below), (below, beside)]
        kept = [
            [
                pltpu.make_async_copy(part(chip, h), own.at[h, 0], local.at[h, 0]),
                pltpu.make_async_copy(part(ways[h][1], h), own.at[h, 1], local.at[h, 1]),
            ]
            for h in range(2)
        ]
        leave = [
            [
                remote(
                    part(across, h), first.at[h, 1], send.at[h, 1], recv.at[h, 1],
                    {"chip": ways[h][0]},
                ),
                remote(
                    part(ways[h][0], h), first.at[h, 0], send.at[h, 0], recv.at[h, 0],
                    {"chip": ways[h][0]},
                ),
            ]
            for h in range(2)
        ]
        follow = [
            remote(
                own.at[h, 1], second.at[h], send.at[h, 2], recv.at[h, 2], {"chip": ways[h][1]}
            )
            for h in range(2)
        ]

        def begin():
            for i in range(2):
                for h in range(2):
                    leave[h][i].start()
            for h in range(2):
                kept[h][1].start()
                kept[h][0].start()

        def middle():
            for h in range(2):
                kept[h][1].wait()
                leave[h][0].wait_recv()
                add(own.at[h, 1], [first.at[h, 1]])
                follow[h].start()

        def finish():
            for h in range(2):
                kept[h][0].wait()
                leave[h][1].wait_recv()
                follow[h].wait_recv()
                add(own.at[h, 0], [first.at[h, 0], second.at[h]])

        def last():
            for h in range(2):
                for copy in leave[h] + [follow[h]]:
                    copy.wait_send()
    else:
        to = [lax.rem(chip + d, nchip) for d in range(nchip)]
        kept = pltpu.make_async_copy(part(chip, 0), own.at[0, 0], local.at[0, 0])
        leave = [
            remote(part(to[d], 0), first.at[0, d], send.at[0, d], recv.at[0, d], {"chip": to[d]})
            for d in range(1, nchip)
        ]

        def begin():
            for copy in leave:
                copy.start()
            kept.start()

        def middle():
            pass

        def finish():
            kept.wait()
            for copy in leave:
                copy.wait_recv()
            add(own.at[0, 0], [first.at[0, d] for d in range(1, nchip)])

        def last():
            for copy in leave:
                copy.wait_send()

    return begin, middle, finish, last


def tail(nz, nchip, ncore, dwo, dwd, dwi, vectors, normed1, grad_project, grad_hidden, tok, w_qkv, w_in, gain1, gain2):
    width = dwo.shape[1]
    ro, rd = dwo.shape[0], dwd.shape[0] // nchip
    halves = 2 if nchip == 4 else 1
    hz = nz // halves
    hd = rd // halves
    ci, cq = dwi.shape[1], grad_project.shape[1] // 3
    wrows = width // nz
    ri = wrows // nchip
    rows = tok.shape[0]
    step = rows // nz
    own = step // ncore
    vr = vectors.shape[0]
    chunk = 512
    dwi = dwi.reshape(nz, nchip, ri, ci)
    dwd = dwd.reshape(nchip, rd, width)

    def kernel(
        dwo_ref, dwd_ref, dwi_ref, vec_ref, n_hbm, gp_hbm, gh_hbm, tok_hbm, wq_hbm, wi_hbm, g1_ref, g2_ref,
        go_ref, gd_ref, gi_ref, gq_ref, e_ref, vsum_ref,
        x_ref, gp_ref, gh_ref, wq_ref, wi_ref, dwq_ref, eb,
        oi, fi, si, oq, fq, sq, od, fd, sd, ti, tq, se, ze, cs, v0, v1, v2, v3,
        ld, ri_s, ri_r, ri_l, rq_s, rq_r, rq_l, rd_s, rd_r, rd_l, x_s, x_r, ez_s, ez_r, t_s, t_r, t_l,
        go_s, go_r, gd_s, gd_r, gi_s, gi_r, gq_s, gq_r, own_l,
        v_s, v_r,
    ):
        z = lax.axis_index("seq")
        chip = lax.axis_index("chip")
        core = lax.axis_index("core")
        sibling = {"core": 1 - core}

        def z_at(d):
            return lax.rem(z + d, nz)

        def chip_at(d):
            return lax.rem(chip + d, nchip)

        loads = [
            pltpu.make_async_copy(a, b, ld.at[i])
            for i, (a, b) in enumerate(
                ((n_hbm, x_ref), (gp_hbm, gp_ref), (gh_hbm, gh_ref), (wi_hbm, wi_ref), (wq_hbm, wq_ref))
            )
        ]
        for copy in loads:
            copy.start()
        greet(
            [{"seq": z_at(d)} for d in range(1, nz)]
            + [{"chip": chip_at(d)} for d in range(1, nchip)]
            + [sibling]
        )

        def turn(kind, part, turned):
            copies = [
                remote(
                    part(z_at(d)), turned.at[z], t_s.at[kind, d], t_r.at[kind, z],
                    {"seq": z_at(d)},
                )
                for d in range(1, nz)
            ]
            copies.append(pltpu.make_async_copy(part(z), turned.at[z], t_l.at[kind]))
            for copy in copies:
                copy.start()
            return copies

        def turned_at(kind, part, turned, source):
            return remote(part, turned.at[source], t_s.at[kind, 0], t_r.at[kind, source], sibling)

        sum_i = scatter_plane(
            nchip, chip, lambda c, h: dwi_ref.at[pl.ds(h * hz, hz), c], oi, fi, si, ri_s, ri_r, ri_l
        )
        sum_q = scatter_plane(
            nchip, chip, lambda c, h: dwq_ref.at[pl.ds(h * hz, hz), pl.ds(c * ri, ri)], oq, fq, sq,
            rq_s, rq_r, rq_l,
        )
        sum_d = scatter_plane(
            nchip, chip, lambda c, h: dwd_ref.at[c, pl.ds(h * hd, hd)], od, fd, sd, rd_s, rd_r, rd_l
        )
        sum_i[0]()

        loads[0].wait()
        loads[1].wait()
        for b in range(nz):
            dwq_ref[b] = lax.dot_general(
                x_ref[:, b * wrows : (b + 1) * wrows], gp_ref[...], TN, preferred_element_type=f32
            ).astype(bf16)
        load_tok = pltpu.make_async_copy(tok_hbm, x_ref, ld.at[5])
        load_tok.start()
        sum_q[0]()
        sum_d[0]()
        sum_i[1]()

        for copy in loads[2:] + [load_tok]:
            copy.wait()
        cs[...] = jnp.zeros_like(cs)
        cs[4:5, : 3 * cq] = jnp.sum(gp_ref[...].astype(f32), axis=0, keepdims=True)

        def norm_back(b):
            at = pl.ds(b * step, step)
            x = x_ref[at, :].astype(f32)
            mean = jnp.mean(x, axis=-1, keepdims=True)
            x = x - mean
            inv = lax.rsqrt(jnp.mean(x * x, axis=-1, keepdims=True) + EPSILON)

            @pl.loop(0, width // chunk)
            def _(c):
                cols = pl.ds(pl.multiple_of(c * chunk, chunk), chunk)
                xhat = (x_ref[at, cols].astype(f32) - mean) * inv
                gn = lax.dot_general(
                    gp_ref[at, :], wq_ref[cols, :], NT, preferred_element_type=f32
                )
                cs[0:1, cols] += jnp.sum(gn * xhat, axis=0, keepdims=True)
                cs[1:2, cols] += jnp.sum(gn, axis=0, keepdims=True)
                e = gn * g1_ref[:, cols]
                gn = lax.dot_general(
                    gh_ref[at, :], wi_ref[cols, :], NT, preferred_element_type=f32
                )
                cs[2:3, cols] += jnp.sum(gn * xhat, axis=0, keepdims=True)
                cs[3:4, cols] += jnp.sum(gn, axis=0, keepdims=True)
                e = (e + gn * g2_ref[:, cols]).astype(bf16)
                for k in range(ncore):
                    eb[b, k, :, cols] = e[k * own : (k + 1) * own]

            copy = remote(eb.at[b, 1 - core], se.at[b], x_s.at[b], x_r.at[b], sibling)
            copy.start()
            return copy

        exchanged = [norm_back(b) for b in range(nz)]
        sum_i[2]()
        turn_i = turn(0, lambda to: oi.at[to // hz, 0, lax.rem(to, hz)], ti)
        sum_q[1]()
        sum_d[1]()

        v0[...] = vec_ref[...]
        lanes = width // 128
        for k in range(4):
            for j in range(lanes):
                v0[k * lanes + j : k * lanes + j + 1, :] = cs[k : k + 1, j * 128 : (j + 1) * 128]
        rank = z * ncore + core
        deep = (3 * cq) // 128 // 3
        for r in range(nz * ncore):

            @pl.when(rank == r)
            def _():
                for g in range(3):
                    for j in range(deep):
                        row = 4 * lanes + (g * nz * ncore + r) * deep + j
                        col = g * cq + j * 128
                        v0[row : row + 1, :] = cs[4:5, col : col + 128]

        v_chips = [
            remote(v0, v1.at[chip], v_s.at[d], v_r.at[chip], {"chip": chip_at(d)})
            for d in range(1, nchip)
        ]
        for copy in v_chips:
            copy.start()
        v1[chip] = v0[...]

        go_at = lambda c, k: go_ref.at[pl.ds(k * (ro * nchip) + c * ro, ro), :]
        gd_at = lambda c, k, h: gd_ref.at[pl.ds(k * (rd * nchip) + c * rd + h * hd, hd), :]
        gi_at = lambda c, k, s: gi_ref.at[
            pl.ds(c * ri, ri), pl.ds((s * ncore + k) * ci, ci)
        ]
        gq_at = lambda c, k, s: gq_ref.at[
            pl.ds(c * ri, ri), pl.ds((s * ncore + k) * 3 * cq, 3 * cq)
        ]
        group = functools.partial(gather_plane, nchip, chip, core)
        rows_o = group(dwo_ref, go_at, go_s, go_r, own_l.at[nz])
        rows_o[0]()

        for b in range(nz):
            exchanged[b].wait_recv()

            @pl.loop(0, own // 16)
            def _(i):
                at = pl.ds(pl.multiple_of(i * 16, 16), 16)
                eb[b, core, at, :] = (
                    eb[b, core, at, :].astype(f32) + se[b, at, :].astype(f32)
                ).astype(bf16)

        sum_q[2]()
        turn_q = turn(1, lambda to: oq.at[to // hz, 0, lax.rem(to, hz)], tq)
        sum_d[2]()
        rows_d = [
            group(od.at[h, 0], functools.partial(gd_at, h=h), gd_s.at[h], gd_r.at[h], own_l.at[nz + 1 + h])
            for h in range(halves)
        ]
        for first, onward, pass_on, last in rows_d:
            first()

        for d in range(1, nchip):
            other = chip_at(d)
            remote(v0, v1.at[other], v_s.at[d], v_r.at[other], sibling).wait_recv()
        total = v1[0]
        for d in range(1, nchip):
            total = total + v1[d]
        v2[core] = total
        v_side = remote(v2.at[core], v2.at[core], v_s.at[nchip], v_r.at[nchip], sibling)
        v_side.start()

        rows_o[1]()
        for first, onward, pass_on, last in rows_d:
            onward()

        groups = []
        for dz in range(1, nz):
            turned_at(0, oi.at[0, 0, 0], ti, z_at(dz)).wait_recv()
        turn_i[-1].wait()
        for source in range(nz):
            groups.append(
                group(
                    ti.at[source], functools.partial(gi_at, s=source), gi_s.at[source],
                    gi_r.at[source], own_l.at[source],
                )
            )
            groups[-1][0]()
        sent_e = [
            remote(
                eb.at[z_at(d), core], ze.at[d], ez_s.at[d], ez_r.at[d], {"seq": z_at(d)}
            )
            for d in range(1, nz)
        ]
        for copy in sent_e:
            copy.start()

        v_side.wait_recv()
        vz = v2[0]
        for c in range(1, ncore):
            vz = vz + v2[c]
        v3[z] = vz
        v_zs = [
            remote(v3.at[z], v3.at[z], v_s.at[nchip + d], v_r.at[nchip + 1 + z], {"seq": z_at(d)})
            for d in range(1, nz)
        ]
        for copy in v_zs:
            copy.start()
        for first, onward, pass_on, last in groups:
            onward()

        for dz in range(1, nz):
            turned_at(1, oq.at[0, 0, 0], tq, z_at(dz)).wait_recv()
        turn_q[-1].wait()
        later = []
        for source in range(nz):
            later.append(
                group(
                    tq.at[source], functools.partial(gq_at, s=source), gq_s.at[source],
                    gq_r.at[source], own_l.at[4 + nz + source],
                )
            )
        for first, onward, pass_on, last in later:
            first()
        rows_o[2]()
        for first, onward, pass_on, last in groups:
            pass_on()
        for first, onward, pass_on, last in later:
            onward()
        for first, onward, pass_on, last in rows_d:
            pass_on()

        for d in range(1, nz):
            other = z_at(d)
            remote(v3.at[0], v3.at[other], v_s.at[0], v_r.at[nchip + 1 + other], sibling).wait_recv()
        total = v3[0]
        for d in range(1, nz):
            total = total + v3[d]
        vsum_ref[...] = total

        for copy in sent_e:
            copy.wait_recv()

        @pl.loop(0, own // 16)
        def _(i):
            at = pl.ds(pl.multiple_of(i * 16, 16), 16)
            acc = eb[z, core, at, :].astype(f32)
            for d in range(1, nz):
                acc = acc + ze[d, at, :].astype(f32)
            e_ref[at, :] = acc

        for first, onward, pass_on, last in later:
            pass_on()

        for first, onward, pass_on, last in [rows_o] + rows_d + groups + later:
            last()
        for begin, middle, finish, last in (sum_i, sum_q, sum_d):
            last()
        for copy in exchanged + sent_e + v_chips + v_zs + [v_side]:
            copy.wait_send()
        for copy in turn_i[:-1] + turn_q[:-1]:
            copy.wait_send()

    dma = pltpu.SemaphoreType.DMA
    anywhere = pl.BlockSpec(memory_space=pl.ANY)
    vmem = pl.BlockSpec(memory_space=pltpu.VMEM)
    out_shape = [
        jax.ShapeDtypeStruct((ncore * nchip * ro, width), bf16),
        jax.ShapeDtypeStruct((ncore * nchip * rd, width), bf16),
        jax.ShapeDtypeStruct((wrows, nz * ncore * ci), bf16),
        jax.ShapeDtypeStruct((wrows, 3 * nz * ncore * cq), bf16),
        jax.ShapeDtypeStruct((own, width), f32),
        jax.ShapeDtypeStruct((vr, 128), f32),
    ]
    slots = max(3 * nchip, 12)
    pair = 2 if nchip == 4 else 1
    nfirst = 2 if nchip == 4 else nchip

    def three(*shape):
        return [
            pltpu.VMEM((halves, pair) + shape, bf16),
            pltpu.VMEM((halves, nfirst) + shape, bf16),
            pltpu.VMEM((halves,) + shape, bf16),
        ]

    return pl.pallas_call(
        kernel,
        in_specs=[anywhere] * 3 + [vmem] + [anywhere] * 6 + [vmem] * 2,
        out_specs=[anywhere] * 4 + [vmem] * 2,
        out_shape=out_shape,
        scratch_shapes=[
            pltpu.VMEM((rows, width), bf16),
            pltpu.VMEM(grad_project.shape, bf16),
            pltpu.VMEM(grad_hidden.shape, bf16),
            pltpu.VMEM(w_qkv.shape, bf16),
            pltpu.VMEM(w_in.shape, bf16),
            pltpu.VMEM((nz, wrows, 3 * cq), bf16),
            pltpu.VMEM((nz, ncore, own, width), bf16),
        ]
        + three(hz, ri, ci)
        + three(hz, ri, 3 * cq)
        + three(hd, width)
        + [
            pltpu.VMEM((nz, ri, ci), bf16),
            pltpu.VMEM((nz, ri, 3 * cq), bf16),
            pltpu.VMEM((nz, own, width), bf16),
            pltpu.VMEM((nz, own, width), bf16),
            pltpu.VMEM((8, width), f32),
            pltpu.VMEM((vr, 128), f32),
            pltpu.VMEM((nchip, vr, 128), f32),
            pltpu.VMEM((ncore, vr, 128), f32),
            pltpu.VMEM((nz, vr, 128), f32),
            dma((6,)),
            dma((halves, nchip)), dma((halves, nchip)), dma((halves, 2)),
            dma((halves, nchip)), dma((halves, nchip)), dma((halves, 2)),
            dma((halves, nchip)), dma((halves, nchip)), dma((halves, 2)),
            dma((nz,)), dma((nz,)),
            dma((nz,)), dma((nz,)),
            dma((2, nz)), dma((2, nz)), dma((2,)),
            dma((slots,)), dma((slots,)),
            dma((halves, slots)), dma((halves, slots)),
            dma((nz, slots)), dma((nz, slots)),
            dma((nz, slots)), dma((nz, slots)),
            dma((4 + 2 * nz,)),
            dma((nchip + nz,)), dma((nchip + nz + 1,)),
        ],
        compiler_params=pltpu.CompilerParams(
            collective_id=2, has_side_effects=True, vmem_limit_bytes=62 * 2**20
        ),
        cost_estimate=cost(4 * rows * width * (3 * cq + ci), 20 * rows * width),
        name="tail",
    )(dwo, dwd, dwi, vectors, normed1, grad_project, grad_hidden, tok, w_qkv, w_in, gain1, gain2)


def on_device(
    nz,
    nchip,
    ncore,
    tokens,
    block_ids,
    cotangent,
    norm1_gain,
    norm1_bias,
    norm2_gain,
    norm2_bias,
    w_qkv,
    b_qkv,
    w_dense,
    b_dense,
    w_in,
    b_in,
    w_out,
    b_out,
):
    own, width = tokens.shape
    z = lax.axis_index("seq")
    chip = lax.axis_index("chip")
    core = lax.axis_index("core")
    ranks = nz * ncore
    rank = z * ncore + core
    rows = ranks * own
    ffr = w_out.shape[0] // ncore
    hc = width // ranks
    split = max(1, HD // hc)
    wrows = width // nz
    blocks = block_ids.shape[1]
    length = blocks * BLOCK
    core_at = core.reshape(1)

    parts = [norm1_gain, norm1_bias, norm2_gain, norm2_bias, b_qkv, b_dense + 0, b_in, b_out,
             block_ids.reshape(-1)]
    sizes = [p.shape[0] for p in parts]
    total = -(-sum(sizes) // 2048) * 2048
    starts = [sum(sizes[:i]) for i in range(len(sizes))]
    small = sum(
        jnp.pad(p.astype(f32), (at, total - at - p.shape[0])) for p, at in zip(parts, starts)
    )
    small = small.astype(bf16).reshape(-1, 128)
    tok, w_in_c, w_qkv_c, small = front(nz, nchip, ncore, tokens, w_in, w_qkv, small)
    tok = tok.reshape(rows, width)
    small = small.reshape(nz, total)

    def vector(i):
        return small[:, starts[i] : starts[i] + sizes[i]].astype(f32).reshape(1, -1)

    gain1, bias1, gain2, bias2 = [vector(i) for i in range(4)]
    bias_c = lax.dynamic_index_in_dim(vector(4).reshape(3, ranks, hc), rank, 1, keepdims=False)
    bias_c = bias_c.reshape(1, 3 * hc)
    bias_in = lax.dynamic_slice_in_dim(vector(6), rank * ffr, ffr, 1)
    ids = vector(8).astype(jnp.int32).reshape(nz, blocks)
    tok, cot_own = lax.optimization_barrier((tok, cotangent))
    cot = lax.all_gather(cot_own, TP, axis=0, tiled=True)

    per_chip = blocks // nchip
    ids_rows = lax.dynamic_slice_in_dim(ids, chip * per_chip, per_chip, 1).reshape(-1)
    ids_seq = lax.dynamic_index_in_dim(ids, chip, 0, keepdims=False)
    slots = jnp.arange(blocks, dtype=jnp.int32)
    order = jnp.sum(jnp.where(ids_seq[None, :] == slots[:, None], slots[None, :], 0), axis=1)
    place = (lax.rem(rank, split) == 0).astype(jnp.int32).reshape(1)
    table = jnp.asarray(turn_table(length))

    def heads_of(x):
        g = x.shape[1] // hc
        if split > 1:
            x = lax.all_gather(x.reshape(rows, g, hc), "core", axis=2, tiled=True)
        x = x.reshape(nz, rows // nz, g * HD)
        return lax.all_to_all(x, "chip", 0, 0, tiled=True).reshape(length, g * HD)

    def heads_back(x):
        g = x.shape[1] // HD
        x = x.reshape(nchip, length // nchip, g * HD)
        x = lax.all_to_all(x, "chip", 0, 0, tiled=True).reshape(rows, g * HD)
        if split > 1:
            x = lax.dynamic_slice_in_dim(x.reshape(rows, g, HD), core * hc, hc, 2)
        return x.reshape(rows, g * hc)

    tile = 256
    normed1, qkv = projections(nz, ids_rows, place, tok, w_qkv_c, bias_c, gain1, bias1, table)
    qkv = heads_of(qkv)
    normed2, active, slope = feed_forward(nz, tok, w_in_c, bias_in, gain2, bias2)
    qkv, active, slope, normed2 = lax.optimization_barrier((qkv, active, slope, normed2))
    attended, lse = attention_forward(ids_seq, order, qkv, tile)
    attended, cot = lax.optimization_barrier((attended, cot))

    if split == 1:
        mixed, g, dw_out = exchange_heads(nz, nchip, ncore, attended, cot, w_dense, active)
    else:
        mixed = heads_back(attended)
        g = heads_of(grad_of_mixed(nz, core_at, cot, w_dense, hc))
        dw_out = lax.dot_general(active, cot, TN, preferred_element_type=f32).astype(bf16)
    mixed, g, dw_out, cot = lax.optimization_barrier((mixed, g, dw_out, cot))
    s_out = lax.psum_scatter(dw_out, "chip", scatter_dimension=0, tiled=True)
    part_out = layer_out(nz, core_at, mixed, w_dense, active, w_out)
    g, part_out = lax.optimization_barrier((g, part_out))
    dqkv = attention_backward(ids_seq, order, qkv, g, lse, table, tile)
    dqkv, cot, mixed, part_out = lax.optimization_barrier((dqkv, cot, mixed, part_out))
    grad_project = heads_back(dqkv)
    grad_hidden, sum_bin = grad_of_hidden(nz, core_at, cot, w_out, slope)
    dw_in = lax.dot_general(normed2, grad_hidden, TN, preferred_element_type=f32).astype(bf16)
    dw_dense = lax.dot_general(mixed, cot, TN, preferred_element_type=f32).astype(bf16)
    grad_project, dw_in, dw_dense, s_out, part_out = lax.optimization_barrier(
        (grad_project, dw_in, dw_dense, s_out, part_out)
    )
    summed_out = lax.psum_scatter(part_out, TP, scatter_dimension=0, tiled=True).astype(f32)

    here = jnp.arange(ranks, dtype=jnp.int32) == rank
    mine_bin = jnp.where(here[:, None], sum_bin.reshape(1, ffr), 0.0)
    vectors = [
        jnp.zeros(7 * width, f32),
        jnp.sum(cotangent.astype(f32), axis=0),
        mine_bin.reshape(-1),
    ]
    vectors = jnp.concatenate([v.reshape(-1, 128) for v in vectors])
    g_wout, g_wdense, g_win, g_wqkv, e, sums = tail(
        nz, nchip, ncore, s_out, dw_dense, dw_in, vectors, normed1, grad_project, grad_hidden, tok,
        w_qkv_c, w_in_c, gain1, gain2
    )
    sums = sums.reshape(-1)
    at = 0
    small_out = []
    for size in (width, width, width, width, 3 * width, width, ranks * ffr):
        small_out.append(lax.dynamic_slice_in_dim(sums, at + z * (size // nz), size // nz))
        at += size
    g_gain1, g_bias1, g_gain2, g_bias2, g_bqkv, g_bdense, g_bin = small_out

    output = (tokens.astype(f32) + summed_out + vector(5) + vector(7)).astype(bf16)
    xhat_own, inv_own = stats(tokens.astype(f32))
    terms = (
        e
        - jnp.mean(e, axis=-1, keepdims=True)
        - xhat_own * jnp.mean(e * xhat_own, axis=-1, keepdims=True)
    ) * inv_own
    grad_tokens = (cotangent.astype(f32) + terms).astype(bf16)
    g_wout, g_wdense, g_win, g_wqkv = widen([g_wout, g_wdense, g_win, g_wqkv], ranks)
    return (
        output,
        grad_tokens,
        g_gain1,
        g_bias1,
        g_gain2,
        g_bias2,
        g_wqkv,
        g_bqkv,
        g_wdense,
        g_bdense,
        g_win,
        g_bin,
        g_wout,
        g_bdense,
    )


def solution(mesh):
    nz, nctx = mesh.shape["seq"], mesh.shape["ctx"]
    ncore = 2
    nchip = nctx // ncore
    fine = Mesh(mesh.devices.reshape(nz, nchip, ncore), ("seq", "chip", "core"))
    own = P(("seq", "chip", "core"), None)
    vec = P("seq")
    mat = P("seq", None)
    return jax.shard_map(
        functools.partial(on_device, nz, nchip, ncore),
        mesh=fine,
        in_specs=(own, mat, own, vec, vec, vec, vec, mat, vec, mat, vec, mat, vec, mat, vec),
        out_specs=(own, own, vec, vec, vec, vec, mat, vec, mat, vec, mat, vec, mat, vec),
        check_vma=False,
    )
```

```python
import functools
import math

import jax
import jax.numpy as jnp
import numpy as np
from jax import lax
from jax.experimental import pallas as pl
from jax.experimental.pallas import tpu as pltpu
from jax.sharding import Mesh, PartitionSpec as P

HD = 256
ROT = 64
BLOCK = 96
EPSILON = 1e-05
ROT_BASE = 10000.0
SCALE = HD ** (-0.5)
f32 = jnp.float32
bf16 = jnp.bfloat16
TP = ("seq", "core")
MESH = pl.DeviceIdType.MESH
NT = (((1,), (1,)), ((), ()))
TN = (((0,), (0,)), ((), ()))
BIG = pltpu.CompilerParams(vmem_limit_bytes=62 * 2**20)


def remote(src, dst, send, recv, target):
    return pltpu.make_async_remote_copy(
        src_ref=src, dst_ref=dst, send_sem=send, recv_sem=recv, device_id=target,
        device_id_type=MESH,
    )


def greet(targets):
    barrier = pltpu.get_barrier_semaphore()
    for target in targets:
        pl.semaphore_signal(barrier, inc=1, device_id=target, device_id_type=MESH)
    pl.semaphore_wait(barrier, len(targets))


def front(nz, nchip, ncore, tokens, w_in, w_qkv, small):
    own, width = tokens.shape
    wrows, ff = w_in.shape
    heads3 = w_qkv.shape[1]
    nctx = nchip * ncore
    piece = wrows // nctx
    half = piece // 2
    zi, zq = ff // nz, heads3 // 3 // nz
    ci, cq = zi // ncore, zq // ncore

    def kernel(
        tok_ref, wi_ref, wq_ref, sm_ref, tok_out, wi_out, wq_out, sm_out, buf_i, buf_q,
        up_s, up_r, dn_s, dn_r, sib_s, sib_r, zi_s, zi_r, zq_s, zq_r, p_s, p_r, r_s, loc, loc_p, sm_s, sm_r,
    ):
        z = lax.axis_index("seq")
        chip = lax.axis_index("chip")
        core = lax.axis_index("core")
        share = chip * ncore + core
        sibling = {"core": 1 - core}

        def z_at(d):
            return lax.rem(z + d, nz)

        def plane_at(d):
            other = lax.rem(share + d, nctx)
            return other // ncore, lax.rem(other, ncore)

        greet(
            [{"seq": z_at(d)} for d in range(1, nz)]
            + [{"chip": plane_at(d)[0], "core": plane_at(d)[1]} for d in range(1, nctx)]
        )

        def around(body, distances=range(1, nz)):
            for distance in distances:
                for other in (z + distance, z - distance):

                    @pl.when(jnp.logical_and(other >= 0, other < nz))
                    def _():
                        body(jnp.clip(other, 0, nz - 1))

        rows = pl.ds(share * piece, piece)

        def hop(to):
            pairs = [(wi_ref.at[rows, pl.ds(to * zi, zi)], buf_i.at[z], zi_s.at[to], zi_r.at[z])]
            for k in range(ncore):
                for g in range(3):
                    pairs.append(
                        (
                            wq_ref.at[rows, pl.ds(g * zq * nz + to * zq + k * cq, cq)],
                            buf_q.at[z, k, :, pl.ds(g * cq, cq)],
                            zq_s.at[to, k, g], zq_r.at[z, k, g],
                        )
                    )
            return pairs

        def hop_to(to):
            return [remote(a, b, c, d, {"seq": to}) for a, b, c, d in hop(to)]

        def send_hop(to):
            for copy in hop_to(to):
                copy.start()

        def hop_left(to):
            for copy in hop_to(to):
                copy.wait_send()

        def hop_arrival(source):
            here = buf_i.at[source]
            remote(here, here, zi_s.at[0], zi_r.at[source], sibling).wait_recv()
            for k in range(ncore):
                for g in range(3):
                    here = buf_q.at[source, k, :, pl.ds(g * cq, cq)]
                    remote(here, here, zq_s.at[0, 0, 0], zq_r.at[source, k, g], sibling).wait_recv()

        def up(s):
            at = jnp.maximum(z - s, 0)
            src = tok_ref if s == 0 else tok_out.at[at, core]
            return remote(
                src, tok_out.at[at, core], up_s.at[s], up_r.at[s],
                {"seq": jnp.minimum(z + 1, nz - 1)},
            )

        def down(s):
            at = jnp.minimum(z + s, nz - 1)
            src = tok_ref if s == 0 else tok_out.at[at, core]
            return remote(
                src, tok_out.at[at, core], dn_s.at[s], dn_r.at[s],
                {"seq": jnp.maximum(z - 1, 0)},
            )

        def side(shard, own_rows=False):
            src = tok_ref if own_rows else tok_out.at[shard, core]
            return remote(src, tok_out.at[shard, core], sib_s.at[shard], sib_r.at[shard], sibling)

        def token_step(s):
            @pl.when(z - 1 - s >= 0)
            def _():
                shard = jnp.maximum(z - 1 - s, 0)
                here = tok_out.at[shard, core]
                remote(here, here, up_s.at[s], up_r.at[s], sibling).wait_recv()
                if s + 1 < nz - 1:

                    @pl.when(z + 1 < nz)
                    def _():
                        up(s + 1).start()

                side(shard).start()

            @pl.when(z + 1 + s < nz)
            def _():
                shard = jnp.minimum(z + 1 + s, nz - 1)
                here = tok_out.at[shard, core]
                remote(here, here, dn_s.at[s], dn_r.at[s], sibling).wait_recv()
                if s + 1 < nz - 1:

                    @pl.when(z > 0)
                    def _():
                        down(s + 1).start()

                side(shard).start()

        def pieces(source, k):
            return buf_i.at[source, :, pl.ds(k * ci, ci)], buf_q.at[source, k]

        def places(source, owner):
            at = pl.ds(source * wrows + owner * piece, piece)
            return wi_out.at[at, :], wq_out.at[at, :]

        def cut(ref, h):
            return ref if h is None else ref.at[pl.ds(h * half, half), :]

        def in_place(source):
            return [
                pltpu.make_async_copy(a, b, loc_p.at[source, i])
                for i, (a, b) in enumerate(zip(pieces(source, core), places(source, share)))
            ]

        if nchip == 4:
            beside = chip + 1 - 2 * lax.rem(chip, 2)
            below = lax.rem(chip + 2, 4)
            across = 3 - chip
            order = ((beside, 0), (below, 1), (beside, 1), (below, 0))

            def spread(source):
                copies = []
                for way, (to, h) in enumerate(order):
                    for k in range(ncore):
                        for i, (a, b) in enumerate(zip(pieces(source, k), places(source, share))):
                            copies.append(
                                remote(
                                    cut(a, h), cut(b, h), p_s.at[source, i, k, way],
                                    p_r.at[source, i, share, h], {"chip": to, "core": k},
                                )
                            )
                return copies

            def relays(source):
                copies = []
                for h, (came, to) in enumerate(((beside, below), (below, beside))):
                    for k in range(ncore):
                        owner = came * ncore + k
                        for i, ref in enumerate(places(source, owner)):
                            part = cut(ref, h)
                            copies.append(
                                remote(
                                    part, part, r_s.at[source, i, k, h],
                                    p_r.at[source, i, owner, h], {"chip": to},
                                )
                            )
                return copies

            def relay(source):
                for copy in relays(source):
                    copy.wait_recv()
                    copy.start()

            rest = [(beside, 1), (below, 0), (across, 0), (across, 1)]
        else:

            def spread(source):
                copies = []
                for d in range(1, nctx):
                    to, k = plane_at(d)
                    for i, (a, b) in enumerate(zip(pieces(source, k), places(source, share))):
                        copies.append(
                            remote(
                                a, b, p_s.at[source, i, 0, d], p_r.at[source, i, share, 0],
                                {"chip": to, "core": k},
                            )
                        )
                return copies

            def relay(source):
                pass

        def to_sibling(source):
            return [
                remote(a, b, p_s.at[source, i, 0, 4], p_r.at[source, i, share, 0], sibling)
                for i, (a, b) in enumerate(zip(pieces(source, 1 - core), places(source, share)))
            ]

        def hand_on(source):
            for copy in spread(source) + in_place(source):
                copy.start()
            if nchip == 4:
                for copy in to_sibling(source):
                    copy.start()

        def arrive(source):
            hop_arrival(source)
            hand_on(source)

        smalls = [
            remote(sm_ref, sm_out.at[z], sm_s.at[d], sm_r.at[z], {"seq": z_at(d)})
            for d in range(1, nz)
        ]
        for copy in smalls:
            copy.start()
        around(send_hop)

        @pl.when(z + 1 < nz)
        def _():
            up(0).start()

        @pl.when(z > 0)
        def _():
            down(0).start()

        side(z, True).start()
        mine = [
            pltpu.make_async_copy(tok_ref, tok_out.at[z, core], loc.at[0]),
            pltpu.make_async_copy(sm_ref, sm_out.at[z], loc.at[1]),
        ]
        held = [
            pltpu.make_async_copy(a, b, loc.at[2 + i]) for i, (a, b, c, d) in enumerate(hop(z))
        ]
        for copy in held + mine:
            copy.start()
        for copy in held:
            copy.wait()
        hand_on(z)
        for distance in range(1, nz):
            around(arrive, [distance])
            if distance == 1:
                relay(z)
            else:
                around(relay, [distance - 1])
            token_step(distance - 1)
        around(relay, [nz - 1])

        for copy in mine:
            copy.wait()
        for shard in range(nz):
            there = tok_out.at[shard, 1 - core]
            remote(there, there, sib_s.at[shard], sib_r.at[shard], sibling).wait_recv()
            side(shard).wait_send()
        for s in range(nz - 1):

            @pl.when(jnp.logical_and(z + 1 < nz, z - s >= 0))
            def _():
                up(s).wait_send()

            @pl.when(jnp.logical_and(z > 0, z + s < nz))
            def _():
                down(s).wait_send()

        around(hop_left)
        for copy in smalls:
            copy.wait_send()
        for d in range(1, nz):
            there = sm_out.at[z_at(d)]
            remote(there, there, sm_s.at[d], sm_r.at[z_at(d)], sibling).wait_recv()
        for source in range(nz):
            for copy in in_place(source):
                copy.wait()
            for copy in spread(source):
                copy.wait_send()
            if nchip == 4:
                for copy in to_sibling(source) + relays(source):
                    copy.wait_send()
                waits = [(chip * ncore + 1 - core, None, 0)] + [
                    (c * ncore + k, h, h) for c, h in rest for k in range(ncore)
                ]
            else:
                waits = [(lax.rem(share + d, nctx), None, 0) for d in range(1, nctx)]
            for owner, h, slot in waits:
                for i, ref in enumerate(places(source, owner)):
                    part = cut(ref, h)
                    remote(
                        part, part, p_s.at[source, i, 0, 0], p_r.at[source, i, owner, slot], sibling
                    ).wait_recv()

    dma = pltpu.SemaphoreType.DMA
    anywhere = pl.BlockSpec(memory_space=pl.ANY)
    return pl.pallas_call(
        kernel,
        in_specs=[anywhere] * 4,
        out_specs=[anywhere] * 4,
        out_shape=[
            jax.ShapeDtypeStruct((nz, ncore, own, width), bf16),
            jax.ShapeDtypeStruct((nz * wrows, ci), bf16),
            jax.ShapeDtypeStruct((nz * wrows, 3 * cq), bf16),
            jax.ShapeDtypeStruct((nz,) + small.shape, bf16),
        ],
        scratch_shapes=[
            pltpu.VMEM((nz, piece, zi), bf16),
            pltpu.VMEM((nz, ncore, piece, 3 * cq), bf16),
            dma((nz,)), dma((nz,)), dma((nz,)), dma((nz,)),
            dma((nz,)), dma((nz,)),
            dma((nz,)), dma((nz,)), dma((nz, ncore, 3)), dma((nz, ncore, 3)),
            dma((nz, 2, ncore, max(5, nctx))), dma((nz, 2, nctx, 2)), dma((nz, 2, ncore, 2)),
            dma((3 + 3 * ncore,)), dma((nz, 2)), dma((nz,)), dma((nz,)),
        ],
        compiler_params=pltpu.CompilerParams(
            collective_id=1, has_side_effects=True, vmem_limit_bytes=62 * 2**20
        ),
        name="front",
    )(tokens, w_in, w_qkv, small)


def turn_table(length):
    half = ROT // 2
    power = -(np.arange(half, dtype=np.float32) * np.float32(2.0)) / np.float32(ROT)
    angles = np.arange(length, dtype=np.float32)[:, None] * np.power(np.float32(ROT_BASE), power)
    table = np.zeros((3, length, 128), np.float32)
    table[0] = 1.0
    table[0, :, :half] = table[0, :, half:ROT] = np.cos(angles)
    table[1, :, :half] = -np.sin(angles)
    table[2, :, half:ROT] = np.sin(angles)
    return table


def turned(u, cosine, minus, plus):
    half = ROT // 2
    return u * cosine + pltpu.roll(u, 128 - half, 1) * minus + pltpu.roll(u, half, 1) * plus


def stats(x):
    center = x - jnp.mean(x, axis=-1, keepdims=True)
    inv = lax.rsqrt(jnp.mean(center * center, axis=-1, keepdims=True) + EPSILON)
    return center * inv, inv


def cost(flops, nbytes, trans=0):
    return pl.CostEstimate(flops=int(flops), bytes_accessed=int(nbytes), transcendentals=int(trans))


def projections(nz, ids, place, tok, w, bias, gain, offset, table):
    rows, width = tok.shape
    step = rows // nz
    blocks = step // BLOCK
    cols = w.shape[1]
    hc = cols // 3

    def kernel(ids_ref, place_ref, tok_ref, w_ref, b_ref, g_ref, o_ref, t_ref, n_ref, out_ref):
        xhat, inv = stats(tok_ref[...].astype(f32))
        normed = (xhat * g_ref[...] + o_ref[...]).astype(bf16)
        n_ref[...] = normed
        project = jnp.dot(normed, w_ref[...], preferred_element_type=f32) + b_ref[...]
        out_ref[...] = project.astype(bf16)
        first = place_ref[0] == 1

        @pl.when(first)
        def _():
            for b in range(blocks):
                at = pl.ds(pl.multiple_of(ids_ref[pl.program_id(0) * blocks + b] * BLOCK, BLOCK), BLOCK)
                c, m, p = t_ref[0, at, :], t_ref[1, at, :], t_ref[2, at, :]
                for g in range(2):
                    u = project[b * BLOCK : (b + 1) * BLOCK, g * hc : g * hc + 128]
                    out_ref[b * BLOCK : (b + 1) * BLOCK, g * hc : g * hc + 128] = turned(
                        u, c, m, p
                    ).astype(bf16)

    whole = lambda shape: pl.BlockSpec(shape, lambda i, *_: (0,) * len(shape))
    return pl.pallas_call(
        kernel,
        grid_spec=pltpu.PrefetchScalarGridSpec(
            num_scalar_prefetch=2,
            grid=(nz,),
            in_specs=[
                pl.BlockSpec((step, width), lambda i, *_: (i, 0)),
                whole((width, cols)),
                whole((1, cols)),
                whole((1, width)),
                whole((1, width)),
                whole(table.shape),
            ],
            out_specs=[
                pl.BlockSpec((step, width), lambda i, *_: (i, 0)),
                pl.BlockSpec((step, cols), lambda i, *_: (i, 0)),
            ],
        ),
        out_shape=[
            jax.ShapeDtypeStruct((rows, width), bf16),
            jax.ShapeDtypeStruct((rows, cols), bf16),
        ],
        compiler_params=BIG,
        cost_estimate=cost(2 * rows * width * cols, 4 * rows * width + 2 * width * cols),
        name="projections",
    )(ids, place, tok, w, bias, gain, offset, table)


def feed_forward(nz, tok, w, bias, gain, offset):
    rows, width = tok.shape
    step = rows // nz
    cols = w.shape[1]

    def kernel(tok_ref, w_ref, b_ref, g_ref, o_ref, n_ref, a_ref, d_ref):
        xhat, inv = stats(tok_ref[...].astype(f32))
        normed = (xhat * g_ref[...] + o_ref[...]).astype(bf16)
        n_ref[...] = normed
        v = jnp.dot(normed, w_ref[...], preferred_element_type=f32) + b_ref[...]
        gate = 0.5 * (1.0 + lax.erf(v * (0.5**0.5)))
        a_ref[...] = (v * gate).astype(bf16)
        bell = jnp.exp(v * v * -0.5) * ((2.0 * math.pi) ** -0.5)
        d_ref[...] = (gate + v * bell).astype(bf16)

    whole = lambda shape: pl.BlockSpec(shape, lambda i: (0, 0))
    part = lambda n: pl.BlockSpec((step, n), lambda i: (i, 0))
    return pl.pallas_call(
        kernel,
        grid=(nz,),
        in_specs=[part(width), whole((width, cols)), whole((1, cols)), whole((1, width)), whole((1, width))],
        out_specs=[part(width), part(cols), part(cols)],
        out_shape=[
            jax.ShapeDtypeStruct((rows, width), bf16),
            jax.ShapeDtypeStruct((rows, cols), bf16),
            jax.ShapeDtypeStruct((rows, cols), bf16),
        ],
        compiler_params=BIG,
        cost_estimate=cost(2 * rows * width * cols, 4 * rows * width + 2 * width * cols, 2 * rows * cols),
        name="feed_forward",
    )(tok, w, bias, gain, offset)


def layer_out(nz, core, mixed, w_dense, active, w_out):
    rows, hc = mixed.shape
    width = w_out.shape[1]
    step = rows // nz
    units = active.shape[1]

    def kernel(core_ref, m_ref, wd_ref, a_ref, wo_ref, out_ref):
        out_ref[...] = (
            jnp.dot(m_ref[...], wd_ref[...], preferred_element_type=f32)
            + jnp.dot(a_ref[...], wo_ref[...], preferred_element_type=f32)
        ).astype(bf16)

    part = lambda n: pl.BlockSpec((step, n), lambda i, c: (i, 0))
    held = lambda n: pl.BlockSpec((n, width), lambda i, c: (c[0], 0))
    return pl.pallas_call(
        kernel,
        grid_spec=pltpu.PrefetchScalarGridSpec(
            num_scalar_prefetch=1,
            grid=(nz,),
            in_specs=[part(hc), held(hc), part(units), held(units)],
            out_specs=part(width),
        ),
        out_shape=jax.ShapeDtypeStruct((rows, width), bf16),
        compiler_params=BIG,
        cost_estimate=cost(2 * rows * width * (hc + units), 4 * rows * width + 2 * width * units),
        name="layer_out",
    )(core, mixed, w_dense, active, w_out)


def widen(arrays, ranks):
    steps = [min(x.shape[0], 128 if x.shape[1] > 4096 else 512) for x in arrays]
    counts = [x.shape[0] // step for x, step in zip(arrays, steps)]
    starts = [sum(counts[:i]) for i in range(len(counts))]

    def kernel(*refs):
        n = len(arrays)
        for i in range(n):
            here = pl.program_id(0) - starts[i]

            @pl.when(jnp.logical_and(here >= 0, here < counts[i]))
            def _():
                if i < n - 1:
                    refs[n + i][...] = refs[i][...].astype(f32)
                else:
                    cols = arrays[i].shape[1] // 3 // ranks
                    for r in range(ranks):
                        for g in range(3):
                            to, at = (g * ranks + r) * cols, (3 * r + g) * cols
                            refs[n + i][:, to : to + cols] = refs[i][:, at : at + cols].astype(f32)

    def part(i):
        return pl.BlockSpec(
            (steps[i], arrays[i].shape[1]),
            lambda s: (jnp.clip(s - starts[i], 0, counts[i] - 1), 0),
        )

    specs = [part(i) for i in range(len(arrays))]
    size = sum(x.size for x in arrays)
    return pl.pallas_call(
        kernel,
        grid=(sum(counts),),
        in_specs=specs,
        out_specs=specs,
        out_shape=[jax.ShapeDtypeStruct(x.shape, f32) for x in arrays],
        compiler_params=BIG,
        cost_estimate=cost(size, 6 * size),
        name="widen",
    )(*arrays)


def grad_of_mixed(nz, core, cot, w_dense, hc):
    rows, width = cot.shape
    step = rows // nz

    def kernel(core_ref, c_ref, w_ref, out_ref):
        out_ref[...] = lax.dot_general(
            c_ref[...], w_ref[...], NT, preferred_element_type=f32
        ).astype(bf16)

    return pl.pallas_call(
        kernel,
        grid_spec=pltpu.PrefetchScalarGridSpec(
            num_scalar_prefetch=1,
            grid=(nz,),
            in_specs=[
                pl.BlockSpec((step, width), lambda i, c: (i, 0)),
                pl.BlockSpec((hc, width), lambda i, c: (c[0], 0)),
            ],
            out_specs=pl.BlockSpec((step, hc), lambda i, c: (i, 0)),
        ),
        out_shape=jax.ShapeDtypeStruct((rows, hc), bf16),
        compiler_params=BIG,
        cost_estimate=cost(2 * rows * width * hc, 2 * rows * width),
        name="grad_of_mixed",
    )(core, cot, w_dense)


def grad_of_hidden(nz, core, cot, w_out, slope):
    rows, width = cot.shape
    step = rows // nz
    units = slope.shape[1]

    def kernel(core_ref, c_ref, w_ref, d_ref, out_ref, sum_ref):
        g = lax.dot_general(c_ref[...], w_ref[...], NT, preferred_element_type=f32)
        g = (g * d_ref[...].astype(f32)).astype(bf16)
        out_ref[...] = g

        @pl.when(pl.program_id(0) == 0)
        def _():
            sum_ref[...] = jnp.zeros_like(sum_ref)

        sum_ref[...] += jnp.sum(g.astype(f32), axis=0, keepdims=True)

    return pl.pallas_call(
        kernel,
        grid_spec=pltpu.PrefetchScalarGridSpec(
            num_scalar_prefetch=1,
            grid=(nz,),
            in_specs=[
                pl.BlockSpec((step, width), lambda i, c: (i, 0)),
                pl.BlockSpec((units, width), lambda i, c: (c[0], 0)),
                pl.BlockSpec((step, units), lambda i, c: (i, 0)),
            ],
            out_specs=[
                pl.BlockSpec((step, units), lambda i, c: (i, 0)),
                pl.BlockSpec((1, units), lambda i, c: (0, 0)),
            ],
        ),
        out_shape=[
            jax.ShapeDtypeStruct((rows, units), bf16),
            jax.ShapeDtypeStruct((1, units), f32),
        ],
        compiler_params=BIG,
        cost_estimate=cost(2 * rows * width * units, 2 * rows * width + 2 * width * units),
        name="grad_of_hidden",
    )(core, cot, w_out, slope)


def norm_back(nz, grad, w, tok, gain, other, sums):
    rows, width = tok.shape
    step = rows // nz
    cols = grad.shape[1]

    def kernel(*refs):
        g_ref, w_ref, t_ref, gain_ref = refs[:4]
        at = 4
        if other is not None:
            other_ref = refs[at]
            at += 1
        e_ref, s_ref = refs[at : at + 2]
        gn = lax.dot_general(g_ref[...], w_ref[...], NT, preferred_element_type=f32)
        xhat, inv = stats(t_ref[...].astype(f32))
        e = gn * gain_ref[...]
        if other is not None:
            e = e + other_ref[...].astype(f32)
        e_ref[...] = e.astype(bf16)

        @pl.when(pl.program_id(0) == 0)
        def _():
            s_ref[...] = jnp.zeros_like(s_ref)
            if sums:
                refs[at + 2][...] = jnp.zeros_like(refs[at + 2])

        s_ref[0:1, :] += jnp.sum(gn * xhat, axis=0, keepdims=True)
        s_ref[1:2, :] += jnp.sum(gn, axis=0, keepdims=True)
        if sums:
            refs[at + 2][...] += jnp.sum(g_ref[...].astype(f32), axis=0, keepdims=True)

    part = lambda n: pl.BlockSpec((step, n), lambda i: (i, 0))
    whole = lambda shape: pl.BlockSpec(shape, lambda i: (0, 0))
    ins = [grad, w, tok, gain] + ([] if other is None else [other])
    return pl.pallas_call(
        kernel,
        grid=(nz,),
        in_specs=[part(cols), whole((width, cols)), part(width), whole((1, width))]
        + ([] if other is None else [part(width)]),
        out_specs=[part(width), whole((2, width))] + ([whole((1, cols))] if sums else []),
        out_shape=[
            jax.ShapeDtypeStruct((rows, width), bf16),
            jax.ShapeDtypeStruct((2, width), f32),
        ]
        + ([jax.ShapeDtypeStruct((1, cols), f32)] if sums else []),
        compiler_params=BIG,
        cost_estimate=cost(2 * rows * width * cols, 6 * rows * width + 2 * width * cols),
        name="norm_back",
    )(*ins)


def attention_forward(ids, order, qkv, tile):
    rows = qkv.shape[0]
    blocks = rows // BLOCK

    def kernel(ids_ref, order_ref, x_ref, o_ref, lse_ref, q_ref, k_ref, v_ref, s_ref):
        for b in range(blocks):
            at = pl.ds(pl.multiple_of(order_ref[b] * BLOCK, BLOCK), BLOCK)
            here = slice(b * BLOCK, (b + 1) * BLOCK)
            for i, ref in enumerate((q_ref, k_ref, v_ref)):
                ref[here, :] = x_ref[at, i * HD : (i + 1) * HD]
        for t in range(rows // tile):
            mine = slice(t * tile, (t + 1) * tile)
            n = (t + 1) * tile
            s = lax.dot_general(q_ref[mine, :], k_ref[:n, :], NT, preferred_element_type=f32)
            s = s * SCALE
            seen = t * tile + lax.broadcasted_iota(jnp.int32, (tile, n), 0) >= (
                lax.broadcasted_iota(jnp.int32, (tile, n), 1)
            )
            s = jnp.where(seen, s, -1e30)
            top = jnp.max(s, axis=-1, keepdims=True)
            e = jnp.exp(s - top)
            total = jnp.sum(e, axis=-1, keepdims=True)
            p = (e * (1.0 / total)).astype(bf16)
            s_ref[mine, :] = jnp.dot(p, v_ref[:n, :], preferred_element_type=f32).astype(bf16)
            lse_ref[mine, :] = top + jnp.log(total)
        for b in range(blocks):
            at = pl.ds(pl.multiple_of(ids_ref[b] * BLOCK, BLOCK), BLOCK)
            o_ref[b * BLOCK : (b + 1) * BLOCK, :] = s_ref[at, :]

    smem = pl.BlockSpec(memory_space=pltpu.SMEM)
    vmem = pl.BlockSpec(memory_space=pltpu.VMEM)
    return pl.pallas_call(
        kernel,
        in_specs=[smem, smem, vmem],
        out_specs=[vmem, vmem],
        out_shape=[
            jax.ShapeDtypeStruct((rows, HD), bf16),
            jax.ShapeDtypeStruct((rows, 1), f32),
        ],
        scratch_shapes=[pltpu.VMEM((rows, HD), bf16)] * 4,
        compiler_params=BIG,
        cost_estimate=cost(2.3 * rows * rows * HD, 8 * rows * HD, rows * rows / 2),
        name="attention_forward",
    )(ids, order, qkv)


def attention_backward(ids, order, qkv, grad, lse, table, tile):
    rows = qkv.shape[0]
    blocks = rows // BLOCK

    def kernel(ids_ref, order_ref, x_ref, g_ref, lse_ref, t_ref, out_ref, q_ref, k_ref, v_ref, m_ref,
               r_ref, dk_ref, dv_ref):
        for b in range(blocks):
            at = pl.ds(pl.multiple_of(order_ref[b] * BLOCK, BLOCK), BLOCK)
            here = slice(b * BLOCK, (b + 1) * BLOCK)
            for i, ref in enumerate((q_ref, k_ref, v_ref)):
                ref[here, :] = x_ref[at, i * HD : (i + 1) * HD]
            m_ref[here, :] = g_ref[at, :]
        for t in reversed(range(rows // tile)):
            mine = slice(t * tile, (t + 1) * tile)
            n = (t + 1) * tile
            q, g = q_ref[mine, :], m_ref[mine, :]
            s = lax.dot_general(q, k_ref[:n, :], NT, preferred_element_type=f32) * SCALE
            seen = t * tile + lax.broadcasted_iota(jnp.int32, (tile, n), 0) >= (
                lax.broadcasted_iota(jnp.int32, (tile, n), 1)
            )
            p = jnp.where(seen, jnp.exp(s - lse_ref[mine, :]), 0.0)
            dp = lax.dot_general(g, v_ref[:n, :], NT, preferred_element_type=f32)
            shift = jnp.sum(p * dp, axis=-1, keepdims=True)
            ds = (p * (dp - shift)).astype(bf16)
            low = p.astype(bf16)
            dq = jnp.dot(ds, k_ref[:n, :], preferred_element_type=f32) * SCALE
            r_ref[mine, :128] = turned(
                dq[:, :128], t_ref[0, mine, :], -t_ref[1, mine, :], -t_ref[2, mine, :]
            ).astype(bf16)
            r_ref[mine, 128:HD] = dq[:, 128:].astype(bf16)
            dk = lax.dot_general(ds, q, TN, preferred_element_type=f32) * SCALE
            dv = lax.dot_general(low, g, TN, preferred_element_type=f32)
            if n == rows:
                dk_ref[...] = dk
                dv_ref[...] = dv
            else:
                dk_ref[:n, :] += dk
                dv_ref[:n, :] += dv
        r_ref[:, HD : HD + 128] = turned(
            dk_ref[:, :128], t_ref[0], -t_ref[1], -t_ref[2]
        ).astype(bf16)
        r_ref[:, HD + 128 : 2 * HD] = dk_ref[:, 128:].astype(bf16)
        r_ref[:, 2 * HD :] = dv_ref[...].astype(bf16)
        for b in range(blocks):
            at = pl.ds(pl.multiple_of(ids_ref[b] * BLOCK, BLOCK), BLOCK)
            out_ref[b * BLOCK : (b + 1) * BLOCK, :] = r_ref[at, :]

    smem = pl.BlockSpec(memory_space=pltpu.SMEM)
    vmem = pl.BlockSpec(memory_space=pltpu.VMEM)
    return pl.pallas_call(
        kernel,
        in_specs=[smem, smem, vmem, vmem, vmem, vmem],
        out_specs=vmem,
        out_shape=jax.ShapeDtypeStruct((rows, 3 * HD), bf16),
        scratch_shapes=[pltpu.VMEM((rows, HD), bf16)] * 4
        + [pltpu.VMEM((rows, 3 * HD), bf16)]
        + [pltpu.VMEM((rows, HD), f32)] * 2,
        compiler_params=BIG,
        cost_estimate=cost(6 * rows * rows * HD, 20 * rows * HD, rows * rows / 2),
        name="attention_backward",
    )(ids, order, qkv, grad, lse, table)


def exchange_heads(nz, nchip, ncore, attended, cot, w_dense, active):
    rows, width = cot.shape
    step = rows // nz
    length, hc = attended.shape
    part = length // nchip
    units = active.shape[1]
    tile = 256

    def kernel(att_ref, cot_hbm, w_hbm, act_hbm, mix_out, g_out, dw_out, cot_ref, w_ref, act_ref, gm_ref, dw_ref,
               ld, m_s, m_r, g_s, g_r, own_l, dw_l):
        chip = lax.axis_index("chip")
        core = lax.axis_index("core")
        loads = [
            pltpu.make_async_copy(w_hbm.at[pl.ds(core * hc, hc), :], w_ref, ld.at[0]),
            pltpu.make_async_copy(act_hbm, act_ref, ld.at[1]),
        ]

        def chip_at(d):
            return lax.rem(chip + d, nchip)

        def rows_of(to):
            return pl.ds(pl.multiple_of(to * step, step), step)

        blocks = [
            pltpu.make_async_copy(
                cot_hbm.at[rows_of(chip_at(d)), :], cot_ref.at[rows_of(chip_at(d)), :], ld.at[1 + d]
            )
            for d in range(1, nchip + 1)
        ]
        for copy in loads[:1] + blocks + loads[1:]:
            copy.start()

        greet([{"chip": chip_at(d)} for d in range(1, nchip)])
        sent = [
            remote(
                att_ref.at[pl.ds(chip_at(d) * part, part), :],
                mix_out.at[pl.ds(chip * step, step), :], m_s.at[d], m_r.at[d], {"chip": chip_at(d)},
            )
            for d in range(1, nchip)
        ]
        kept = [
            pltpu.make_async_copy(
                att_ref.at[pl.ds(chip * part, part), :], mix_out.at[pl.ds(chip * step, step), :],
                own_l.at[0],
            )
        ]
        for copy in sent + kept:
            copy.start()
        loads[0].wait()
        for d in range(1, nchip + 1):
            to = chip_at(d)
            at = rows_of(to)
            blocks[d - 1].wait()
            gm_ref[at, :] = lax.dot_general(
                cot_ref[at, :], w_ref[...], NT, preferred_element_type=f32
            ).astype(bf16)
            there = g_out.at[pl.ds(chip * part, part), :]
            if d < nchip:
                copy = remote(gm_ref.at[at, :], there, g_s.at[d], g_r.at[d], {"chip": to})
                sent.append(copy)
            else:
                copy = pltpu.make_async_copy(gm_ref.at[at, :], there, own_l.at[1])
                kept.append(copy)
            copy.start()
        loads[1].wait()
        for t in range(units // tile):
            at = pl.ds(t * tile, tile)
            dw_ref[at, :] = lax.dot_general(
                act_ref[:, at], cot_ref[...], TN, preferred_element_type=f32
            ).astype(bf16)
            copy = pltpu.make_async_copy(dw_ref.at[at, :], dw_out.at[at, :], dw_l.at[t])
            copy.start()
            kept.append(copy)
        for copy in kept + sent:
            copy.wait()

    dma = pltpu.SemaphoreType.DMA
    anywhere = pl.BlockSpec(memory_space=pl.ANY)
    return pl.pallas_call(
        kernel,
        in_specs=[anywhere] * 4,
        out_specs=[anywhere] * 3,
        out_shape=[
            jax.ShapeDtypeStruct((rows, hc), bf16),
            jax.ShapeDtypeStruct((length, hc), bf16),
            jax.ShapeDtypeStruct((units, width), bf16),
        ],
        scratch_shapes=[
            pltpu.VMEM((rows, width), bf16),
            pltpu.VMEM((hc, width), bf16),
            pltpu.VMEM((rows, units), bf16),
            pltpu.VMEM((rows, hc), bf16),
            pltpu.VMEM((units, width), bf16),
            dma((2 + nchip,)), dma((nchip,)), dma((nchip,)), dma((nchip,)), dma((nchip,)), dma((2,)),
            dma((units // tile,)),
        ],
        compiler_params=pltpu.CompilerParams(
            collective_id=3, has_side_effects=True, vmem_limit_bytes=62 * 2**20
        ),
        cost_estimate=cost(2 * rows * width * (hc + units), 4 * rows * width),
        name="exchange_heads",
    )(attended, cot, w_dense, active)


def gather_plane(nchip, chip, core, src, dst_of, send, recv, local):
    sibling = {"core": 1 - core}
    rows = src.shape[0]
    half = rows // 2
    here = dst_of(chip, core)
    begun = [pltpu.make_async_copy(src, here, local)]
    begun.append(remote(src, here, send.at[0], recv.at[0], sibling))
    relays = []
    arrivals = []

    def cut(ref, h):
        return ref.at[pl.ds(h * half, half), :]

    if nchip == 4:
        beside = chip + 1 - 2 * lax.rem(chip, 2)
        below = lax.rem(chip + 2, 4)
        across = 3 - chip
        order = ((beside, 0, 1), (below, 1, 2), (beside, 1, 1), (below, 0, 2))
        for i, (to, h, d) in enumerate(order):
            slot = 4 + 2 * d + h
            begun.append(
                remote(cut(src, h), cut(here, h), send.at[slot], recv.at[slot], {"chip": to})
            )

        def passing(owner, h, to):
            part = cut(dst_of(owner, core), h)
            return remote(part, part, send.at[10 + h], recv.at[10 + h], {"chip": to})

        relays = [(passing(beside, 0, below), beside, 0, 6), (passing(below, 1, beside), below, 1, 9)]
        arrivals = [(beside, 1, 7, 1), (below, 0, 8, 2), (across, 0, 10, 3), (across, 1, 11, 3)]
        others = [(beside, 1), (below, 2), (across, 3)]
    else:
        others = [(lax.rem(chip + d, nchip), d) for d in range(1, nchip)]
        for to, d in others:
            begun.append(
                remote(src, here, send.at[nchip + d], recv.at[nchip + chip], {"chip": to})
            )

    def side(owner, slot):
        part = dst_of(owner, core)
        return remote(part, part, send.at[slot], recv.at[slot], sibling)

    def slot_of(owner, d):
        return d if nchip == 4 else 2 * nchip + owner

    def first():
        for copy in begun:
            copy.start()

    def onward():
        if nchip == 4:
            for copy, owner, h, slot in relays:
                part = cut(dst_of(owner, core), h)
                remote(part, part, send.at[0], recv.at[slot], sibling).wait_recv()
                copy.start()

    def pass_on():
        if nchip == 4:
            for owner, h, slot, d in arrivals:
                part = cut(dst_of(owner, core), h)
                remote(part, part, send.at[0], recv.at[slot], sibling).wait_recv()
                if slot != 10:
                    side(owner, d).start()
        else:
            for owner, d in others:
                part = dst_of(owner, core)
                remote(part, part, send.at[0], recv.at[nchip + owner], sibling).wait_recv()
                side(owner, slot_of(owner, d)).start()

    def last():
        begun[0].wait()
        for copy in begun[1:]:
            copy.wait_send()
        for copy, owner, h, slot in relays:
            copy.wait_send()
        there = dst_of(chip, 1 - core)
        remote(there, there, send.at[0], recv.at[0], sibling).wait_recv()
        for owner, d in others:
            side(owner, slot_of(owner, d)).wait_send()
            there = dst_of(owner, 1 - core)
            remote(there, there, send.at[0], recv.at[slot_of(owner, d)], sibling).wait_recv()

    return first, onward, pass_on, last


def scatter_plane(nchip, chip, part, own, first, second, send, recv, local):
    halves = own.shape[0]
    copies = []
    shape = own.shape[2:]

    def add(dst, terms):
        def rows(lead):
            @pl.loop(0, shape[-2] // 16)
            def _(i):
                at = lead + (pl.ds(pl.multiple_of(i * 16, 16), 16), slice(None))
                acc = dst[at].astype(f32)
                for term in terms:
                    acc = acc + term[at].astype(f32)
                dst[at] = acc.astype(bf16)

        if len(shape) == 2:
            rows(())
        else:

            @pl.loop(0, shape[0])
            def _(b):
                rows((b,))

    if nchip == 4:
        beside = chip + 1 - 2 * lax.rem(chip, 2)
        below = lax.rem(chip + 2, 4)
        across = 3 - chip
        ways = [(beside, below), (below, beside)]
        kept = [
            [
                pltpu.make_async_copy(part(chip, h), own.at[h, 0], local.at[h, 0]),
                pltpu.make_async_copy(part(ways[h][1], h), own.at[h, 1], local.at[h, 1]),
            ]
            for h in range(2)
        ]
        leave = [
            [
                remote(
                    part(across, h), first.at[h, 1], send.at[h, 1], recv.at[h, 1],
                    {"chip": ways[h][0]},
                ),
                remote(
                    part(ways[h][0], h), first.at[h, 0], send.at[h, 0], recv.at[h, 0],
                    {"chip": ways[h][0]},
                ),
            ]
            for h in range(2)
        ]
        follow = [
            remote(
                own.at[h, 1], second.at[h], send.at[h, 2], recv.at[h, 2], {"chip": ways[h][1]}
            )
            for h in range(2)
        ]

        def begin():
            for i in range(2):
                for h in range(2):
                    leave[h][i].start()
            for h in range(2):
                kept[h][1].start()
                kept[h][0].start()

        def middle():
            for h in range(2):
                kept[h][1].wait()
                leave[h][0].wait_recv()
                add(own.at[h, 1], [first.at[h, 1]])
                follow[h].start()

        def finish():
            for h in range(2):
                kept[h][0].wait()
                leave[h][1].wait_recv()
                follow[h].wait_recv()
                add(own.at[h, 0], [first.at[h, 0], second.at[h]])

        def last():
            for h in range(2):
                for copy in leave[h] + [follow[h]]:
                    copy.wait_send()
    else:
        to = [lax.rem(chip + d, nchip) for d in range(nchip)]
        kept = pltpu.make_async_copy(part(chip, 0), own.at[0, 0], local.at[0, 0])
        leave = [
            remote(part(to[d], 0), first.at[0, d], send.at[0, d], recv.at[0, d], {"chip": to[d]})
            for d in range(1, nchip)
        ]

        def begin():
            for copy in leave:
                copy.start()
            kept.start()

        def middle():
            pass

        def finish():
            kept.wait()
            for copy in leave:
                copy.wait_recv()
            add(own.at[0, 0], [first.at[0, d] for d in range(1, nchip)])

        def last():
            for copy in leave:
                copy.wait_send()

    return begin, middle, finish, last


def tail(nz, nchip, ncore, dwo, dwd, dwi, vectors, normed1, grad_project, grad_hidden, tok, w_qkv, w_in, gain1, gain2):
    width = dwo.shape[1]
    ro, rd = dwo.shape[0], dwd.shape[0] // nchip
    halves = 2 if nchip == 4 else 1
    hz = nz // halves
    hd = rd // halves
    ci, cq = dwi.shape[1], grad_project.shape[1] // 3
    wrows = width // nz
    ri = wrows // nchip
    rows = tok.shape[0]
    step = rows // nz
    own = step // ncore
    vr = vectors.shape[0]
    chunk = 512
    dwi = dwi.reshape(nz, nchip, ri, ci)
    dwd = dwd.reshape(nchip, rd, width)

    def kernel(
        dwo_ref, dwd_ref, dwi_ref, vec_ref, n_hbm, gp_hbm, gh_hbm, tok_hbm, wq_hbm, wi_hbm, g1_ref, g2_ref,
        go_ref, gd_ref, gi_ref, gq_ref, e_ref, vsum_ref,
        x_ref, gp_ref, gh_ref, wq_ref, wi_ref, dwq_ref, eb,
        oi, fi, si, oq, fq, sq, od, fd, sd, ti, tq, se, ze, cs, v0, v1, v2, v3,
        ld, ri_s, ri_r, ri_l, rq_s, rq_r, rq_l, rd_s, rd_r, rd_l, x_s, x_r, ez_s, ez_r, t_s, t_r, t_l,
        go_s, go_r, gd_s, gd_r, gi_s, gi_r, gq_s, gq_r, own_l,
        v_s, v_r,
    ):
        z = lax.axis_index("seq")
        chip = lax.axis_index("chip")
        core = lax.axis_index("core")
        sibling = {"core": 1 - core}

        def z_at(d):
            return lax.rem(z + d, nz)

        def chip_at(d):
            return lax.rem(chip + d, nchip)

        loads = [
            pltpu.make_async_copy(a, b, ld.at[i])
            for i, (a, b) in enumerate(
                ((n_hbm, x_ref), (gp_hbm, gp_ref), (gh_hbm, gh_ref), (wi_hbm, wi_ref), (wq_hbm, wq_ref))
            )
        ]
        for copy in loads:
            copy.start()
        greet(
            [{"seq": z_at(d)} for d in range(1, nz)]
            + [{"chip": chip_at(d)} for d in range(1, nchip)]
            + [sibling]
        )

        def turn(kind, part, turned):
            copies = [
                remote(
                    part(z_at(d)), turned.at[z], t_s.at[kind, d], t_r.at[kind, z],
                    {"seq": z_at(d)},
                )
                for d in range(1, nz)
            ]
            copies.append(pltpu.make_async_copy(part(z), turned.at[z], t_l.at[kind]))
            for copy in copies:
                copy.start()
            return copies

        def turned_at(kind, part, turned, source):
            return remote(part, turned.at[source], t_s.at[kind, 0], t_r.at[kind, source], sibling)

        sum_i = scatter_plane(
            nchip, chip, lambda c, h: dwi_ref.at[pl.ds(h * hz, hz), c], oi, fi, si, ri_s, ri_r, ri_l
        )
        sum_q = scatter_plane(
            nchip, chip, lambda c, h: dwq_ref.at[pl.ds(h * hz, hz), pl.ds(c * ri, ri)], oq, fq, sq,
            rq_s, rq_r, rq_l,
        )
        sum_d = scatter_plane(
            nchip, chip, lambda c, h: dwd_ref.at[c, pl.ds(h * hd, hd)], od, fd, sd, rd_s, rd_r, rd_l
        )
        sum_i[0]()

        loads[0].wait()
        loads[1].wait()
        for b in range(nz):
            dwq_ref[b] = lax.dot_general(
                x_ref[:, b * wrows : (b + 1) * wrows], gp_ref[...], TN, preferred_element_type=f32
            ).astype(bf16)
        load_tok = pltpu.make_async_copy(tok_hbm, x_ref, ld.at[5])
        load_tok.start()
        sum_q[0]()
        sum_d[0]()
        sum_i[1]()

        for copy in loads[2:] + [load_tok]:
            copy.wait()
        cs[...] = jnp.zeros_like(cs)
        cs[4:5, : 3 * cq] = jnp.sum(gp_ref[...].astype(f32), axis=0, keepdims=True)

        def norm_back(b):
            at = pl.ds(b * step, step)
            x = x_ref[at, :].astype(f32)
            mean = jnp.mean(x, axis=-1, keepdims=True)
            x = x - mean
            inv = lax.rsqrt(jnp.mean(x * x, axis=-1, keepdims=True) + EPSILON)

            @pl.loop(0, width // chunk)
            def _(c):
                cols = pl.ds(pl.multiple_of(c * chunk, chunk), chunk)
                xhat = (x_ref[at, cols].astype(f32) - mean) * inv
                gn = lax.dot_general(
                    gp_ref[at, :], wq_ref[cols, :], NT, preferred_element_type=f32
                )
                cs[0:1, cols] += jnp.sum(gn * xhat, axis=0, keepdims=True)
                cs[1:2, cols] += jnp.sum(gn, axis=0, keepdims=True)
                e = gn * g1_ref[:, cols]
                gn = lax.dot_general(
                    gh_ref[at, :], wi_ref[cols, :], NT, preferred_element_type=f32
                )
                cs[2:3, cols] += jnp.sum(gn * xhat, axis=0, keepdims=True)
                cs[3:4, cols] += jnp.sum(gn, axis=0, keepdims=True)
                e = (e + gn * g2_ref[:, cols]).astype(bf16)
                for k in range(ncore):
                    eb[b, k, :, cols] = e[k * own : (k + 1) * own]

            copy = remote(eb.at[b, 1 - core], se.at[b], x_s.at[b], x_r.at[b], sibling)
            copy.start()
            return copy

        exchanged = [norm_back(b) for b in range(nz)]
        sum_i[2]()
        turn_i = turn(0, lambda to: oi.at[to // hz, 0, lax.rem(to, hz)], ti)
        sum_q[1]()
        sum_d[1]()

        v0[...] = vec_ref[...]
        lanes = width // 128
        for k in range(4):
            for j in range(lanes):
                v0[k * lanes + j : k * lanes + j + 1, :] = cs[k : k + 1, j * 128 : (j + 1) * 128]
        rank = z * ncore + core
        deep = (3 * cq) // 128 // 3
        for r in range(nz * ncore):

            @pl.when(rank == r)
            def _():
                for g in range(3):
                    for j in range(deep):
                        row = 4 * lanes + (g * nz * ncore + r) * deep + j
                        col = g * cq + j * 128
                        v0[row : row + 1, :] = cs[4:5, col : col + 128]

        v_chips = [
            remote(v0, v1.at[chip], v_s.at[d], v_r.at[chip], {"chip": chip_at(d)})
            for d in range(1, nchip)
        ]
        for copy in v_chips:
            copy.start()
        v1[chip] = v0[...]

        go_at = lambda c, k: go_ref.at[pl.ds(k * (ro * nchip) + c * ro, ro), :]
        gd_at = lambda c, k, h: gd_ref.at[pl.ds(k * (rd * nchip) + c * rd + h * hd, hd), :]
        gi_at = lambda c, k, s: gi_ref.at[
            pl.ds(c * ri, ri), pl.ds((s * ncore + k) * ci, ci)
        ]
        gq_at = lambda c, k, s: gq_ref.at[
            pl.ds(c * ri, ri), pl.ds((s * ncore + k) * 3 * cq, 3 * cq)
        ]
        group = functools.partial(gather_plane, nchip, chip, core)
        rows_o = group(dwo_ref, go_at, go_s, go_r, own_l.at[nz])
        rows_o[0]()

        for b in range(nz):
            exchanged[b].wait_recv()

            @pl.loop(0, own // 16)
            def _(i):
                at = pl.ds(pl.multiple_of(i * 16, 16), 16)
                eb[b, core, at, :] = (
                    eb[b, core, at, :].astype(f32) + se[b, at, :].astype(f32)
                ).astype(bf16)

        sum_q[2]()
        turn_q = turn(1, lambda to: oq.at[to // hz, 0, lax.rem(to, hz)], tq)
        sum_d[2]()
        rows_d = [
            group(od.at[h, 0], functools.partial(gd_at, h=h), gd_s.at[h], gd_r.at[h], own_l.at[nz + 1 + h])
            for h in range(halves)
        ]
        for first, onward, pass_on, last in rows_d:
            first()

        for d in range(1, nchip):
            other = chip_at(d)
            remote(v0, v1.at[other], v_s.at[d], v_r.at[other], sibling).wait_recv()
        total = v1[0]
        for d in range(1, nchip):
            total = total + v1[d]
        v2[core] = total
        v_side = remote(v2.at[core], v2.at[core], v_s.at[nchip], v_r.at[nchip], sibling)
        v_side.start()

        rows_o[1]()
        for first, onward, pass_on, last in rows_d:
            onward()

        groups = []
        for dz in range(1, nz):
            turned_at(0, oi.at[0, 0, 0], ti, z_at(dz)).wait_recv()
        turn_i[-1].wait()
        for source in range(nz):
            groups.append(
                group(
                    ti.at[source], functools.partial(gi_at, s=source), gi_s.at[source],
                    gi_r.at[source], own_l.at[source],
                )
            )
            groups[-1][0]()
        sent_e = [
            remote(
                eb.at[z_at(d), core], ze.at[d], ez_s.at[d], ez_r.at[d], {"seq": z_at(d)}
            )
            for d in range(1, nz)
        ]
        for copy in sent_e:
            copy.start()

        v_side.wait_recv()
        vz = v2[0]
        for c in range(1, ncore):
            vz = vz + v2[c]
        v3[z] = vz
        v_zs = [
            remote(v3.at[z], v3.at[z], v_s.at[nchip + d], v_r.at[nchip + 1 + z], {"seq": z_at(d)})
            for d in range(1, nz)
        ]
        for copy in v_zs:
            copy.start()
        for first, onward, pass_on, last in groups:
            onward()

        for dz in range(1, nz):
            turned_at(1, oq.at[0, 0, 0], tq, z_at(dz)).wait_recv()
        turn_q[-1].wait()
        later = []
        for source in range(nz):
            later.append(
                group(
                    tq.at[source], functools.partial(gq_at, s=source), gq_s.at[source],
                    gq_r.at[source], own_l.at[4 + nz + source],
                )
            )
        for first, onward, pass_on, last in later:
            first()
        rows_o[2]()
        for first, onward, pass_on, last in groups:
            pass_on()
        for first, onward, pass_on, last in later:
            onward()
        for first, onward, pass_on, last in rows_d:
            pass_on()

        for d in range(1, nz):
            other = z_at(d)
            remote(v3.at[0], v3.at[other], v_s.at[0], v_r.at[nchip + 1 + other], sibling).wait_recv()
        total = v3[0]
        for d in range(1, nz):
            total = total + v3[d]
        vsum_ref[...] = total

        for copy in sent_e:
            copy.wait_recv()

        @pl.loop(0, own // 16)
        def _(i):
            at = pl.ds(pl.multiple_of(i * 16, 16), 16)
            acc = eb[z, core, at, :].astype(f32)
            for d in range(1, nz):
                acc = acc + ze[d, at, :].astype(f32)
            e_ref[at, :] = acc

        for first, onward, pass_on, last in later:
            pass_on()

        for first, onward, pass_on, last in [rows_o] + rows_d + groups + later:
            last()
        for begin, middle, finish, last in (sum_i, sum_q, sum_d):
            last()
        for copy in exchanged + sent_e + v_chips + v_zs + [v_side]:
            copy.wait_send()
        for copy in turn_i[:-1] + turn_q[:-1]:
            copy.wait_send()

    dma = pltpu.SemaphoreType.DMA
    anywhere = pl.BlockSpec(memory_space=pl.ANY)
    vmem = pl.BlockSpec(memory_space=pltpu.VMEM)
    out_shape = [
        jax.ShapeDtypeStruct((ncore * nchip * ro, width), bf16),
        jax.ShapeDtypeStruct((ncore * nchip * rd, width), bf16),
        jax.ShapeDtypeStruct((wrows, nz * ncore * ci), bf16),
        jax.ShapeDtypeStruct((wrows, 3 * nz * ncore * cq), bf16),
        jax.ShapeDtypeStruct((own, width), f32),
        jax.ShapeDtypeStruct((vr, 128), f32),
    ]
    slots = max(3 * nchip, 12)
    pair = 2 if nchip == 4 else 1
    nfirst = 2 if nchip == 4 else nchip

    def three(*shape):
        return [
            pltpu.VMEM((halves, pair) + shape, bf16),
            pltpu.VMEM((halves, nfirst) + shape, bf16),
            pltpu.VMEM((halves,) + shape, bf16),
        ]

    return pl.pallas_call(
        kernel,
        in_specs=[anywhere] * 3 + [vmem] + [anywhere] * 6 + [vmem] * 2,
        out_specs=[anywhere] * 4 + [vmem] * 2,
        out_shape=out_shape,
        scratch_shapes=[
            pltpu.VMEM((rows, width), bf16),
            pltpu.VMEM(grad_project.shape, bf16),
            pltpu.VMEM(grad_hidden.shape, bf16),
            pltpu.VMEM(w_qkv.shape, bf16),
            pltpu.VMEM(w_in.shape, bf16),
            pltpu.VMEM((nz, wrows, 3 * cq), bf16),
            pltpu.VMEM((nz, ncore, own, width), bf16),
        ]
        + three(hz, ri, ci)
        + three(hz, ri, 3 * cq)
        + three(hd, width)
        + [
            pltpu.VMEM((nz, ri, ci), bf16),
            pltpu.VMEM((nz, ri, 3 * cq), bf16),
            pltpu.VMEM((nz, own, width), bf16),
            pltpu.VMEM((nz, own, width), bf16),
            pltpu.VMEM((8, width), f32),
            pltpu.VMEM((vr, 128), f32),
            pltpu.VMEM((nchip, vr, 128), f32),
            pltpu.VMEM((ncore, vr, 128), f32),
            pltpu.VMEM((nz, vr, 128), f32),
            dma((6,)),
            dma((halves, nchip)), dma((halves, nchip)), dma((halves, 2)),
            dma((halves, nchip)), dma((halves, nchip)), dma((halves, 2)),
            dma((halves, nchip)), dma((halves, nchip)), dma((halves, 2)),
            dma((nz,)), dma((nz,)),
            dma((nz,)), dma((nz,)),
            dma((2, nz)), dma((2, nz)), dma((2,)),
            dma((slots,)), dma((slots,)),
            dma((halves, slots)), dma((halves, slots)),
            dma((nz, slots)), dma((nz, slots)),
            dma((nz, slots)), dma((nz, slots)),
            dma((4 + 2 * nz,)),
            dma((nchip + nz,)), dma((nchip + nz + 1,)),
        ],
        compiler_params=pltpu.CompilerParams(
            collective_id=2, has_side_effects=True, vmem_limit_bytes=62 * 2**20
        ),
        cost_estimate=cost(4 * rows * width * (3 * cq + ci), 20 * rows * width),
        name="tail",
    )(dwo, dwd, dwi, vectors, normed1, grad_project, grad_hidden, tok, w_qkv, w_in, gain1, gain2)


def on_device(
    nz,
    nchip,
    ncore,
    tokens,
    block_ids,
    cotangent,
    norm1_gain,
    norm1_bias,
    norm2_gain,
    norm2_bias,
    w_qkv,
    b_qkv,
    w_dense,
    b_dense,
    w_in,
    b_in,
    w_out,
    b_out,
):
    own, width = tokens.shape
    z = lax.axis_index("seq")
    chip = lax.axis_index("chip")
    core = lax.axis_index("core")
    ranks = nz * ncore
    rank = z * ncore + core
    rows = ranks * own
    ffr = w_out.shape[0] // ncore
    hc = width // ranks
    split = max(1, HD // hc)
    wrows = width // nz
    blocks = block_ids.shape[1]
    length = blocks * BLOCK
    core_at = core.reshape(1)

    parts = [norm1_gain, norm1_bias, norm2_gain, norm2_bias, b_qkv, b_dense + 0, b_in, b_out,
             block_ids.reshape(-1)]
    sizes = [p.shape[0] for p in parts]
    total = -(-sum(sizes) // 2048) * 2048
    starts = [sum(sizes[:i]) for i in range(len(sizes))]
    small = sum(
        jnp.pad(p.astype(f32), (at, total - at - p.shape[0])) for p, at in zip(parts, starts)
    )
    small = small.astype(bf16).reshape(-1, 128)
    tok, w_in_c, w_qkv_c, small = front(nz, nchip, ncore, tokens, w_in, w_qkv, small)
    tok = tok.reshape(rows, width)
    small = small.reshape(nz, total)

    def vector(i):
        return small[:, starts[i] : starts[i] + sizes[i]].astype(f32).reshape(1, -1)

    gain1, bias1, gain2, bias2 = [vector(i) for i in range(4)]
    bias_c = lax.dynamic_index_in_dim(vector(4).reshape(3, ranks, hc), rank, 1, keepdims=False)
    bias_c = bias_c.reshape(1, 3 * hc)
    bias_in = lax.dynamic_slice_in_dim(vector(6), rank * ffr, ffr, 1)
    ids = vector(8).astype(jnp.int32).reshape(nz, blocks)
    tok, cot_own = lax.optimization_barrier((tok, cotangent))
    cot = lax.all_gather(cot_own, TP, axis=0, tiled=True)

    per_chip = blocks // nchip
    ids_rows = lax.dynamic_slice_in_dim(ids, chip * per_chip, per_chip, 1).reshape(-1)
    ids_seq = lax.dynamic_index_in_dim(ids, chip, 0, keepdims=False)
    slots = jnp.arange(blocks, dtype=jnp.int32)
    order = jnp.sum(jnp.where(ids_seq[None, :] == slots[:, None], slots[None, :], 0), axis=1)
    place = (lax.rem(rank, split) == 0).astype(jnp.int32).reshape(1)
    table = jnp.asarray(turn_table(length))

    def heads_of(x):
        g = x.shape[1] // hc
        if split > 1:
            x = lax.all_gather(x.reshape(rows, g, hc), "core", axis=2, tiled=True)
        x = x.reshape(nz, rows // nz, g * HD)
        return lax.all_to_all(x, "chip", 0, 0, tiled=True).reshape(length, g * HD)

    def heads_back(x):
        g = x.shape[1] // HD
        x = x.reshape(nchip, length // nchip, g * HD)
        x = lax.all_to_all(x, "chip", 0, 0, tiled=True).reshape(rows, g * HD)
        if split > 1:
            x = lax.dynamic_slice_in_dim(x.reshape(rows, g, HD), core * hc, hc, 2)
        return x.reshape(rows, g * hc)

    tile = 256
    normed1, qkv = projections(nz, ids_rows, place, tok, w_qkv_c, bias_c, gain1, bias1, table)
    qkv = heads_of(qkv)
    normed2, active, slope = feed_forward(nz, tok, w_in_c, bias_in, gain2, bias2)
    qkv, active, slope, normed2 = lax.optimization_barrier((qkv, active, slope, normed2))
    attended, lse = attention_forward(ids_seq, order, qkv, tile)
    attended, cot = lax.optimization_barrier((attended, cot))

    if split == 1:
        mixed, g, dw_out = exchange_heads(nz, nchip, ncore, attended, cot, w_dense, active)
    else:
        mixed = heads_back(attended)
        g = heads_of(grad_of_mixed(nz, core_at, cot, w_dense, hc))
        dw_out = lax.dot_general(active, cot, TN, preferred_element_type=f32).astype(bf16)
    mixed, g, dw_out, cot = lax.optimization_barrier((mixed, g, dw_out, cot))
    s_out = lax.psum_scatter(dw_out, "chip", scatter_dimension=0, tiled=True)
    part_out = layer_out(nz, core_at, mixed, w_dense, active, w_out)
    g, part_out = lax.optimization_barrier((g, part_out))
    dqkv = attention_backward(ids_seq, order, qkv, g, lse, table, tile)
    dqkv, cot, mixed, part_out = lax.optimization_barrier((dqkv, cot, mixed, part_out))
    grad_project = heads_back(dqkv)
    grad_hidden, sum_bin = grad_of_hidden(nz, core_at, cot, w_out, slope)
    dw_in = lax.dot_general(normed2, grad_hidden, TN, preferred_element_type=f32).astype(bf16)
    dw_dense = lax.dot_general(mixed, cot, TN, preferred_element_type=f32).astype(bf16)
    grad_project, dw_in, dw_dense, s_out, part_out = lax.optimization_barrier(
        (grad_project, dw_in, dw_dense, s_out, part_out)
    )
    summed_out = lax.psum_scatter(part_out, TP, scatter_dimension=0, tiled=True).astype(f32)

    here = jnp.arange(ranks, dtype=jnp.int32) == rank
    mine_bin = jnp.where(here[:, None], sum_bin.reshape(1, ffr), 0.0)
    vectors = [
        jnp.zeros(7 * width, f32),
        jnp.sum(cotangent.astype(f32), axis=0),
        mine_bin.reshape(-1),
    ]
    vectors = jnp.concatenate([v.reshape(-1, 128) for v in vectors])
    g_wout, g_wdense, g_win, g_wqkv, e, sums = tail(
        nz, nchip, ncore, s_out, dw_dense, dw_in, vectors, normed1, grad_project, grad_hidden, tok,
        w_qkv_c, w_in_c, gain1, gain2
    )
    sums = sums.reshape(-1)
    at = 0
    small_out = []
    for size in (width, width, width, width, 3 * width, width, ranks * ffr):
        small_out.append(lax.dynamic_slice_in_dim(sums, at + z * (size // nz), size // nz))
        at += size
    g_gain1, g_bias1, g_gain2, g_bias2, g_bqkv, g_bdense, g_bin = small_out

    output = (tokens.astype(f32) + summed_out + vector(5) + vector(7)).astype(bf16)
    xhat_own, inv_own = stats(tokens.astype(f32))
    terms = (
        e
        - jnp.mean(e, axis=-1, keepdims=True)
        - xhat_own * jnp.mean(e * xhat_own, axis=-1, keepdims=True)
    ) * inv_own
    grad_tokens = (cotangent.astype(f32) + terms).astype(bf16)
    g_wout, g_wdense, g_win, g_wqkv = widen([g_wout, g_wdense, g_win, g_wqkv], ranks)
    return (
        output,
        grad_tokens,
        g_gain1,
        g_bias1,
        g_gain2,
        g_bias2,
        g_wqkv,
        g_bqkv,
        g_wdense,
        g_bdense,
        g_win,
        g_bin,
        g_wout,
        g_bdense,
    )


def solution(mesh):
    nz, nctx = mesh.shape["seq"], mesh.shape["ctx"]
    ncore = 2
    nchip = nctx // ncore
    fine = Mesh(mesh.devices.reshape(nz, nchip, ncore), ("seq", "chip", "core"))
    own = P(("seq", "chip", "core"), None)
    vec = P("seq")
    mat = P("seq", None)
    return jax.shard_map(
        functools.partial(on_device, nz, nchip, ncore),
        mesh=fine,
        in_specs=(own, mat, own, vec, vec, vec, vec, mat, vec, mat, vec, mat, vec, mat, vec),
        out_specs=(own, own, vec, vec, vec, vec, mat, vec, mat, vec, mat, vec, mat, vec),
        check_vma=False,
    )
```
